32 devices in a mesh: dp: 8 (over z, y), rep: 4 (over x, core).
Axes of the slice: x: 2, y: 2, z: 4, core: 2. Of those that a mesh axis runs over, the one named last changes fastest.
Arguments:
- item_table: bfloat16 [4096, 512], P(('dp', 'rep')), may hold values from -6 to 6
- requests: int32 [32, 32, 2], P(('dp', 'rep')), may hold values from 0 to 127, as said below
- event_slot: int32 [16384], P(('dp', 'rep')), may hold values from 0 to 63, as said below
- lengths: int32 [32, 4], P(('dp', 'rep')), may hold values from 1 to 256, 512 in all within a row
- leaf_ids: int32 [16384, 8], P(('dp', 'rep')), may hold values from 0 to 31
- leaf_table: bfloat16 [256, 512], replicated, may hold values from -2.09375 to 2.09375
- w_in: bfloat16 [512, 2048], replicated, may hold values from -0.25 to 0.25
- w_out: bfloat16 [512, 512], replicated, may hold values from -0.25 to 0.25
- cotangent: bfloat16 [16384, 512], P(('dp', 'rep')), may hold values from -6 to 6
Outputs:
- output: bfloat16 [16384, 512], P(('dp', 'rep'))
- table_grad: float32 [4096, 512], P(('dp', 'rep'))
- leaf_grad: float32 [256, 512], replicated
- w_in_grad: float32 [512, 2048], replicated
- w_out_grad: float32 [512, 512], replicated
The draws below stay inside these ranges and needn't reach their ends.
Inputs may be any that keep to these rules, and one draw needn't show every extreme that they name: `requests`: for each device and owner the 2 requested rows are distinct. `event_slot`: every one of a device's 64 slots is named by at least one of its events.
All inputs are finite; a program needn't handle non-finite values.
Results may differ from the reference program's by a relative error of at most 0.014.
Values may be sent and summed in bfloat16 or wider, within the bound.
No kernel may reach another device: no remote copies, remote signals or barrier semaphores. Data moves between devices by JAX's collectives and lax.ppermute only.
A program may use at most 64 MiB of HBM per device.

```python
import math
import jax
import jax.numpy as jnp
import numpy as np
from jax import lax

D = 512
HEADS = 4
TREES = 8
LEAVES = 32
CAP = 2
TOK_DEV = 512
MAXLEN = 256
SEQS_DEV = 4
SLOTS = 64
ROWS_DEV = 128
ROWS = 4096
TOKENS = 16384
DEVICES = 32


def draw_requests(key, part):
    first_key, second_key = jax.random.split(key)
    starts = jax.random.randint(first_key, (DEVICES, DEVICES, 1), 0, ROWS_DEV)
    starts = starts.at[0, 0, 0].set(ROWS_DEV - 1).at[0, 1, 0].set(0)
    strides = 2 * jax.random.randint(second_key, (DEVICES, DEVICES, 1), 0, ROWS_DEV // 2) + 1
    offsets = jnp.arange(CAP, dtype=jnp.int32)[None, None, :]
    return ((starts + offsets * strides) % ROWS_DEV).astype(jnp.int32)


def draw_event_slot(key, part):
    device_keys = jax.random.split(key, DEVICES)

    def one_device(device_key):
        extra_key, order_key = jax.random.split(device_key)
        extra = jax.random.randint(extra_key, (TOK_DEV - SLOTS,), 0, SLOTS)
        listing = jnp.concatenate([jnp.arange(SLOTS, dtype=jnp.int32), extra.astype(jnp.int32)])
        return jax.random.permutation(order_key, listing)
    return jax.vmap(one_device)(device_keys).reshape(-1).astype(jnp.int32)


def with_ends(entries, rng, least, high):
    longest = entries.shape.index(max(entries.shape))
    spots = []
    for shift in (0, 1):
        where = [jax.random.randint(jax.random.fold_in(rng, axis), (), 0, length) for axis, length in enumerate(entries.shape)]
        where[longest] = (where[longest] + shift) % entries.shape[longest]
        spots.append(tuple(where))
    return entries.at[spots[0]].set(least).at[spots[1]].set(high)


def levels(rng, extent, cuts, smallest, high):
    level = 1.0
    for axis_at, shards_of in cuts:
        heights = jax.random.uniform(jax.random.fold_in(jax.random.fold_in(rng, 6), axis_at), (shards_of,), jnp.float32, smallest / len(cuts), high / len(cuts))
        level = level * jnp.repeat(jnp.exp(heights), extent[axis_at] // shards_of).reshape((-1,) + (1,) * (len(extent) - 1 - axis_at))
    return level


def split_up(count, total, reach, slope):
    weights = [(1 << 20) // math.isqrt(rank ** slope) + 1 for rank in range(2, count + 1)]
    spare, counts = total - reach - (count - 1), [1] * (count - 1)
    while spare > 0:
        candidates = [i for i in range(count - 1) if counts[i] < reach]
        whole, remaining = sum([weights[i] for i in candidates]), spare
        for i in candidates:
            more = min(reach - counts[i], max(1, remaining * weights[i] // whole), spare)
            counts[i] = counts[i] + more
            spare = spare - more
    return np.array([reach] + counts)


def uneven(stream_key, amount, total, most, lean):
    if amount == 2:
        one = jax.random.randint(stream_key, (), max(1, total - most), min(most, total - 1) + 1)
        return jnp.stack([one, total - one])
    sizes = jnp.asarray(split_up(amount, total, most, lean), jnp.int32)
    pairs = (amount - 1) // 2
    donor, taker = sizes[1:1 + 2 * pairs:2], sizes[2:2 + 2 * pairs:2]
    margin = jnp.minimum(donor - 1, most - taker)
    moved = jax.random.randint(jax.random.fold_in(stream_key, 1), (pairs,), 0, 1 << 20) % (margin + 1)
    sizes = sizes.at[1:1 + 2 * pairs:2].set(donor - moved).at[2:2 + 2 * pairs:2].set(taker + moved)
    return sizes[jax.random.permutation(jax.random.fold_in(stream_key, 2), amount)]


def gaussian(key, dims, scale, bound, cuts=(), kind=jnp.bfloat16):
    gain = levels(key, dims, cuts, -0.22, 0.18) if cuts else 1.0
    values = jax.random.normal(key, dims, jnp.float32) * scale * gain
    return jnp.minimum(jnp.maximum(values, -bound), bound).astype(kind)


def setup_inputs(seed: int = 0) -> dict:
    splits = jax.random.split(jax.random.key(seed), 10)
    return {
        "item_table": gaussian(splits[0], (ROWS, D), 1.0, 6.0, ((0, 32),)),
        "requests": draw_requests(jax.random.fold_in(splits[9], 71), 0),
        "event_slot": draw_event_slot(jax.random.fold_in(splits[9], 71), 0),
        "lengths": jax.vmap(lambda own: uneven(own, SEQS_DEV, TOK_DEV, MAXLEN, 2))(jax.random.split(splits[3], DEVICES)).reshape((DEVICES, SEQS_DEV)).astype(jnp.int32),
        "leaf_ids": with_ends(jax.random.randint(splits[4], (TOKENS, TREES), 0, LEAVES), jax.random.fold_in(splits[4], 1), 0, LEAVES - 1).astype(jnp.int32),
        "leaf_table": gaussian(splits[5], (TREES * LEAVES, D), 0.35, 2.09375),
        "w_in": gaussian(splits[6], (D, 4 * D), D ** -0.5, 0.25),
        "w_out": gaussian(splits[7], (D, D), D ** -0.5, 0.25),
        "cotangent": gaussian(splits[8], (TOKENS, D), 1.0, 6.0, ((0, 32),)),
    }


epsilon = 1e-06

def normalize(values):
    center = values - lax.optimization_barrier(jnp.mean(values, axis=-1, keepdims=True))
    spread = lax.optimization_barrier(jnp.mean(center * center, axis=-1, keepdims=True))
    return center * lax.rsqrt(spread + epsilon)

def visible(lengths, count):
    ends = jnp.cumsum(lengths)
    places = jnp.arange(count, dtype=jnp.int32)
    segment = lax.optimization_barrier(jnp.sum((places[:, None] >= ends[None, :]).astype(jnp.int32), axis=1))
    same = segment[:, None] == segment[None, :]
    return jnp.logical_and(same, places[None, :] <= places[:, None])

def front(rows, event_slot, lengths, leaf_ids, leaf_table, w_in):
    count = event_slot.shape[0]
    picker = (event_slot[:, None] == jnp.arange(rows.shape[0], dtype=jnp.int32)[None, :]).astype(jnp.bfloat16)
    leaves = leaf_table.shape[0] // leaf_ids.shape[1]
    onehot = (leaf_ids[:, :, None] == jnp.arange(leaves, dtype=jnp.int32)[None, None, :]).reshape(count, -1).astype(jnp.bfloat16)
    inputs = (jnp.dot(picker, rows, preferred_element_type=jnp.float32) + jnp.dot(onehot, leaf_table, preferred_element_type=jnp.float32)).astype(jnp.bfloat16)
    normed = normalize(inputs.astype(jnp.float32)).astype(jnp.bfloat16)
    hidden = jax.nn.silu(jnp.dot(normed, w_in, preferred_element_type=jnp.float32)).astype(jnp.bfloat16)
    width = w_in.shape[0]
    head_size = width // HEADS
    gates = hidden[:, 0:width]
    value_heads = hidden[:, width:2 * width].reshape(count, HEADS, head_size)
    query_heads = hidden[:, 2 * width:3 * width].reshape(count, HEADS, head_size)
    key_heads = hidden[:, 3 * width:4 * width].reshape(count, HEADS, head_size)
    scores = jnp.einsum('qhd,khd->hqk', query_heads.astype(jnp.float32), key_heads.astype(jnp.float32)) * head_size ** (-0.5)
    allowed = visible(lengths, count)
    weights = jnp.where(allowed[None], jax.nn.silu(scores), 0.0).astype(jnp.bfloat16)
    mixed = jnp.einsum('hqk,khd->qhd', weights.astype(jnp.float32), value_heads.astype(jnp.float32)).reshape(count, width)
    gated = (normalize(mixed) * gates.astype(jnp.float32)).astype(jnp.bfloat16)
    return (inputs, gated)

def back(inputs, gated, w_out):
    return (jnp.dot(gated, w_out, preferred_element_type=jnp.float32) + inputs.astype(jnp.float32)).astype(jnp.bfloat16)

def reference(item_table, requests, event_slot, lengths, leaf_ids, leaf_table, w_in, w_out, cotangent):
    owner_rows = item_table.reshape(DEVICES, ROWS_DEV, D)
    owners = jnp.arange(DEVICES, dtype=jnp.int32)[None, :, None]
    fetched = owner_rows[owners, requests].reshape(DEVICES, SLOTS, D)

    def one_device(carry, items):
        rows, slots, history, leaf_rows, tangent = items

        def local_front(arrived, table_leaf, weight_in):
            return front(arrived, slots, history, leaf_rows, table_leaf, weight_in)
        (inputs, gated), pull_front = jax.vjp(local_front, rows, leaf_table, w_in)
        output, pull_back = jax.vjp(back, inputs, gated, w_out)
        d_inputs, d_gated, d_out = pull_back(tangent)
        d_rows, d_leaf, d_in = pull_front((d_inputs, d_gated))
        carry = (carry[0] + d_leaf.astype(jnp.float32), carry[1] + d_in.astype(jnp.float32), carry[2] + d_out.astype(jnp.float32))
        return (carry, (output, d_rows))
    start = (jnp.zeros(leaf_table.shape, jnp.float32), jnp.zeros(w_in.shape, jnp.float32), jnp.zeros(w_out.shape, jnp.float32))
    items = (fetched, event_slot.reshape(DEVICES, TOK_DEV), lengths, leaf_ids.reshape(DEVICES, TOK_DEV, TREES), cotangent.reshape(DEVICES, TOK_DEV, D))
    sums, stacked = lax.scan(one_device, start, items)
    outputs, row_grads = stacked
    flat_index = (owners * ROWS_DEV + requests).reshape(-1).astype(jnp.int32)
    table_grad = jnp.zeros((ROWS, D), jnp.float32).at[flat_index].add(row_grads.reshape(-1, D).astype(jnp.float32))
    share = 1.0 / DEVICES
    return (outputs.reshape(TOKENS, D), table_grad, sums[0] * share, sums[1] * share, sums[2] * share)
```

```python
import jax
import jax.numpy as jnp
from jax import lax
from jax.sharding import PartitionSpec as P

HEADS = 4


epsilon = 1e-06


def normalize(values):
    center = values - jnp.mean(values, axis=-1, keepdims=True)
    spread = jnp.mean(center * center, axis=-1, keepdims=True)
    return center * lax.rsqrt(spread + epsilon)


def visible(lengths, count):
    ends = jnp.cumsum(lengths)
    places = jnp.arange(count, dtype=jnp.int32)
    segment = jnp.sum((places[:, None] >= ends[None, :]).astype(jnp.int32), axis=1)
    same = segment[:, None] == segment[None, :]
    return jnp.logical_and(same, places[None, :] <= places[:, None])


def front(rows, event_slot, lengths, leaf_ids, leaf_table, w_in):
    count = event_slot.shape[0]
    picker = (event_slot[:, None] == jnp.arange(rows.shape[0], dtype=jnp.int32)[None, :]).astype(
        jnp.bfloat16
    )
    leaves = leaf_table.shape[0] // leaf_ids.shape[1]
    onehot = (
        (leaf_ids[:, :, None] == jnp.arange(leaves, dtype=jnp.int32)[None, None, :])
        .reshape(count, -1)
        .astype(jnp.bfloat16)
    )
    inputs = (
        jnp.dot(picker, rows, preferred_element_type=jnp.float32)
        + jnp.dot(onehot, leaf_table, preferred_element_type=jnp.float32)
    ).astype(jnp.bfloat16)
    normed = normalize(inputs.astype(jnp.float32)).astype(jnp.bfloat16)
    hidden = jax.nn.silu(jnp.dot(normed, w_in, preferred_element_type=jnp.float32)).astype(
        jnp.bfloat16
    )
    width = w_in.shape[0]
    head_size = width // HEADS
    gates = hidden[:, 0:width]
    value_heads = hidden[:, width : 2 * width].reshape(count, HEADS, head_size)
    query_heads = hidden[:, 2 * width : 3 * width].reshape(count, HEADS, head_size)
    key_heads = hidden[:, 3 * width : 4 * width].reshape(count, HEADS, head_size)
    scores = jnp.einsum(
        "qhd,khd->hqk", query_heads, key_heads, preferred_element_type=jnp.float32
    ) * head_size ** (-0.5)
    allowed = visible(lengths, count)
    weights = jnp.where(allowed[None], jax.nn.silu(scores), 0.0).astype(jnp.bfloat16)
    mixed = jnp.einsum(
        "hqk,khd->qhd", weights, value_heads, preferred_element_type=jnp.float32
    ).reshape(count, width)
    gated = (normalize(mixed) * gates.astype(jnp.float32)).astype(jnp.bfloat16)
    return (inputs, gated)


def back(inputs, gated, w_out):
    return (
        jnp.dot(gated, w_out, preferred_element_type=jnp.float32) + inputs.astype(jnp.float32)
    ).astype(jnp.bfloat16)


def exchange(blocks):
    return lax.all_to_all(blocks, ("dp", "rep"), split_axis=0, concat_axis=0, tiled=True)


ROUTES = ((0,), (1, 2), (3, 4))


def chunk_order(groups):
    masks = [0]
    for group in groups:
        digits = [
            sum(((digit >> k) & 1) << bit for k, bit in enumerate(group))
            for digit in range(2 ** len(group))
        ]
        masks = [mask ^ digit for mask in masks for digit in digits]
    return masks


def swap(block, mask, count):
    return lax.ppermute(block, ("dp", "rep"), [(i, i ^ mask) for i in range(count)])


def reduce_scatter(parts, groups, count):
    parts = [parts]
    for group in groups:
        size = 2 ** len(group)
        split = [part.reshape((size, -1) + part.shape[1:]) for part in parts]
        received = []
        for digit in range(1, size):
            mask = sum(((digit >> k) & 1) << bit for k, bit in enumerate(group))
            block = sum(part[digit].astype(jnp.float32) for part in split).astype(jnp.bfloat16)
            received.append(swap(block, mask, count))
        parts = [part[0] for part in split] + received
    return sum(part.astype(jnp.float32) for part in parts)


def gather(block, groups, count):
    for group in groups[::-1]:
        pieces = [block]
        for digit in range(1, 2 ** len(group)):
            mask = sum(((digit >> k) & 1) << bit for k, bit in enumerate(group))
            pieces.append(swap(block, mask, count))
        block = jnp.concatenate(pieces, axis=0)
    return block


def mean_over_devices(d_leaf, d_in, d_out, place, count):
    groups = ROUTES
    chunks = 2 ** sum(len(group) for group in groups)
    width = d_in.shape[0]
    half = d_leaf.shape[1] // 2
    grads = jnp.concatenate(
        [d_in, d_out, jnp.concatenate([d_leaf[:, :half], d_leaf[:, half:]], axis=0)], axis=1
    )
    order = jnp.asarray(chunk_order(groups), jnp.int32) ^ (place % chunks)
    moved = grads.reshape(chunks, -1, grads.shape[1])[order]
    own = reduce_scatter(moved, groups, count)
    far = chunks
    while far < count:
        own = own + swap(own, far, count)
        far *= 2
    own = (own * (1.0 / count)).astype(jnp.bfloat16)
    full = gather(own, groups, count)
    back_order = jnp.argsort(order)
    full = full[back_order].reshape(grads.shape).astype(jnp.float32)
    leaf = full[:, -half:]
    return (
        jnp.concatenate([leaf[: d_leaf.shape[0]], leaf[d_leaf.shape[0] :]], axis=1),
        full[:, : d_in.shape[1]],
        full[:, d_in.shape[1] : d_in.shape[1] + width],
    )


def on_device(
    item_table, requests, event_slot, lengths, leaf_ids, leaf_table, w_in, w_out, cotangent
):
    data_count = lax.axis_size("dp")
    replica_count = lax.axis_size("rep")
    width = item_table.shape[1]
    count = data_count * replica_count
    place = lax.axis_index(("dp", "rep"))
    asked = exchange(requests[0])
    fetched = item_table[asked]
    arrived = exchange(fetched).reshape(-1, width)

    def local_front(rows, table_leaf, weight_in):
        return front(rows, event_slot, lengths[0], leaf_ids, table_leaf, weight_in)

    (inputs, gated), pull_front = jax.vjp(local_front, arrived, leaf_table, w_in)
    output, pull_back = jax.vjp(back, inputs, gated, w_out)
    d_inputs, d_gated, d_out = pull_back(cotangent)
    d_rows, d_leaf, d_in = pull_front((d_inputs, d_gated))
    returned = exchange(d_rows.reshape(count, -1, width))
    leaf_mean, in_mean, out_mean = mean_over_devices(d_leaf, d_in, d_out, place, count)
    table_grad = (
        jnp.zeros(item_table.shape, jnp.float32)
        .at[asked.reshape(-1)]
        .add(returned.reshape(-1, width).astype(jnp.float32))
    )
    return (output, table_grad, leaf_mean, in_mean, out_mean)


def solution(mesh):
    return jax.shard_map(
        on_device,
        mesh=mesh,
        in_specs=(
            P(("dp", "rep"), None),
            P(("dp", "rep"), None, None),
            P(("dp", "rep")),
            P(("dp", "rep"), None),
            P(("dp", "rep"), None),
            P(),
            P(),
            P(),
            P(("dp", "rep"), None),
        ),
        out_specs=(P(("dp", "rep"), None), P(("dp", "rep"), None), P(), P(), P()),
        check_vma=False,
    )
```

```python
import functools
import jax
import jax.numpy as jnp
from jax import lax
from jax.experimental import pallas as pl
from jax.experimental.pallas import tpu as pltpu
from jax.sharding import PartitionSpec as P

HEADS = 4
MAXLEN = 256
BLOCK = 128
ROWS = 16
epsilon = 1e-06
f32 = jnp.float32
bf16 = jnp.bfloat16

ROUTE_IN = ((0,), (1, 2), (3, 4))
ROUTE_OUT = ((0,), (3, 4), (1, 2))


def dot(a, b, contract):
    return lax.dot_general(a, b, ((contract[0], contract[1]), ((), ())), preferred_element_type=f32)


def mm(a, b):
    return dot(a, b, ((1,), (0,)))


def mm_nt(a, b):
    return dot(a, b, ((1,), (1,)))


def mm_tn(a, b):
    return dot(a, b, ((0,), (0,)))


def mask_of(group, digit):
    return sum(((digit >> k) & 1) << bit for k, bit in enumerate(group))


def chunk_order(groups):
    masks = [0]
    for group in groups:
        masks = [mask ^ mask_of(group, digit) for mask in masks for digit in range(2 ** len(group))]
    return masks


def spans(count):
    for start in range(0, count, BLOCK):
        low = max(0, start - (MAXLEN - 1)) // BLOCK * BLOCK
        yield start, low, start + BLOCK


def center(values):
    values = values - jnp.mean(values, axis=-1, keepdims=True)
    return values, lax.rsqrt(jnp.mean(values * values, axis=-1, keepdims=True) + epsilon)


def pull_normalize(change, normed, scale):
    return scale * (
        change
        - jnp.mean(change, axis=-1, keepdims=True)
        - normed * jnp.mean(change * normed, axis=-1, keepdims=True)
    )


def pickers(slots, slot_ref, leaf_ref, leaves):
    count = slot_ref.shape[1]
    picker = lax.broadcasted_iota(jnp.int32, (slots, count), 0) == slot_ref[...]
    trees = leaf_ref.shape[0]
    each = leaves // trees
    spots = lax.broadcasted_iota(jnp.int32, (each, count), 0)
    onehot = [(spots == leaf_ref[t : t + 1, :]).astype(f32).astype(bf16) for t in range(trees)]
    return picker.astype(f32).astype(bf16), jnp.concatenate(onehot, axis=0)


def permute_rows(me, order, source, target):
    for place, mask in enumerate(order):
        start = pl.multiple_of((me ^ mask) * ROWS, ROWS)
        target[place * ROWS : (place + 1) * ROWS, :] = source[pl.ds(start, ROWS), :]


def layer_kernel(
    me_ref, lengths_ref, slot_ref, leaf_ref, rows_ref, table_ref, in_ref, out_ref, tangent_ref,
    inputs_ref, gated_ref, d_pre_ref, keep_ref, send_ref,
    normed, normed_t, moved, hidden, slope, weights, weights_slope, mixed, d_mixed, d_gated,
    d_score, allowed,
):
    count, width = inputs_ref.shape
    head = width // HEADS
    picker, onehot = pickers(rows_ref.shape[0], slot_ref, leaf_ref, table_ref.shape[0])
    d_gated[...] = mm_nt(tangent_ref[...], out_ref[...]).astype(bf16)
    inputs_ref[...] = (mm_tn(picker, rows_ref[...]) + mm_tn(onehot, table_ref[...])).astype(bf16)
    for start in range(0, count, BLOCK):
        at = slice(start, start + BLOCK)
        values, scale = center(inputs_ref[at, :].astype(f32))
        normed[at, :] = (values * scale).astype(bf16)
    normed_t[...] = normed[...].T
    for block in range(4):
        for start in range(0, count, BLOCK):
            at = slice(start, start + BLOCK)
            to = slice(block * width, (block + 1) * width)
            half = mm(normed[at, :], in_ref[:, to]) * 0.5
            curve = jnp.tanh(half)
            upper = 1.0 + curve
            hidden[at, to] = (half * upper).astype(bf16)
            slope[at, to] = (0.5 * upper * (1.0 + half * (1.0 - curve))).astype(bf16)
    weights[...] = jnp.zeros_like(weights)
    d_score[...] = jnp.zeros_like(d_score)
    ends = []
    total = 0
    for place in range(lengths_ref.shape[1]):
        total = total + lengths_ref[0, place]
        ends.append(total)
    half_scale = 0.5 * head ** (-0.5)
    for start, low, high in spans(count):
        at = slice(start, start + BLOCK)
        row = start + lax.broadcasted_iota(jnp.int32, (BLOCK, high - low), 0)
        column = low + lax.broadcasted_iota(jnp.int32, (BLOCK, high - low), 1)
        first = jnp.zeros_like(row)
        for end in ends[:-1]:
            first = jnp.where(row >= end, end, first)
        allowed[at, low:high] = jnp.where(
            jnp.logical_and(column >= first, column <= row), 1.0, 0.0
        ).astype(f32)
    for h in range(HEADS):
        value_at = slice(width + h * head, width + (h + 1) * head)
        query_at = slice(2 * width + h * head, 2 * width + (h + 1) * head)
        key_at = slice(3 * width + h * head, 3 * width + (h + 1) * head)
        for start, low, high in spans(count):
            at = slice(start, start + BLOCK)
            half = mm_nt(hidden[at, query_at], hidden[low:high, key_at]) * half_scale
            curve = jnp.tanh(half)
            upper = (1.0 + curve) * allowed[at, low:high]
            weights[h, at, low:high] = (half * upper).astype(bf16)
            weights_slope[h, at, low:high] = (
                half_scale * upper * (1.0 + half * (1.0 - curve))
            ).astype(bf16)
        for start in range(0, count, 2 * BLOCK):
            at = slice(start, start + 2 * BLOCK)
            high = start + 2 * BLOCK
            mixed[at, h * head : (h + 1) * head] = mm(
                weights[h, at, :high], hidden[:high, value_at]
            )
    for start in range(0, count, BLOCK):
        at = slice(start, start + BLOCK)
        values, scale = center(mixed[at, :])
        values = values * scale
        gates = hidden[at, :width].astype(f32)
        change = d_gated[at, :].astype(f32)
        gated_ref[at, :] = (values * gates).astype(bf16)
        d_pre_ref[at, :width] = (change * values * slope[at, :width].astype(f32)).astype(bf16)
        d_mixed[at, :] = pull_normalize(change * gates, values, scale).astype(bf16)
    for h in range(HEADS):
        own = slice(h * head, (h + 1) * head)
        value_at = slice(width + h * head, width + (h + 1) * head)
        query_at = slice(2 * width + h * head, 2 * width + (h + 1) * head)
        key_at = slice(3 * width + h * head, 3 * width + (h + 1) * head)
        for start, low, high in spans(count):
            at = slice(start, start + BLOCK)
            d_score[h, at, low:high] = (
                mm_nt(d_mixed[at, own], hidden[low:high, value_at])
                * weights_slope[h, at, low:high].astype(f32)
            ).astype(bf16)
        for start in range(0, count, 2 * BLOCK):
            at = slice(start, start + 2 * BLOCK)
            high = start + 2 * BLOCK
            d_query = mm(d_score[h, at, :high], hidden[:high, key_at])
            d_pre_ref[at, query_at] = (d_query * slope[at, query_at].astype(f32)).astype(bf16)
            d_key = mm_tn(d_score[h, start:, at], hidden[start:, query_at])
            d_pre_ref[at, key_at] = (d_key * slope[at, key_at].astype(f32)).astype(bf16)
            d_value = mm_tn(weights[h, start:, at], d_mixed[start:, own])
            d_pre_ref[at, value_at] = (d_value * slope[at, value_at].astype(f32)).astype(bf16)
    permute_rows(me_ref[0], chunk_order(ROUTE_IN), normed_t, moved)
    half_rows = keep_ref.shape[0]
    for block in range(4):
        to = slice(block * width, (block + 1) * width)
        send_ref[:, to] = mm(moved[half_rows:, :], d_pre_ref[:, to]).astype(bf16)
        keep_ref[:, to] = mm(moved[:half_rows, :], d_pre_ref[:, to]).astype(bf16)


def run_layer(me, lengths, slot, leaf, rows, table, w_in, w_out, tangent):
    count, width = tangent.shape
    smem = pl.BlockSpec(memory_space=pltpu.SMEM)
    vmem = pl.BlockSpec(memory_space=pltpu.VMEM)
    shape = jax.ShapeDtypeStruct
    return pl.pallas_call(
        layer_kernel,
        name="layer",
        out_shape=(
            shape((count, width), bf16),
            shape((count, width), bf16),
            shape((count, 4 * width), bf16),
            shape((width // 2, 4 * width), bf16),
            shape((width // 2, 4 * width), bf16),
        ),
        in_specs=[smem, smem] + [vmem] * 7,
        out_specs=(vmem,) * 5,
        scratch_shapes=[
            pltpu.VMEM((count, width), bf16),
            pltpu.VMEM((width, count), bf16),
            pltpu.VMEM((width, count), bf16),
            pltpu.VMEM((count, 4 * width), bf16),
            pltpu.VMEM((count, 4 * width), bf16),
            pltpu.VMEM((HEADS, count, count), bf16),
            pltpu.VMEM((HEADS, count, count), bf16),
            pltpu.VMEM((count, width), f32),
            pltpu.VMEM((count, width), bf16),
            pltpu.VMEM((count, width), bf16),
            pltpu.VMEM((HEADS, count, count), bf16),
            pltpu.VMEM((count, count), f32),
        ],
        compiler_params=pltpu.CompilerParams(vmem_limit_bytes=40 * 2**20),
        cost_estimate=pl.CostEstimate(flops=4 * 10**9, bytes_accessed=10**7, transcendentals=10**6),
    )(me, lengths, slot, leaf, rows, table, w_in, w_out, tangent)


def tail_kernel(
    me_ref, slot_ref, leaf_ref, inputs_ref, gated_ref, d_pre_ref, in_ref, out_ref, tangent_ref,
    output_ref, d_rows_ref, keep_ref, send_ref,
    d_inputs, turned, moved, leaf_grad,
):
    count, width = inputs_ref.shape
    slots = d_rows_ref.shape[0]
    order = chunk_order(ROUTE_OUT)
    half_rows = keep_ref.shape[0]
    turned[...] = gated_ref[...].T
    permute_rows(me_ref[0], order, turned, moved)
    send_ref[:, :width] = mm(moved[half_rows:, :], tangent_ref[...]).astype(bf16)
    keep_ref[:, :width] = mm(moved[:half_rows, :], tangent_ref[...]).astype(bf16)
    for start in range(0, count, BLOCK):
        at = slice(start, start + BLOCK)
        values, scale = center(inputs_ref[at, :].astype(f32))
        change = mm_nt(d_pre_ref[at, :], in_ref[...])
        change = pull_normalize(change, values * scale, scale)
        d_inputs[at, :] = (change + tangent_ref[at, :].astype(f32)).astype(bf16)
    leaves = leaf_grad.shape[0] // 2
    picker, onehot = pickers(slots, slot_ref, leaf_ref, leaves)
    d_leaf = mm(onehot, d_inputs[...]).astype(bf16)
    leaf_grad[:leaves, :] = d_leaf[:, : width // 2]
    leaf_grad[leaves:, :] = d_leaf[:, width // 2 :]
    for place, mask in enumerate(order):
        start = pl.multiple_of((me_ref[0] ^ mask) * ROWS, ROWS)
        target = send_ref if place * ROWS >= half_rows else keep_ref
        at = place * ROWS % half_rows
        target[at : at + ROWS, width:] = leaf_grad[pl.ds(start, ROWS), :]
    d_rows_ref[...] = mm(picker, d_inputs[...]).astype(bf16)
    for start in range(0, count, BLOCK):
        at = slice(start, start + BLOCK)
        output_ref[at, :] = (
            mm(gated_ref[at, :], out_ref[...]) + inputs_ref[at, :].astype(f32)
        ).astype(bf16)


def run_tail(me, slot, leaf, inputs, gated, d_pre, w_in, w_out, tangent, slots):
    count, width = tangent.shape
    smem = pl.BlockSpec(memory_space=pltpu.SMEM)
    vmem = pl.BlockSpec(memory_space=pltpu.VMEM)
    shape = jax.ShapeDtypeStruct
    return pl.pallas_call(
        tail_kernel,
        name="tail",
        out_shape=(
            shape((count, width), bf16),
            shape((slots, width), bf16),
            shape((width // 2, width + width // 2), bf16),
            shape((width // 2, width + width // 2), bf16),
        ),
        in_specs=[smem] + [vmem] * 8,
        out_specs=(vmem,) * 4,
        scratch_shapes=[
            pltpu.VMEM((count, width), bf16),
            pltpu.VMEM((width, count), bf16),
            pltpu.VMEM((width, count), bf16),
            pltpu.VMEM((width, width // 2), bf16),
        ],
        compiler_params=pltpu.CompilerParams(vmem_limit_bytes=32 * 2**20),
        cost_estimate=pl.CostEstimate(flops=2 * 10**9, bytes_accessed=10**7, transcendentals=0),
    )(me, slot, leaf, inputs, gated, d_pre, w_in, w_out, tangent)


def finish_kernel(
    me_ref, asked_ref, returned_ref, in_own, in_other, out_own, out_other,
    table_ref, leaf_ref, in_ref, out_ref,
):
    width = in_ref.shape[0]
    leaves = leaf_ref.shape[0]
    me = me_ref[0]
    half_rows = in_own.shape[0]
    places = in_own.shape[0] // ROWS
    order = chunk_order(ROUTE_IN)
    for place, mask in enumerate(order):
        source = in_own if place < places else in_other
        start = pl.multiple_of((me ^ mask) * ROWS, ROWS)
        at = slice(place % places * ROWS, (place % places + 1) * ROWS)
        in_ref[pl.ds(start, ROWS), :] = source[at, :].astype(f32)
    order = chunk_order(ROUTE_OUT)
    for place, mask in enumerate(order):
        source = out_own if place < places else out_other
        chunk = me ^ mask
        start = pl.multiple_of(chunk * ROWS, ROWS)
        at = slice(place % places * ROWS, (place % places + 1) * ROWS)
        out_ref[pl.ds(start, ROWS), :] = source[at, :width].astype(f32)
        low = chunk < leaves // ROWS

        @pl.when(low)
        def _():
            leaf_ref[pl.ds(start, ROWS), : width // 2] = source[at, width:].astype(f32)

        @pl.when(jnp.logical_not(low))
        def _():
            spot = pl.multiple_of(start - leaves, ROWS)
            leaf_ref[pl.ds(spot, ROWS), width // 2 :] = source[at, width:].astype(f32)

    rows = lax.broadcasted_iota(jnp.int32, (table_ref.shape[0], asked_ref.shape[1]), 0)
    table_ref[...] = mm((rows == asked_ref[...]).astype(f32).astype(bf16), returned_ref[...])


def run_finish(me, asked, returned, in_own, in_other, out_own, out_other, owned, leaves):
    smem = pl.BlockSpec(memory_space=pltpu.SMEM)
    vmem = pl.BlockSpec(memory_space=pltpu.VMEM)
    shape = jax.ShapeDtypeStruct
    width = returned.shape[1]
    return pl.pallas_call(
        finish_kernel,
        name="finish",
        out_shape=(
            shape((owned, width), f32),
            shape((leaves, width), f32),
            shape((width, 4 * width), f32),
            shape((width, width), f32),
        ),
        in_specs=[smem] + [vmem] * 6,
        out_specs=(vmem,) * 4,
        compiler_params=pltpu.CompilerParams(vmem_limit_bytes=32 * 2**20),
    )(me, asked, returned, in_own, in_other, out_own, out_other)


def exchange(blocks):
    return lax.all_to_all(blocks, ("dp", "rep"), split_axis=0, concat_axis=0, tiled=True)


def swap(block, mask, count):
    return lax.ppermute(block, ("dp", "rep"), [(i, i ^ mask) for i in range(count)])


def add(parts):
    return sum(part.astype(f32) for part in parts)


def reduce_scatter(keep, send, groups, count):
    parts = [keep, swap(send, mask_of(groups[0], 1), count)]
    for group in groups[1:]:
        size = 2 ** len(group)
        rows = parts[0].shape[0] // size
        received = []
        for digit in range(1, size):
            at = slice(digit * rows, (digit + 1) * rows)
            block = add(part[at] for part in parts).astype(bf16)
            received.append(swap(block, mask_of(group, digit), count))
        parts = [part[:rows] for part in parts] + received
    own = add(parts)
    far = 2 ** sum(len(group) for group in groups)
    while far < count:
        own = own + swap(own, far, count)
        far *= 2
    return (own * (1.0 / count)).astype(bf16)


def gather(block, groups, count):
    for group in groups[:0:-1]:
        pieces = [block]
        for digit in range(1, 2 ** len(group)):
            pieces.append(swap(block, mask_of(group, digit), count))
        block = jnp.concatenate(pieces, axis=0)
    return block, swap(block, mask_of(groups[0], 1), count)


def on_device(
    item_table, requests, event_slot, lengths, leaf_ids, leaf_table, w_in, w_out, cotangent
):
    count = lax.axis_size("dp") * lax.axis_size("rep")
    owned, width = item_table.shape
    place = lax.axis_index(("dp", "rep"))
    me = (place % 2 ** sum(len(group) for group in ROUTE_IN)).astype(jnp.int32).reshape(1)
    slot = event_slot.reshape(1, -1)
    leaf = leaf_ids.T
    asked = exchange(requests[0])
    fetched = item_table[asked]
    arrived = exchange(fetched).reshape(-1, width)
    inputs, gated, d_pre, keep_in, send_in = run_layer(
        me, lengths, slot, leaf, arrived, leaf_table, w_in, w_out, cotangent
    )
    output, d_rows, keep_out, send_out = run_tail(
        me, slot, leaf, inputs, gated, d_pre, w_in, w_out, cotangent, arrived.shape[0]
    )
    returned = exchange(d_rows.reshape(count, -1, width)).reshape(-1, width)
    in_part = reduce_scatter(keep_in, send_in, ROUTE_IN, count)
    out_part = reduce_scatter(keep_out, send_out, ROUTE_OUT, count)
    in_own, in_other = gather(in_part, ROUTE_IN, count)
    out_own, out_other = gather(out_part, ROUTE_OUT, count)
    table_grad, leaf_mean, in_mean, out_mean = run_finish(
        me, asked.reshape(1, -1), returned, in_own, in_other, out_own, out_other, owned,
        leaf_table.shape[0],
    )
    return (output, table_grad, leaf_mean, in_mean, out_mean)


def solution(mesh):
    return jax.shard_map(
        on_device,
        mesh=mesh,
        in_specs=(
            P(("dp", "rep"), None),
            P(("dp", "rep"), None, None),
            P(("dp", "rep")),
            P(("dp", "rep"), None),
            P(("dp", "rep"), None),
            P(),
            P(),
            P(),
            P(("dp", "rep"), None),
        ),
        out_specs=(P(("dp", "rep"), None), P(("dp", "rep"), None), P(), P(), P()),
        check_vma=False,
    )
```

```python
import functools
import jax
import jax.numpy as jnp
from jax import lax
from jax.experimental import pallas as pl
from jax.experimental.pallas import tpu as pltpu
from jax.sharding import PartitionSpec as P

HEADS = 4
MAXLEN = 256
BLOCK = 128
ROWS = 16
epsilon = 1e-06
f32 = jnp.float32
bf16 = jnp.bfloat16

ROUTE_IN = ((0, 1, 3, 2, 4), (0, 2, 1, 3, 4))
ROUTE_OUT = ((0, 3, 2, 1, 4), (0, 3, 2, 1, 4))
CHUNKS = 2 ** len(ROUTE_IN[0])


def dot(a, b, contract):
    return lax.dot_general(a, b, ((contract[0], contract[1]), ((), ())), preferred_element_type=f32)


def mm(a, b):
    return dot(a, b, ((1,), (0,)))


def mm_nt(a, b):
    return dot(a, b, ((1,), (1,)))


def mm_tn(a, b):
    return dot(a, b, ((0,), (0,)))


def place_masks(bits):
    masks = [0]
    for bit in bits:
        masks = [mask ^ (digit << bit) for mask in masks for digit in (0, 1)]
    return masks


def chunk_at(me, route):
    chunks = []
    for owner in (me, me ^ 1):
        odd = owner & 1 == 1
        for even, other in zip(place_masks(route[0][1:]), place_masks(route[1][1:])):
            chunks.append(owner ^ (even if even == other else jnp.where(odd, other, even)))
    return chunks


def spans(count):
    for start in range(0, count, BLOCK):
        low = max(0, start - (MAXLEN - 1)) // BLOCK * BLOCK
        yield start, low, start + BLOCK


def center(values):
    values = values - jnp.mean(values, axis=-1, keepdims=True)
    return values, lax.rsqrt(jnp.mean(values * values, axis=-1, keepdims=True) + epsilon)


def pull_normalize(change, normed, scale):
    return scale * (
        change
        - jnp.mean(change, axis=-1, keepdims=True)
        - normed * jnp.mean(change * normed, axis=-1, keepdims=True)
    )


def pickers(slots, slot_ref, leaf_ref, leaves):
    count = slot_ref.shape[1]
    picker = lax.broadcasted_iota(jnp.int32, (slots, count), 0) == slot_ref[...]
    trees = leaf_ref.shape[0]
    each = leaves // trees
    spots = lax.broadcasted_iota(jnp.int32, (each, count), 0)
    onehot = [(spots == leaf_ref[t : t + 1, :]).astype(f32).astype(bf16) for t in range(trees)]
    return picker.astype(f32).astype(bf16), jnp.concatenate(onehot, axis=0)


def permute_rows(chunks, source, target):
    for place, chunk in enumerate(chunks):
        start = pl.multiple_of(chunk * ROWS, ROWS)
        target[place * ROWS : (place + 1) * ROWS, :] = source[pl.ds(start, ROWS), :]


def prepare_kernel(
    lengths_ref, slot_ref, leaf_ref, table_hbm, in_hbm, out_hbm, tangent_hbm,
    in_ref, out_ref, tangent_ref, d_gated_ref, leaf_sum_ref, picker_ref, onehot_ref, allowed,
    table, sems,
):
    count, width = tangent_ref.shape
    copies = [
        pltpu.make_async_copy(source, target, sems.at[k])
        for k, (source, target) in enumerate(
            ((table_hbm, table), (out_hbm, out_ref), (tangent_hbm, tangent_ref), (in_hbm, in_ref))
        )
    ]
    for copy in copies:
        copy.start()
    picker, onehot = pickers(picker_ref.shape[0], slot_ref, leaf_ref, onehot_ref.shape[0])
    picker_ref[...] = picker
    onehot_ref[...] = onehot
    ends = []
    total = 0
    for place in range(lengths_ref.shape[1]):
        total = total + lengths_ref[0, place]
        ends.append(total)
    for start, low, high in spans(count):
        at = slice(start, start + BLOCK)
        row = start + lax.broadcasted_iota(jnp.int32, (BLOCK, high - low), 0)
        column = low + lax.broadcasted_iota(jnp.int32, (BLOCK, high - low), 1)
        first = jnp.zeros_like(row)
        for end in ends[:-1]:
            first = jnp.where(row >= end, end, first)
        allowed[at, low:high] = jnp.where(
            jnp.logical_and(column >= first, column <= row), 1.0, 0.0
        ).astype(f32)
    copies[0].wait()
    leaf_sum_ref[...] = mm_tn(onehot_ref[...], table[...])
    copies[1].wait()
    copies[2].wait()
    d_gated_ref[...] = mm_nt(tangent_ref[...], out_ref[...]).astype(bf16)
    copies[3].wait()


def run_prepare(lengths, slot, leaf, table, w_in, w_out, tangent, slots):
    count, width = tangent.shape
    smem = pl.BlockSpec(memory_space=pltpu.SMEM)
    vmem = pl.BlockSpec(memory_space=pltpu.VMEM)
    hbm = pl.BlockSpec(memory_space=pltpu.HBM)
    shape = jax.ShapeDtypeStruct
    return pl.pallas_call(
        prepare_kernel,
        name="prepare",
        out_shape=(
            shape(w_in.shape, bf16),
            shape(w_out.shape, bf16),
            shape(tangent.shape, bf16),
            shape(tangent.shape, bf16),
            shape(tangent.shape, f32),
            shape((slots, count), bf16),
            shape((table.shape[0], count), bf16),
            shape((count, count), f32),
        ),
        in_specs=[smem, vmem, vmem] + [hbm] * 4,
        out_specs=(vmem,) * 8,
        scratch_shapes=[pltpu.VMEM(table.shape, bf16), pltpu.SemaphoreType.DMA((4,))],
        compiler_params=pltpu.CompilerParams(vmem_limit_bytes=24 * 2**20),
        cost_estimate=pl.CostEstimate(flops=10**9, bytes_accessed=10**7, transcendentals=0),
    )(lengths, slot, leaf, table, w_in, w_out, tangent)


def lookup_kernel(me_ref, asked_ref, table_ref, rows_ref, chosen_ref):
    count, many = asked_ref.shape
    each = many // count
    owned = table_ref.shape[0]
    me = me_ref[0]
    lane = lax.broadcasted_iota(jnp.int32, (count, many), 1)
    spot = lax.broadcasted_iota(jnp.int32, (count, owned), 1)
    parts = []
    for k in range(each):
        wanted = jnp.sum(
            jnp.where(lane == me * each + k, asked_ref[...], 0), axis=1, keepdims=True
        )
        parts.append((spot == wanted).astype(f32).astype(bf16))
    chosen = jnp.concatenate(parts, axis=0)
    to = lax.broadcasted_iota(jnp.int32, (many, many), 0)
    source = (to % each) * count + ((to // each) ^ me)
    order = (source == lax.broadcasted_iota(jnp.int32, (many, many), 1)).astype(f32).astype(bf16)
    chosen_ref[...] = mm(order, chosen).astype(bf16)
    rows_ref[...] = mm(chosen_ref[...], table_ref[...]).astype(bf16)


def run_lookup(me, asked, table):
    smem = pl.BlockSpec(memory_space=pltpu.SMEM)
    vmem = pl.BlockSpec(memory_space=pltpu.VMEM)
    shape = jax.ShapeDtypeStruct
    return pl.pallas_call(
        lookup_kernel,
        name="lookup",
        out_shape=(
            shape((asked.shape[1], table.shape[1]), bf16),
            shape((asked.shape[1], table.shape[0]), bf16),
        ),
        in_specs=[smem, vmem, vmem],
        out_specs=(vmem,) * 2,
        compiler_params=pltpu.CompilerParams(vmem_limit_bytes=16 * 2**20),
    )(me, asked, table)


def layer_kernel(
    me_ref, rows_ref, picker_ref, leaf_sum_ref, in_ref, d_gated, allowed,
    inputs_ref, gated_ref, d_pre_ref, keep_ref, send_ref,
    normed, normed_t, moved, hidden, slope, weights, weights_slope, mixed, d_mixed, d_score,
):
    count, width = inputs_ref.shape
    head = width // HEADS
    inputs_ref[...] = (mm_tn(picker_ref[...], rows_ref[...]) + leaf_sum_ref[...]).astype(bf16)
    for start in range(0, count, BLOCK):
        at = slice(start, start + BLOCK)
        values, scale = center(inputs_ref[at, :].astype(f32))
        normed[at, :] = (values * scale).astype(bf16)
    normed_t[...] = normed[...].T
    for start in range(0, 4 * width, 2 * BLOCK):
        to = slice(start, start + 2 * BLOCK)
        half = mm(normed[...], in_ref[:, to]) * 0.5
        curve = jnp.tanh(half)
        upper = 1.0 + curve
        hidden[:, to] = (half * upper).astype(bf16)
        slope[:, to] = (0.5 * upper * (1.0 + half * (1.0 - curve))).astype(bf16)
    weights[...] = jnp.zeros_like(weights)
    d_score[...] = jnp.zeros_like(d_score)
    half_scale = 0.5 * head ** (-0.5)
    for h in range(HEADS):
        value_at = slice(width + h * head, width + (h + 1) * head)
        query_at = slice(2 * width + h * head, 2 * width + (h + 1) * head)
        key_at = slice(3 * width + h * head, 3 * width + (h + 1) * head)
        for start, low, high in spans(count):
            at = slice(start, start + BLOCK)
            half = mm_nt(hidden[at, query_at], hidden[low:high, key_at]) * half_scale
            curve = jnp.tanh(half)
            upper = (1.0 + curve) * allowed[at, low:high]
            weights[h, at, low:high] = (half * upper).astype(bf16)
            weights_slope[h, at, low:high] = (
                half_scale * upper * (1.0 + half * (1.0 - curve))
            ).astype(bf16)
        for start in range(0, count, 2 * BLOCK):
            at = slice(start, start + 2 * BLOCK)
            high = start + 2 * BLOCK
            mixed[at, h * head : (h + 1) * head] = mm(
                weights[h, at, :high], hidden[:high, value_at]
            )
    for start in range(0, count, BLOCK):
        at = slice(start, start + BLOCK)
        values, scale = center(mixed[at, :])
        values = values * scale
        gates = hidden[at, :width].astype(f32)
        change = d_gated[at, :].astype(f32)
        gated_ref[at, :] = (values * gates).astype(bf16)
        d_pre_ref[at, :width] = (change * values * slope[at, :width].astype(f32)).astype(bf16)
        d_mixed[at, :] = pull_normalize(change * gates, values, scale).astype(bf16)
    for h in range(HEADS):
        own = slice(h * head, (h + 1) * head)
        value_at = slice(width + h * head, width + (h + 1) * head)
        query_at = slice(2 * width + h * head, 2 * width + (h + 1) * head)
        key_at = slice(3 * width + h * head, 3 * width + (h + 1) * head)
        for start, low, high in spans(count):
            at = slice(start, start + BLOCK)
            d_score[h, at, low:high] = (
                mm_nt(d_mixed[at, own], hidden[low:high, value_at])
                * weights_slope[h, at, low:high].astype(f32)
            ).astype(bf16)
        for start in range(0, count, 2 * BLOCK):
            at = slice(start, start + 2 * BLOCK)
            high = start + 2 * BLOCK
            d_query = mm(d_score[h, at, :high], hidden[:high, key_at])
            d_pre_ref[at, query_at] = (d_query * slope[at, query_at].astype(f32)).astype(bf16)
            d_key = mm_tn(d_score[h, start:, at], hidden[start:, query_at])
            d_pre_ref[at, key_at] = (d_key * slope[at, key_at].astype(f32)).astype(bf16)
            d_value = mm_tn(weights[h, start:, at], d_mixed[start:, own])
            d_pre_ref[at, value_at] = (d_value * slope[at, value_at].astype(f32)).astype(bf16)
    permute_rows(chunk_at(me_ref[0], ROUTE_IN), normed_t, moved)
    half_rows = keep_ref.shape[0]
    for start in range(0, 4 * width, 2 * BLOCK):
        to = slice(start, start + 2 * BLOCK)
        grad = mm(moved[...], d_pre_ref[:, to]).astype(bf16)
        keep_ref[:, to] = grad[:half_rows, :]
        send_ref[:, to] = grad[half_rows:, :]


def run_layer(me, rows, picker, leaf_sum, w_in, d_gated, allowed):
    count, width = leaf_sum.shape
    smem = pl.BlockSpec(memory_space=pltpu.SMEM)
    vmem = pl.BlockSpec(memory_space=pltpu.VMEM)
    shape = jax.ShapeDtypeStruct
    return pl.pallas_call(
        layer_kernel,
        name="layer",
        out_shape=(
            shape((count, width), bf16),
            shape((count, width), bf16),
            shape((count, 4 * width), bf16),
            shape((width // 2, 4 * width), bf16),
            shape((width // 2, 4 * width), bf16),
        ),
        in_specs=[smem] + [vmem] * 6,
        out_specs=(vmem,) * 5,
        scratch_shapes=[
            pltpu.VMEM((count, width), bf16),
            pltpu.VMEM((width, count), bf16),
            pltpu.VMEM((width, count), bf16),
            pltpu.VMEM((count, 4 * width), bf16),
            pltpu.VMEM((count, 4 * width), bf16),
            pltpu.VMEM((HEADS, count, count), bf16),
            pltpu.VMEM((HEADS, count, count), bf16),
            pltpu.VMEM((count, width), f32),
            pltpu.VMEM((count, width), bf16),
            pltpu.VMEM((HEADS, count, count), bf16),
        ],
        compiler_params=pltpu.CompilerParams(vmem_limit_bytes=32 * 2**20),
        cost_estimate=pl.CostEstimate(flops=4 * 10**9, bytes_accessed=10**7, transcendentals=10**6),
    )(me, rows, picker, leaf_sum, w_in, d_gated, allowed)


def tail_kernel(
    me_ref, picker_ref, onehot_ref, inputs_ref, gated_ref, d_pre_ref, in_ref, out_ref, tangent_ref,
    output_ref, d_rows_ref, keep_ref, send_ref,
    d_inputs, turned, moved, leaf_grad,
):
    count, width = inputs_ref.shape
    chunks = chunk_at(me_ref[0], ROUTE_OUT)
    half_rows = keep_ref.shape[0]
    turned[...] = gated_ref[...].T
    permute_rows(chunks, turned, moved)
    grad = mm(moved[...], tangent_ref[...]).astype(bf16)
    keep_ref[:, :width] = grad[:half_rows, :]
    send_ref[:, :width] = grad[half_rows:, :]
    normed_change = mm_nt(d_pre_ref[...], in_ref[...])
    for start in range(0, count, BLOCK):
        at = slice(start, start + BLOCK)
        values, scale = center(inputs_ref[at, :].astype(f32))
        change = pull_normalize(normed_change[at, :], values * scale, scale)
        d_inputs[at, :] = (change + tangent_ref[at, :].astype(f32)).astype(bf16)
    leaves = leaf_grad.shape[0] // 2
    d_leaf = mm(onehot_ref[...], d_inputs[...]).astype(bf16)
    leaf_grad[:leaves, :] = d_leaf[:, : width // 2]
    leaf_grad[leaves:, :] = d_leaf[:, width // 2 :]
    for place, chunk in enumerate(chunks):
        start = pl.multiple_of(chunk * ROWS, ROWS)
        target = send_ref if place * ROWS >= half_rows else keep_ref
        at = place * ROWS % half_rows
        target[at : at + ROWS, width:] = leaf_grad[pl.ds(start, ROWS), :]
    d_rows_ref[...] = mm(picker_ref[...], d_inputs[...]).astype(bf16)
    output_ref[...] = (
        mm(gated_ref[...], out_ref[...]) + inputs_ref[...].astype(f32)
    ).astype(bf16)


def run_tail(me, picker, onehot, inputs, gated, d_pre, w_in, w_out, tangent):
    count, width = tangent.shape
    smem = pl.BlockSpec(memory_space=pltpu.SMEM)
    vmem = pl.BlockSpec(memory_space=pltpu.VMEM)
    shape = jax.ShapeDtypeStruct
    return pl.pallas_call(
        tail_kernel,
        name="tail",
        out_shape=(
            shape((count, width), bf16),
            shape((picker.shape[0], width), bf16),
            shape((width // 2, width + width // 2), bf16),
            shape((width // 2, width + width // 2), bf16),
        ),
        in_specs=[smem] + [vmem] * 8,
        out_specs=(vmem,) * 4,
        scratch_shapes=[
            pltpu.VMEM((count, width), bf16),
            pltpu.VMEM((width, count), bf16),
            pltpu.VMEM((width, count), bf16),
            pltpu.VMEM((width, width // 2), bf16),
        ],
        compiler_params=pltpu.CompilerParams(vmem_limit_bytes=24 * 2**20),
        cost_estimate=pl.CostEstimate(flops=2 * 10**9, bytes_accessed=10**7, transcendentals=0),
    )(me, picker, onehot, inputs, gated, d_pre, w_in, w_out, tangent)


def finish_kernel(
    me_ref, chosen_ref, returned_ref, in_own, in_other, out_own, out_other,
    table_ref, leaf_ref, in_ref, out_ref,
):
    width = in_ref.shape[0]
    leaves = leaf_ref.shape[0]
    me = me_ref[0]
    places = in_own.shape[0] // ROWS
    for place, chunk in enumerate(chunk_at(me, ROUTE_IN)):
        source = in_own if place < places else in_other
        at = slice(place % places * ROWS, (place % places + 1) * ROWS)
        start = pl.multiple_of(chunk * ROWS, ROWS)
        in_ref[pl.ds(start, ROWS), :] = source[at, :].astype(f32)
    for place, chunk in enumerate(chunk_at(me, ROUTE_OUT)):
        source = out_own if place < places else out_other
        at = slice(place % places * ROWS, (place % places + 1) * ROWS)
        start = pl.multiple_of(chunk * ROWS, ROWS)
        out_ref[pl.ds(start, ROWS), :] = source[at, :width].astype(f32)
        low = chunk < leaves // ROWS

        @pl.when(low)
        def _():
            leaf_ref[pl.ds(start, ROWS), : width // 2] = source[at, width:].astype(f32)

        @pl.when(jnp.logical_not(low))
        def _():
            spot = pl.multiple_of(start - leaves, ROWS)
            leaf_ref[pl.ds(spot, ROWS), width // 2 :] = source[at, width:].astype(f32)

    table_ref[...] = mm_tn(chosen_ref[...], returned_ref[...])


def run_finish(me, chosen, returned, in_own, in_other, out_own, out_other, leaves):
    smem = pl.BlockSpec(memory_space=pltpu.SMEM)
    vmem = pl.BlockSpec(memory_space=pltpu.VMEM)
    shape = jax.ShapeDtypeStruct
    width = returned.shape[1]
    return pl.pallas_call(
        finish_kernel,
        name="finish",
        out_shape=(
            shape((chosen.shape[1], width), f32),
            shape((leaves, width), f32),
            shape((width, 4 * width), f32),
            shape((width, width), f32),
        ),
        in_specs=[smem] + [vmem] * 6,
        out_specs=(vmem,) * 4,
        compiler_params=pltpu.CompilerParams(vmem_limit_bytes=32 * 2**20),
    )(me, chosen, returned, in_own, in_other, out_own, out_other)


def exchange(blocks):
    return lax.all_to_all(blocks, ("dp", "rep"), split_axis=0, concat_axis=0, tiled=True)


def swap(block, masks, count):
    return lax.ppermute(block, ("dp", "rep"), [(i, i ^ masks[i % 2]) for i in range(count)])


def step(route, k):
    return (1 << route[0][k], 1 << route[1][k])


def add(parts):
    return sum(part.astype(f32) for part in parts)


def halve(parts, route, k, count):
    rows = parts[0].shape[0] // 2
    block = add(part[rows:] for part in parts).astype(bf16)
    return [part[:rows] for part in parts] + [swap(block, step(route, k), count)]


def double(block, route, k, count):
    return jnp.concatenate([block, swap(block, step(route, k), count)], axis=0)


def reduce_and_gather(keep_in, send_in, keep_out, send_out, count):
    last = len(ROUTE_IN[0]) - 1
    split = keep_in.shape[1]
    in_parts = [keep_in, swap(send_in, step(ROUTE_IN, 0), count)]
    out_parts = [keep_out, swap(send_out, step(ROUTE_OUT, 0), count)]
    for k in range(1, last):
        in_parts = halve(in_parts, ROUTE_IN, k, count)
        out_parts = halve(out_parts, ROUTE_OUT, k, count)
    both = jnp.concatenate([add(in_parts), add(out_parts)], axis=1)
    rows = both.shape[0] // 2
    own = both[:rows] + swap(both[rows:].astype(bf16), step(ROUTE_IN, last), count).astype(f32)
    far = CHUNKS
    while far < count:
        own = own + swap(own, (far, far), count)
        far *= 2
    own = (own * (1.0 / count)).astype(bf16)
    both = double(own, ROUTE_IN, last, count)
    in_block, out_block = both[:, :split], both[:, split:]
    for k in range(last - 1, 0, -1):
        in_block = double(in_block, ROUTE_IN, k, count)
        out_block = double(out_block, ROUTE_OUT, k, count)
    return (
        in_block,
        swap(in_block, step(ROUTE_IN, 0), count),
        out_block,
        swap(out_block, step(ROUTE_OUT, 0), count),
    )


def gather_requests(requests, count):
    block = requests.reshape(1, -1)
    far = 1
    while far < count:
        block = jnp.concatenate([block, swap(block, (far, far), count)], axis=0)
        far *= 2
    return block


def on_device(
    item_table, requests, event_slot, lengths, leaf_ids, leaf_table, w_in, w_out, cotangent
):
    count = lax.axis_size("dp") * lax.axis_size("rep")
    place = lax.axis_index(("dp", "rep")).astype(jnp.int32)
    me = (place & (CHUNKS - 1)).reshape(1)
    slots = requests.shape[1] * requests.shape[2]
    w_in, w_out, cotangent, d_gated, leaf_sum, picker, onehot, allowed = run_prepare(
        lengths, event_slot.reshape(1, -1), leaf_ids.T, leaf_table, w_in, w_out, cotangent, slots
    )
    asked = gather_requests(requests, count)
    fetched, chosen = run_lookup(place.reshape(1), asked, item_table)
    arrived = exchange(fetched)
    inputs, gated, d_pre, keep_in, send_in = run_layer(
        me, arrived, picker, leaf_sum, w_in, d_gated, allowed
    )
    output, d_rows, keep_out, send_out = run_tail(
        me, picker, onehot, inputs, gated, d_pre, w_in, w_out, cotangent
    )
    returned = exchange(d_rows)
    in_own, in_other, out_own, out_other = reduce_and_gather(
        keep_in, send_in, keep_out, send_out, count
    )
    table_grad, leaf_mean, in_mean, out_mean = run_finish(
        me, chosen, returned, in_own, in_other, out_own, out_other, leaf_table.shape[0]
    )
    return (output, table_grad, leaf_mean, in_mean, out_mean)


def solution(mesh):
    return jax.shard_map(
        on_device,
        mesh=mesh,
        in_specs=(
            P(("dp", "rep"), None),
            P(("dp", "rep"), None, None),
            P(("dp", "rep")),
            P(("dp", "rep"), None),
            P(("dp", "rep"), None),
            P(),
            P(),
            P(),
            P(("dp", "rep"), None),
        ),
        out_specs=(P(("dp", "rep"), None), P(("dp", "rep"), None), P(), P(), P()),
        check_vma=False,
    )
```

```python
import functools
import jax
import jax.numpy as jnp
from jax import lax
from jax.experimental import pallas as pl
from jax.experimental.pallas import tpu as pltpu
from jax.sharding import PartitionSpec as P

HEADS = 4
MAXLEN = 256
BLOCK = 128
ROWS = 16
epsilon = 1e-06
f32 = jnp.float32
bf16 = jnp.bfloat16

ROUTES = (((0,), (1, 2), (3, 4)), ((0,), (3, 4), (1, 2)))
SPLIT = 2048
CHUNKS = 32
LAYER_VMEM = 60 * 2**20


def dot(a, b, contract):
    return lax.dot_general(a, b, ((contract[0], contract[1]), ((), ())), preferred_element_type=f32)


def mm(a, b):
    return dot(a, b, ((1,), (0,)))


def mm_nt(a, b):
    return dot(a, b, ((1,), (1,)))


def mm_tn(a, b):
    return dot(a, b, ((0,), (0,)))


def mask_of(group, digit):
    return sum(((digit >> k) & 1) << bit for k, bit in enumerate(group))


def chunk_order(groups):
    masks = [0]
    for group in groups:
        masks = [mask ^ mask_of(group, digit) for mask in masks for digit in range(2 ** len(group))]
    return masks


def spans(count):
    for start in range(0, count, BLOCK):
        low = max(0, start - (MAXLEN - 1)) // BLOCK * BLOCK
        yield start, low, start + BLOCK


def center(values):
    values = values - jnp.mean(values, axis=-1, keepdims=True)
    return values, lax.rsqrt(jnp.mean(values * values, axis=-1, keepdims=True) + epsilon)


def pull_normalize(change, normed, scale):
    return scale * (
        change
        - jnp.mean(change, axis=-1, keepdims=True)
        - normed * jnp.mean(change * normed, axis=-1, keepdims=True)
    )


def pickers(slots, slot_ref, leaf_ref, leaves):
    count = slot_ref.shape[1]
    picker = lax.broadcasted_iota(jnp.int32, (slots, count), 0) == slot_ref[...]
    trees = leaf_ref.shape[0]
    each = leaves // trees
    spots = lax.broadcasted_iota(jnp.int32, (each, count), 0)
    onehot = [(spots == leaf_ref[t : t + 1, :]).astype(f32).astype(bf16) for t in range(trees)]
    return picker.astype(f32).astype(bf16), jnp.concatenate(onehot, axis=0)


def permute_rows(me, order, source, target):
    for place, mask in enumerate(order):
        start = pl.multiple_of((me ^ mask) * ROWS, ROWS)
        target[place * ROWS : (place + 1) * ROWS, :] = source[pl.ds(start, ROWS), :]


def lookup_kernel(asked_ref, table_ref, rows_ref, chosen_ref):
    count, each = asked_ref.shape
    many = count * each
    spot = lax.broadcasted_iota(jnp.int32, (count, table_ref.shape[0]), 1)
    parts = [(spot == asked_ref[:, k : k + 1]).astype(f32).astype(bf16) for k in range(each)]
    chosen = jnp.concatenate(parts, axis=0)
    to = lax.broadcasted_iota(jnp.int32, (many, many), 0)
    source = (to % each) * count + to // each
    order = (source == lax.broadcasted_iota(jnp.int32, (many, many), 1)).astype(f32).astype(bf16)
    chosen_ref[...] = mm(order, chosen).astype(bf16)
    rows_ref[...] = mm(chosen_ref[...], table_ref[...]).astype(bf16)


def run_lookup(asked, table):
    vmem = pl.BlockSpec(memory_space=pltpu.VMEM)
    shape = jax.ShapeDtypeStruct
    many = asked.shape[0] * asked.shape[1]
    return pl.pallas_call(
        lookup_kernel,
        name="lookup",
        out_shape=(shape((many, table.shape[1]), bf16), shape((many, table.shape[0]), bf16)),
        in_specs=[vmem, vmem],
        out_specs=(vmem,) * 2,
        compiler_params=pltpu.CompilerParams(vmem_limit_bytes=16 * 2**20),
    )(asked, table)


def layer_kernel(
    me_ref, lengths_ref, slot_ref, leaf_ref, rows_ref, table_hbm, in_hbm, out_hbm, tangent_hbm,
    output_hbm, d_rows_ref, keep_hbm, send_hbm,
    inputs, gated, d_pre, grads, output,
    normed, turned, moved, hidden, slope, weights, weights_slope, mixed, d_mixed,
    d_score, d_gated, allowed, d_inputs, leaf_grad, table, w_in, w_out, tangent, sems, out_sems,
):
    count, width = inputs.shape
    head = width // HEADS
    half_rows = width // 2
    copies = [
        pltpu.make_async_copy(source, target, sems.at[k])
        for k, (source, target) in enumerate(
            ((table_hbm, table), (in_hbm, w_in), (out_hbm, w_out), (tangent_hbm, tangent))
        )
    ]
    for copy in copies:
        copy.start()
    leaving = []

    def leave(source, target):
        copy = pltpu.make_async_copy(source, target, out_sems.at[len(leaving)])
        copy.start()
        leaving.append(copy)

    picker, onehot = pickers(rows_ref.shape[0], slot_ref, leaf_ref, table.shape[0])
    ends = []
    total = 0
    for place in range(lengths_ref.shape[1]):
        total = total + lengths_ref[0, place]
        ends.append(total)
    for start, low, high in spans(count):
        at = slice(start, start + BLOCK)
        row = start + lax.broadcasted_iota(jnp.int32, (BLOCK, high - low), 0)
        column = low + lax.broadcasted_iota(jnp.int32, (BLOCK, high - low), 1)
        first = jnp.zeros_like(row)
        for end in ends[:-1]:
            first = jnp.where(row >= end, end, first)
        allowed[at, low:high] = jnp.where(
            jnp.logical_and(column >= first, column <= row), 1.0, 0.0
        ).astype(f32)
    copies[0].wait()
    inputs[...] = (mm_tn(picker, rows_ref[...]) + mm_tn(onehot, table[...])).astype(bf16)
    for start in range(0, count, BLOCK):
        at = slice(start, start + BLOCK)
        values, scale = center(inputs[at, :].astype(f32))
        normed[at, :] = (values * scale).astype(bf16)
    turned[...] = normed[...].T
    copies[1].wait()
    for start in range(0, 4 * width, 2 * BLOCK):
        to = slice(start, start + 2 * BLOCK)
        half = mm(normed[...], w_in[:, to]) * 0.5
        curve = jnp.tanh(half)
        upper = 1.0 + curve
        hidden[:, to] = (half * upper).astype(bf16)
        slope[:, to] = (0.5 * upper * (1.0 + half * (1.0 - curve))).astype(bf16)
    weights[...] = jnp.zeros_like(weights)
    d_score[...] = jnp.zeros_like(d_score)
    half_scale = 0.5 * head ** (-0.5)
    for h in range(HEADS):
        value_at = slice(width + h * head, width + (h + 1) * head)
        query_at = slice(2 * width + h * head, 2 * width + (h + 1) * head)
        key_at = slice(3 * width + h * head, 3 * width + (h + 1) * head)
        for start, low, high in spans(count):
            at = slice(start, start + BLOCK)
            half = mm_nt(hidden[at, query_at], hidden[low:high, key_at]) * half_scale
            curve = jnp.tanh(half)
            upper = (1.0 + curve) * allowed[at, low:high]
            weights[h, at, low:high] = (half * upper).astype(bf16)
            weights_slope[h, at, low:high] = (
                half_scale * upper * (1.0 + half * (1.0 - curve))
            ).astype(bf16)
        for start in range(0, count, 2 * BLOCK):
            at = slice(start, start + 2 * BLOCK)
            high = start + 2 * BLOCK
            mixed[at, h * head : (h + 1) * head] = mm(
                weights[h, at, :high], hidden[:high, value_at]
            )
    copies[2].wait()
    copies[3].wait()
    d_gated[...] = mm_nt(tangent[...], w_out[...]).astype(bf16)
    for start in range(0, count, BLOCK):
        at = slice(start, start + BLOCK)
        values, scale = center(mixed[at, :])
        values = values * scale
        gates = hidden[at, :width].astype(f32)
        change = d_gated[at, :].astype(f32)
        gated[at, :] = (values * gates).astype(bf16)
        d_pre[at, :width] = (change * values * slope[at, :width].astype(f32)).astype(bf16)
        d_mixed[at, :] = pull_normalize(change * gates, values, scale).astype(bf16)
    for h in range(HEADS):
        own = slice(h * head, (h + 1) * head)
        value_at = slice(width + h * head, width + (h + 1) * head)
        query_at = slice(2 * width + h * head, 2 * width + (h + 1) * head)
        key_at = slice(3 * width + h * head, 3 * width + (h + 1) * head)
        for start, low, high in spans(count):
            at = slice(start, start + BLOCK)
            d_score[h, at, low:high] = (
                mm_nt(d_mixed[at, own], hidden[low:high, value_at])
                * weights_slope[h, at, low:high].astype(f32)
            ).astype(bf16)
        for start in range(0, count, 2 * BLOCK):
            at = slice(start, start + 2 * BLOCK)
            high = start + 2 * BLOCK
            d_query = mm(d_score[h, at, :high], hidden[:high, key_at])
            d_pre[at, query_at] = (d_query * slope[at, query_at].astype(f32)).astype(bf16)
            d_key = mm_tn(d_score[h, start:, at], hidden[start:, query_at])
            d_pre[at, key_at] = (d_key * slope[at, key_at].astype(f32)).astype(bf16)
            d_value = mm_tn(weights[h, start:, at], d_mixed[start:, own])
            d_pre[at, value_at] = (d_value * slope[at, value_at].astype(f32)).astype(bf16)
    me = me_ref[0]
    early, late = (chunk_order(route) for route in ROUTES)
    permute_rows(me, early, turned, moved)
    for start in range(0, 4 * width, 2 * BLOCK):
        to = slice(start, start + 2 * BLOCK)
        grads[:, to] = mm(moved[...], d_pre[:, to]).astype(bf16)
    leave(grads.at[half_rows:, : 4 * width], send_hbm.at[:, : 4 * width])
    leave(grads.at[:half_rows, : 4 * width], keep_hbm.at[:, : 4 * width])
    turned[...] = gated[...].T
    permute_rows(me, late, turned, moved)
    grads[:, 4 * width : 5 * width] = mm(moved[...], tangent[...]).astype(bf16)
    normed_change = mm_nt(d_pre[...], w_in[...])
    for start in range(0, count, BLOCK):
        at = slice(start, start + BLOCK)
        values, scale = center(inputs[at, :].astype(f32))
        change = pull_normalize(normed_change[at, :], values * scale, scale)
        d_inputs[at, :] = (change + tangent[at, :].astype(f32)).astype(bf16)
    leaves = table.shape[0]
    d_leaf = mm(onehot, d_inputs[...]).astype(bf16)
    leaf_grad[:leaves, :] = d_leaf[:, : width // 2]
    leaf_grad[leaves:, :] = d_leaf[:, width // 2 :]
    permute_rows(me, late, leaf_grad, grads.at[:, 5 * width :])
    leave(grads.at[half_rows:, 4 * width :], send_hbm.at[:, 4 * width :])
    leave(grads.at[:half_rows, 4 * width :], keep_hbm.at[:, 4 * width :])
    d_rows_ref[...] = mm(picker, d_inputs[...]).astype(bf16)
    output[...] = (mm(gated[...], w_out[...]) + inputs[...].astype(f32)).astype(bf16)
    leave(output, output_hbm)
    for copy in leaving:
        copy.wait()


def run_layer(me, lengths, slot, leaf, rows, table, w_in, w_out, tangent):
    count, width = tangent.shape
    smem = pl.BlockSpec(memory_space=pltpu.SMEM)
    vmem = pl.BlockSpec(memory_space=pltpu.VMEM)
    hbm = pl.BlockSpec(memory_space=pltpu.HBM)
    shape = jax.ShapeDtypeStruct
    columns = 5 * width + width // 2
    return pl.pallas_call(
        layer_kernel,
        name="layer",
        out_shape=(
            shape((count, width), bf16),
            shape((rows.shape[0], width), bf16),
            shape((width // 2, columns), bf16),
            shape((width // 2, columns), bf16),
        ),
        in_specs=[smem, smem] + [vmem] * 3 + [hbm] * 4,
        out_specs=(hbm, vmem, hbm, hbm),
        scratch_shapes=[
            pltpu.VMEM((count, width), bf16),
            pltpu.VMEM((count, width), bf16),
            pltpu.VMEM((count, 4 * width), bf16),
            pltpu.VMEM((width, columns), bf16),
            pltpu.VMEM((count, width), bf16),
            pltpu.VMEM((count, width), bf16),
            pltpu.VMEM((width, count), bf16),
            pltpu.VMEM((width, count), bf16),
            pltpu.VMEM((count, 4 * width), bf16),
            pltpu.VMEM((count, 4 * width), bf16),
            pltpu.VMEM((HEADS, count, count), bf16),
            pltpu.VMEM((HEADS, count, count), bf16),
            pltpu.VMEM((count, width), f32),
            pltpu.VMEM((count, width), bf16),
            pltpu.VMEM((HEADS, count, count), bf16),
            pltpu.VMEM((count, width), bf16),
            pltpu.VMEM((count, count), f32),
            pltpu.VMEM((count, width), bf16),
            pltpu.VMEM((width, width // 2), bf16),
            pltpu.VMEM(table.shape, bf16),
            pltpu.VMEM(w_in.shape, bf16),
            pltpu.VMEM(w_out.shape, bf16),
            pltpu.VMEM(tangent.shape, bf16),
            pltpu.SemaphoreType.DMA((4,)),
            pltpu.SemaphoreType.DMA((5,)),
        ],
        compiler_params=pltpu.CompilerParams(vmem_limit_bytes=LAYER_VMEM),
        cost_estimate=pl.CostEstimate(flops=6 * 10**9, bytes_accessed=10**7, transcendentals=10**6),
    )(me, lengths, slot, leaf, rows, table, w_in, w_out, tangent)


def finish_kernel(
    me_ref, chosen_ref, returned_ref, early_own, early_other, late_own, late_other,
    table_ref, leaf_ref, in_hbm, out_hbm, grads, sems,
):
    width, columns = grads.shape
    leaves = leaf_ref.shape[0]
    me = me_ref[0]
    half_rows = width // 2
    leaving = []

    def leave(source, target):
        copy = pltpu.make_async_copy(source, target, sems.at[len(leaving)])
        copy.start()
        leaving.append(copy)

    def place(route, own, other, low, high, at):
        for spot, mask in enumerate(chunk_order(route)):
            source = own if spot * ROWS < half_rows else other
            row = spot * ROWS % half_rows
            start = pl.multiple_of((me ^ mask) * ROWS, ROWS)
            grads[pl.ds(start, ROWS), at + low : at + high] = source[
                row : row + ROWS, low:high
            ].astype(f32)

    for low in range(0, SPLIT, width):
        place(ROUTES[0], early_own, early_other, low, low + width, 0)
        leave(grads.at[:, low : low + width], in_hbm.at[:, low : low + width])
    place(ROUTES[1], late_own, late_other, 0, width, SPLIT)
    leave(grads.at[:, SPLIT : SPLIT + width], out_hbm)
    place(ROUTES[1], late_own, late_other, width, columns - SPLIT, SPLIT)
    leaf_ref[:, : width // 2] = grads[:leaves, 5 * width :]
    leaf_ref[:, width // 2 :] = grads[leaves:, 5 * width :]
    table_ref[...] = mm_tn(chosen_ref[...], returned_ref[...])
    for copy in leaving:
        copy.wait()


def run_finish(me, chosen, returned, early_own, early_other, late_own, late_other, leaves):
    smem = pl.BlockSpec(memory_space=pltpu.SMEM)
    vmem = pl.BlockSpec(memory_space=pltpu.VMEM)
    hbm = pl.BlockSpec(memory_space=pltpu.HBM)
    shape = jax.ShapeDtypeStruct
    width = returned.shape[1]
    return pl.pallas_call(
        finish_kernel,
        name="finish",
        out_shape=(
            shape((chosen.shape[1], width), f32),
            shape((leaves, width), f32),
            shape((width, 4 * width), f32),
            shape((width, width), f32),
        ),
        in_specs=[smem] + [vmem] * 6,
        out_specs=(vmem, vmem, hbm, hbm),
        scratch_shapes=[
            pltpu.VMEM((width, early_own.shape[1] + late_own.shape[1]), f32),
            pltpu.SemaphoreType.DMA((5,)),
        ],
        compiler_params=pltpu.CompilerParams(vmem_limit_bytes=32 * 2**20),
    )(me, chosen, returned, early_own, early_other, late_own, late_other)


def exchange(blocks):
    return lax.all_to_all(blocks, ("dp", "rep"), split_axis=0, concat_axis=0, tiled=True)


def swap(block, mask, count):
    return lax.ppermute(block, ("dp", "rep"), [(i, i ^ mask) for i in range(count)])


def add(parts):
    return sum(part.astype(f32) for part in parts)


def shares(parts, group):
    size = 2 ** len(group)
    rows = parts[0].shape[0] // size
    return [
        add(part[digit * rows : (digit + 1) * rows] for part in parts).astype(bf16)
        for digit in range(1, size)
    ]


def swap_all(blocks, group, count):
    return [
        swap(block, mask_of(group, digit), count) for digit, block in enumerate(blocks, start=1)
    ]


def reduce_and_gather(keep, send, d_rows, count):
    other = swap(send, 1, count)
    early = [keep[:, :SPLIT], other[:, :SPLIT]]
    late = [keep[:, SPLIT:], other[:, SPLIT:]]
    for k in (1, 2):
        early_route, late_route = ROUTES[0][k], ROUTES[1][k]
        blocks = shares(early, early_route), shares(late, late_route)
        if k == 1:
            (early_blocks, late_blocks), d_rows = lax.optimization_barrier((blocks, d_rows))
            returned = exchange(d_rows)
        else:
            early_blocks, late_blocks = lax.optimization_barrier(blocks)
        got = swap_all(early_blocks, early_route, count), swap_all(late_blocks, late_route, count)
        if k == 1:
            got, returned = lax.optimization_barrier((got, returned))
        else:
            got = lax.optimization_barrier(got)
        early = [part[: part.shape[0] // 2 ** len(early_route)] for part in early] + got[0]
        late = [part[: part.shape[0] // 2 ** len(late_route)] for part in late] + got[1]
    own = [add(early), add(late)]
    far = CHUNKS
    while far < count:
        own = [part + swap(part, far, count) for part in own]
        far *= 2
    early, late = ((part * (1.0 / count)).astype(bf16) for part in own)
    for k in (2, 1):
        early, late = lax.optimization_barrier((early, late))
        routes = ROUTES[0][k], ROUTES[1][k]
        got = lax.optimization_barrier(
            tuple(
                swap_all([block] * (2 ** len(route) - 1), route, count)
                for block, route in zip((early, late), routes)
            )
        )
        early = jnp.concatenate([early] + got[0], axis=0)
        late = jnp.concatenate([late] + got[1], axis=0)
    return returned, early, swap(early, 1, count), late, swap(late, 1, count)


def on_device(
    item_table, requests, event_slot, lengths, leaf_ids, leaf_table, w_in, w_out, cotangent
):
    count = lax.axis_size("dp") * lax.axis_size("rep")
    place = lax.axis_index(("dp", "rep")).astype(jnp.int32)
    me = (place & (CHUNKS - 1)).reshape(1)
    slot = event_slot.reshape(1, -1)
    leaf = leaf_ids.T
    asked = exchange(requests[0])
    fetched, chosen = run_lookup(asked, item_table)
    arrived = exchange(fetched)
    output, d_rows, keep, send = run_layer(
        me, lengths, slot, leaf, arrived, leaf_table, w_in, w_out, cotangent
    )
    returned, early, early_other, late, late_other = reduce_and_gather(keep, send, d_rows, count)
    table_grad, leaf_mean, in_mean, out_mean = run_finish(
        me, chosen, returned, early, early_other, late, late_other, leaf_table.shape[0]
    )
    return (output, table_grad, leaf_mean, in_mean, out_mean)


def solution(mesh):
    return jax.shard_map(
        on_device,
        mesh=mesh,
        in_specs=(
            P(("dp", "rep"), None),
            P(("dp", "rep"), None, None),
            P(("dp", "rep")),
            P(("dp", "rep"), None),
            P(("dp", "rep"), None),
            P(),
            P(),
            P(),
            P(("dp", "rep"), None),
        ),
        out_specs=(P(("dp", "rep"), None), P(("dp", "rep"), None), P(), P(), P()),
        check_vma=False,
    )
```

```python
import functools
import jax
import jax.numpy as jnp
from jax import lax
from jax.experimental import pallas as pl
from jax.experimental.pallas import tpu as pltpu
from jax.sharding import PartitionSpec as P

HEADS = 4
MAXLEN = 256
BLOCK = 128
ROWS = 16
epsilon = 1e-06
f32 = jnp.float32
bf16 = jnp.bfloat16

ROUTES = (((0,), (1, 2), (3, 4)), ((0,), (3, 4), (1, 2)))
CHUNKS = 32
LAYER_VMEM = 60 * 2**20


def dot(a, b, contract):
    return lax.dot_general(a, b, ((contract[0], contract[1]), ((), ())), preferred_element_type=f32)


def mm(a, b):
    return dot(a, b, ((1,), (0,)))


def mm_nt(a, b):
    return dot(a, b, ((1,), (1,)))


def mm_tn(a, b):
    return dot(a, b, ((0,), (0,)))


def mask_of(group, digit):
    return sum(((digit >> k) & 1) << bit for k, bit in enumerate(group))


def masks_of(groups):
    masks = [0]
    for group in groups:
        masks = [mask ^ mask_of(group, digit) for mask in masks for digit in range(2 ** len(group))]
    return masks


def chunk_order(me):
    chunks = []
    for owner in (me, me ^ 1):
        odd = owner & 1 == 1
        for one, other in zip(masks_of(ROUTES[0][1:]), masks_of(ROUTES[1][1:])):
            chunks.append(owner ^ (one if one == other else jnp.where(odd, other, one)))
    return chunks


def spans(count):
    for start in range(0, count, BLOCK):
        low = max(0, start - (MAXLEN - 1)) // BLOCK * BLOCK
        yield start, low, start + BLOCK


def center(values):
    values = values - jnp.mean(values, axis=-1, keepdims=True)
    return values, lax.rsqrt(jnp.mean(values * values, axis=-1, keepdims=True) + epsilon)


def pull_normalize(change, normed, scale):
    return scale * (
        change
        - jnp.mean(change, axis=-1, keepdims=True)
        - normed * jnp.mean(change * normed, axis=-1, keepdims=True)
    )


def pickers(slots, slot_ref, leaf_ref, leaves):
    count = slot_ref.shape[1]
    picker = lax.broadcasted_iota(jnp.int32, (slots, count), 0) == slot_ref[...]
    trees = leaf_ref.shape[0]
    each = leaves // trees
    spots = lax.broadcasted_iota(jnp.int32, (each, count), 0)
    onehot = [(spots == leaf_ref[t : t + 1, :]).astype(f32).astype(bf16) for t in range(trees)]
    return picker.astype(f32).astype(bf16), jnp.concatenate(onehot, axis=0)


def permute_rows(chunks, source, *targets):
    rows = targets[0].shape[0]
    for place, chunk in enumerate(chunks):
        start = pl.multiple_of(chunk * ROWS, ROWS)
        at = place * ROWS % rows
        targets[place * ROWS // rows][at : at + ROWS, :] = source[pl.ds(start, ROWS), :]


def lookup_kernel(asked_ref, table_ref, rows_ref, chosen_ref):
    count, each = asked_ref.shape
    many = count * each
    spot = lax.broadcasted_iota(jnp.int32, (count, table_ref.shape[0]), 1)
    parts = [(spot == asked_ref[:, k : k + 1]).astype(f32).astype(bf16) for k in range(each)]
    chosen = jnp.concatenate(parts, axis=0)
    to = lax.broadcasted_iota(jnp.int32, (many, many), 0)
    source = (to % each) * count + to // each
    order = (source == lax.broadcasted_iota(jnp.int32, (many, many), 1)).astype(f32).astype(bf16)
    chosen_ref[...] = mm(order, chosen).astype(bf16)
    rows_ref[...] = mm(chosen_ref[...], table_ref[...]).astype(bf16)


def run_lookup(asked, table):
    vmem = pl.BlockSpec(memory_space=pltpu.VMEM)
    shape = jax.ShapeDtypeStruct
    many = asked.shape[0] * asked.shape[1]
    return pl.pallas_call(
        lookup_kernel,
        name="lookup",
        out_shape=(shape((many, table.shape[1]), bf16), shape((many, table.shape[0]), bf16)),
        in_specs=[vmem, vmem],
        out_specs=(vmem,) * 2,
        compiler_params=pltpu.CompilerParams(vmem_limit_bytes=16 * 2**20),
    )(asked, table)


def layer_kernel(
    me_ref, lengths_ref, slot_ref, leaf_ref, rows_ref, table_hbm, in_hbm, out_hbm, tangent_hbm,
    output_hbm, d_rows_ref, keep_hbm, send_hbm,
    inputs, gated, d_pre, output, keep_ref, send_ref,
    normed, turned, moved, hidden, slope, weights, weights_slope, mixed, d_mixed,
    d_score, d_gated, allowed, d_inputs, leaf_grad, table, w_in, w_out, tangent, sems, out_sems,
):
    count, width = inputs.shape
    head = width // HEADS
    half_rows = width // 2
    copies = [
        pltpu.make_async_copy(source, target, sems.at[k])
        for k, (source, target) in enumerate(
            ((table_hbm, table), (in_hbm, w_in), (out_hbm, w_out), (tangent_hbm, tangent))
        )
    ]
    for copy in copies:
        copy.start()
    picker, onehot = pickers(rows_ref.shape[0], slot_ref, leaf_ref, table.shape[0])
    ends = []
    total = 0
    for place in range(lengths_ref.shape[1]):
        total = total + lengths_ref[0, place]
        ends.append(total)
    for start, low, high in spans(count):
        at = slice(start, start + BLOCK)
        row = start + lax.broadcasted_iota(jnp.int32, (BLOCK, high - low), 0)
        column = low + lax.broadcasted_iota(jnp.int32, (BLOCK, high - low), 1)
        first = jnp.zeros_like(row)
        for end in ends[:-1]:
            first = jnp.where(row >= end, end, first)
        allowed[at, low:high] = jnp.where(
            jnp.logical_and(column >= first, column <= row), 1.0, 0.0
        ).astype(f32)
    copies[0].wait()
    inputs[...] = (mm_tn(picker, rows_ref[...]) + mm_tn(onehot, table[...])).astype(bf16)
    for start in range(0, count, BLOCK):
        at = slice(start, start + BLOCK)
        values, scale = center(inputs[at, :].astype(f32))
        normed[at, :] = (values * scale).astype(bf16)
    turned[...] = normed[...].T
    copies[1].wait()
    for start in range(0, 4 * width, 2 * BLOCK):
        to = slice(start, start + 2 * BLOCK)
        half = mm(normed[...], w_in[:, to]) * 0.5
        curve = jnp.tanh(half)
        upper = 1.0 + curve
        hidden[:, to] = (half * upper).astype(bf16)
        slope[:, to] = (0.5 * upper * (1.0 + half * (1.0 - curve))).astype(bf16)
    weights[...] = jnp.zeros_like(weights)
    d_score[...] = jnp.zeros_like(d_score)
    half_scale = 0.5 * head ** (-0.5)
    for h in range(HEADS):
        value_at = slice(width + h * head, width + (h + 1) * head)
        query_at = slice(2 * width + h * head, 2 * width + (h + 1) * head)
        key_at = slice(3 * width + h * head, 3 * width + (h + 1) * head)
        for start, low, high in spans(count):
            at = slice(start, start + BLOCK)
            half = mm_nt(hidden[at, query_at], hidden[low:high, key_at]) * half_scale
            curve = jnp.tanh(half)
            upper = (1.0 + curve) * allowed[at, low:high]
            weights[h, at, low:high] = (half * upper).astype(bf16)
            weights_slope[h, at, low:high] = (
                half_scale * upper * (1.0 + half * (1.0 - curve))
            ).astype(bf16)
        for start in range(0, count, 2 * BLOCK):
            at = slice(start, start + 2 * BLOCK)
            high = start + 2 * BLOCK
            mixed[at, h * head : (h + 1) * head] = mm(
                weights[h, at, :high], hidden[:high, value_at]
            )
    copies[2].wait()
    copies[3].wait()
    d_gated[...] = mm_nt(tangent[...], w_out[...]).astype(bf16)
    for start in range(0, count, BLOCK):
        at = slice(start, start + BLOCK)
        values, scale = center(mixed[at, :])
        values = values * scale
        gates = hidden[at, :width].astype(f32)
        change = d_gated[at, :].astype(f32)
        gated[at, :] = (values * gates).astype(bf16)
        d_pre[at, :width] = (change * values * slope[at, :width].astype(f32)).astype(bf16)
        d_mixed[at, :] = pull_normalize(change * gates, values, scale).astype(bf16)
    for h in range(HEADS):
        own = slice(h * head, (h + 1) * head)
        value_at = slice(width + h * head, width + (h + 1) * head)
        query_at = slice(2 * width + h * head, 2 * width + (h + 1) * head)
        key_at = slice(3 * width + h * head, 3 * width + (h + 1) * head)
        for start, low, high in spans(count):
            at = slice(start, start + BLOCK)
            d_score[h, at, low:high] = (
                mm_nt(d_mixed[at, own], hidden[low:high, value_at])
                * weights_slope[h, at, low:high].astype(f32)
            ).astype(bf16)
        for start in range(0, count, 2 * BLOCK):
            at = slice(start, start + 2 * BLOCK)
            high = start + 2 * BLOCK
            d_query = mm(d_score[h, at, :high], hidden[:high, key_at])
            d_pre[at, query_at] = (d_query * slope[at, query_at].astype(f32)).astype(bf16)
            d_key = mm_tn(d_score[h, start:, at], hidden[start:, query_at])
            d_pre[at, key_at] = (d_key * slope[at, key_at].astype(f32)).astype(bf16)
            d_value = mm_tn(weights[h, start:, at], d_mixed[start:, own])
            d_pre[at, value_at] = (d_value * slope[at, value_at].astype(f32)).astype(bf16)
    chunks = chunk_order(me_ref[0])
    permute_rows(chunks, turned, moved)
    for start in range(0, 4 * width, 2 * BLOCK):
        to = slice(start, start + 2 * BLOCK)
        grad = mm(moved[...], d_pre[:, to]).astype(bf16)
        keep_ref[:, to] = grad[:half_rows, :]
        send_ref[:, to] = grad[half_rows:, :]
    leaving = []

    def leave(source, target):
        copy = pltpu.make_async_copy(source, target, out_sems.at[len(leaving)])
        copy.start()
        leaving.append(copy)

    leave(send_ref.at[:, : 4 * width], send_hbm.at[:, : 4 * width])
    leave(keep_ref.at[:, : 4 * width], keep_hbm.at[:, : 4 * width])
    turned[...] = gated[...].T
    permute_rows(chunks, turned, moved)
    grad = mm(moved[...], tangent[...]).astype(bf16)
    keep_ref[:, 4 * width : 5 * width] = grad[:half_rows, :]
    send_ref[:, 4 * width : 5 * width] = grad[half_rows:, :]
    output[...] = (mm(gated[...], w_out[...]) + inputs[...].astype(f32)).astype(bf16)
    leave(output, output_hbm)
    normed_change = mm_nt(d_pre[...], w_in[...])
    for start in range(0, count, BLOCK):
        at = slice(start, start + BLOCK)
        values, scale = center(inputs[at, :].astype(f32))
        change = pull_normalize(normed_change[at, :], values * scale, scale)
        d_inputs[at, :] = (change + tangent[at, :].astype(f32)).astype(bf16)
    leaves = table.shape[0]
    d_leaf = mm(onehot, d_inputs[...]).astype(bf16)
    leaf_grad[:leaves, :] = d_leaf[:, : width // 2]
    leaf_grad[leaves:, :] = d_leaf[:, width // 2 :]
    permute_rows(chunks, leaf_grad, keep_ref.at[:, 5 * width :], send_ref.at[:, 5 * width :])
    leave(send_ref.at[:, 4 * width :], send_hbm.at[:, 4 * width :])
    leave(keep_ref.at[:, 4 * width :], keep_hbm.at[:, 4 * width :])
    d_rows_ref[...] = mm(picker, d_inputs[...]).astype(bf16)
    for copy in leaving:
        copy.wait()


def run_layer(me, lengths, slot, leaf, rows, table, w_in, w_out, tangent):
    count, width = tangent.shape
    smem = pl.BlockSpec(memory_space=pltpu.SMEM)
    vmem = pl.BlockSpec(memory_space=pltpu.VMEM)
    hbm = pl.BlockSpec(memory_space=pltpu.HBM)
    shape = jax.ShapeDtypeStruct
    columns = 5 * width + width // 2
    return pl.pallas_call(
        layer_kernel,
        name="layer",
        out_shape=(
            shape((count, width), bf16),
            shape((rows.shape[0], width), bf16),
            shape((width // 2, columns), bf16),
            shape((width // 2, columns), bf16),
        ),
        in_specs=[smem, smem] + [vmem] * 3 + [hbm] * 4,
        out_specs=(hbm, vmem, hbm, hbm),
        scratch_shapes=[
            pltpu.VMEM((count, width), bf16),
            pltpu.VMEM((count, width), bf16),
            pltpu.VMEM((count, 4 * width), bf16),
            pltpu.VMEM((count, width), bf16),
            pltpu.VMEM((width // 2, columns), bf16),
            pltpu.VMEM((width // 2, columns), bf16),
            pltpu.VMEM((count, width), bf16),
            pltpu.VMEM((width, count), bf16),
            pltpu.VMEM((width, count), bf16),
            pltpu.VMEM((count, 4 * width), bf16),
            pltpu.VMEM((count, 4 * width), bf16),
            pltpu.VMEM((HEADS, count, count), bf16),
            pltpu.VMEM((HEADS, count, count), bf16),
            pltpu.VMEM((count, width), f32),
            pltpu.VMEM((count, width), bf16),
            pltpu.VMEM((HEADS, count, count), bf16),
            pltpu.VMEM((count, width), bf16),
            pltpu.VMEM((count, count), f32),
            pltpu.VMEM((count, width), bf16),
            pltpu.VMEM((width, width // 2), bf16),
            pltpu.VMEM(table.shape, bf16),
            pltpu.VMEM(w_in.shape, bf16),
            pltpu.VMEM(w_out.shape, bf16),
            pltpu.VMEM(tangent.shape, bf16),
            pltpu.SemaphoreType.DMA((4,)),
            pltpu.SemaphoreType.DMA((5,)),
        ],
        compiler_params=pltpu.CompilerParams(vmem_limit_bytes=LAYER_VMEM),
        cost_estimate=pl.CostEstimate(flops=6 * 10**9, bytes_accessed=10**7, transcendentals=10**6),
    )(me, lengths, slot, leaf, rows, table, w_in, w_out, tangent)


def finish_kernel(
    me_ref, chosen_ref, returned_ref, own_ref, other_ref,
    table_ref, leaf_ref, in_hbm, out_hbm, grads, sems,
):
    width, columns = grads.shape
    leaves = leaf_ref.shape[0]
    half_rows = width // 2
    chunks = chunk_order(me_ref[0])
    leaving = []
    for low in range(0, columns, width):
        high = min(low + width, columns)
        for place, chunk in enumerate(chunks):
            source = own_ref if place * ROWS < half_rows else other_ref
            at = place * ROWS % half_rows
            start = pl.multiple_of(chunk * ROWS, ROWS)
            grads[pl.ds(start, ROWS), low:high] = source[at : at + ROWS, low:high].astype(f32)
        if low < 5 * width:
            target = in_hbm.at[:, low:high] if low < 4 * width else out_hbm
            copy = pltpu.make_async_copy(grads.at[:, low:high], target, sems.at[len(leaving)])
            copy.start()
            leaving.append(copy)
    leaf_ref[:, : width // 2] = grads[:leaves, 5 * width :]
    leaf_ref[:, width // 2 :] = grads[leaves:, 5 * width :]
    table_ref[...] = mm_tn(chosen_ref[...], returned_ref[...])
    for copy in leaving:
        copy.wait()


def run_finish(me, chosen, returned, own, other, leaves):
    smem = pl.BlockSpec(memory_space=pltpu.SMEM)
    vmem = pl.BlockSpec(memory_space=pltpu.VMEM)
    hbm = pl.BlockSpec(memory_space=pltpu.HBM)
    shape = jax.ShapeDtypeStruct
    width = returned.shape[1]
    return pl.pallas_call(
        finish_kernel,
        name="finish",
        out_shape=(
            shape((chosen.shape[1], width), f32),
            shape((leaves, width), f32),
            shape((width, 4 * width), f32),
            shape((width, width), f32),
        ),
        in_specs=[smem] + [vmem] * 4,
        out_specs=(vmem, vmem, hbm, hbm),
        scratch_shapes=[
            pltpu.VMEM((width, own.shape[1]), f32),
            pltpu.SemaphoreType.DMA((5,)),
        ],
        compiler_params=pltpu.CompilerParams(vmem_limit_bytes=32 * 2**20),
    )(me, chosen, returned, own, other)


def exchange(blocks):
    return lax.all_to_all(blocks, ("dp", "rep"), split_axis=0, concat_axis=0, tiled=True)


def swap(block, masks, count):
    return lax.ppermute(block, ("dp", "rep"), [(i, i ^ masks[i % 2]) for i in range(count)])


def partners(k):
    size = 2 ** len(ROUTES[0][k])
    return [tuple(mask_of(route[k], digit) for route in ROUTES) for digit in range(1, size)]


def add(parts):
    return sum(part.astype(f32) for part in parts)


def reduce_and_gather(keep, send, d_rows, count):
    parts = [keep, swap(send, (1, 1), count)]
    returned = None
    for k in (1, 2):
        masks = partners(k)
        rows = parts[0].shape[0] // (1 + len(masks))
        blocks = [
            add(part[digit * rows : (digit + 1) * rows] for part in parts).astype(bf16)
            for digit in range(1, 1 + len(masks))
        ]
        if returned is None:
            blocks, d_rows = lax.optimization_barrier((blocks, d_rows))
            returned = exchange(d_rows)
        got = [swap(block, mask, count) for block, mask in zip(blocks, masks)]
        if k == 1:
            got, returned = lax.optimization_barrier((got, returned))
        parts = [part[:rows] for part in parts] + got
    own = add(parts)
    far = CHUNKS
    while far < count:
        own = own + swap(own, (far, far), count)
        far *= 2
    own = (own * (1.0 / count)).astype(bf16)
    for k in (2, 1):
        got = lax.optimization_barrier([swap(own, mask, count) for mask in partners(k)])
        own = jnp.concatenate([own] + got, axis=0)
    return returned, own, swap(own, (1, 1), count)


def on_device(
    item_table, requests, event_slot, lengths, leaf_ids, leaf_table, w_in, w_out, cotangent
):
    count = lax.axis_size("dp") * lax.axis_size("rep")
    place = lax.axis_index(("dp", "rep")).astype(jnp.int32)
    me = (place & (CHUNKS - 1)).reshape(1)
    slot = event_slot.reshape(1, -1)
    leaf = leaf_ids.T
    asked = exchange(requests[0])
    fetched, chosen = run_lookup(asked, item_table)
    arrived = exchange(fetched)
    output, d_rows, keep, send = run_layer(
        me, lengths, slot, leaf, arrived, leaf_table, w_in, w_out, cotangent
    )
    returned, own, other = reduce_and_gather(keep, send, d_rows, count)
    table_grad, leaf_mean, in_mean, out_mean = run_finish(
        me, chosen, returned, own, other, leaf_table.shape[0]
    )
    return (output, table_grad, leaf_mean, in_mean, out_mean)


def solution(mesh):
    return jax.shard_map(
        on_device,
        mesh=mesh,
        in_specs=(
            P(("dp", "rep"), None),
            P(("dp", "rep"), None, None),
            P(("dp", "rep")),
            P(("dp", "rep"), None),
            P(("dp", "rep"), None),
            P(),
            P(),
            P(),
            P(("dp", "rep"), None),
        ),
        out_specs=(P(("dp", "rep"), None), P(("dp", "rep"), None), P(), P(), P()),
        check_vma=False,
    )
```

```python
import functools
import jax
import jax.numpy as jnp
from jax import lax
from jax.experimental import pallas as pl
from jax.experimental.pallas import tpu as pltpu
from jax.sharding import PartitionSpec as P

HEADS = 4
MAXLEN = 256
BLOCK = 128
ROWS = 16
epsilon = 1e-06
f32 = jnp.float32
bf16 = jnp.bfloat16

GROUP_BITS = (1, 2, 3)
FAR_BIT = 4
GROUP = 2 ** len(GROUP_BITS)
CHUNKS = 4 * GROUP
LAYER_VMEM = 60 * 2**20


def dot(a, b, contract):
    return lax.dot_general(a, b, ((contract[0], contract[1]), ((), ())), preferred_element_type=f32)


def mm(a, b):
    return dot(a, b, ((1,), (0,)))


def mm_nt(a, b):
    return dot(a, b, ((1,), (1,)))


def mm_tn(a, b):
    return dot(a, b, ((0,), (0,)))


def chunk_order(me):
    side = me & (1 << FAR_BIT)
    return [
        (me & 1 ^ other) + (member << GROUP_BITS[0]) + (side ^ far)
        for other in (0, 1)
        for member in range(GROUP)
        for far in (0, 1 << FAR_BIT)
    ]


def spans(count):
    for start in range(0, count, BLOCK):
        low = max(0, start - (MAXLEN - 1)) // BLOCK * BLOCK
        yield start, low, start + BLOCK


def center(values):
    values = values - jnp.mean(values, axis=-1, keepdims=True)
    return values, lax.rsqrt(jnp.mean(values * values, axis=-1, keepdims=True) + epsilon)


def pull_normalize(change, normed, scale):
    return scale * (
        change
        - jnp.mean(change, axis=-1, keepdims=True)
        - normed * jnp.mean(change * normed, axis=-1, keepdims=True)
    )


def pickers(slots, slot_ref, leaf_ref, leaves):
    count = slot_ref.shape[1]
    picker = lax.broadcasted_iota(jnp.int32, (slots, count), 0) == slot_ref[...]
    trees = leaf_ref.shape[0]
    each = leaves // trees
    spots = lax.broadcasted_iota(jnp.int32, (each, count), 0)
    onehot = [(spots == leaf_ref[t : t + 1, :]).astype(f32).astype(bf16) for t in range(trees)]
    return picker.astype(f32).astype(bf16), jnp.concatenate(onehot, axis=0)


def permute_rows(chunks, source, *targets):
    rows = targets[0].shape[0]
    for place, chunk in enumerate(chunks):
        start = pl.multiple_of(chunk * ROWS, ROWS)
        at = place * ROWS % rows
        targets[place * ROWS // rows][at : at + ROWS, :] = source[pl.ds(start, ROWS), :]


def lookup_kernel(asked_ref, table_ref, rows_ref, chosen_ref):
    count, each = asked_ref.shape
    many = count * each
    spot = lax.broadcasted_iota(jnp.int32, (count, table_ref.shape[0]), 1)
    parts = [(spot == asked_ref[:, k : k + 1]).astype(f32).astype(bf16) for k in range(each)]
    chosen = jnp.concatenate(parts, axis=0)
    to = lax.broadcasted_iota(jnp.int32, (many, many), 0)
    source = (to % each) * count + to // each
    order = (source == lax.broadcasted_iota(jnp.int32, (many, many), 1)).astype(f32).astype(bf16)
    chosen_ref[...] = mm(order, chosen).astype(bf16)
    rows_ref[...] = mm(chosen_ref[...], table_ref[...]).astype(bf16)


def run_lookup(asked, table):
    vmem = pl.BlockSpec(memory_space=pltpu.VMEM)
    shape = jax.ShapeDtypeStruct
    many = asked.shape[0] * asked.shape[1]
    return pl.pallas_call(
        lookup_kernel,
        name="lookup",
        out_shape=(shape((many, table.shape[1]), bf16), shape((many, table.shape[0]), bf16)),
        in_specs=[vmem, vmem],
        out_specs=(vmem,) * 2,
        compiler_params=pltpu.CompilerParams(vmem_limit_bytes=16 * 2**20),
    )(asked, table)


def layer_kernel(
    me_ref, lengths_ref, slot_ref, leaf_ref, rows_ref, table_hbm, in_hbm, out_hbm, tangent_hbm,
    output_hbm, d_rows_ref, keep_hbm, send_hbm,
    inputs, gated, d_pre, output, keep_ref, send_ref,
    normed, turned, moved, hidden, slope, weights, weights_slope, mixed, d_mixed,
    d_score, d_gated, allowed, d_inputs, leaf_grad, table, w_in, w_out, tangent, sems, out_sems,
):
    count, width = inputs.shape
    head = width // HEADS
    half_rows = width // 2
    copies = [
        pltpu.make_async_copy(source, target, sems.at[k])
        for k, (source, target) in enumerate(
            ((table_hbm, table), (in_hbm, w_in), (out_hbm, w_out), (tangent_hbm, tangent))
        )
    ]
    for copy in copies:
        copy.start()
    picker, onehot = pickers(rows_ref.shape[0], slot_ref, leaf_ref, table.shape[0])
    ends = []
    total = 0
    for place in range(lengths_ref.shape[1]):
        total = total + lengths_ref[0, place]
        ends.append(total)
    for start, low, high in spans(count):
        at = slice(start, start + BLOCK)
        row = start + lax.broadcasted_iota(jnp.int32, (BLOCK, high - low), 0)
        column = low + lax.broadcasted_iota(jnp.int32, (BLOCK, high - low), 1)
        first = jnp.zeros_like(row)
        for end in ends[:-1]:
            first = jnp.where(row >= end, end, first)
        allowed[at, low:high] = jnp.where(
            jnp.logical_and(column >= first, column <= row), 1.0, 0.0
        ).astype(f32)
    copies[0].wait()
    inputs[...] = (mm_tn(picker, rows_ref[...]) + mm_tn(onehot, table[...])).astype(bf16)
    for start in range(0, count, BLOCK):
        at = slice(start, start + BLOCK)
        values, scale = center(inputs[at, :].astype(f32))
        normed[at, :] = (values * scale).astype(bf16)
    turned[...] = normed[...].T
    copies[1].wait()
    for start in range(0, 4 * width, 2 * BLOCK):
        to = slice(start, start + 2 * BLOCK)
        half = mm(normed[...], w_in[:, to]) * 0.5
        curve = jnp.tanh(half)
        upper = 1.0 + curve
        hidden[:, to] = (half * upper).astype(bf16)
        slope[:, to] = (0.5 * upper * (1.0 + half * (1.0 - curve))).astype(bf16)
    weights[...] = jnp.zeros_like(weights)
    d_score[...] = jnp.zeros_like(d_score)
    half_scale = 0.5 * head ** (-0.5)
    for h in range(HEADS):
        value_at = slice(width + h * head, width + (h + 1) * head)
        query_at = slice(2 * width + h * head, 2 * width + (h + 1) * head)
        key_at = slice(3 * width + h * head, 3 * width + (h + 1) * head)
        for start, low, high in spans(count):
            at = slice(start, start + BLOCK)
            half = mm_nt(hidden[at, query_at], hidden[low:high, key_at]) * half_scale
            curve = jnp.tanh(half)
            upper = (1.0 + curve) * allowed[at, low:high]
            weights[h, at, low:high] = (half * upper).astype(bf16)
            weights_slope[h, at, low:high] = (
                half_scale * upper * (1.0 + half * (1.0 - curve))
            ).astype(bf16)
        for start in range(0, count, 2 * BLOCK):
            at = slice(start, start + 2 * BLOCK)
            high = start + 2 * BLOCK
            mixed[at, h * head : (h + 1) * head] = mm(
                weights[h, at, :high], hidden[:high, value_at]
            )
    copies[2].wait()
    copies[3].wait()
    d_gated[...] = mm_nt(tangent[...], w_out[...]).astype(bf16)
    for start in range(0, count, BLOCK):
        at = slice(start, start + BLOCK)
        values, scale = center(mixed[at, :])
        values = values * scale
        gates = hidden[at, :width].astype(f32)
        change = d_gated[at, :].astype(f32)
        gated[at, :] = (values * gates).astype(bf16)
        d_pre[at, :width] = (change * values * slope[at, :width].astype(f32)).astype(bf16)
        d_mixed[at, :] = pull_normalize(change * gates, values, scale).astype(bf16)
    for h in range(HEADS):
        own = slice(h * head, (h + 1) * head)
        value_at = slice(width + h * head, width + (h + 1) * head)
        query_at = slice(2 * width + h * head, 2 * width + (h + 1) * head)
        key_at = slice(3 * width + h * head, 3 * width + (h + 1) * head)
        for start, low, high in spans(count):
            at = slice(start, start + BLOCK)
            d_score[h, at, low:high] = (
                mm_nt(d_mixed[at, own], hidden[low:high, value_at])
                * weights_slope[h, at, low:high].astype(f32)
            ).astype(bf16)
        for start in range(0, count, 2 * BLOCK):
            at = slice(start, start + 2 * BLOCK)
            high = start + 2 * BLOCK
            d_query = mm(d_score[h, at, :high], hidden[:high, key_at])
            d_pre[at, query_at] = (d_query * slope[at, query_at].astype(f32)).astype(bf16)
            d_key = mm_tn(d_score[h, start:, at], hidden[start:, query_at])
            d_pre[at, key_at] = (d_key * slope[at, key_at].astype(f32)).astype(bf16)
            d_value = mm_tn(weights[h, start:, at], d_mixed[start:, own])
            d_pre[at, value_at] = (d_value * slope[at, value_at].astype(f32)).astype(bf16)
    chunks = chunk_order(me_ref[0])
    permute_rows(chunks, turned, moved)
    for start in range(0, 4 * width, 2 * BLOCK):
        to = slice(start, start + 2 * BLOCK)
        grad = mm(moved[...], d_pre[:, to]).astype(bf16)
        keep_ref[:, to] = grad[:half_rows, :]
        send_ref[:, to] = grad[half_rows:, :]
    leaving = []

    def leave(source, target):
        copy = pltpu.make_async_copy(source, target, out_sems.at[len(leaving)])
        copy.start()
        leaving.append(copy)

    leave(send_ref.at[:, : 4 * width], send_hbm.at[:, : 4 * width])
    leave(keep_ref.at[:, : 4 * width], keep_hbm.at[:, : 4 * width])
    turned[...] = gated[...].T
    permute_rows(chunks, turned, moved)
    grad = mm(moved[...], tangent[...]).astype(bf16)
    keep_ref[:, 4 * width : 5 * width] = grad[:half_rows, :]
    send_ref[:, 4 * width : 5 * width] = grad[half_rows:, :]
    output[...] = (mm(gated[...], w_out[...]) + inputs[...].astype(f32)).astype(bf16)
    leave(output, output_hbm)
    normed_change = mm_nt(d_pre[...], w_in[...])
    for start in range(0, count, BLOCK):
        at = slice(start, start + BLOCK)
        values, scale = center(inputs[at, :].astype(f32))
        change = pull_normalize(normed_change[at, :], values * scale, scale)
        d_inputs[at, :] = (change + tangent[at, :].astype(f32)).astype(bf16)
    leaves = table.shape[0]
    d_leaf = mm(onehot, d_inputs[...]).astype(bf16)
    leaf_grad[:leaves, :] = d_leaf[:, : width // 2]
    leaf_grad[leaves:, :] = d_leaf[:, width // 2 :]
    permute_rows(chunks, leaf_grad, keep_ref.at[:, 5 * width :], send_ref.at[:, 5 * width :])
    leave(send_ref.at[:, 4 * width :], send_hbm.at[:, 4 * width :])
    leave(keep_ref.at[:, 4 * width :], keep_hbm.at[:, 4 * width :])
    d_rows_ref[...] = mm(picker, d_inputs[...]).astype(bf16)
    for copy in leaving:
        copy.wait()


def run_layer(me, lengths, slot, leaf, rows, table, w_in, w_out, tangent):
    count, width = tangent.shape
    smem = pl.BlockSpec(memory_space=pltpu.SMEM)
    vmem = pl.BlockSpec(memory_space=pltpu.VMEM)
    hbm = pl.BlockSpec(memory_space=pltpu.HBM)
    shape = jax.ShapeDtypeStruct
    columns = 5 * width + width // 2
    return pl.pallas_call(
        layer_kernel,
        name="layer",
        out_shape=(
            shape((count, width), bf16),
            shape((rows.shape[0], width), bf16),
            shape((width // 2, columns), bf16),
            shape((width // 2, columns), bf16),
        ),
        in_specs=[smem, smem] + [vmem] * 3 + [hbm] * 4,
        out_specs=(hbm, vmem, hbm, hbm),
        scratch_shapes=[
            pltpu.VMEM((count, width), bf16),
            pltpu.VMEM((count, width), bf16),
            pltpu.VMEM((count, 4 * width), bf16),
            pltpu.VMEM((count, width), bf16),
            pltpu.VMEM((width // 2, columns), bf16),
            pltpu.VMEM((width // 2, columns), bf16),
            pltpu.VMEM((count, width), bf16),
            pltpu.VMEM((width, count), bf16),
            pltpu.VMEM((width, count), bf16),
            pltpu.VMEM((count, 4 * width), bf16),
            pltpu.VMEM((count, 4 * width), bf16),
            pltpu.VMEM((HEADS, count, count), bf16),
            pltpu.VMEM((HEADS, count, count), bf16),
            pltpu.VMEM((count, width), f32),
            pltpu.VMEM((count, width), bf16),
            pltpu.VMEM((HEADS, count, count), bf16),
            pltpu.VMEM((count, width), bf16),
            pltpu.VMEM((count, count), f32),
            pltpu.VMEM((count, width), bf16),
            pltpu.VMEM((width, width // 2), bf16),
            pltpu.VMEM(table.shape, bf16),
            pltpu.VMEM(w_in.shape, bf16),
            pltpu.VMEM(w_out.shape, bf16),
            pltpu.VMEM(tangent.shape, bf16),
            pltpu.SemaphoreType.DMA((4,)),
            pltpu.SemaphoreType.DMA((5,)),
        ],
        compiler_params=pltpu.CompilerParams(vmem_limit_bytes=LAYER_VMEM),
        cost_estimate=pl.CostEstimate(flops=6 * 10**9, bytes_accessed=10**7, transcendentals=10**6),
    )(me, lengths, slot, leaf, rows, table, w_in, w_out, tangent)


def finish_kernel(
    me_ref, chosen_ref, returned_ref, own_ref, other_ref,
    table_ref, leaf_ref, in_hbm, out_hbm, grads, sems,
):
    width, columns = grads.shape
    leaves = leaf_ref.shape[0]
    half_rows = width // 2
    chunks = chunk_order(me_ref[0])
    leaving = []
    for low in range(0, columns, width):
        high = min(low + width, columns)
        for place, chunk in enumerate(chunks):
            source = own_ref if place * ROWS < half_rows else other_ref
            at = place * ROWS % half_rows
            start = pl.multiple_of(chunk * ROWS, ROWS)
            grads[pl.ds(start, ROWS), low:high] = source[at : at + ROWS, low:high].astype(f32)
        if low < 5 * width:
            target = in_hbm.at[:, low:high] if low < 4 * width else out_hbm
            copy = pltpu.make_async_copy(grads.at[:, low:high], target, sems.at[len(leaving)])
            copy.start()
            leaving.append(copy)
    leaf_ref[:, : width // 2] = grads[:leaves, 5 * width :]
    leaf_ref[:, width // 2 :] = grads[leaves:, 5 * width :]
    table_ref[...] = mm_tn(chosen_ref[...], returned_ref[...])
    for copy in leaving:
        copy.wait()


def run_finish(me, chosen, returned, own, other, leaves):
    smem = pl.BlockSpec(memory_space=pltpu.SMEM)
    vmem = pl.BlockSpec(memory_space=pltpu.VMEM)
    hbm = pl.BlockSpec(memory_space=pltpu.HBM)
    shape = jax.ShapeDtypeStruct
    width = returned.shape[1]
    return pl.pallas_call(
        finish_kernel,
        name="finish",
        out_shape=(
            shape((chosen.shape[1], width), f32),
            shape((leaves, width), f32),
            shape((width, 4 * width), f32),
            shape((width, width), f32),
        ),
        in_specs=[smem] + [vmem] * 4,
        out_specs=(vmem, vmem, hbm, hbm),
        scratch_shapes=[
            pltpu.VMEM((width, own.shape[1]), f32),
            pltpu.SemaphoreType.DMA((5,)),
        ],
        compiler_params=pltpu.CompilerParams(vmem_limit_bytes=32 * 2**20),
    )(me, chosen, returned, own, other)


def exchange(blocks):
    return lax.all_to_all(blocks, ("dp", "rep"), split_axis=0, concat_axis=0, tiled=True)


def swap(block, mask, count):
    return lax.ppermute(block, ("dp", "rep"), [(i, i ^ mask) for i in range(count)])


def trade(blocks, count):
    low = GROUP_BITS[0]
    span = GROUP << low
    groups = [
        [base + rest + (member << low) for member in range(GROUP)]
        for base in range(0, count, span)
        for rest in range(1 << low)
    ]
    return lax.all_to_all(
        blocks, ("dp", "rep"), split_axis=0, concat_axis=0, axis_index_groups=groups, tiled=True
    )


def add(parts):
    return sum(part.astype(f32) for part in parts)


def reduce_and_gather(keep, send, d_rows, count):
    blocks = add((keep, swap(send, 1, count))).astype(bf16)
    blocks, d_rows = lax.optimization_barrier((blocks, d_rows))
    returned = exchange(d_rows)
    got = trade(blocks, count)
    got, returned = lax.optimization_barrier((got, returned))
    rows = got.shape[0] // GROUP
    total = add(got[member * rows : (member + 1) * rows] for member in range(GROUP))
    near, far = total[: rows // 2], total[rows // 2 :]
    own = near + swap(far.astype(bf16), 1 << FAR_BIT, count).astype(f32)
    reach = CHUNKS
    while reach < count:
        own = own + swap(own, reach, count)
        reach *= 2
    own = (own * (1.0 / count)).astype(bf16)
    own = jnp.concatenate([own, swap(own, 1 << FAR_BIT, count)], axis=0)
    copies = jnp.broadcast_to(own[None], (GROUP,) + own.shape).reshape(-1, own.shape[1])
    full = trade(copies, count)
    return returned, full, swap(full, 1, count)


def on_device(
    item_table, requests, event_slot, lengths, leaf_ids, leaf_table, w_in, w_out, cotangent
):
    count = lax.axis_size("dp") * lax.axis_size("rep")
    place = lax.axis_index(("dp", "rep")).astype(jnp.int32)
    me = (place & (CHUNKS - 1)).reshape(1)
    slot = event_slot.reshape(1, -1)
    leaf = leaf_ids.T
    asked = exchange(requests[0])
    fetched, chosen = run_lookup(asked, item_table)
    arrived = exchange(fetched)
    output, d_rows, keep, send = run_layer(
        me, lengths, slot, leaf, arrived, leaf_table, w_in, w_out, cotangent
    )
    returned, own, other = reduce_and_gather(keep, send, d_rows, count)
    table_grad, leaf_mean, in_mean, out_mean = run_finish(
        me, chosen, returned, own, other, leaf_table.shape[0]
    )
    return (output, table_grad, leaf_mean, in_mean, out_mean)


def solution(mesh):
    return jax.shard_map(
        on_device,
        mesh=mesh,
        in_specs=(
            P(("dp", "rep"), None),
            P(("dp", "rep"), None, None),
            P(("dp", "rep")),
            P(("dp", "rep"), None),
            P(("dp", "rep"), None),
            P(),
            P(),
            P(),
            P(("dp", "rep"), None),
        ),
        out_specs=(P(("dp", "rep"), None), P(("dp", "rep"), None), P(), P(), P()),
        check_vma=False,
    )
```

```python
import functools
import jax
import jax.numpy as jnp
from jax import lax
from jax.experimental import pallas as pl
from jax.experimental.pallas import tpu as pltpu
from jax.sharding import PartitionSpec as P

HEADS = 4
MAXLEN = 256
BLOCK = 128
ROWS = 16
epsilon = 1e-06
f32 = jnp.float32
bf16 = jnp.bfloat16

ROUTES = (((0,), (1, 2), (3, 4)), ((0,), (3,), (4,), (2,), (1,)))
SPLIT = 2048
CHUNKS = 32
LAYER_VMEM = 60 * 2**20


def dot(a, b, contract):
    return lax.dot_general(a, b, ((contract[0], contract[1]), ((), ())), preferred_element_type=f32)


def mm(a, b):
    return dot(a, b, ((1,), (0,)))


def mm_nt(a, b):
    return dot(a, b, ((1,), (1,)))


def mm_tn(a, b):
    return dot(a, b, ((0,), (0,)))


def mask_of(group, digit):
    return sum(((digit >> k) & 1) << bit for k, bit in enumerate(group))


def chunk_order(groups):
    masks = [0]
    for group in groups:
        masks = [mask ^ mask_of(group, digit) for mask in masks for digit in range(2 ** len(group))]
    return masks


def spans(count):
    for start in range(0, count, BLOCK):
        low = max(0, start - (MAXLEN - 1)) // BLOCK * BLOCK
        yield start, low, start + BLOCK


def center(values):
    values = values - jnp.mean(values, axis=-1, keepdims=True)
    return values, lax.rsqrt(jnp.mean(values * values, axis=-1, keepdims=True) + epsilon)


def pull_normalize(change, normed, scale):
    return scale * (
        change
        - jnp.mean(change, axis=-1, keepdims=True)
        - normed * jnp.mean(change * normed, axis=-1, keepdims=True)
    )


def pickers(slots, slot_ref, leaf_ref, leaves):
    count = slot_ref.shape[1]
    picker = lax.broadcasted_iota(jnp.int32, (slots, count), 0) == slot_ref[...]
    trees = leaf_ref.shape[0]
    each = leaves // trees
    spots = lax.broadcasted_iota(jnp.int32, (each, count), 0)
    onehot = [(spots == leaf_ref[t : t + 1, :]).astype(f32).astype(bf16) for t in range(trees)]
    return picker.astype(f32).astype(bf16), jnp.concatenate(onehot, axis=0)


def permute_rows(me, order, source, target):
    for place, mask in enumerate(order):
        start = pl.multiple_of((me ^ mask) * ROWS, ROWS)
        target[place * ROWS : (place + 1) * ROWS, :] = source[pl.ds(start, ROWS), :]


def lookup_kernel(asked_ref, table_ref, rows_ref, chosen_ref):
    count, each = asked_ref.shape
    many = count * each
    spot = lax.broadcasted_iota(jnp.int32, (count, table_ref.shape[0]), 1)
    parts = [(spot == asked_ref[:, k : k + 1]).astype(f32).astype(bf16) for k in range(each)]
    chosen = jnp.concatenate(parts, axis=0)
    to = lax.broadcasted_iota(jnp.int32, (many, many), 0)
    source = (to % each) * count + to // each
    order = (source == lax.broadcasted_iota(jnp.int32, (many, many), 1)).astype(f32).astype(bf16)
    chosen_ref[...] = mm(order, chosen).astype(bf16)
    rows_ref[...] = mm(chosen_ref[...], table_ref[...]).astype(bf16)


def run_lookup(asked, table):
    vmem = pl.BlockSpec(memory_space=pltpu.VMEM)
    shape = jax.ShapeDtypeStruct
    many = asked.shape[0] * asked.shape[1]
    return pl.pallas_call(
        lookup_kernel,
        name="lookup",
        out_shape=(shape((many, table.shape[1]), bf16), shape((many, table.shape[0]), bf16)),
        in_specs=[vmem, vmem],
        out_specs=(vmem,) * 2,
        compiler_params=pltpu.CompilerParams(vmem_limit_bytes=16 * 2**20),
    )(asked, table)


def layer_kernel(
    me_ref, lengths_ref, slot_ref, leaf_ref, rows_ref, table_hbm, in_hbm, out_hbm, tangent_hbm,
    output_hbm, d_rows_ref, keep_hbm, send_hbm, keep_late_hbm, send_late_hbm,
    inputs, gated, d_pre, grads, output,
    normed, turned, moved, hidden, slope, weights, weights_slope, mixed, d_mixed,
    d_score, d_gated, allowed, d_inputs, leaf_grad, table, w_in, w_out, tangent, sems, out_sems,
):
    count, width = inputs.shape
    head = width // HEADS
    half_rows = width // 2
    copies = [
        pltpu.make_async_copy(source, target, sems.at[k])
        for k, (source, target) in enumerate(
            ((table_hbm, table), (in_hbm, w_in), (out_hbm, w_out), (tangent_hbm, tangent))
        )
    ]
    for copy in copies:
        copy.start()
    leaving = []

    def leave(source, target):
        copy = pltpu.make_async_copy(source, target, out_sems.at[len(leaving)])
        copy.start()
        leaving.append(copy)

    picker, onehot = pickers(rows_ref.shape[0], slot_ref, leaf_ref, table.shape[0])
    ends = []
    total = 0
    for place in range(lengths_ref.shape[1]):
        total = total + lengths_ref[0, place]
        ends.append(total)
    for start, low, high in spans(count):
        at = slice(start, start + BLOCK)
        row = start + lax.broadcasted_iota(jnp.int32, (BLOCK, high - low), 0)
        column = low + lax.broadcasted_iota(jnp.int32, (BLOCK, high - low), 1)
        first = jnp.zeros_like(row)
        for end in ends[:-1]:
            first = jnp.where(row >= end, end, first)
        allowed[at, low:high] = jnp.where(
            jnp.logical_and(column >= first, column <= row), 1.0, 0.0
        ).astype(f32)
    copies[0].wait()
    inputs[...] = (mm_tn(picker, rows_ref[...]) + mm_tn(onehot, table[...])).astype(bf16)
    for start in range(0, count, BLOCK):
        at = slice(start, start + BLOCK)
        values, scale = center(inputs[at, :].astype(f32))
        normed[at, :] = (values * scale).astype(bf16)
    turned[...] = normed[...].T
    copies[1].wait()
    for start in range(0, 4 * width, 2 * BLOCK):
        to = slice(start, start + 2 * BLOCK)
        half = mm(normed[...], w_in[:, to]) * 0.5
        curve = jnp.tanh(half)
        upper = 1.0 + curve
        hidden[:, to] = (half * upper).astype(bf16)
        slope[:, to] = (0.5 * upper * (1.0 + half * (1.0 - curve))).astype(bf16)
    weights[...] = jnp.zeros_like(weights)
    d_score[...] = jnp.zeros_like(d_score)
    half_scale = 0.5 * head ** (-0.5)
    for h in range(HEADS):
        value_at = slice(width + h * head, width + (h + 1) * head)
        query_at = slice(2 * width + h * head, 2 * width + (h + 1) * head)
        key_at = slice(3 * width + h * head, 3 * width + (h + 1) * head)
        for start, low, high in spans(count):
            at = slice(start, start + BLOCK)
            half = mm_nt(hidden[at, query_at], hidden[low:high, key_at]) * half_scale
            curve = jnp.tanh(half)
            upper = (1.0 + curve) * allowed[at, low:high]
            weights[h, at, low:high] = (half * upper).astype(bf16)
            weights_slope[h, at, low:high] = (
                half_scale * upper * (1.0 + half * (1.0 - curve))
            ).astype(bf16)
        for start in range(0, count, 2 * BLOCK):
            at = slice(start, start + 2 * BLOCK)
            high = start + 2 * BLOCK
            mixed[at, h * head : (h + 1) * head] = mm(
                weights[h, at, :high], hidden[:high, value_at]
            )
    copies[2].wait()
    copies[3].wait()
    d_gated[...] = mm_nt(tangent[...], w_out[...]).astype(bf16)
    for start in range(0, count, BLOCK):
        at = slice(start, start + BLOCK)
        values, scale = center(mixed[at, :])
        values = values * scale
        gates = hidden[at, :width].astype(f32)
        change = d_gated[at, :].astype(f32)
        gated[at, :] = (values * gates).astype(bf16)
        d_pre[at, :width] = (change * values * slope[at, :width].astype(f32)).astype(bf16)
        d_mixed[at, :] = pull_normalize(change * gates, values, scale).astype(bf16)
    for h in range(HEADS):
        own = slice(h * head, (h + 1) * head)
        value_at = slice(width + h * head, width + (h + 1) * head)
        query_at = slice(2 * width + h * head, 2 * width + (h + 1) * head)
        key_at = slice(3 * width + h * head, 3 * width + (h + 1) * head)
        for start, low, high in spans(count):
            at = slice(start, start + BLOCK)
            d_score[h, at, low:high] = (
                mm_nt(d_mixed[at, own], hidden[low:high, value_at])
                * weights_slope[h, at, low:high].astype(f32)
            ).astype(bf16)
        for start in range(0, count, 2 * BLOCK):
            at = slice(start, start + 2 * BLOCK)
            high = start + 2 * BLOCK
            d_query = mm(d_score[h, at, :high], hidden[:high, key_at])
            d_pre[at, query_at] = (d_query * slope[at, query_at].astype(f32)).astype(bf16)
            d_key = mm_tn(d_score[h, start:, at], hidden[start:, query_at])
            d_pre[at, key_at] = (d_key * slope[at, key_at].astype(f32)).astype(bf16)
            d_value = mm_tn(weights[h, start:, at], d_mixed[start:, own])
            d_pre[at, value_at] = (d_value * slope[at, value_at].astype(f32)).astype(bf16)
    me = me_ref[0]
    early, late = (chunk_order(route) for route in ROUTES)
    permute_rows(me, early, turned, moved)
    for start in range(0, 4 * width, 2 * BLOCK):
        to = slice(start, start + 2 * BLOCK)
        grads[:, to] = mm(moved[...], d_pre[:, to]).astype(bf16)
    leave(grads.at[half_rows:, :SPLIT], send_hbm)
    leave(grads.at[:half_rows, :SPLIT], keep_hbm)
    turned[...] = gated[...].T
    permute_rows(me, late, turned, moved)
    grads[:, 4 * width : 5 * width] = mm(moved[...], tangent[...]).astype(bf16)
    normed_change = mm_nt(d_pre[...], w_in[...])
    for start in range(0, count, BLOCK):
        at = slice(start, start + BLOCK)
        values, scale = center(inputs[at, :].astype(f32))
        change = pull_normalize(normed_change[at, :], values * scale, scale)
        d_inputs[at, :] = (change + tangent[at, :].astype(f32)).astype(bf16)
    leaves = table.shape[0]
    d_leaf = mm(onehot, d_inputs[...]).astype(bf16)
    leaf_grad[:leaves, :] = d_leaf[:, : width // 2]
    leaf_grad[leaves:, :] = d_leaf[:, width // 2 :]
    permute_rows(me, late, leaf_grad, grads.at[:, 5 * width :])
    leave(grads.at[half_rows:, SPLIT:], send_late_hbm)
    leave(grads.at[:half_rows, SPLIT:], keep_late_hbm)
    d_rows_ref[...] = mm(picker, d_inputs[...]).astype(bf16)
    output[...] = (mm(gated[...], w_out[...]) + inputs[...].astype(f32)).astype(bf16)
    leave(output, output_hbm)
    for copy in leaving:
        copy.wait()


def run_layer(me, lengths, slot, leaf, rows, table, w_in, w_out, tangent):
    count, width = tangent.shape
    smem = pl.BlockSpec(memory_space=pltpu.SMEM)
    vmem = pl.BlockSpec(memory_space=pltpu.VMEM)
    hbm = pl.BlockSpec(memory_space=pltpu.HBM)
    shape = jax.ShapeDtypeStruct
    columns = 5 * width + width // 2
    return pl.pallas_call(
        layer_kernel,
        name="layer",
        out_shape=(
            shape((count, width), bf16),
            shape((rows.shape[0], width), bf16),
            shape((width // 2, SPLIT), bf16),
            shape((width // 2, SPLIT), bf16),
            shape((width // 2, columns - SPLIT), bf16),
            shape((width // 2, columns - SPLIT), bf16),
        ),
        in_specs=[smem, smem] + [vmem] * 3 + [hbm] * 4,
        out_specs=(hbm, vmem, hbm, hbm, hbm, hbm),
        scratch_shapes=[
            pltpu.VMEM((count, width), bf16),
            pltpu.VMEM((count, width), bf16),
            pltpu.VMEM((count, 4 * width), bf16),
            pltpu.VMEM((width, columns), bf16),
            pltpu.VMEM((count, width), bf16),
            pltpu.VMEM((count, width), bf16),
            pltpu.VMEM((width, count), bf16),
            pltpu.VMEM((width, count), bf16),
            pltpu.VMEM((count, 4 * width), bf16),
            pltpu.VMEM((count, 4 * width), bf16),
            pltpu.VMEM((HEADS, count, count), bf16),
            pltpu.VMEM((HEADS, count, count), bf16),
            pltpu.VMEM((count, width), f32),
            pltpu.VMEM((count, width), bf16),
            pltpu.VMEM((HEADS, count, count), bf16),
            pltpu.VMEM((count, width), bf16),
            pltpu.VMEM((count, count), f32),
            pltpu.VMEM((count, width), bf16),
            pltpu.VMEM((width, width // 2), bf16),
            pltpu.VMEM(table.shape, bf16),
            pltpu.VMEM(w_in.shape, bf16),
            pltpu.VMEM(w_out.shape, bf16),
            pltpu.VMEM(tangent.shape, bf16),
            pltpu.SemaphoreType.DMA((4,)),
            pltpu.SemaphoreType.DMA((5,)),
        ],
        compiler_params=pltpu.CompilerParams(vmem_limit_bytes=LAYER_VMEM),
        cost_estimate=pl.CostEstimate(flops=6 * 10**9, bytes_accessed=10**7, transcendentals=10**6),
    )(me, lengths, slot, leaf, rows, table, w_in, w_out, tangent)


def finish_kernel(
    me_ref, chosen_ref, returned_ref, early_own, early_other, late_own, late_other,
    table_ref, leaf_ref, in_hbm, out_hbm, grads, sems,
):
    width, columns = grads.shape
    leaves = leaf_ref.shape[0]
    me = me_ref[0]
    half_rows = width // 2
    leaving = []

    def leave(source, target):
        copy = pltpu.make_async_copy(source, target, sems.at[len(leaving)])
        copy.start()
        leaving.append(copy)

    def place(route, own, other, low, high, at):
        for spot, mask in enumerate(chunk_order(route)):
            source = own if spot * ROWS < half_rows else other
            row = spot * ROWS % half_rows
            start = pl.multiple_of((me ^ mask) * ROWS, ROWS)
            grads[pl.ds(start, ROWS), at + low : at + high] = source[
                row : row + ROWS, low:high
            ].astype(f32)

    for low in range(0, SPLIT, width):
        place(ROUTES[0], early_own, early_other, low, low + width, 0)
        leave(grads.at[:, low : low + width], in_hbm.at[:, low : low + width])
    place(ROUTES[1], late_own, late_other, 0, width, SPLIT)
    leave(grads.at[:, SPLIT : SPLIT + width], out_hbm)
    place(ROUTES[1], late_own, late_other, width, columns - SPLIT, SPLIT)
    leaf_ref[:, : width // 2] = grads[:leaves, 5 * width :]
    leaf_ref[:, width // 2 :] = grads[leaves:, 5 * width :]
    table_ref[...] = mm_tn(chosen_ref[...], returned_ref[...])
    for copy in leaving:
        copy.wait()


def run_finish(me, chosen, returned, early_own, early_other, late_own, late_other, leaves):
    smem = pl.BlockSpec(memory_space=pltpu.SMEM)
    vmem = pl.BlockSpec(memory_space=pltpu.VMEM)
    hbm = pl.BlockSpec(memory_space=pltpu.HBM)
    shape = jax.ShapeDtypeStruct
    width = returned.shape[1]
    return pl.pallas_call(
        finish_kernel,
        name="finish",
        out_shape=(
            shape((chosen.shape[1], width), f32),
            shape((leaves, width), f32),
            shape((width, 4 * width), f32),
            shape((width, width), f32),
        ),
        in_specs=[smem] + [vmem] * 6,
        out_specs=(vmem, vmem, hbm, hbm),
        scratch_shapes=[
            pltpu.VMEM((width, early_own.shape[1] + late_own.shape[1]), f32),
            pltpu.SemaphoreType.DMA((5,)),
        ],
        compiler_params=pltpu.CompilerParams(vmem_limit_bytes=32 * 2**20),
    )(me, chosen, returned, early_own, early_other, late_own, late_other)


def exchange(blocks):
    return lax.all_to_all(blocks, ("dp", "rep"), split_axis=0, concat_axis=0, tiled=True)


def swap(block, mask, count):
    return lax.ppermute(block, ("dp", "rep"), [(i, i ^ mask) for i in range(count)])


def add(parts):
    return sum(part.astype(f32) for part in parts)


def shares(parts, group):
    size = 2 ** len(group)
    rows = parts[0].shape[0] // size
    return [
        add(part[digit * rows : (digit + 1) * rows] for part in parts).astype(bf16)
        for digit in range(1, size)
    ]


def swap_all(blocks, group, count):
    return [
        swap(block, mask_of(group, digit), count) for digit, block in enumerate(blocks, start=1)
    ]


def extend(parts, got):
    return [part[: got[0].shape[0]] for part in parts] + got


def split_up(parts, group, count):
    return extend(parts, swap_all(shares(parts, group), group, count))


def join(block, group, count):
    pieces = swap_all([block] * (2 ** len(group) - 1), group, count)
    return jnp.concatenate([block] + pieces, axis=0)


def reduce_and_gather(early, late, d_rows, count):
    _, near, far = ROUTES[0]
    _, first, second, third, fourth = ROUTES[1]
    early = [early[0], swap(early[1], 1, count)]
    late = [late[0], swap(late[1], 1, count)]
    early_blocks, late_blocks, d_rows = lax.optimization_barrier(
        (shares(early, near), shares(late, first), d_rows)
    )
    early_got = swap_all(early_blocks, near, count)
    late = split_up(extend(late, swap_all(late_blocks, first, count)), second, count)
    returned = exchange(d_rows)
    early_got, late, returned = lax.optimization_barrier((early_got, late, returned))
    early = split_up(extend(early, early_got), far, count)
    late = split_up(split_up(late, third, count), fourth, count)
    own = [add(early), add(late)]
    reach = CHUNKS
    while reach < count:
        own = [part + swap(part, reach, count) for part in own]
        reach *= 2
    early, late = lax.optimization_barrier(
        tuple((part * (1.0 / count)).astype(bf16) for part in own)
    )
    early = join(early, far, count)
    late = join(join(late, fourth, count), third, count)
    early, late = lax.optimization_barrier((early, late))
    pieces = swap_all([early] * (2 ** len(near) - 1), near, count)
    late = join(join(late, second, count), first, count)
    pieces, late = lax.optimization_barrier((pieces, late))
    early = jnp.concatenate([early] + pieces, axis=0)
    return returned, early, swap(early, 1, count), late, swap(late, 1, count)


def on_device(
    item_table, requests, event_slot, lengths, leaf_ids, leaf_table, w_in, w_out, cotangent
):
    count = lax.axis_size("dp") * lax.axis_size("rep")
    place = lax.axis_index(("dp", "rep")).astype(jnp.int32)
    me = (place & (CHUNKS - 1)).reshape(1)
    slot = event_slot.reshape(1, -1)
    leaf = leaf_ids.T
    asked = exchange(requests[0])
    fetched, chosen = run_lookup(asked, item_table)
    arrived = exchange(fetched)
    output, d_rows, keep, send, keep_late, send_late = run_layer(
        me, lengths, slot, leaf, arrived, leaf_table, w_in, w_out, cotangent
    )
    returned, early, early_other, late, late_other = reduce_and_gather(
        (keep, send), (keep_late, send_late), d_rows, count
    )
    table_grad, leaf_mean, in_mean, out_mean = run_finish(
        me, chosen, returned, early, early_other, late, late_other, leaf_table.shape[0]
    )
    return (output, table_grad, leaf_mean, in_mean, out_mean)


def solution(mesh):
    return jax.shard_map(
        on_device,
        mesh=mesh,
        in_specs=(
            P(("dp", "rep"), None),
            P(("dp", "rep"), None, None),
            P(("dp", "rep")),
            P(("dp", "rep"), None),
            P(("dp", "rep"), None),
            P(),
            P(),
            P(),
            P(("dp", "rep"), None),
        ),
        out_specs=(P(("dp", "rep"), None), P(("dp", "rep"), None), P(), P(), P()),
        check_vma=False,
    )
```

```python
import functools
import jax
import jax.numpy as jnp
from jax import lax
from jax.experimental import pallas as pl
from jax.experimental.pallas import tpu as pltpu
from jax.sharding import PartitionSpec as P

HEADS = 4
MAXLEN = 256
BLOCK = 128
ROWS = 16
epsilon = 1e-06
f32 = jnp.float32
bf16 = jnp.bfloat16

ROUTES = (((0,), (1, 2), (3, 4)), ((0,), (3,), (4,), (2,), (1,)))
SPLIT = 2048
CHUNKS = 32
LAYER_VMEM = 60 * 2**20


def dot(a, b, contract):
    return lax.dot_general(a, b, ((contract[0], contract[1]), ((), ())), preferred_element_type=f32)


def mm(a, b):
    return dot(a, b, ((1,), (0,)))


def mm_nt(a, b):
    return dot(a, b, ((1,), (1,)))


def mm_tn(a, b):
    return dot(a, b, ((0,), (0,)))


def mask_of(group, digit):
    return sum(((digit >> k) & 1) << bit for k, bit in enumerate(group))


def chunk_order(groups):
    masks = [0]
    for group in groups:
        masks = [mask ^ mask_of(group, digit) for mask in masks for digit in range(2 ** len(group))]
    return masks


def spans(count):
    for start in range(0, count, BLOCK):
        low = max(0, start - (MAXLEN - 1)) // BLOCK * BLOCK
        yield start, low, start + BLOCK


def center(values):
    values = values - jnp.mean(values, axis=-1, keepdims=True)
    return values, lax.rsqrt(jnp.mean(values * values, axis=-1, keepdims=True) + epsilon)


def pull_normalize(change, normed, scale):
    return scale * (
        change
        - jnp.mean(change, axis=-1, keepdims=True)
        - normed * jnp.mean(change * normed, axis=-1, keepdims=True)
    )


def pickers(slots, slot_ref, leaf_ref, leaves):
    count = slot_ref.shape[1]
    picker = lax.broadcasted_iota(jnp.int32, (slots, count), 0) == slot_ref[...]
    trees = leaf_ref.shape[0]
    each = leaves // trees
    spots = lax.broadcasted_iota(jnp.int32, (each, count), 0)
    onehot = [(spots == leaf_ref[t : t + 1, :]).astype(f32).astype(bf16) for t in range(trees)]
    return picker.astype(f32).astype(bf16), jnp.concatenate(onehot, axis=0)


def permute_rows(me, order, source, target):
    for place, mask in enumerate(order):
        start = pl.multiple_of((me ^ mask) * ROWS, ROWS)
        target[place * ROWS : (place + 1) * ROWS, :] = source[pl.ds(start, ROWS), :]


def lookup_kernel(asked_ref, table_ref, rows_ref, chosen_ref):
    count, each = asked_ref.shape
    many = count * each
    spot = lax.broadcasted_iota(jnp.int32, (count, table_ref.shape[0]), 1)
    parts = [(spot == asked_ref[:, k : k + 1]).astype(f32).astype(bf16) for k in range(each)]
    chosen = jnp.concatenate(parts, axis=0)
    to = lax.broadcasted_iota(jnp.int32, (many, many), 0)
    source = (to % each) * count + to // each
    order = (source == lax.broadcasted_iota(jnp.int32, (many, many), 1)).astype(f32).astype(bf16)
    chosen_ref[...] = mm(order, chosen).astype(bf16)
    rows = mm(chosen_ref[...], table_ref[...]).astype(bf16)
    rows_ref[...] = rows.reshape(rows_ref.shape)


def run_lookup(asked, table):
    vmem = pl.BlockSpec(memory_space=pltpu.VMEM)
    shape = jax.ShapeDtypeStruct
    many = asked.shape[0] * asked.shape[1]
    return pl.pallas_call(
        lookup_kernel,
        name="lookup",
        out_shape=(
            shape(asked.shape + table.shape[1:], bf16),
            shape((many, table.shape[0]), bf16),
        ),
        in_specs=[vmem, vmem],
        out_specs=(vmem,) * 2,
        compiler_params=pltpu.CompilerParams(vmem_limit_bytes=16 * 2**20),
    )(asked, table)


def layer_kernel(
    me_ref, lengths_ref, slot_ref, leaf_ref, rows_ref, table_hbm, in_hbm, out_hbm, tangent_hbm,
    output_hbm, d_rows_ref, keep_hbm, send_hbm, keep_late_hbm, send_late_hbm,
    inputs, gated, d_pre, grads, output,
    normed, turned, moved, hidden, slope, weights, weights_slope, mixed, d_mixed,
    d_score, d_gated, allowed, d_inputs, leaf_grad, table, w_in, w_out, tangent, sems, out_sems,
):
    count, width = inputs.shape
    head = width // HEADS
    half_rows = width // 2
    copies = [
        pltpu.make_async_copy(source, target, sems.at[k])
        for k, (source, target) in enumerate(
            ((table_hbm, table), (in_hbm, w_in), (out_hbm, w_out), (tangent_hbm, tangent))
        )
    ]
    for copy in copies:
        copy.start()
    leaving = []

    def leave(source, target):
        copy = pltpu.make_async_copy(source, target, out_sems.at[len(leaving)])
        copy.start()
        leaving.append(copy)

    rows = rows_ref[...].reshape(-1, width)
    picker, onehot = pickers(rows.shape[0], slot_ref, leaf_ref, table.shape[0])
    ends = []
    total = 0
    for place in range(lengths_ref.shape[1]):
        total = total + lengths_ref[0, place]
        ends.append(total)
    for start, low, high in spans(count):
        at = slice(start, start + BLOCK)
        row = start + lax.broadcasted_iota(jnp.int32, (BLOCK, high - low), 0)
        column = low + lax.broadcasted_iota(jnp.int32, (BLOCK, high - low), 1)
        first = jnp.zeros_like(row)
        for end in ends[:-1]:
            first = jnp.where(row >= end, end, first)
        allowed[at, low:high] = jnp.where(
            jnp.logical_and(column >= first, column <= row), 1.0, 0.0
        ).astype(f32)
    copies[0].wait()
    inputs[...] = (mm_tn(picker, rows) + mm_tn(onehot, table[...])).astype(bf16)
    for start in range(0, count, BLOCK):
        at = slice(start, start + BLOCK)
        values, scale = center(inputs[at, :].astype(f32))
        normed[at, :] = (values * scale).astype(bf16)
    turned[...] = normed[...].T
    copies[1].wait()
    for start in range(0, 4 * width, 2 * BLOCK):
        to = slice(start, start + 2 * BLOCK)
        half = mm(normed[...], w_in[:, to]) * 0.5
        curve = jnp.tanh(half)
        upper = 1.0 + curve
        hidden[:, to] = (half * upper).astype(bf16)
        slope[:, to] = (0.5 * upper * (1.0 + half * (1.0 - curve))).astype(bf16)
    for start, low, high in spans(count):
        at = slice(start, start + BLOCK)
        end = start // (2 * BLOCK) * 2 * BLOCK + 2 * BLOCK
        for out in (slice(0, low), slice(high, end)):
            if out.start < out.stop:
                nothing = jnp.zeros((HEADS, BLOCK, out.stop - out.start), bf16)
                weights[:, at, out] = nothing
                d_score[:, at, out] = nothing
    half_scale = 0.5 * head ** (-0.5)
    for h in range(HEADS):
        value_at = slice(width + h * head, width + (h + 1) * head)
        query_at = slice(2 * width + h * head, 2 * width + (h + 1) * head)
        key_at = slice(3 * width + h * head, 3 * width + (h + 1) * head)
        for start, low, high in spans(count):
            at = slice(start, start + BLOCK)
            half = mm_nt(hidden[at, query_at], hidden[low:high, key_at]) * half_scale
            curve = jnp.tanh(half)
            upper = (1.0 + curve) * allowed[at, low:high]
            weights[h, at, low:high] = (half * upper).astype(bf16)
            weights_slope[h, at, low:high] = (
                half_scale * upper * (1.0 + half * (1.0 - curve))
            ).astype(bf16)
        for start in range(0, count, 2 * BLOCK):
            at = slice(start, start + 2 * BLOCK)
            high = start + 2 * BLOCK
            mixed[at, h * head : (h + 1) * head] = mm(
                weights[h, at, :high], hidden[:high, value_at]
            )
    copies[2].wait()
    copies[3].wait()
    d_gated[...] = mm_nt(tangent[...], w_out[...]).astype(bf16)
    for start in range(0, count, BLOCK):
        at = slice(start, start + BLOCK)
        values, scale = center(mixed[at, :])
        values = values * scale
        gates = hidden[at, :width].astype(f32)
        change = d_gated[at, :].astype(f32)
        gated[at, :] = (values * gates).astype(bf16)
        d_pre[at, :width] = (change * values * slope[at, :width].astype(f32)).astype(bf16)
        d_mixed[at, :] = pull_normalize(change * gates, values, scale).astype(bf16)
    for h in range(HEADS):
        own = slice(h * head, (h + 1) * head)
        value_at = slice(width + h * head, width + (h + 1) * head)
        query_at = slice(2 * width + h * head, 2 * width + (h + 1) * head)
        key_at = slice(3 * width + h * head, 3 * width + (h + 1) * head)
        for start, low, high in spans(count):
            at = slice(start, start + BLOCK)
            d_score[h, at, low:high] = (
                mm_nt(d_mixed[at, own], hidden[low:high, value_at])
                * weights_slope[h, at, low:high].astype(f32)
            ).astype(bf16)
        for start in range(0, count, 2 * BLOCK):
            at = slice(start, start + 2 * BLOCK)
            high = start + 2 * BLOCK
            d_query = mm(d_score[h, at, :high], hidden[:high, key_at])
            d_pre[at, query_at] = (d_query * slope[at, query_at].astype(f32)).astype(bf16)
            d_key = mm_tn(d_score[h, start:, at], hidden[start:, query_at])
            d_pre[at, key_at] = (d_key * slope[at, key_at].astype(f32)).astype(bf16)
            d_value = mm_tn(weights[h, start:, at], d_mixed[start:, own])
            d_pre[at, value_at] = (d_value * slope[at, value_at].astype(f32)).astype(bf16)
    me = me_ref[0]
    early, late = (chunk_order(route) for route in ROUTES)
    permute_rows(me, early, turned, moved)
    for start in range(0, 4 * width, 2 * BLOCK):
        to = slice(start, start + 2 * BLOCK)
        grads[:, to] = mm(moved[...], d_pre[:, to]).astype(bf16)
    leave(grads.at[half_rows:, :SPLIT], send_hbm)
    leave(grads.at[:half_rows, :SPLIT], keep_hbm)
    turned[...] = gated[...].T
    permute_rows(me, late, turned, moved)
    grads[:, 4 * width : 5 * width] = mm(moved[...], tangent[...]).astype(bf16)
    normed_change = mm_nt(d_pre[...], w_in[...])
    for start in range(0, count, BLOCK):
        at = slice(start, start + BLOCK)
        values, scale = center(inputs[at, :].astype(f32))
        change = pull_normalize(normed_change[at, :], values * scale, scale)
        d_inputs[at, :] = (change + tangent[at, :].astype(f32)).astype(bf16)
    leaves = table.shape[0]
    d_leaf = mm(onehot, d_inputs[...]).astype(bf16)
    leaf_grad[:leaves, :] = d_leaf[:, : width // 2]
    leaf_grad[leaves:, :] = d_leaf[:, width // 2 :]
    permute_rows(me, late, leaf_grad, grads.at[:, 5 * width :])
    leave(grads.at[half_rows:, SPLIT:], send_late_hbm)
    leave(grads.at[:half_rows, SPLIT:], keep_late_hbm)
    d_rows = mm(picker, d_inputs[...]).astype(bf16)
    d_rows_ref[...] = d_rows.reshape(d_rows_ref.shape)
    output[...] = (mm(gated[...], w_out[...]) + inputs[...].astype(f32)).astype(bf16)
    leave(output, output_hbm)
    for copy in leaving:
        copy.wait()


def run_layer(me, lengths, slot, leaf, rows, table, w_in, w_out, tangent):
    count, width = tangent.shape
    smem = pl.BlockSpec(memory_space=pltpu.SMEM)
    vmem = pl.BlockSpec(memory_space=pltpu.VMEM)
    hbm = pl.BlockSpec(memory_space=pltpu.HBM)
    shape = jax.ShapeDtypeStruct
    columns = 5 * width + width // 2
    return pl.pallas_call(
        layer_kernel,
        name="layer",
        out_shape=(
            shape((count, width), bf16),
            shape(rows.shape, bf16),
            shape((width // 2, SPLIT), bf16),
            shape((width // 2, SPLIT), bf16),
            shape((width // 2, columns - SPLIT), bf16),
            shape((width // 2, columns - SPLIT), bf16),
        ),
        in_specs=[smem, smem] + [vmem] * 3 + [hbm] * 4,
        out_specs=(hbm, vmem, hbm, hbm, hbm, hbm),
        scratch_shapes=[
            pltpu.VMEM((count, width), bf16),
            pltpu.VMEM((count, width), bf16),
            pltpu.VMEM((count, 4 * width), bf16),
            pltpu.VMEM((width, columns), bf16),
            pltpu.VMEM((count, width), bf16),
            pltpu.VMEM((count, width), bf16),
            pltpu.VMEM((width, count), bf16),
            pltpu.VMEM((width, count), bf16),
            pltpu.VMEM((count, 4 * width), bf16),
            pltpu.VMEM((count, 4 * width), bf16),
            pltpu.VMEM((HEADS, count, count), bf16),
            pltpu.VMEM((HEADS, count, count), bf16),
            pltpu.VMEM((count, width), f32),
            pltpu.VMEM((count, width), bf16),
            pltpu.VMEM((HEADS, count, count), bf16),
            pltpu.VMEM((count, width), bf16),
            pltpu.VMEM((count, count), f32),
            pltpu.VMEM((count, width), bf16),
            pltpu.VMEM((width, width // 2), bf16),
            pltpu.VMEM(table.shape, bf16),
            pltpu.VMEM(w_in.shape, bf16),
            pltpu.VMEM(w_out.shape, bf16),
            pltpu.VMEM(tangent.shape, bf16),
            pltpu.SemaphoreType.DMA((4,)),
            pltpu.SemaphoreType.DMA((5,)),
        ],
        compiler_params=pltpu.CompilerParams(vmem_limit_bytes=LAYER_VMEM),
        cost_estimate=pl.CostEstimate(flops=6 * 10**9, bytes_accessed=10**7, transcendentals=10**6),
    )(me, lengths, slot, leaf, rows, table, w_in, w_out, tangent)


def finish_kernel(
    me_ref, chosen_ref, returned_ref, early_own, early_other, late_own, late_other,
    table_ref, leaf_ref, in_hbm, out_hbm, grads, sems,
):
    width, columns = grads.shape
    leaves = leaf_ref.shape[0]
    me = me_ref[0]
    half_rows = width // 2
    leaving = []

    def leave(source, target):
        copy = pltpu.make_async_copy(source, target, sems.at[len(leaving)])
        copy.start()
        leaving.append(copy)

    def place(route, own, other, low, high, at):
        for spot, mask in enumerate(chunk_order(route)):
            source = own if spot * ROWS < half_rows else other
            row = spot * ROWS % half_rows
            start = pl.multiple_of((me ^ mask) * ROWS, ROWS)
            grads[pl.ds(start, ROWS), at + low : at + high] = source[
                row : row + ROWS, low:high
            ].astype(f32)

    for low in range(0, SPLIT, width):
        place(ROUTES[0], early_own, early_other, low, low + width, 0)
        leave(grads.at[:, low : low + width], in_hbm.at[:, low : low + width])
    place(ROUTES[1], late_own, late_other, 0, width, SPLIT)
    leave(grads.at[:, SPLIT : SPLIT + width], out_hbm)
    place(ROUTES[1], late_own, late_other, width, columns - SPLIT, SPLIT)
    leaf_ref[:, : width // 2] = grads[:leaves, 5 * width :]
    leaf_ref[:, width // 2 :] = grads[leaves:, 5 * width :]
    table_ref[...] = mm_tn(chosen_ref[...], returned_ref[...].reshape(-1, width))
    for copy in leaving:
        copy.wait()


def run_finish(me, chosen, returned, early_own, early_other, late_own, late_other, leaves):
    smem = pl.BlockSpec(memory_space=pltpu.SMEM)
    vmem = pl.BlockSpec(memory_space=pltpu.VMEM)
    hbm = pl.BlockSpec(memory_space=pltpu.HBM)
    shape = jax.ShapeDtypeStruct
    width = returned.shape[2]
    return pl.pallas_call(
        finish_kernel,
        name="finish",
        out_shape=(
            shape((chosen.shape[1], width), f32),
            shape((leaves, width), f32),
            shape((width, 4 * width), f32),
            shape((width, width), f32),
        ),
        in_specs=[smem] + [vmem] * 6,
        out_specs=(vmem, vmem, hbm, hbm),
        scratch_shapes=[
            pltpu.VMEM((width, early_own.shape[1] + late_own.shape[1]), f32),
            pltpu.SemaphoreType.DMA((5,)),
        ],
        compiler_params=pltpu.CompilerParams(vmem_limit_bytes=32 * 2**20),
    )(me, chosen, returned, early_own, early_other, late_own, late_other)


def load_kernel(*refs):
    for source, target in zip(refs[: len(refs) // 2], refs[len(refs) // 2 :]):
        target[...] = source[...]


def run_load(*arrays):
    vmem = pl.BlockSpec(memory_space=pltpu.VMEM)
    return pl.pallas_call(
        load_kernel,
        name="load",
        out_shape=tuple(jax.ShapeDtypeStruct(array.shape, array.dtype) for array in arrays),
        in_specs=[vmem] * len(arrays),
        out_specs=(vmem,) * len(arrays),
        compiler_params=pltpu.CompilerParams(vmem_limit_bytes=8 * 2**20),
        cost_estimate=pl.CostEstimate(flops=0, bytes_accessed=4 * 2**20, transcendentals=0),
    )(*arrays)


def merge_kernel(keep_ref, other_ref, *outs):
    rows = outs[0].shape[0]
    for part, out in enumerate(outs):
        at = slice(part * rows, (part + 1) * rows)
        out[...] = (keep_ref[at, :].astype(f32) + other_ref[at, :].astype(f32)).astype(bf16)


def run_merge(keep, other, parts):
    vmem = pl.BlockSpec(memory_space=pltpu.VMEM)
    part = jax.ShapeDtypeStruct((keep.shape[0] // parts, keep.shape[1]), bf16)
    return pl.pallas_call(
        merge_kernel,
        name="merge",
        out_shape=(part,) * parts,
        in_specs=[vmem] * 2,
        out_specs=(vmem,) * parts,
        compiler_params=pltpu.CompilerParams(vmem_limit_bytes=8 * 2**20),
    )(keep, other)


def exchange(blocks):
    return lax.all_to_all(blocks, ("dp", "rep"), split_axis=0, concat_axis=0, tiled=True)


def swap(block, mask, count):
    return lax.ppermute(block, ("dp", "rep"), [(i, i ^ mask) for i in range(count)])


def add(parts):
    return sum(part.astype(f32) for part in parts)


def shares(parts, group):
    size = 2 ** len(group)
    rows = parts[0].shape[0] // size
    return [
        add(part[digit * rows : (digit + 1) * rows] for part in parts).astype(bf16)
        for digit in range(1, size)
    ]


def swap_all(blocks, group, count):
    return [
        swap(block, mask_of(group, digit), count) for digit, block in enumerate(blocks, start=1)
    ]


def extend(parts, got):
    return [part[: got[0].shape[0]] for part in parts] + got


def split_up(parts, group, count):
    return extend(parts, swap_all(shares(parts, group), group, count))


def join(block, group, count):
    pieces = swap_all([block] * (2 ** len(group) - 1), group, count)
    return jnp.concatenate([block] + pieces, axis=0)


def reduce_and_gather(early, late, d_rows, count):
    _, near, far = ROUTES[0]
    _, first, second, third, fourth = ROUTES[1]
    early_other, late_other = swap(early[1], 1, count), swap(late[1], 1, count)
    early_own, late_own, d_rows = run_load(early[0], late[0], d_rows)
    early, *early_blocks = run_merge(early_own, early_other, 2 ** len(near))
    late, *late_blocks = run_merge(late_own, late_other, 2 ** len(first))
    early_blocks, late_blocks = lax.optimization_barrier((early_blocks, late_blocks))
    early_got = swap_all(early_blocks, near, count)
    late = [late] + swap_all(late_blocks, first, count)
    late_blocks, d_rows = lax.optimization_barrier((shares(late, second), d_rows))
    returned = exchange(d_rows)
    late = extend(late, swap_all(late_blocks, second, count))
    early_got, late, returned = lax.optimization_barrier((early_got, late, returned))
    early = split_up([early] + early_got, far, count)
    late = split_up(split_up(late, third, count), fourth, count)
    own = [add(early), add(late)]
    reach = CHUNKS
    while reach < count:
        own = [part + swap(part, reach, count) for part in own]
        reach *= 2
    early, late = lax.optimization_barrier(
        tuple((part * (1.0 / count)).astype(bf16) for part in own)
    )
    early = join(early, far, count)
    late = join(join(late, fourth, count), third, count)
    early, late = lax.optimization_barrier((early, late))
    pieces = swap_all([early] * (2 ** len(near) - 1), near, count)
    late = join(join(late, second, count), first, count)
    pieces, late = lax.optimization_barrier((pieces, late))
    early = jnp.concatenate([early] + pieces, axis=0)
    return returned, early, swap(early, 1, count), late, swap(late, 1, count)


def on_device(
    item_table, requests, event_slot, lengths, leaf_ids, leaf_table, w_in, w_out, cotangent
):
    count = lax.axis_size("dp") * lax.axis_size("rep")
    place = lax.axis_index(("dp", "rep")).astype(jnp.int32)
    me = (place & (CHUNKS - 1)).reshape(1)
    slot = event_slot.reshape(1, -1)
    leaf = leaf_ids.T
    asked = exchange(requests[0])
    fetched, chosen = run_lookup(asked, item_table)
    arrived = exchange(fetched)
    output, d_rows, keep, send, keep_late, send_late = run_layer(
        me, lengths, slot, leaf, arrived, leaf_table, w_in, w_out, cotangent
    )
    returned, early, early_other, late, late_other = reduce_and_gather(
        (keep, send), (keep_late, send_late), d_rows, count
    )
    table_grad, leaf_mean, in_mean, out_mean = run_finish(
        me, chosen, returned, early, early_other, late, late_other, leaf_table.shape[0]
    )
    return (output, table_grad, leaf_mean, in_mean, out_mean)


def solution(mesh):
    return jax.shard_map(
        on_device,
        mesh=mesh,
        in_specs=(
            P(("dp", "rep"), None),
            P(("dp", "rep"), None, None),
            P(("dp", "rep")),
            P(("dp", "rep"), None),
            P(("dp", "rep"), None),
            P(),
            P(),
            P(),
            P(("dp", "rep"), None),
        ),
        out_specs=(P(("dp", "rep"), None), P(("dp", "rep"), None), P(), P(), P()),
        check_vma=False,
    )
```

```python
import functools
import jax
import jax.numpy as jnp
from jax import lax
from jax.experimental import pallas as pl
from jax.experimental.pallas import tpu as pltpu
from jax.sharding import PartitionSpec as P

HEADS = 4
MAXLEN = 256
BLOCK = 128
ROWS = 16
epsilon = 1e-06
f32 = jnp.float32
bf16 = jnp.bfloat16

ROUTES = (((0,), (1, 2), (3, 4)), ((0,), (3,), (4,), (2,), (1,)))
SPLIT = 2048
CHUNKS = 32
STRIP = 32
LAYER_VMEM = 60 * 2**20


def dot(a, b, contract):
    return lax.dot_general(a, b, ((contract[0], contract[1]), ((), ())), preferred_element_type=f32)


def mm(a, b):
    return dot(a, b, ((1,), (0,)))


def mm_nt(a, b):
    return dot(a, b, ((1,), (1,)))


def mm_tn(a, b):
    return dot(a, b, ((0,), (0,)))


def mask_of(group, digit):
    return sum(((digit >> k) & 1) << bit for k, bit in enumerate(group))


def chunk_order(groups):
    masks = [0]
    for group in groups:
        masks = [mask ^ mask_of(group, digit) for mask in masks for digit in range(2 ** len(group))]
    return masks


def spans(count):
    for start in range(0, count, BLOCK):
        low = max(0, start - (MAXLEN - 1)) // BLOCK * BLOCK
        yield start, low, start + BLOCK


def strips(start, stop):
    return [slice(at, at + STRIP) for at in range(start, stop, STRIP)]


def silu(half):
    curve = jnp.tanh(half)
    value = (half + half * curve).astype(bf16)
    half, curve = half.astype(bf16), curve.astype(bf16)
    return value, (0.5 + 0.5 * curve) * (1.0 + half * (1.0 - curve))


def center(values):
    values = values - jnp.mean(values, axis=-1, keepdims=True)
    return values, lax.rsqrt(jnp.mean(values * values, axis=-1, keepdims=True) + epsilon)


def pull_normalize(change, normed, scale):
    return scale * (
        change
        - jnp.mean(change, axis=-1, keepdims=True)
        - normed * jnp.mean(change * normed, axis=-1, keepdims=True)
    )


def pickers(slots, slot_ref, leaf_ref, leaves):
    count = slot_ref.shape[1]
    picker = lax.broadcasted_iota(jnp.int32, (slots, count), 0) == slot_ref[...]
    trees = leaf_ref.shape[0]
    each = leaves // trees
    spots = lax.broadcasted_iota(jnp.int32, (each, count), 0)
    onehot = [(spots == leaf_ref[t : t + 1, :]).astype(f32).astype(bf16) for t in range(trees)]
    return picker.astype(f32).astype(bf16), jnp.concatenate(onehot, axis=0)


def permute_rows(me, order, source, target):
    for place, mask in enumerate(order):
        start = pl.multiple_of((me ^ mask) * ROWS, ROWS)
        target[place * ROWS : (place + 1) * ROWS, :] = source[pl.ds(start, ROWS), :]


def lookup_kernel(asked_ref, table_ref, rows_ref, chosen_ref):
    count, each = asked_ref.shape
    many = count * each
    spot = lax.broadcasted_iota(jnp.int32, (count, table_ref.shape[0]), 1)
    parts = [(spot == asked_ref[:, k : k + 1]).astype(f32).astype(bf16) for k in range(each)]
    chosen = jnp.concatenate(parts, axis=0)
    to = lax.broadcasted_iota(jnp.int32, (many, many), 0)
    source = (to % each) * count + to // each
    order = (source == lax.broadcasted_iota(jnp.int32, (many, many), 1)).astype(f32).astype(bf16)
    chosen_ref[...] = mm(order, chosen).astype(bf16)
    rows = mm(chosen_ref[...], table_ref[...]).astype(bf16)
    rows_ref[...] = rows.reshape(rows_ref.shape)


def run_lookup(asked, table):
    vmem = pl.BlockSpec(memory_space=pltpu.VMEM)
    shape = jax.ShapeDtypeStruct
    many = asked.shape[0] * asked.shape[1]
    return pl.pallas_call(
        lookup_kernel,
        name="lookup",
        out_shape=(
            shape(asked.shape + table.shape[1:], bf16),
            shape((many, table.shape[0]), bf16),
        ),
        in_specs=[vmem, vmem],
        out_specs=(vmem,) * 2,
        compiler_params=pltpu.CompilerParams(vmem_limit_bytes=16 * 2**20),
    )(asked, table)


def layer_kernel(
    me_ref, lengths_ref, slot_ref, leaf_ref, rows_ref, table_hbm, in_hbm, out_hbm, tangent_hbm,
    output_hbm, d_rows_ref, keep_hbm, send_hbm, keep_late_hbm, send_late_hbm,
    inputs, gated, d_pre, grads, output,
    normed, turned, moved, hidden, slope, weights, weights_slope, mixed, d_mixed,
    d_score, d_gated, allowed, allowed_scale, d_inputs, leaf_grad, table, w_in, w_out, tangent, sems, out_sems,
):
    count, width = inputs.shape
    head = width // HEADS
    half_scale = 0.5 * head ** (-0.5)
    half_rows = width // 2
    copies = [
        pltpu.make_async_copy(source, target, sems.at[k])
        for k, (source, target) in enumerate(
            ((table_hbm, table), (in_hbm, w_in), (out_hbm, w_out), (tangent_hbm, tangent))
        )
    ]
    for copy in copies:
        copy.start()
    leaving = []

    def leave(source, target):
        copy = pltpu.make_async_copy(source, target, out_sems.at[len(leaving)])
        copy.start()
        leaving.append(copy)

    rows = rows_ref[...].reshape(-1, width)
    picker, onehot = pickers(rows.shape[0], slot_ref, leaf_ref, table.shape[0])
    ends = []
    total = 0
    for place in range(lengths_ref.shape[1]):
        total = total + lengths_ref[0, place]
        ends.append(total)
    for start, low, high in spans(count):
        at = slice(start, start + BLOCK)
        row = start + lax.broadcasted_iota(jnp.int32, (BLOCK, high - low), 0)
        column = low + lax.broadcasted_iota(jnp.int32, (BLOCK, high - low), 1)
        first = jnp.zeros_like(row)
        for end in ends[:-1]:
            first = jnp.where(row >= end, end, first)
        seen = jnp.logical_and(column >= first, column <= row)
        allowed[at, low:high] = jnp.where(seen, 1.0, 0.0).astype(bf16)
        allowed_scale[at, low:high] = jnp.where(seen, 2.0 * half_scale, 0.0).astype(bf16)
    copies[0].wait()
    inputs[...] = (mm_tn(picker, rows) + mm_tn(onehot, table[...])).astype(bf16)
    for at in strips(0, count):
        values, scale = center(inputs[at, :].astype(f32))
        normed[at, :] = (values * scale).astype(bf16)
    turned[...] = normed[...].T
    copies[1].wait()
    for start in range(0, 4 * width, 2 * BLOCK):
        to = slice(start, start + 2 * BLOCK)
        halves = mm(normed[...], w_in[:, to]) * 0.5
        for at in strips(0, count):
            value, slope_at = silu(halves[at, :])
            hidden[at, to] = value
            slope[at, to] = slope_at
    for start, low, high in spans(count):
        at = slice(start, start + BLOCK)
        end = start // (2 * BLOCK) * 2 * BLOCK + 2 * BLOCK
        for out in (slice(0, low), slice(high, end)):
            if out.start < out.stop:
                nothing = jnp.zeros((HEADS, BLOCK, out.stop - out.start), bf16)
                weights[:, at, out] = nothing
                d_score[:, at, out] = nothing
    for h in range(HEADS):
        value_at = slice(width + h * head, width + (h + 1) * head)
        query_at = slice(2 * width + h * head, 2 * width + (h + 1) * head)
        key_at = slice(3 * width + h * head, 3 * width + (h + 1) * head)
        for start, low, high in spans(count):
            at = slice(start, start + BLOCK)
            halves = mm_nt(hidden[at, query_at], hidden[low:high, key_at]) * half_scale
            for strip in strips(0, BLOCK):
                to = slice(start + strip.start, start + strip.stop)
                value, slope_at = silu(halves[strip, :])
                weights[h, to, low:high] = value * allowed[to, low:high]
                weights_slope[h, to, low:high] = slope_at * allowed_scale[to, low:high]
        for start in range(0, count, 2 * BLOCK):
            at = slice(start, start + 2 * BLOCK)
            high = start + 2 * BLOCK
            mixed[at, h * head : (h + 1) * head] = mm(
                weights[h, at, :high], hidden[:high, value_at]
            )
    copies[2].wait()
    copies[3].wait()
    d_gated[...] = mm_nt(tangent[...], w_out[...]).astype(bf16)
    for at in strips(0, count):
        values, scale = center(mixed[at, :])
        values = values * scale
        gates = hidden[at, :width].astype(f32)
        change = d_gated[at, :].astype(f32)
        gated[at, :] = (values * gates).astype(bf16)
        d_pre[at, :width] = (change * values).astype(bf16) * slope[at, :width]
        d_mixed[at, :] = pull_normalize(change * gates, values, scale).astype(bf16)
    for h in range(HEADS):
        own = slice(h * head, (h + 1) * head)
        value_at = slice(width + h * head, width + (h + 1) * head)
        query_at = slice(2 * width + h * head, 2 * width + (h + 1) * head)
        key_at = slice(3 * width + h * head, 3 * width + (h + 1) * head)
        for start, low, high in spans(count):
            at = slice(start, start + BLOCK)
            d_weights = mm_nt(d_mixed[at, own], hidden[low:high, value_at]).astype(bf16)
            d_score[h, at, low:high] = d_weights * weights_slope[h, at, low:high]
        for start in range(0, count, 2 * BLOCK):
            at = slice(start, start + 2 * BLOCK)
            high = start + 2 * BLOCK
            d_query = mm(d_score[h, at, :high], hidden[:high, key_at])
            d_pre[at, query_at] = d_query.astype(bf16) * slope[at, query_at]
            d_key = mm_tn(d_score[h, start:, at], hidden[start:, query_at])
            d_pre[at, key_at] = d_key.astype(bf16) * slope[at, key_at]
            d_value = mm_tn(weights[h, start:, at], d_mixed[start:, own])
            d_pre[at, value_at] = d_value.astype(bf16) * slope[at, value_at]
    me = me_ref[0]
    early, late = (chunk_order(route) for route in ROUTES)
    permute_rows(me, early, turned, moved)
    for start in range(0, 4 * width, 2 * BLOCK):
        to = slice(start, start + 2 * BLOCK)
        grads[:, to] = mm(moved[...], d_pre[:, to]).astype(bf16)
    leave(grads.at[half_rows:, :SPLIT], send_hbm)
    leave(grads.at[:half_rows, :SPLIT], keep_hbm)
    turned[...] = gated[...].T
    permute_rows(me, late, turned, moved)
    grads[:, 4 * width : 5 * width] = mm(moved[...], tangent[...]).astype(bf16)
    output[...] = (mm(gated[...], w_out[...]) + inputs[...].astype(f32)).astype(bf16)
    leave(output, output_hbm)
    normed_change = mm_nt(d_pre[...], w_in[...])
    for at in strips(0, count):
        values, scale = center(inputs[at, :].astype(f32))
        change = pull_normalize(normed_change[at, :], values * scale, scale)
        d_inputs[at, :] = (change + tangent[at, :].astype(f32)).astype(bf16)
    leaves = table.shape[0]
    d_leaf = mm(onehot, d_inputs[...]).astype(bf16)
    leaf_grad[:leaves, :] = d_leaf[:, : width // 2]
    leaf_grad[leaves:, :] = d_leaf[:, width // 2 :]
    permute_rows(me, late, leaf_grad, grads.at[:, 5 * width :])
    leave(grads.at[half_rows:, SPLIT:], send_late_hbm)
    leave(grads.at[:half_rows, SPLIT:], keep_late_hbm)
    d_rows = mm(picker, d_inputs[...]).astype(bf16)
    d_rows_ref[...] = d_rows.reshape(d_rows_ref.shape)
    for copy in leaving:
        copy.wait()


def run_layer(me, lengths, slot, leaf, rows, table, w_in, w_out, tangent):
    count, width = tangent.shape
    smem = pl.BlockSpec(memory_space=pltpu.SMEM)
    vmem = pl.BlockSpec(memory_space=pltpu.VMEM)
    hbm = pl.BlockSpec(memory_space=pltpu.HBM)
    shape = jax.ShapeDtypeStruct
    columns = 5 * width + width // 2
    return pl.pallas_call(
        layer_kernel,
        name="layer",
        out_shape=(
            shape((count, width), bf16),
            shape(rows.shape, bf16),
            shape((width // 2, SPLIT), bf16),
            shape((width // 2, SPLIT), bf16),
            shape((width // 2, columns - SPLIT), bf16),
            shape((width // 2, columns - SPLIT), bf16),
        ),
        in_specs=[smem, smem] + [vmem] * 3 + [hbm] * 4,
        out_specs=(hbm, vmem, hbm, hbm, hbm, hbm),
        scratch_shapes=[
            pltpu.VMEM((count, width), bf16),
            pltpu.VMEM((count, width), bf16),
            pltpu.VMEM((count, 4 * width), bf16),
            pltpu.VMEM((width, columns), bf16),
            pltpu.VMEM((count, width), bf16),
            pltpu.VMEM((count, width), bf16),
            pltpu.VMEM((width, count), bf16),
            pltpu.VMEM((width, count), bf16),
            pltpu.VMEM((count, 4 * width), bf16),
            pltpu.VMEM((count, 4 * width), bf16),
            pltpu.VMEM((HEADS, count, count), bf16),
            pltpu.VMEM((HEADS, count, count), bf16),
            pltpu.VMEM((count, width), f32),
            pltpu.VMEM((count, width), bf16),
            pltpu.VMEM((HEADS, count, count), bf16),
            pltpu.VMEM((count, width), bf16),
            pltpu.VMEM((count, count), bf16),
            pltpu.VMEM((count, count), bf16),
            pltpu.VMEM((count, width), bf16),
            pltpu.VMEM((width, width // 2), bf16),
            pltpu.VMEM(table.shape, bf16),
            pltpu.VMEM(w_in.shape, bf16),
            pltpu.VMEM(w_out.shape, bf16),
            pltpu.VMEM(tangent.shape, bf16),
            pltpu.SemaphoreType.DMA((4,)),
            pltpu.SemaphoreType.DMA((5,)),
        ],
        compiler_params=pltpu.CompilerParams(vmem_limit_bytes=LAYER_VMEM),
        cost_estimate=pl.CostEstimate(flops=6 * 10**9, bytes_accessed=10**7, transcendentals=10**6),
    )(me, lengths, slot, leaf, rows, table, w_in, w_out, tangent)


def finish_kernel(
    me_ref, chosen_ref, returned_ref, early_own, early_other, late_own, late_other,
    table_hbm, leaf_hbm, in_hbm, out_hbm, grads, table, sems,
):
    width, columns = grads.shape
    leaves = leaf_hbm.shape[0]
    me = me_ref[0]
    half_rows = width // 2
    leaving = []

    def leave(source, target):
        copy = pltpu.make_async_copy(source, target, sems.at[len(leaving)])
        copy.start()
        leaving.append(copy)

    def place(route, own, other, low, high, at):
        for spot, mask in enumerate(chunk_order(route)):
            source = own if spot * ROWS < half_rows else other
            row = spot * ROWS % half_rows
            start = pl.multiple_of((me ^ mask) * ROWS, ROWS)
            grads[pl.ds(start, ROWS), at + low : at + high] = source[
                row : row + ROWS, low:high
            ].astype(f32)

    place(ROUTES[1], late_own, late_other, 0, width, SPLIT)
    leave(grads.at[:, SPLIT : SPLIT + width], out_hbm)
    place(ROUTES[1], late_own, late_other, width, columns - SPLIT, SPLIT)
    for half in range(2):
        leave(
            grads.at[half * leaves : (half + 1) * leaves, SPLIT + width :],
            leaf_hbm.at[:, half * (width // 2) : (half + 1) * (width // 2)],
        )
    table[...] = mm_tn(chosen_ref[...], returned_ref[...].reshape(-1, width))
    leave(table, table_hbm)
    for low in range(0, SPLIT, width):
        place(ROUTES[0], early_own, early_other, low, low + width, 0)
        leave(grads.at[:, low : low + width], in_hbm.at[:, low : low + width])
    for copy in leaving:
        copy.wait()


def run_finish(me, chosen, returned, early_own, early_other, late_own, late_other, leaves):
    smem = pl.BlockSpec(memory_space=pltpu.SMEM)
    vmem = pl.BlockSpec(memory_space=pltpu.VMEM)
    hbm = pl.BlockSpec(memory_space=pltpu.HBM)
    shape = jax.ShapeDtypeStruct
    width = returned.shape[2]
    return pl.pallas_call(
        finish_kernel,
        name="finish",
        out_shape=(
            shape((chosen.shape[1], width), f32),
            shape((leaves, width), f32),
            shape((width, 4 * width), f32),
            shape((width, width), f32),
        ),
        in_specs=[smem] + [vmem] * 6,
        out_specs=(hbm,) * 4,
        scratch_shapes=[
            pltpu.VMEM((width, early_own.shape[1] + late_own.shape[1]), f32),
            pltpu.VMEM((chosen.shape[1], width), f32),
            pltpu.SemaphoreType.DMA((8,)),
        ],
        compiler_params=pltpu.CompilerParams(vmem_limit_bytes=32 * 2**20),
    )(me, chosen, returned, early_own, early_other, late_own, late_other)


def load_kernel(*refs):
    for source, target in zip(refs[: len(refs) // 2], refs[len(refs) // 2 :]):
        target[...] = source[...]


def run_load(*arrays):
    vmem = pl.BlockSpec(memory_space=pltpu.VMEM)
    return pl.pallas_call(
        load_kernel,
        name="load",
        out_shape=tuple(jax.ShapeDtypeStruct(array.shape, array.dtype) for array in arrays),
        in_specs=[vmem] * len(arrays),
        out_specs=(vmem,) * len(arrays),
        compiler_params=pltpu.CompilerParams(vmem_limit_bytes=8 * 2**20),
        cost_estimate=pl.CostEstimate(flops=0, bytes_accessed=4 * 2**20, transcendentals=0),
    )(*arrays)


def merge_kernel(keep_ref, other_ref, *outs):
    rows = outs[0].shape[0]
    for part, out in enumerate(outs):
        at = slice(part * rows, (part + 1) * rows)
        out[...] = (keep_ref[at, :].astype(f32) + other_ref[at, :].astype(f32)).astype(bf16)


def run_merge(keep, other, parts):
    vmem = pl.BlockSpec(memory_space=pltpu.VMEM)
    part = jax.ShapeDtypeStruct((keep.shape[0] // parts, keep.shape[1]), bf16)
    return pl.pallas_call(
        merge_kernel,
        name="merge",
        out_shape=(part,) * parts,
        in_specs=[vmem] * 2,
        out_specs=(vmem,) * parts,
        compiler_params=pltpu.CompilerParams(vmem_limit_bytes=8 * 2**20),
    )(keep, other)


def exchange(blocks):
    return lax.all_to_all(blocks, ("dp", "rep"), split_axis=0, concat_axis=0, tiled=True)


def swap(block, mask, count):
    return lax.ppermute(block, ("dp", "rep"), [(i, i ^ mask) for i in range(count)])


def add(parts):
    return sum(part.astype(f32) for part in parts)


def shares(parts, group):
    size = 2 ** len(group)
    rows = parts[0].shape[0] // size
    return [
        add(part[digit * rows : (digit + 1) * rows] for part in parts).astype(bf16)
        for digit in range(1, size)
    ]


def swap_all(blocks, group, count):
    return [
        swap(block, mask_of(group, digit), count) for digit, block in enumerate(blocks, start=1)
    ]


def extend(parts, got):
    return [part[: got[0].shape[0]] for part in parts] + got


def split_up(parts, group, count):
    return extend(parts, swap_all(shares(parts, group), group, count))


def join(block, group, count):
    pieces = swap_all([block] * (2 ** len(group) - 1), group, count)
    return jnp.concatenate([block] + pieces, axis=0)


def reduce_and_gather(early, late, d_rows, count):
    _, near, far = ROUTES[0]
    _, first, second, third, fourth = ROUTES[1]
    early_other, late_other = swap(early[1], 1, count), swap(late[1], 1, count)
    early_own, late_own, d_rows = run_load(early[0], late[0], d_rows)
    early, *early_blocks = run_merge(early_own, early_other, 2 ** len(near))
    late, *late_blocks = run_merge(late_own, late_other, 2 ** len(first))
    early_blocks, late_blocks = lax.optimization_barrier((early_blocks, late_blocks))
    early_got = swap_all(early_blocks, near, count)
    late = [late] + swap_all(late_blocks, first, count)
    late = split_up(late, second, count)
    early_got[0], d_rows = lax.optimization_barrier((early_got[0], d_rows))
    returned = exchange(d_rows)
    early_got, late, returned = lax.optimization_barrier((early_got, late, returned))
    early = split_up([early] + early_got, far, count)
    late = split_up(split_up(late, third, count), fourth, count)
    own = [add(early), add(late)]
    reach = CHUNKS
    while reach < count:
        own = [part + swap(part, reach, count) for part in own]
        reach *= 2
    early, late = lax.optimization_barrier(
        tuple((part * (1.0 / count)).astype(bf16) for part in own)
    )
    early = join(early, far, count)
    late = join(join(late, fourth, count), third, count)
    early, late = lax.optimization_barrier((early, late))
    pieces = swap_all([early] * (2 ** len(near) - 1), near, count)
    late = join(join(late, second, count), first, count)
    pieces, late = lax.optimization_barrier((pieces, late))
    early = jnp.concatenate([early] + pieces, axis=0)
    return returned, early, swap(early, 1, count), late, swap(late, 1, count)


def on_device(
    item_table, requests, event_slot, lengths, leaf_ids, leaf_table, w_in, w_out, cotangent
):
    count = lax.axis_size("dp") * lax.axis_size("rep")
    place = lax.axis_index(("dp", "rep")).astype(jnp.int32)
    me = (place & (CHUNKS - 1)).reshape(1)
    slot = event_slot.reshape(1, -1)
    leaf = leaf_ids.T
    asked = exchange(requests[0])
    fetched, chosen = run_lookup(asked, item_table)
    arrived = exchange(fetched)
    output, d_rows, keep, send, keep_late, send_late = run_layer(
        me, lengths, slot, leaf, arrived, leaf_table, w_in, w_out, cotangent
    )
    returned, early, early_other, late, late_other = reduce_and_gather(
        (keep, send), (keep_late, send_late), d_rows, count
    )
    table_grad, leaf_mean, in_mean, out_mean = run_finish(
        me, chosen, returned, early, early_other, late, late_other, leaf_table.shape[0]
    )
    return (output, table_grad, leaf_mean, in_mean, out_mean)


def solution(mesh):
    return jax.shard_map(
        on_device,
        mesh=mesh,
        in_specs=(
            P(("dp", "rep"), None),
            P(("dp", "rep"), None, None),
            P(("dp", "rep")),
            P(("dp", "rep"), None),
            P(("dp", "rep"), None),
            P(),
            P(),
            P(),
            P(("dp", "rep"), None),
        ),
        out_specs=(P(("dp", "rep"), None), P(("dp", "rep"), None), P(), P(), P()),
        check_vma=False,
    )
```

```python
import functools
import jax
import jax.numpy as jnp
from jax import lax
from jax.experimental import pallas as pl
from jax.experimental.pallas import tpu as pltpu
from jax.sharding import PartitionSpec as P

HEADS = 4
MAXLEN = 256
BLOCK = 128
ROWS = 16
epsilon = 1e-06
f32 = jnp.float32
bf16 = jnp.bfloat16

EARLY = ((0,), (1, 2), (3, 4))
LATE = ((0,), (3,), (4,))
SHARED = ((2,), (1,))
SPLIT = 2048
CHUNKS = 32
STRIP = 32
LAYER_VMEM = 60 * 2**20


def dot(a, b, contract):
    return lax.dot_general(a, b, ((contract[0], contract[1]), ((), ())), preferred_element_type=f32)


def mm(a, b):
    return dot(a, b, ((1,), (0,)))


def mm_nt(a, b):
    return dot(a, b, ((1,), (1,)))


def mm_tn(a, b):
    return dot(a, b, ((0,), (0,)))


def mask_of(group, digit):
    return sum(((digit >> k) & 1) << bit for k, bit in enumerate(group))


def chunk_order(me, route, shared=()):
    masks = [0]
    for group in route + shared:
        masks = [mask ^ mask_of(group, digit) for mask in masks for digit in range(2 ** len(group))]
    for group in shared:
        me = me & ~mask_of(group, 1)
    return [me ^ mask for mask in masks]


def spans(count):
    for start in range(0, count, BLOCK):
        low = max(0, start - (MAXLEN - 1)) // BLOCK * BLOCK
        yield start, low, start + BLOCK


def strips(start, stop):
    return [slice(at, at + STRIP) for at in range(start, stop, STRIP)]


def silu(half):
    curve = jnp.tanh(half)
    value = (half + half * curve).astype(bf16)
    half, curve = half.astype(bf16), curve.astype(bf16)
    return value, (0.5 + 0.5 * curve) * (1.0 + half * (1.0 - curve))


def center(values):
    values = values - jnp.mean(values, axis=-1, keepdims=True)
    return values, lax.rsqrt(jnp.mean(values * values, axis=-1, keepdims=True) + epsilon)


def pull_normalize(change, normed, scale):
    return scale * (
        change
        - jnp.mean(change, axis=-1, keepdims=True)
        - normed * jnp.mean(change * normed, axis=-1, keepdims=True)
    )


def pickers(slots, slot_ref, leaf_ref, leaves):
    count = slot_ref.shape[1]
    picker = lax.broadcasted_iota(jnp.int32, (slots, count), 0) == slot_ref[...]
    trees = leaf_ref.shape[0]
    each = leaves // trees
    spots = lax.broadcasted_iota(jnp.int32, (each, count), 0)
    onehot = [(spots == leaf_ref[t : t + 1, :]).astype(f32).astype(bf16) for t in range(trees)]
    return picker.astype(f32).astype(bf16), jnp.concatenate(onehot, axis=0)


def permute_rows(chunks, source, target):
    for place, chunk in enumerate(chunks):
        start = pl.multiple_of(chunk * ROWS, ROWS)
        target[place * ROWS : (place + 1) * ROWS, :] = source[pl.ds(start, ROWS), :]


def lookup_kernel(asked_ref, table_ref, rows_ref, chosen_ref):
    count, each = asked_ref.shape
    many = count * each
    spot = lax.broadcasted_iota(jnp.int32, (count, table_ref.shape[0]), 1)
    parts = [(spot == asked_ref[:, k : k + 1]).astype(f32).astype(bf16) for k in range(each)]
    chosen = jnp.concatenate(parts, axis=0)
    to = lax.broadcasted_iota(jnp.int32, (many, many), 0)
    source = (to % each) * count + to // each
    order = (source == lax.broadcasted_iota(jnp.int32, (many, many), 1)).astype(f32).astype(bf16)
    chosen_ref[...] = mm(order, chosen).astype(bf16)
    rows = mm(chosen_ref[...], table_ref[...]).astype(bf16)
    rows_ref[...] = rows.reshape(rows_ref.shape)


def run_lookup(asked, table):
    vmem = pl.BlockSpec(memory_space=pltpu.VMEM)
    shape = jax.ShapeDtypeStruct
    many = asked.shape[0] * asked.shape[1]
    return pl.pallas_call(
        lookup_kernel,
        name="lookup",
        out_shape=(
            shape(asked.shape + table.shape[1:], bf16),
            shape((many, table.shape[0]), bf16),
        ),
        in_specs=[vmem, vmem],
        out_specs=(vmem,) * 2,
        compiler_params=pltpu.CompilerParams(vmem_limit_bytes=16 * 2**20),
    )(asked, table)


def layer_kernel(
    me_ref, lengths_ref, slot_ref, leaf_ref, rows_ref, table_hbm, in_hbm, out_hbm, tangent_hbm,
    output_hbm, d_rows_ref, keep_hbm, send_hbm, keep_late_hbm, send_late_hbm,
    inputs, gated, d_pre, grads, output,
    normed, turned, moved, hidden, slope, weights, weights_slope, mixed, d_mixed,
    d_score, d_gated, allowed, allowed_scale, d_inputs, leaf_grad, table, w_in, w_out, tangent, sems, out_sems,
):
    count, width = inputs.shape
    head = width // HEADS
    half_scale = 0.5 * head ** (-0.5)
    half_rows = width // 2
    copies = [
        pltpu.make_async_copy(source, target, sems.at[k])
        for k, (source, target) in enumerate(
            ((table_hbm, table), (in_hbm, w_in), (out_hbm, w_out), (tangent_hbm, tangent))
        )
    ]
    for copy in copies:
        copy.start()
    leaving = []

    def leave(source, target):
        copy = pltpu.make_async_copy(source, target, out_sems.at[len(leaving)])
        copy.start()
        leaving.append(copy)

    rows = rows_ref[...].reshape(-1, width)
    picker, onehot = pickers(rows.shape[0], slot_ref, leaf_ref, table.shape[0])
    ends = []
    total = 0
    for place in range(lengths_ref.shape[1]):
        total = total + lengths_ref[0, place]
        ends.append(total)
    for start, low, high in spans(count):
        at = slice(start, start + BLOCK)
        row = start + lax.broadcasted_iota(jnp.int32, (BLOCK, high - low), 0)
        column = low + lax.broadcasted_iota(jnp.int32, (BLOCK, high - low), 1)
        first = jnp.zeros_like(row)
        for end in ends[:-1]:
            first = jnp.where(row >= end, end, first)
        seen = jnp.logical_and(column >= first, column <= row)
        allowed[at, low:high] = jnp.where(seen, 1.0, 0.0).astype(bf16)
        allowed_scale[at, low:high] = jnp.where(seen, 2.0 * half_scale, 0.0).astype(bf16)
    copies[0].wait()
    inputs[...] = (mm_tn(picker, rows) + mm_tn(onehot, table[...])).astype(bf16)
    for at in strips(0, count):
        values, scale = center(inputs[at, :].astype(f32))
        normed[at, :] = (values * scale).astype(bf16)
    turned[...] = normed[...].T
    copies[1].wait()
    for start in range(0, 4 * width, 2 * BLOCK):
        to = slice(start, start + 2 * BLOCK)
        halves = mm(normed[...], w_in[:, to]) * 0.5
        for at in strips(0, count):
            value, slope_at = silu(halves[at, :])
            hidden[at, to] = value
            slope[at, to] = slope_at
    for start, low, high in spans(count):
        at = slice(start, start + BLOCK)
        end = start // (2 * BLOCK) * 2 * BLOCK + 2 * BLOCK
        for out in (slice(0, low), slice(high, end)):
            if out.start < out.stop:
                nothing = jnp.zeros((HEADS, BLOCK, out.stop - out.start), bf16)
                weights[:, at, out] = nothing
                d_score[:, at, out] = nothing
    for h in range(HEADS):
        value_at = slice(width + h * head, width + (h + 1) * head)
        query_at = slice(2 * width + h * head, 2 * width + (h + 1) * head)
        key_at = slice(3 * width + h * head, 3 * width + (h + 1) * head)
        for start, low, high in spans(count):
            at = slice(start, start + BLOCK)
            halves = mm_nt(hidden[at, query_at], hidden[low:high, key_at]) * half_scale
            for strip in strips(0, BLOCK):
                to = slice(start + strip.start, start + strip.stop)
                value, slope_at = silu(halves[strip, :])
                weights[h, to, low:high] = value * allowed[to, low:high]
                weights_slope[h, to, low:high] = slope_at * allowed_scale[to, low:high]
        for start in range(0, count, 2 * BLOCK):
            at = slice(start, start + 2 * BLOCK)
            high = start + 2 * BLOCK
            mixed[at, h * head : (h + 1) * head] = mm(
                weights[h, at, :high], hidden[:high, value_at]
            )
    copies[2].wait()
    copies[3].wait()
    d_gated[...] = mm_nt(tangent[...], w_out[...]).astype(bf16)
    for at in strips(0, count):
        values, scale = center(mixed[at, :])
        values = values * scale
        gates = hidden[at, :width].astype(f32)
        change = d_gated[at, :].astype(f32)
        gated[at, :] = (values * gates).astype(bf16)
        d_pre[at, :width] = (change * values).astype(bf16) * slope[at, :width]
        d_mixed[at, :] = pull_normalize(change * gates, values, scale).astype(bf16)
    for h in range(HEADS):
        own = slice(h * head, (h + 1) * head)
        value_at = slice(width + h * head, width + (h + 1) * head)
        query_at = slice(2 * width + h * head, 2 * width + (h + 1) * head)
        key_at = slice(3 * width + h * head, 3 * width + (h + 1) * head)
        for start, low, high in spans(count):
            at = slice(start, start + BLOCK)
            d_weights = mm_nt(d_mixed[at, own], hidden[low:high, value_at]).astype(bf16)
            d_score[h, at, low:high] = d_weights * weights_slope[h, at, low:high]
        for start in range(0, count, 2 * BLOCK):
            at = slice(start, start + 2 * BLOCK)
            high = start + 2 * BLOCK
            d_query = mm(d_score[h, at, :high], hidden[:high, key_at])
            d_pre[at, query_at] = d_query.astype(bf16) * slope[at, query_at]
            d_key = mm_tn(d_score[h, start:, at], hidden[start:, query_at])
            d_pre[at, key_at] = d_key.astype(bf16) * slope[at, key_at]
            d_value = mm_tn(weights[h, start:, at], d_mixed[start:, own])
            d_pre[at, value_at] = d_value.astype(bf16) * slope[at, value_at]
    me = me_ref[0]
    early, late = chunk_order(me, EARLY), chunk_order(me, LATE, SHARED)
    permute_rows(early, turned, moved)
    for start in range(0, 4 * width, 2 * BLOCK):
        to = slice(start, start + 2 * BLOCK)
        grads[:, to] = mm(moved[...], d_pre[:, to]).astype(bf16)
    leave(grads.at[half_rows:, :SPLIT], send_hbm)
    leave(grads.at[:half_rows, :SPLIT], keep_hbm)
    turned[...] = gated[...].T
    permute_rows(late, turned, moved)
    grads[:, 4 * width : 5 * width] = mm(moved[...], tangent[...]).astype(bf16)
    output[...] = (mm(gated[...], w_out[...]) + inputs[...].astype(f32)).astype(bf16)
    leave(output, output_hbm)
    normed_change = mm_nt(d_pre[...], w_in[...])
    for at in strips(0, count):
        values, scale = center(inputs[at, :].astype(f32))
        change = pull_normalize(normed_change[at, :], values * scale, scale)
        d_inputs[at, :] = (change + tangent[at, :].astype(f32)).astype(bf16)
    leaves = table.shape[0]
    d_leaf = mm(onehot, d_inputs[...]).astype(bf16)
    leaf_grad[:leaves, :] = d_leaf[:, : width // 2]
    leaf_grad[leaves:, :] = d_leaf[:, width // 2 :]
    permute_rows(late, leaf_grad, grads.at[:, 5 * width :])
    leave(grads.at[half_rows:, SPLIT:], send_late_hbm)
    leave(grads.at[:half_rows, SPLIT:], keep_late_hbm)
    d_rows = mm(picker, d_inputs[...]).astype(bf16)
    d_rows_ref[...] = d_rows.reshape(d_rows_ref.shape)
    for copy in leaving:
        copy.wait()


def run_layer(me, lengths, slot, leaf, rows, table, w_in, w_out, tangent):
    count, width = tangent.shape
    smem = pl.BlockSpec(memory_space=pltpu.SMEM)
    vmem = pl.BlockSpec(memory_space=pltpu.VMEM)
    hbm = pl.BlockSpec(memory_space=pltpu.HBM)
    shape = jax.ShapeDtypeStruct
    columns = 5 * width + width // 2
    return pl.pallas_call(
        layer_kernel,
        name="layer",
        out_shape=(
            shape((count, width), bf16),
            shape(rows.shape, bf16),
            shape((width // 2, SPLIT), bf16),
            shape((width // 2, SPLIT), bf16),
            shape((width // 2, columns - SPLIT), bf16),
            shape((width // 2, columns - SPLIT), bf16),
        ),
        in_specs=[smem, smem] + [vmem] * 3 + [hbm] * 4,
        out_specs=(hbm, vmem, hbm, hbm, hbm, hbm),
        scratch_shapes=[
            pltpu.VMEM((count, width), bf16),
            pltpu.VMEM((count, width), bf16),
            pltpu.VMEM((count, 4 * width), bf16),
            pltpu.VMEM((width, columns), bf16),
            pltpu.VMEM((count, width), bf16),
            pltpu.VMEM((count, width), bf16),
            pltpu.VMEM((width, count), bf16),
            pltpu.VMEM((width, count), bf16),
            pltpu.VMEM((count, 4 * width), bf16),
            pltpu.VMEM((count, 4 * width), bf16),
            pltpu.VMEM((HEADS, count, count), bf16),
            pltpu.VMEM((HEADS, count, count), bf16),
            pltpu.VMEM((count, width), f32),
            pltpu.VMEM((count, width), bf16),
            pltpu.VMEM((HEADS, count, count), bf16),
            pltpu.VMEM((count, width), bf16),
            pltpu.VMEM((count, count), bf16),
            pltpu.VMEM((count, count), bf16),
            pltpu.VMEM((count, width), bf16),
            pltpu.VMEM((width, width // 2), bf16),
            pltpu.VMEM(table.shape, bf16),
            pltpu.VMEM(w_in.shape, bf16),
            pltpu.VMEM(w_out.shape, bf16),
            pltpu.VMEM(tangent.shape, bf16),
            pltpu.SemaphoreType.DMA((4,)),
            pltpu.SemaphoreType.DMA((5,)),
        ],
        compiler_params=pltpu.CompilerParams(vmem_limit_bytes=LAYER_VMEM),
        cost_estimate=pl.CostEstimate(flops=6 * 10**9, bytes_accessed=10**7, transcendentals=10**6),
    )(me, lengths, slot, leaf, rows, table, w_in, w_out, tangent)


def finish_kernel(
    me_ref, chosen_ref, returned_ref, early_own, early_other, late_own, late_other,
    table_hbm, leaf_hbm, in_hbm, out_hbm, grads, table, sems,
):
    width, columns = grads.shape
    leaves = leaf_hbm.shape[0]
    me = me_ref[0]
    half_rows = width // 2
    leaving = []

    def leave(source, target):
        copy = pltpu.make_async_copy(source, target, sems.at[len(leaving)])
        copy.start()
        leaving.append(copy)

    early, late = chunk_order(me, EARLY), chunk_order(me, LATE, SHARED)

    def place(chunks, own, other, low, high, at):
        for spot, chunk in enumerate(chunks):
            source = own if spot * ROWS < half_rows else other
            row = spot * ROWS % half_rows
            start = pl.multiple_of(chunk * ROWS, ROWS)
            grads[pl.ds(start, ROWS), at + low : at + high] = source[
                row : row + ROWS, low:high
            ].astype(f32)

    place(late, late_own, late_other, 0, width, SPLIT)
    leave(grads.at[:, SPLIT : SPLIT + width], out_hbm)
    place(late, late_own, late_other, width, columns - SPLIT, SPLIT)
    for half in range(2):
        leave(
            grads.at[half * leaves : (half + 1) * leaves, SPLIT + width :],
            leaf_hbm.at[:, half * (width // 2) : (half + 1) * (width // 2)],
        )
    table[...] = mm_tn(chosen_ref[...], returned_ref[...].reshape(-1, width))
    leave(table, table_hbm)
    for low in range(0, SPLIT, width):
        place(early, early_own, early_other, low, low + width, 0)
        leave(grads.at[:, low : low + width], in_hbm.at[:, low : low + width])
    for copy in leaving:
        copy.wait()


def run_finish(me, chosen, returned, early_own, early_other, late_own, late_other, leaves):
    smem = pl.BlockSpec(memory_space=pltpu.SMEM)
    vmem = pl.BlockSpec(memory_space=pltpu.VMEM)
    hbm = pl.BlockSpec(memory_space=pltpu.HBM)
    shape = jax.ShapeDtypeStruct
    width = returned.shape[2]
    return pl.pallas_call(
        finish_kernel,
        name="finish",
        out_shape=(
            shape((chosen.shape[1], width), f32),
            shape((leaves, width), f32),
            shape((width, 4 * width), f32),
            shape((width, width), f32),
        ),
        in_specs=[smem] + [vmem] * 6,
        out_specs=(hbm,) * 4,
        scratch_shapes=[
            pltpu.VMEM((width, early_own.shape[1] + late_own.shape[1]), f32),
            pltpu.VMEM((chosen.shape[1], width), f32),
            pltpu.SemaphoreType.DMA((8,)),
        ],
        compiler_params=pltpu.CompilerParams(vmem_limit_bytes=32 * 2**20),
    )(me, chosen, returned, early_own, early_other, late_own, late_other)


def load_kernel(*refs):
    for source, target in zip(refs[: len(refs) // 2], refs[len(refs) // 2 :]):
        target[...] = source[...]


def run_load(*arrays):
    vmem = pl.BlockSpec(memory_space=pltpu.VMEM)
    return pl.pallas_call(
        load_kernel,
        name="load",
        out_shape=tuple(jax.ShapeDtypeStruct(array.shape, array.dtype) for array in arrays),
        in_specs=[vmem] * len(arrays),
        out_specs=(vmem,) * len(arrays),
        compiler_params=pltpu.CompilerParams(vmem_limit_bytes=8 * 2**20),
        cost_estimate=pl.CostEstimate(flops=0, bytes_accessed=4 * 2**20, transcendentals=0),
    )(*arrays)


def merge_kernel(keep_ref, other_ref, *outs):
    rows = outs[0].shape[0]
    for part, out in enumerate(outs):
        at = slice(part * rows, (part + 1) * rows)
        out[...] = (keep_ref[at, :].astype(f32) + other_ref[at, :].astype(f32)).astype(bf16)


def run_merge(keep, other, parts):
    vmem = pl.BlockSpec(memory_space=pltpu.VMEM)
    part = jax.ShapeDtypeStruct((keep.shape[0] // parts, keep.shape[1]), bf16)
    return pl.pallas_call(
        merge_kernel,
        name="merge",
        out_shape=(part,) * parts,
        in_specs=[vmem] * 2,
        out_specs=(vmem,) * parts,
        compiler_params=pltpu.CompilerParams(vmem_limit_bytes=8 * 2**20),
    )(keep, other)


def exchange(blocks):
    return lax.all_to_all(blocks, ("dp", "rep"), split_axis=0, concat_axis=0, tiled=True)


def swap(block, mask, count):
    return lax.ppermute(block, ("dp", "rep"), [(i, i ^ mask) for i in range(count)])


def add(parts):
    return sum(part.astype(f32) for part in parts)


def shares(parts, group):
    size = 2 ** len(group)
    rows = parts[0].shape[0] // size
    return [
        add(part[digit * rows : (digit + 1) * rows] for part in parts).astype(bf16)
        for digit in range(1, size)
    ]


def swap_all(blocks, group, count):
    return [
        swap(block, mask_of(group, digit), count) for digit, block in enumerate(blocks, start=1)
    ]


def extend(parts, got):
    return [part[: got[0].shape[0]] for part in parts] + got


def split_up(parts, group, count):
    return extend(parts, swap_all(shares(parts, group), group, count))


def sum_with(block, group, count):
    return block.astype(f32) + swap(block, mask_of(group, 1), count).astype(f32)


def join(block, group, count):
    pieces = swap_all([block] * (2 ** len(group) - 1), group, count)
    return jnp.concatenate([block] + pieces, axis=0)


def reduce_and_gather(early, late, d_rows, count):
    _, near, far = EARLY
    _, first, second = LATE
    early_other, late_other = swap(early[1], 1, count), swap(late[1], 1, count)
    early_own, late_own, d_rows = run_load(early[0], late[0], d_rows)
    early, *early_blocks = run_merge(early_own, early_other, 2 ** len(near))
    late, *late_blocks = run_merge(late_own, late_other, 2 ** len(first))
    early_blocks, late_blocks = lax.optimization_barrier((early_blocks, late_blocks))
    early_got = swap_all(early_blocks, near, count)
    late = [late] + swap_all(late_blocks, first, count)
    late_blocks, d_rows = lax.optimization_barrier((shares(late, second), d_rows))
    returned = exchange(d_rows)
    late = extend(late, swap_all(late_blocks, second, count))
    early_got, late, returned = lax.optimization_barrier((early_got, late, returned))
    early, late = split_up([early] + early_got, far, count), add(late).astype(bf16)
    late = sum_with(late, SHARED[0], count).astype(bf16)
    early, late = add(early), sum_with(late, SHARED[1], count)
    reach = CHUNKS
    while reach < count:
        early, late = early + swap(early, reach, count), late + swap(late, reach, count)
        reach *= 2
    early = join((early * (1.0 / count)).astype(bf16), far, count)
    early, late = lax.optimization_barrier((early, (late * (1.0 / count)).astype(bf16)))
    pieces = swap_all([early] * (2 ** len(near) - 1), near, count)
    late = join(join(late, second, count), first, count)
    pieces, late = lax.optimization_barrier((pieces, late))
    early = jnp.concatenate([early] + pieces, axis=0)
    return returned, early, swap(early, 1, count), late, swap(late, 1, count)


def on_device(
    item_table, requests, event_slot, lengths, leaf_ids, leaf_table, w_in, w_out, cotangent
):
    count = lax.axis_size("dp") * lax.axis_size("rep")
    place = lax.axis_index(("dp", "rep")).astype(jnp.int32)
    me = (place & (CHUNKS - 1)).reshape(1)
    slot = event_slot.reshape(1, -1)
    leaf = leaf_ids.T
    asked = exchange(requests[0])
    fetched, chosen = run_lookup(asked, item_table)
    arrived = exchange(fetched)
    output, d_rows, keep, send, keep_late, send_late = run_layer(
        me, lengths, slot, leaf, arrived, leaf_table, w_in, w_out, cotangent
    )
    returned, early, early_other, late, late_other = reduce_and_gather(
        (keep, send), (keep_late, send_late), d_rows, count
    )
    table_grad, leaf_mean, in_mean, out_mean = run_finish(
        me, chosen, returned, early, early_other, late, late_other, leaf_table.shape[0]
    )
    return (output, table_grad, leaf_mean, in_mean, out_mean)


def solution(mesh):
    return jax.shard_map(
        on_device,
        mesh=mesh,
        in_specs=(
            P(("dp", "rep"), None),
            P(("dp", "rep"), None, None),
            P(("dp", "rep")),
            P(("dp", "rep"), None),
            P(("dp", "rep"), None),
            P(),
            P(),
            P(),
            P(("dp", "rep"), None),
        ),
        out_specs=(P(("dp", "rep"), None), P(("dp", "rep"), None), P(), P(), P()),
        check_vma=False,
    )
```

```python
import functools
import jax
import jax.numpy as jnp
from jax import lax
from jax.experimental import pallas as pl
from jax.experimental.pallas import tpu as pltpu
from jax.sharding import PartitionSpec as P

HEADS = 4
MAXLEN = 256
BLOCK = 128
ROWS = 16
epsilon = 1e-06
f32 = jnp.float32
bf16 = jnp.bfloat16

EARLY = ((0,), (1, 2), (3, 4))
LATE = ((0,), (3,), (4,))
SHARED = ((2,), (1,))
SPLIT = 2048
CHUNKS = 32
STRIP = 32
LAYER_VMEM = 60 * 2**20


def dot(a, b, contract):
    return lax.dot_general(a, b, ((contract[0], contract[1]), ((), ())), preferred_element_type=f32)


def mm(a, b):
    return dot(a, b, ((1,), (0,)))


def mm_nt(a, b):
    return dot(a, b, ((1,), (1,)))


def mm_tn(a, b):
    return dot(a, b, ((0,), (0,)))


def mask_of(group, digit):
    return sum(((digit >> k) & 1) << bit for k, bit in enumerate(group))


def chunk_order(me, route, shared=()):
    masks = [0]
    for group in route + shared:
        masks = [mask ^ mask_of(group, digit) for mask in masks for digit in range(2 ** len(group))]
    for group in shared:
        me = me & ~mask_of(group, 1)
    return [me ^ mask for mask in masks]


def spans(count):
    for start in range(0, count, BLOCK):
        low = max(0, start - (MAXLEN - 1)) // BLOCK * BLOCK
        yield start, low, start + BLOCK


def strips(start, stop):
    return [slice(at, at + STRIP) for at in range(start, stop, STRIP)]


def silu(half):
    curve = jnp.tanh(half)
    value = (half + half * curve).astype(bf16)
    half, curve = half.astype(bf16), curve.astype(bf16)
    return value, (0.5 + 0.5 * curve) * (1.0 + half * (1.0 - curve))


def center(values):
    values = values - jnp.mean(values, axis=-1, keepdims=True)
    return values, lax.rsqrt(jnp.mean(values * values, axis=-1, keepdims=True) + epsilon)


def pull_normalize(change, normed, scale):
    return scale * (
        change
        - jnp.mean(change, axis=-1, keepdims=True)
        - normed * jnp.mean(change * normed, axis=-1, keepdims=True)
    )


def pickers(slots, slot_ref, leaf_ref, leaves):
    count = slot_ref.shape[1]
    picker = lax.broadcasted_iota(jnp.int32, (slots, count), 0) == slot_ref[...]
    trees = leaf_ref.shape[0]
    each = leaves // trees
    spots = lax.broadcasted_iota(jnp.int32, (each, count), 0)
    onehot = [(spots == leaf_ref[t : t + 1, :]).astype(f32).astype(bf16) for t in range(trees)]
    return picker.astype(f32).astype(bf16), jnp.concatenate(onehot, axis=0)


def permute_rows(chunks, source, target):
    for place, chunk in enumerate(chunks):
        start = pl.multiple_of(chunk * ROWS, ROWS)
        target[place * ROWS : (place + 1) * ROWS, :] = source[pl.ds(start, ROWS), :]


def zero_one(condition):
    return jnp.where(condition, 1.0, 0.0).astype(bf16)


def to_tiles(rows):
    parts = rows.shape[1] // BLOCK
    shape = (rows.shape[0] * parts, rows.shape[0])
    row, column = (lax.broadcasted_iota(jnp.int32, shape, axis) for axis in (0, 1))
    total = jnp.zeros((shape[0], BLOCK), f32)
    for part in range(parts):
        place = zero_one(row == column * parts + part)
        total = total + mm(place, rows[:, part * BLOCK : (part + 1) * BLOCK])
    return total.astype(bf16)


def from_tiles(block, width):
    parts = width // BLOCK
    shape = (block.shape[0] // parts, block.shape[0])
    row, column = (lax.broadcasted_iota(jnp.int32, shape, axis) for axis in (0, 1))
    pieces = [mm(zero_one(column == row * parts + part), block) for part in range(parts)]
    return jnp.concatenate(pieces, axis=1).astype(bf16)


def lookup_kernel(asked_ref, table_ref, rows_ref, chosen_ref):
    count, each = asked_ref.shape
    owned, width = table_ref.shape
    parts = width // BLOCK
    many = count * each * parts
    row = lax.broadcasted_iota(jnp.int32, (many, count), 0)
    device = lax.broadcasted_iota(jnp.int32, (many, count), 1)
    own = zero_one(row // (each * parts) == device)
    wanted = mm(own, asked_ref[...].astype(f32).astype(bf16)).astype(jnp.int32)
    spot = lax.broadcasted_iota(jnp.int32, (many, owned), 1)
    row = lax.broadcasted_iota(jnp.int32, (many, owned), 0)
    found = jnp.zeros((many, owned), jnp.bool_)
    for k in range(each):
        here = jnp.logical_and(row // parts % each == k, spot == wanted[:, k : k + 1])
        found = jnp.logical_or(found, here)
    chosen_ref[...] = zero_one(found)
    total = jnp.zeros((many, BLOCK), f32)
    for part in range(parts):
        mine = zero_one(jnp.logical_and(found, row % parts == part))
        total = total + mm(mine, table_ref[:, part * BLOCK : (part + 1) * BLOCK])
    rows_ref[...] = total.astype(bf16)


def run_lookup(asked, table):
    vmem = pl.BlockSpec(memory_space=pltpu.VMEM)
    shape = jax.ShapeDtypeStruct
    many = asked.shape[0] * asked.shape[1] * table.shape[1] // BLOCK
    return pl.pallas_call(
        lookup_kernel,
        name="lookup",
        out_shape=(
            shape((many, BLOCK), bf16),
            shape((many, table.shape[0]), bf16),
        ),
        in_specs=[vmem, vmem],
        out_specs=(vmem,) * 2,
        compiler_params=pltpu.CompilerParams(vmem_limit_bytes=16 * 2**20),
    )(asked, table)


def layer_kernel(
    me_ref, lengths_ref, slot_ref, leaf_ref, rows_ref, table_hbm, in_hbm, out_hbm, tangent_hbm,
    output_hbm, d_rows_ref, keep_hbm, send_hbm, keep_late_hbm, send_late_hbm,
    inputs, gated, d_pre, grads, output,
    normed, turned, moved, hidden, slope, weights, weights_slope, mixed, d_mixed,
    d_score, d_gated, allowed, allowed_scale, keys_t, values_t, d_inputs, leaf_grad, table, w_in, w_out, tangent, sems, out_sems,
):
    count, width = inputs.shape
    head = width // HEADS
    half_scale = 0.5 * head ** (-0.5)
    half_rows = width // 2
    copies = [
        pltpu.make_async_copy(source, target, sems.at[k])
        for k, (source, target) in enumerate(
            ((table_hbm, table), (in_hbm, w_in), (out_hbm, w_out), (tangent_hbm, tangent))
        )
    ]
    for copy in copies:
        copy.start()
    leaving = []

    def leave(source, target):
        copy = pltpu.make_async_copy(source, target, out_sems.at[len(leaving)])
        copy.start()
        leaving.append(copy)

    rows = from_tiles(rows_ref[...], width)
    picker, onehot = pickers(rows.shape[0], slot_ref, leaf_ref, table.shape[0])
    ends = []
    total = 0
    for place in range(lengths_ref.shape[1]):
        total = total + lengths_ref[0, place]
        ends.append(total)
    for start, low, high in spans(count):
        at = slice(start, start + BLOCK)
        row = start + lax.broadcasted_iota(jnp.int32, (BLOCK, high - low), 0)
        column = low + lax.broadcasted_iota(jnp.int32, (BLOCK, high - low), 1)
        first = jnp.zeros_like(row)
        for end in ends[:-1]:
            first = jnp.where(row >= end, end, first)
        seen = jnp.logical_and(column >= first, column <= row)
        allowed[at, low:high] = jnp.where(seen, 1.0, 0.0).astype(bf16)
        allowed_scale[at, low:high] = jnp.where(seen, 2.0 * half_scale, 0.0).astype(bf16)
    copies[0].wait()
    inputs[...] = (mm_tn(picker, rows) + mm_tn(onehot, table[...])).astype(bf16)
    for at in strips(0, count):
        values, scale = center(inputs[at, :].astype(f32))
        normed[at, :] = (values * scale).astype(bf16)
    turned[...] = normed[...].T
    copies[1].wait()
    for start in range(0, 4 * width, 2 * BLOCK):
        to = slice(start, start + 2 * BLOCK)
        halves = mm(normed[...], w_in[:, to]) * 0.5
        for at in strips(0, count):
            value, slope_at = silu(halves[at, :])
            hidden[at, to] = value
            slope[at, to] = slope_at
    keys_t[...] = hidden[:, 3 * width :].T
    values_t[...] = hidden[:, width : 2 * width].T
    for start, low, high in spans(count):
        at = slice(start, start + BLOCK)
        end = start // (2 * BLOCK) * 2 * BLOCK + 2 * BLOCK
        for out in (slice(0, low), slice(high, end)):
            if out.start < out.stop:
                nothing = jnp.zeros((HEADS, BLOCK, out.stop - out.start), bf16)
                weights[:, at, out] = nothing
                d_score[:, at, out] = nothing
    for h in range(HEADS):
        own = slice(h * head, (h + 1) * head)
        value_at = slice(width + h * head, width + (h + 1) * head)
        query_at = slice(2 * width + h * head, 2 * width + (h + 1) * head)
        key_at = slice(3 * width + h * head, 3 * width + (h + 1) * head)
        for start, low, high in spans(count):
            at = slice(start, start + BLOCK)
            halves = mm(hidden[at, query_at], keys_t[own, low:high]) * half_scale
            for strip in strips(0, BLOCK):
                to = slice(start + strip.start, start + strip.stop)
                value, slope_at = silu(halves[strip, :])
                weights[h, to, low:high] = value * allowed[to, low:high]
                weights_slope[h, to, low:high] = slope_at * allowed_scale[to, low:high]
        for start in range(0, count, 2 * BLOCK):
            at = slice(start, start + 2 * BLOCK)
            high = start + 2 * BLOCK
            mixed[at, h * head : (h + 1) * head] = mm(
                weights[h, at, :high], hidden[:high, value_at]
            )
    copies[2].wait()
    copies[3].wait()
    d_gated[...] = mm_nt(tangent[...], w_out[...]).astype(bf16)
    for at in strips(0, count):
        values, scale = center(mixed[at, :])
        values = values * scale
        gates = hidden[at, :width].astype(f32)
        change = d_gated[at, :].astype(f32)
        gated[at, :] = (values * gates).astype(bf16)
        d_pre[at, :width] = (change * values).astype(bf16) * slope[at, :width]
        d_mixed[at, :] = pull_normalize(change * gates, values, scale).astype(bf16)
    for h in range(HEADS):
        own = slice(h * head, (h + 1) * head)
        value_at = slice(width + h * head, width + (h + 1) * head)
        query_at = slice(2 * width + h * head, 2 * width + (h + 1) * head)
        key_at = slice(3 * width + h * head, 3 * width + (h + 1) * head)
        for start, low, high in spans(count):
            at = slice(start, start + BLOCK)
            d_weights = mm(d_mixed[at, own], values_t[own, low:high]).astype(bf16)
            d_score[h, at, low:high] = d_weights * weights_slope[h, at, low:high]
        for start in range(0, count, 2 * BLOCK):
            at = slice(start, start + 2 * BLOCK)
            high = start + 2 * BLOCK
            d_query = mm(d_score[h, at, :high], hidden[:high, key_at])
            d_pre[at, query_at] = d_query.astype(bf16) * slope[at, query_at]
            d_key = mm_tn(d_score[h, start:, at], hidden[start:, query_at])
            d_pre[at, key_at] = d_key.astype(bf16) * slope[at, key_at]
            d_value = mm_tn(weights[h, start:, at], d_mixed[start:, own])
            d_pre[at, value_at] = d_value.astype(bf16) * slope[at, value_at]
    me = me_ref[0]
    early, late = chunk_order(me, EARLY), chunk_order(me, LATE, SHARED)
    permute_rows(early, turned, moved)
    for start in range(0, 4 * width, 2 * BLOCK):
        to = slice(start, start + 2 * BLOCK)
        grads[:, to] = mm(moved[...], d_pre[:, to]).astype(bf16)
    leave(grads.at[half_rows:, :SPLIT], send_hbm)
    leave(grads.at[:half_rows, :SPLIT], keep_hbm)
    turned[...] = gated[...].T
    permute_rows(late, turned, moved)
    grads[:, 4 * width : 5 * width] = mm(moved[...], tangent[...]).astype(bf16)
    output[...] = (mm(gated[...], w_out[...]) + inputs[...].astype(f32)).astype(bf16)
    leave(output, output_hbm)
    normed_change = mm_nt(d_pre[...], w_in[...])
    for at in strips(0, count):
        values, scale = center(inputs[at, :].astype(f32))
        change = pull_normalize(normed_change[at, :], values * scale, scale)
        d_inputs[at, :] = (change + tangent[at, :].astype(f32)).astype(bf16)
    leaves = table.shape[0]
    d_leaf = mm(onehot, d_inputs[...]).astype(bf16)
    leaf_grad[:leaves, :] = d_leaf[:, : width // 2]
    leaf_grad[leaves:, :] = d_leaf[:, width // 2 :]
    permute_rows(late, leaf_grad, grads.at[:, 5 * width :])
    leave(grads.at[half_rows:, SPLIT:], send_late_hbm)
    leave(grads.at[:half_rows, SPLIT:], keep_late_hbm)
    d_rows_ref[...] = to_tiles(mm(picker, d_inputs[...]).astype(bf16))
    for copy in leaving:
        copy.wait()


def run_layer(me, lengths, slot, leaf, rows, table, w_in, w_out, tangent):
    count, width = tangent.shape
    smem = pl.BlockSpec(memory_space=pltpu.SMEM)
    vmem = pl.BlockSpec(memory_space=pltpu.VMEM)
    hbm = pl.BlockSpec(memory_space=pltpu.HBM)
    shape = jax.ShapeDtypeStruct
    columns = 5 * width + width // 2
    return pl.pallas_call(
        layer_kernel,
        name="layer",
        out_shape=(
            shape((count, width), bf16),
            shape(rows.shape, bf16),
            shape((width // 2, SPLIT), bf16),
            shape((width // 2, SPLIT), bf16),
            shape((width // 2, columns - SPLIT), bf16),
            shape((width // 2, columns - SPLIT), bf16),
        ),
        in_specs=[smem, smem] + [vmem] * 3 + [hbm] * 4,
        out_specs=(hbm, vmem, hbm, hbm, hbm, hbm),
        scratch_shapes=[
            pltpu.VMEM((count, width), bf16),
            pltpu.VMEM((count, width), bf16),
            pltpu.VMEM((count, 4 * width), bf16),
            pltpu.VMEM((width, columns), bf16),
            pltpu.VMEM((count, width), bf16),
            pltpu.VMEM((count, width), bf16),
            pltpu.VMEM((width, count), bf16),
            pltpu.VMEM((width, count), bf16),
            pltpu.VMEM((count, 4 * width), bf16),
            pltpu.VMEM((count, 4 * width), bf16),
            pltpu.VMEM((HEADS, count, count), bf16),
            pltpu.VMEM((HEADS, count, count), bf16),
            pltpu.VMEM((count, width), f32),
            pltpu.VMEM((count, width), bf16),
            pltpu.VMEM((HEADS, count, count), bf16),
            pltpu.VMEM((count, width), bf16),
            pltpu.VMEM((count, count), bf16),
            pltpu.VMEM((count, count), bf16),
            pltpu.VMEM((width, count), bf16),
            pltpu.VMEM((width, count), bf16),
            pltpu.VMEM((count, width), bf16),
            pltpu.VMEM((width, width // 2), bf16),
            pltpu.VMEM(table.shape, bf16),
            pltpu.VMEM(w_in.shape, bf16),
            pltpu.VMEM(w_out.shape, bf16),
            pltpu.VMEM(tangent.shape, bf16),
            pltpu.SemaphoreType.DMA((4,)),
            pltpu.SemaphoreType.DMA((5,)),
        ],
        compiler_params=pltpu.CompilerParams(vmem_limit_bytes=LAYER_VMEM),
        cost_estimate=pl.CostEstimate(flops=6 * 10**9, bytes_accessed=10**7, transcendentals=10**6),
    )(me, lengths, slot, leaf, rows, table, w_in, w_out, tangent)


def finish_kernel(
    me_ref, chosen_ref, returned_ref, early_own, early_other, late_own, late_other,
    table_hbm, leaf_hbm, in_hbm, out_hbm, grads, table, sems,
):
    width, columns = grads.shape
    leaves = leaf_hbm.shape[0]
    me = me_ref[0]
    half_rows = width // 2
    leaving = []

    def leave(source, target):
        copy = pltpu.make_async_copy(source, target, sems.at[len(leaving)])
        copy.start()
        leaving.append(copy)

    early, late = chunk_order(me, EARLY), chunk_order(me, LATE, SHARED)

    def place(chunks, own, other, low, high, at):
        for spot, chunk in enumerate(chunks):
            source = own if spot * ROWS < half_rows else other
            row = spot * ROWS % half_rows
            start = pl.multiple_of(chunk * ROWS, ROWS)
            grads[pl.ds(start, ROWS), at + low : at + high] = source[
                row : row + ROWS, low:high
            ].astype(f32)

    place(late, late_own, late_other, 0, width, SPLIT)
    leave(grads.at[:, SPLIT : SPLIT + width], out_hbm)
    place(late, late_own, late_other, width, columns - SPLIT, SPLIT)
    for half in range(2):
        leave(
            grads.at[half * leaves : (half + 1) * leaves, SPLIT + width :],
            leaf_hbm.at[:, half * (width // 2) : (half + 1) * (width // 2)],
        )
    row = lax.broadcasted_iota(jnp.int32, chosen_ref.shape, 0)
    parts = width // BLOCK
    for part in range(parts):
        mine = jnp.where(row % parts == part, chosen_ref[...].astype(f32), 0.0).astype(bf16)
        table[:, part * BLOCK : (part + 1) * BLOCK] = mm_tn(mine, returned_ref[...])
    leave(table, table_hbm)
    for low in range(0, SPLIT, width):
        place(early, early_own, early_other, low, low + width, 0)
        leave(grads.at[:, low : low + width], in_hbm.at[:, low : low + width])
    for copy in leaving:
        copy.wait()


def run_finish(me, chosen, returned, early_own, early_other, late_own, late_other, leaves):
    smem = pl.BlockSpec(memory_space=pltpu.SMEM)
    vmem = pl.BlockSpec(memory_space=pltpu.VMEM)
    hbm = pl.BlockSpec(memory_space=pltpu.HBM)
    shape = jax.ShapeDtypeStruct
    width = early_own.shape[1] // 4
    return pl.pallas_call(
        finish_kernel,
        name="finish",
        out_shape=(
            shape((chosen.shape[1], width), f32),
            shape((leaves, width), f32),
            shape((width, 4 * width), f32),
            shape((width, width), f32),
        ),
        in_specs=[smem] + [vmem] * 6,
        out_specs=(hbm,) * 4,
        scratch_shapes=[
            pltpu.VMEM((width, early_own.shape[1] + late_own.shape[1]), f32),
            pltpu.VMEM((chosen.shape[1], width), f32),
            pltpu.SemaphoreType.DMA((8,)),
        ],
        compiler_params=pltpu.CompilerParams(vmem_limit_bytes=32 * 2**20),
    )(me, chosen, returned, early_own, early_other, late_own, late_other)


def load_kernel(*refs):
    for source, target in zip(refs[: len(refs) // 2], refs[len(refs) // 2 :]):
        target[...] = source[...]


def run_load(*arrays):
    vmem = pl.BlockSpec(memory_space=pltpu.VMEM)
    return pl.pallas_call(
        load_kernel,
        name="load",
        out_shape=tuple(jax.ShapeDtypeStruct(array.shape, array.dtype) for array in arrays),
        in_specs=[vmem] * len(arrays),
        out_specs=(vmem,) * len(arrays),
        compiler_params=pltpu.CompilerParams(vmem_limit_bytes=8 * 2**20),
        cost_estimate=pl.CostEstimate(flops=0, bytes_accessed=4 * 2**20, transcendentals=0),
    )(*arrays)


def merge_kernel(keep_ref, other_ref, *outs):
    rows = outs[0].shape[0]
    for part, out in enumerate(outs):
        at = slice(part * rows, (part + 1) * rows)
        out[...] = (keep_ref[at, :].astype(f32) + other_ref[at, :].astype(f32)).astype(bf16)


def run_merge(keep, other, parts):
    vmem = pl.BlockSpec(memory_space=pltpu.VMEM)
    part = jax.ShapeDtypeStruct((keep.shape[0] // parts, keep.shape[1]), bf16)
    return pl.pallas_call(
        merge_kernel,
        name="merge",
        out_shape=(part,) * parts,
        in_specs=[vmem] * 2,
        out_specs=(vmem,) * parts,
        compiler_params=pltpu.CompilerParams(vmem_limit_bytes=8 * 2**20),
    )(keep, other)


def exchange(blocks):
    return lax.all_to_all(blocks, ("dp", "rep"), split_axis=0, concat_axis=0, tiled=True)


def swap(block, mask, count):
    return lax.ppermute(block, ("dp", "rep"), [(i, i ^ mask) for i in range(count)])


def add(parts):
    return sum(part.astype(f32) for part in parts)


def shares(parts, group):
    size = 2 ** len(group)
    rows = parts[0].shape[0] // size
    return [
        add(part[digit * rows : (digit + 1) * rows] for part in parts).astype(bf16)
        for digit in range(1, size)
    ]


def swap_all(blocks, group, count):
    return [
        swap(block, mask_of(group, digit), count) for digit, block in enumerate(blocks, start=1)
    ]


def extend(parts, got):
    return [part[: got[0].shape[0]] for part in parts] + got


def split_up(parts, group, count):
    return extend(parts, swap_all(shares(parts, group), group, count))


def sum_with(block, group, count):
    return block.astype(f32) + swap(block, mask_of(group, 1), count).astype(f32)


def join(block, group, count):
    pieces = swap_all([block] * (2 ** len(group) - 1), group, count)
    return jnp.concatenate([block] + pieces, axis=0)


def reduce_and_gather(early, late, d_rows, count):
    _, near, far = EARLY
    _, first, second = LATE
    early_other, late_other = swap(early[1], 1, count), swap(late[1], 1, count)
    early_own, late_own = run_load(early[0], late[0])
    early, *early_blocks = run_merge(early_own, early_other, 2 ** len(near))
    late, *late_blocks = run_merge(late_own, late_other, 2 ** len(first))
    early_blocks, late_blocks = lax.optimization_barrier((early_blocks, late_blocks))
    early_got = swap_all(early_blocks, near, count)
    late = split_up([late] + swap_all(late_blocks, first, count), second, count)
    early_got, late = lax.optimization_barrier((early_got, late))
    early, late = split_up([early] + early_got, far, count), add(late).astype(bf16)
    late = sum_with(late, SHARED[0], count).astype(bf16)
    early, late = add(early), sum_with(late, SHARED[1], count)
    reach = CHUNKS
    while reach < count:
        early, late = early + swap(early, reach, count), late + swap(late, reach, count)
        reach *= 2
    early = join((early * (1.0 / count)).astype(bf16), far, count)
    early, late = lax.optimization_barrier((early, (late * (1.0 / count)).astype(bf16)))
    pieces = swap_all([early] * (2 ** len(near) - 1), near, count)
    late, d_rows = lax.optimization_barrier((join(late, second, count), d_rows))
    returned = exchange(d_rows)
    late = join(late, first, count)
    pieces, late, returned = lax.optimization_barrier((pieces, late, returned))
    early = jnp.concatenate([early] + pieces, axis=0)
    return returned, early, swap(early, 1, count), late, swap(late, 1, count)


def on_device(
    item_table, requests, event_slot, lengths, leaf_ids, leaf_table, w_in, w_out, cotangent
):
    count = lax.axis_size("dp") * lax.axis_size("rep")
    place = lax.axis_index(("dp", "rep")).astype(jnp.int32)
    me = (place & (CHUNKS - 1)).reshape(1)
    slot = event_slot.reshape(1, -1)
    leaf = leaf_ids.T
    asked = exchange(requests[0])
    fetched, chosen = run_lookup(asked, item_table)
    arrived = exchange(fetched)
    output, d_rows, keep, send, keep_late, send_late = run_layer(
        me, lengths, slot, leaf, arrived, leaf_table, w_in, w_out, cotangent
    )
    returned, early, early_other, late, late_other = reduce_and_gather(
        (keep, send), (keep_late, send_late), d_rows, count
    )
    table_grad, leaf_mean, in_mean, out_mean = run_finish(
        me, chosen, returned, early, early_other, late, late_other, leaf_table.shape[0]
    )
    return (output, table_grad, leaf_mean, in_mean, out_mean)


def solution(mesh):
    return jax.shard_map(
        on_device,
        mesh=mesh,
        in_specs=(
            P(("dp", "rep"), None),
            P(("dp", "rep"), None, None),
            P(("dp", "rep")),
            P(("dp", "rep"), None),
            P(("dp", "rep"), None),
            P(),
            P(),
            P(),
            P(("dp", "rep"), None),
        ),
        out_specs=(P(("dp", "rep"), None), P(("dp", "rep"), None), P(), P(), P()),
        check_vma=False,
    )
```

```python
import functools
import jax
import jax.numpy as jnp
from jax import lax
from jax.experimental import pallas as pl
from jax.experimental.pallas import tpu as pltpu
from jax.sharding import PartitionSpec as P

HEADS = 4
MAXLEN = 256
BLOCK = 128
ROWS = 16
epsilon = 1e-06
f32 = jnp.float32
bf16 = jnp.bfloat16

EARLY = ((0,), (1, 2), (3, 4))
LATE = ((0,), (3,), (4,))
SHARED = ((2,), (1,))
SPLIT = 2048
CHUNKS = 32
STRIP = 32
LAYER_VMEM = 60 * 2**20


def dot(a, b, contract):
    return lax.dot_general(a, b, ((contract[0], contract[1]), ((), ())), preferred_element_type=f32)


def mm(a, b):
    return dot(a, b, ((1,), (0,)))


def mm_nt(a, b):
    return dot(a, b, ((1,), (1,)))


def mm_tn(a, b):
    return dot(a, b, ((0,), (0,)))


def mask_of(group, digit):
    return sum(((digit >> k) & 1) << bit for k, bit in enumerate(group))


def chunk_order(me, route, shared=()):
    masks = [0]
    for group in route + shared:
        masks = [mask ^ mask_of(group, digit) for mask in masks for digit in range(2 ** len(group))]
    for group in shared:
        me = me & ~mask_of(group, 1)
    return [me ^ mask for mask in masks]


def spans(count):
    for start in range(0, count, BLOCK):
        low = max(0, start - (MAXLEN - 1)) // BLOCK * BLOCK
        yield start, low, start + BLOCK


def strips(start, stop):
    return [slice(at, at + STRIP) for at in range(start, stop, STRIP)]


def silu(half):
    curve = jnp.tanh(half)
    value = (half + half * curve).astype(bf16)
    half, curve = half.astype(bf16), curve.astype(bf16)
    return value, (0.5 + 0.5 * curve) * (1.0 + half * (1.0 - curve))


def center(values):
    values = values - jnp.mean(values, axis=-1, keepdims=True)
    return values, lax.rsqrt(jnp.mean(values * values, axis=-1, keepdims=True) + epsilon)


def pull_normalize(change, normed, scale):
    return scale * (
        change
        - jnp.mean(change, axis=-1, keepdims=True)
        - normed * jnp.mean(change * normed, axis=-1, keepdims=True)
    )


def pickers(slots, slot_ref, leaf_ref, leaves):
    count = slot_ref.shape[1]
    picker = lax.broadcasted_iota(jnp.int32, (slots, count), 0) == slot_ref[...]
    trees = leaf_ref.shape[0]
    each = leaves // trees
    spots = lax.broadcasted_iota(jnp.int32, (each, count), 0)
    onehot = [(spots == leaf_ref[t : t + 1, :]).astype(f32).astype(bf16) for t in range(trees)]
    return picker.astype(f32).astype(bf16), jnp.concatenate(onehot, axis=0)


def permute_rows(chunks, source, target):
    for place, chunk in enumerate(chunks):
        start = pl.multiple_of(chunk * ROWS, ROWS)
        target[place * ROWS : (place + 1) * ROWS, :] = source[pl.ds(start, ROWS), :]


def zero_one(condition):
    return jnp.where(condition, 1.0, 0.0).astype(bf16)


def to_tiles(rows):
    parts = rows.shape[1] // BLOCK
    shape = (rows.shape[0] * parts, rows.shape[0])
    row, column = (lax.broadcasted_iota(jnp.int32, shape, axis) for axis in (0, 1))
    total = jnp.zeros((shape[0], BLOCK), f32)
    for part in range(parts):
        place = zero_one(row == column * parts + part)
        total = total + mm(place, rows[:, part * BLOCK : (part + 1) * BLOCK])
    return total.astype(bf16)


def from_tiles(block, width):
    parts = width // BLOCK
    shape = (block.shape[0] // parts, block.shape[0])
    row, column = (lax.broadcasted_iota(jnp.int32, shape, axis) for axis in (0, 1))
    pieces = [mm(zero_one(column == row * parts + part), block) for part in range(parts)]
    return jnp.concatenate(pieces, axis=1).astype(bf16)


def lookup_kernel(asked_ref, table_ref, rows_ref, chosen_ref):
    count, each = asked_ref.shape
    owned, width = table_ref.shape
    parts = width // BLOCK
    many = count * each * parts
    spot = lax.broadcasted_iota(jnp.int32, (count, owned), 1)
    row = lax.broadcasted_iota(jnp.int32, (many, count), 0)
    device = lax.broadcasted_iota(jnp.int32, (many, count), 1)
    chosen = jnp.zeros((many, owned), f32)
    for k in range(each):
        base = (device * each + k) * parts
        here = zero_one(jnp.logical_and(row >= base, row < base + parts))
        chosen = chosen + mm(here, zero_one(spot == asked_ref[:, k : k + 1]))
    chosen_ref[...] = chosen.astype(bf16)
    part_of = lax.broadcasted_iota(jnp.int32, (many, owned), 0) & (parts - 1)
    total = jnp.zeros((many, BLOCK), f32)
    for part in range(parts):
        mine = jnp.where(part_of == part, chosen, 0.0).astype(bf16)
        total = total + mm(mine, table_ref[:, part * BLOCK : (part + 1) * BLOCK])
    rows_ref[...] = total.astype(bf16)


def run_lookup(asked, table):
    vmem = pl.BlockSpec(memory_space=pltpu.VMEM)
    shape = jax.ShapeDtypeStruct
    many = asked.shape[0] * asked.shape[1] * table.shape[1] // BLOCK
    return pl.pallas_call(
        lookup_kernel,
        name="lookup",
        out_shape=(
            shape((many, BLOCK), bf16),
            shape((many, table.shape[0]), bf16),
        ),
        in_specs=[vmem, vmem],
        out_specs=(vmem,) * 2,
        compiler_params=pltpu.CompilerParams(vmem_limit_bytes=16 * 2**20),
    )(asked, table)


def layer_kernel(
    me_ref, lengths_ref, slot_ref, leaf_ref, rows_ref, table_hbm, in_hbm, out_hbm, tangent_hbm,
    output_hbm, d_rows_ref, keep_hbm, send_hbm, keep_late_hbm, send_late_hbm,
    inputs, gated, d_pre, grads, output,
    normed, turned, moved, hidden, slope, weights, weights_slope, mixed, d_mixed,
    d_score, d_gated, allowed, allowed_scale, keys_t, values_t, d_inputs, leaf_grad, table, w_in, w_out, tangent, sems, out_sems,
):
    count, width = inputs.shape
    head = width // HEADS
    half_scale = 0.5 * head ** (-0.5)
    half_rows = width // 2
    copies = [
        pltpu.make_async_copy(source, target, sems.at[k])
        for k, (source, target) in enumerate(
            ((table_hbm, table), (in_hbm, w_in), (out_hbm, w_out), (tangent_hbm, tangent))
        )
    ]
    for copy in copies:
        copy.start()
    leaving = []

    def leave(source, target):
        copy = pltpu.make_async_copy(source, target, out_sems.at[len(leaving)])
        copy.start()
        leaving.append(copy)

    rows = from_tiles(rows_ref[...], width)
    picker, onehot = pickers(rows.shape[0], slot_ref, leaf_ref, table.shape[0])
    ends = []
    total = 0
    for place in range(lengths_ref.shape[1]):
        total = total + lengths_ref[0, place]
        ends.append(total)
    for start, low, high in spans(count):
        at = slice(start, start + BLOCK)
        row = start + lax.broadcasted_iota(jnp.int32, (BLOCK, high - low), 0)
        column = low + lax.broadcasted_iota(jnp.int32, (BLOCK, high - low), 1)
        first = jnp.zeros_like(row)
        for end in ends[:-1]:
            first = jnp.where(row >= end, end, first)
        seen = jnp.logical_and(column >= first, column <= row)
        allowed[at, low:high] = jnp.where(seen, 1.0, 0.0).astype(bf16)
        allowed_scale[at, low:high] = jnp.where(seen, 2.0 * half_scale, 0.0).astype(bf16)
    copies[0].wait()
    inputs[...] = (mm_tn(picker, rows) + mm_tn(onehot, table[...])).astype(bf16)
    for at in strips(0, count):
        values, scale = center(inputs[at, :].astype(f32))
        normed[at, :] = (values * scale).astype(bf16)
    turned[...] = normed[...].T
    copies[1].wait()
    for start in range(0, 4 * width, 2 * BLOCK):
        to = slice(start, start + 2 * BLOCK)
        halves = mm(normed[...], w_in[:, to]) * 0.5
        for at in strips(0, count):
            value, slope_at = silu(halves[at, :])
            hidden[at, to] = value
            slope[at, to] = slope_at
    keys_t[...] = hidden[:, 3 * width :].T
    values_t[...] = hidden[:, width : 2 * width].T
    for start, low, high in spans(count):
        at = slice(start, start + BLOCK)
        end = start // (2 * BLOCK) * 2 * BLOCK + 2 * BLOCK
        for out in (slice(0, low), slice(high, end)):
            if out.start < out.stop:
                nothing = jnp.zeros((HEADS, BLOCK, out.stop - out.start), bf16)
                weights[:, at, out] = nothing
                d_score[:, at, out] = nothing
    for h in range(HEADS):
        own = slice(h * head, (h + 1) * head)
        value_at = slice(width + h * head, width + (h + 1) * head)
        query_at = slice(2 * width + h * head, 2 * width + (h + 1) * head)
        key_at = slice(3 * width + h * head, 3 * width + (h + 1) * head)
        for start, low, high in spans(count):
            at = slice(start, start + BLOCK)
            halves = mm(hidden[at, query_at], keys_t[own, low:high]) * half_scale
            for strip in strips(0, BLOCK):
                to = slice(start + strip.start, start + strip.stop)
                value, slope_at = silu(halves[strip, :])
                weights[h, to, low:high] = value * allowed[to, low:high]
                weights_slope[h, to, low:high] = slope_at * allowed_scale[to, low:high]
        for start in range(0, count, 2 * BLOCK):
            at = slice(start, start + 2 * BLOCK)
            high = start + 2 * BLOCK
            mixed[at, h * head : (h + 1) * head] = mm(
                weights[h, at, :high], hidden[:high, value_at]
            )
    copies[2].wait()
    copies[3].wait()
    d_gated[...] = mm_nt(tangent[...], w_out[...]).astype(bf16)
    for at in strips(0, count):
        values, scale = center(mixed[at, :])
        values = values * scale
        gates = hidden[at, :width].astype(f32)
        change = d_gated[at, :].astype(f32)
        gated[at, :] = (values * gates).astype(bf16)
        d_pre[at, :width] = (change * values).astype(bf16) * slope[at, :width]
        d_mixed[at, :] = pull_normalize(change * gates, values, scale).astype(bf16)
    for h in range(HEADS):
        own = slice(h * head, (h + 1) * head)
        value_at = slice(width + h * head, width + (h + 1) * head)
        query_at = slice(2 * width + h * head, 2 * width + (h + 1) * head)
        key_at = slice(3 * width + h * head, 3 * width + (h + 1) * head)
        for start, low, high in spans(count):
            at = slice(start, start + BLOCK)
            d_weights = mm(d_mixed[at, own], values_t[own, low:high]).astype(bf16)
            d_score[h, at, low:high] = d_weights * weights_slope[h, at, low:high]
        for start in range(0, count, 2 * BLOCK):
            at = slice(start, start + 2 * BLOCK)
            high = start + 2 * BLOCK
            d_query = mm(d_score[h, at, :high], hidden[:high, key_at])
            d_pre[at, query_at] = d_query.astype(bf16) * slope[at, query_at]
            d_key = mm_tn(d_score[h, start:, at], hidden[start:, query_at])
            d_pre[at, key_at] = d_key.astype(bf16) * slope[at, key_at]
            d_value = mm_tn(weights[h, start:, at], d_mixed[start:, own])
            d_pre[at, value_at] = d_value.astype(bf16) * slope[at, value_at]
    me = me_ref[0]
    early, late = chunk_order(me, EARLY), chunk_order(me, LATE, SHARED)
    permute_rows(early, turned, moved)
    for start in range(0, 4 * width, 2 * BLOCK):
        to = slice(start, start + 2 * BLOCK)
        grads[:, to] = mm(moved[...], d_pre[:, to]).astype(bf16)
    leave(grads.at[half_rows:, :SPLIT], send_hbm)
    leave(grads.at[:half_rows, :SPLIT], keep_hbm)
    turned[...] = gated[...].T
    permute_rows(late, turned, moved)
    grads[:, 4 * width : 5 * width] = mm(moved[...], tangent[...]).astype(bf16)
    output[...] = (mm(gated[...], w_out[...]) + inputs[...].astype(f32)).astype(bf16)
    leave(output, output_hbm)
    normed_change = mm_nt(d_pre[...], w_in[...])
    for at in strips(0, count):
        values, scale = center(inputs[at, :].astype(f32))
        change = pull_normalize(normed_change[at, :], values * scale, scale)
        d_inputs[at, :] = (change + tangent[at, :].astype(f32)).astype(bf16)
    leaves = table.shape[0]
    d_leaf = mm(onehot, d_inputs[...]).astype(bf16)
    leaf_grad[:leaves, :] = d_leaf[:, : width // 2]
    leaf_grad[leaves:, :] = d_leaf[:, width // 2 :]
    permute_rows(late, leaf_grad, grads.at[:, 5 * width :])
    leave(grads.at[half_rows:, SPLIT:], send_late_hbm)
    leave(grads.at[:half_rows, SPLIT:], keep_late_hbm)
    d_rows_ref[...] = to_tiles(mm(picker, d_inputs[...]).astype(bf16))
    for copy in leaving:
        copy.wait()


def run_layer(me, lengths, slot, leaf, rows, table, w_in, w_out, tangent):
    count, width = tangent.shape
    smem = pl.BlockSpec(memory_space=pltpu.SMEM)
    vmem = pl.BlockSpec(memory_space=pltpu.VMEM)
    hbm = pl.BlockSpec(memory_space=pltpu.HBM)
    shape = jax.ShapeDtypeStruct
    columns = 5 * width + width // 2
    return pl.pallas_call(
        layer_kernel,
        name="layer",
        out_shape=(
            shape((count, width), bf16),
            shape(rows.shape, bf16),
            shape((width // 2, SPLIT), bf16),
            shape((width // 2, SPLIT), bf16),
            shape((width // 2, columns - SPLIT), bf16),
            shape((width // 2, columns - SPLIT), bf16),
        ),
        in_specs=[smem, smem] + [vmem] * 3 + [hbm] * 4,
        out_specs=(hbm, vmem, hbm, hbm, hbm, hbm),
        scratch_shapes=[
            pltpu.VMEM((count, width), bf16),
            pltpu.VMEM((count, width), bf16),
            pltpu.VMEM((count, 4 * width), bf16),
            pltpu.VMEM((width, columns), bf16),
            pltpu.VMEM((count, width), bf16),
            pltpu.VMEM((count, width), bf16),
            pltpu.VMEM((width, count), bf16),
            pltpu.VMEM((width, count), bf16),
            pltpu.VMEM((count, 4 * width), bf16),
            pltpu.VMEM((count, 4 * width), bf16),
            pltpu.VMEM((HEADS, count, count), bf16),
            pltpu.VMEM((HEADS, count, count), bf16),
            pltpu.VMEM((count, width), f32),
            pltpu.VMEM((count, width), bf16),
            pltpu.VMEM((HEADS, count, count), bf16),
            pltpu.VMEM((count, width), bf16),
            pltpu.VMEM((count, count), bf16),
            pltpu.VMEM((count, count), bf16),
            pltpu.VMEM((width, count), bf16),
            pltpu.VMEM((width, count), bf16),
            pltpu.VMEM((count, width), bf16),
            pltpu.VMEM((width, width // 2), bf16),
            pltpu.VMEM(table.shape, bf16),
            pltpu.VMEM(w_in.shape, bf16),
            pltpu.VMEM(w_out.shape, bf16),
            pltpu.VMEM(tangent.shape, bf16),
            pltpu.SemaphoreType.DMA((4,)),
            pltpu.SemaphoreType.DMA((5,)),
        ],
        compiler_params=pltpu.CompilerParams(vmem_limit_bytes=LAYER_VMEM),
        cost_estimate=pl.CostEstimate(flops=6 * 10**9, bytes_accessed=10**7, transcendentals=10**6),
    )(me, lengths, slot, leaf, rows, table, w_in, w_out, tangent)


def finish_kernel(
    me_ref, chosen_ref, returned_ref, early_own, early_other, late_own, late_other,
    table_hbm, leaf_hbm, in_hbm, out_hbm, grads, table, sems,
):
    width, columns = grads.shape
    leaves = leaf_hbm.shape[0]
    me = me_ref[0]
    half_rows = width // 2
    leaving = []

    def leave(source, target):
        copy = pltpu.make_async_copy(source, target, sems.at[len(leaving)])
        copy.start()
        leaving.append(copy)

    early, late = chunk_order(me, EARLY), chunk_order(me, LATE, SHARED)

    def place(chunks, own, other, low, high, at):
        for spot, chunk in enumerate(chunks):
            source = own if spot * ROWS < half_rows else other
            row = spot * ROWS % half_rows
            start = pl.multiple_of(chunk * ROWS, ROWS)
            grads[pl.ds(start, ROWS), at + low : at + high] = source[
                row : row + ROWS, low:high
            ].astype(f32)

    place(late, late_own, late_other, 0, width, SPLIT)
    leave(grads.at[:, SPLIT : SPLIT + width], out_hbm)
    place(late, late_own, late_other, width, columns - SPLIT, SPLIT)
    for half in range(2):
        leave(
            grads.at[half * leaves : (half + 1) * leaves, SPLIT + width :],
            leaf_hbm.at[:, half * (width // 2) : (half + 1) * (width // 2)],
        )
    parts = width // BLOCK
    part_of = lax.broadcasted_iota(jnp.int32, chosen_ref.shape, 0) & (parts - 1)
    for part in range(parts):
        mine = jnp.where(part_of == part, chosen_ref[...].astype(f32), 0.0).astype(bf16)
        table[:, part * BLOCK : (part + 1) * BLOCK] = mm_tn(mine, returned_ref[...])
    leave(table, table_hbm)
    for low in range(0, SPLIT, width):
        place(early, early_own, early_other, low, low + width, 0)
        leave(grads.at[:, low : low + width], in_hbm.at[:, low : low + width])
    for copy in leaving:
        copy.wait()


def run_finish(me, chosen, returned, early_own, early_other, late_own, late_other, leaves):
    smem = pl.BlockSpec(memory_space=pltpu.SMEM)
    vmem = pl.BlockSpec(memory_space=pltpu.VMEM)
    hbm = pl.BlockSpec(memory_space=pltpu.HBM)
    shape = jax.ShapeDtypeStruct
    width = early_own.shape[1] // 4
    return pl.pallas_call(
        finish_kernel,
        name="finish",
        out_shape=(
            shape((chosen.shape[1], width), f32),
            shape((leaves, width), f32),
            shape((width, 4 * width), f32),
            shape((width, width), f32),
        ),
        in_specs=[smem] + [vmem] * 6,
        out_specs=(hbm,) * 4,
        scratch_shapes=[
            pltpu.VMEM((width, early_own.shape[1] + late_own.shape[1]), f32),
            pltpu.VMEM((chosen.shape[1], width), f32),
            pltpu.SemaphoreType.DMA((8,)),
        ],
        compiler_params=pltpu.CompilerParams(vmem_limit_bytes=32 * 2**20),
    )(me, chosen, returned, early_own, early_other, late_own, late_other)


def load_kernel(*refs):
    for source, target in zip(refs[: len(refs) // 2], refs[len(refs) // 2 :]):
        target[...] = source[...]


def run_load(*arrays):
    vmem = pl.BlockSpec(memory_space=pltpu.VMEM)
    return pl.pallas_call(
        load_kernel,
        name="load",
        out_shape=tuple(jax.ShapeDtypeStruct(array.shape, array.dtype) for array in arrays),
        in_specs=[vmem] * len(arrays),
        out_specs=(vmem,) * len(arrays),
        compiler_params=pltpu.CompilerParams(vmem_limit_bytes=8 * 2**20),
        cost_estimate=pl.CostEstimate(flops=0, bytes_accessed=4 * 2**20, transcendentals=0),
    )(*arrays)


def merge_kernel(keep_ref, other_ref, *outs):
    rows = outs[0].shape[0]
    for part, out in enumerate(outs):
        at = slice(part * rows, (part + 1) * rows)
        out[...] = (keep_ref[at, :].astype(f32) + other_ref[at, :].astype(f32)).astype(bf16)


def run_merge(keep, other, parts):
    vmem = pl.BlockSpec(memory_space=pltpu.VMEM)
    part = jax.ShapeDtypeStruct((keep.shape[0] // parts, keep.shape[1]), bf16)
    return pl.pallas_call(
        merge_kernel,
        name="merge",
        out_shape=(part,) * parts,
        in_specs=[vmem] * 2,
        out_specs=(vmem,) * parts,
        compiler_params=pltpu.CompilerParams(vmem_limit_bytes=8 * 2**20),
    )(keep, other)


def exchange(blocks):
    return lax.all_to_all(blocks, ("dp", "rep"), split_axis=0, concat_axis=0, tiled=True)


def swap(block, mask, count):
    return lax.ppermute(block, ("dp", "rep"), [(i, i ^ mask) for i in range(count)])


def add(parts):
    return sum(part.astype(f32) for part in parts)


def shares(parts, group):
    size = 2 ** len(group)
    rows = parts[0].shape[0] // size
    return [
        add(part[digit * rows : (digit + 1) * rows] for part in parts).astype(bf16)
        for digit in range(1, size)
    ]


def swap_all(blocks, group, count):
    return [
        swap(block, mask_of(group, digit), count) for digit, block in enumerate(blocks, start=1)
    ]


def extend(parts, got):
    return [part[: got[0].shape[0]] for part in parts] + got


def split_up(parts, group, count):
    return extend(parts, swap_all(shares(parts, group), group, count))


def sum_with(block, group, count):
    return block.astype(f32) + swap(block, mask_of(group, 1), count).astype(f32)


def join(block, group, count):
    pieces = swap_all([block] * (2 ** len(group) - 1), group, count)
    return jnp.concatenate([block] + pieces, axis=0)


def reduce_and_gather(early, late, d_rows, count):
    _, near, far = EARLY
    _, first, second = LATE
    early_other, late_other = swap(early[1], 1, count), swap(late[1], 1, count)
    early_own, late_own = run_load(early[0], late[0])
    early, *early_blocks = run_merge(early_own, early_other, 2 ** len(near))
    late, *late_blocks = run_merge(late_own, late_other, 2 ** len(first))
    early_blocks, late_blocks = lax.optimization_barrier((early_blocks, late_blocks))
    early_got = swap_all(early_blocks, near, count)
    late = [late] + swap_all(late_blocks, first, count)
    late_got = swap_all(shares(late, second), second, count)
    early_got[0], late, d_rows = lax.optimization_barrier((early_got[0], late, d_rows))
    returned = exchange(d_rows)
    early_got, late = lax.optimization_barrier((early_got, extend(late, late_got)))
    early, late = split_up([early] + early_got, far, count), add(late).astype(bf16)
    late = sum_with(late, SHARED[0], count).astype(bf16)
    early, late = add(early), sum_with(late, SHARED[1], count)
    reach = CHUNKS
    while reach < count:
        early, late = early + swap(early, reach, count), late + swap(late, reach, count)
        reach *= 2
    early = join((early * (1.0 / count)).astype(bf16), far, count)
    early, late = lax.optimization_barrier((early, (late * (1.0 / count)).astype(bf16)))
    pieces = swap_all([early] * (2 ** len(near) - 1), near, count)
    late = join(join(late, second, count), first, count)
    pieces, late = lax.optimization_barrier((pieces, late))
    early = jnp.concatenate([early] + pieces, axis=0)
    return returned, early, swap(early, 1, count), late, swap(late, 1, count)


def on_device(
    item_table, requests, event_slot, lengths, leaf_ids, leaf_table, w_in, w_out, cotangent
):
    count = lax.axis_size("dp") * lax.axis_size("rep")
    place = lax.axis_index(("dp", "rep")).astype(jnp.int32)
    me = (place & (CHUNKS - 1)).reshape(1)
    slot = event_slot.reshape(1, -1)
    leaf = leaf_ids.T
    asked = exchange(requests[0])
    (table,) = run_load(item_table)
    fetched, chosen = run_lookup(asked, table)
    arrived = exchange(fetched)
    output, d_rows, keep, send, keep_late, send_late = run_layer(
        me, lengths, slot, leaf, arrived, leaf_table, w_in, w_out, cotangent
    )
    returned, early, early_other, late, late_other = reduce_and_gather(
        (keep, send), (keep_late, send_late), d_rows, count
    )
    table_grad, leaf_mean, in_mean, out_mean = run_finish(
        me, chosen, returned, early, early_other, late, late_other, leaf_table.shape[0]
    )
    return (output, table_grad, leaf_mean, in_mean, out_mean)


def solution(mesh):
    return jax.shard_map(
        on_device,
        mesh=mesh,
        in_specs=(
            P(("dp", "rep"), None),
            P(("dp", "rep"), None, None),
            P(("dp", "rep")),
            P(("dp", "rep"), None),
            P(("dp", "rep"), None),
            P(),
            P(),
            P(),
            P(("dp", "rep"), None),
        ),
        out_specs=(P(("dp", "rep"), None), P(("dp", "rep"), None), P(), P(), P()),
        check_vma=False,
    )
```

```python
import functools
import jax
import jax.numpy as jnp
from jax import lax
from jax.experimental import pallas as pl
from jax.experimental.pallas import tpu as pltpu
from jax.sharding import PartitionSpec as P

HEADS = 4
MAXLEN = 256
BLOCK = 128
ROWS = 16
epsilon = 1e-06
f32 = jnp.float32
bf16 = jnp.bfloat16

EARLY = ((0,), (1, 2), (3, 4))
LATE = ((0,), (3,), (4,))
SHARED = ((2,), (1,))
SPLIT = 2048
CHUNKS = 32
STRIP = 32
LAYER_VMEM = 60 * 2**20


def dot(a, b, contract):
    return lax.dot_general(a, b, ((contract[0], contract[1]), ((), ())), preferred_element_type=f32)


def mm(a, b):
    return dot(a, b, ((1,), (0,)))


def mm_nt(a, b):
    return dot(a, b, ((1,), (1,)))


def mm_tn(a, b):
    return dot(a, b, ((0,), (0,)))


def mask_of(group, digit):
    return sum(((digit >> k) & 1) << bit for k, bit in enumerate(group))


def chunk_order(me, route, shared=()):
    masks = [0]
    for group in route + shared:
        masks = [mask ^ mask_of(group, digit) for mask in masks for digit in range(2 ** len(group))]
    for group in shared:
        me = me & ~mask_of(group, 1)
    return [me ^ mask for mask in masks]


def spans(count):
    for start in range(0, count, BLOCK):
        low = max(0, start - (MAXLEN - 1)) // BLOCK * BLOCK
        yield start, low, start + BLOCK


def strips(start, stop):
    return [slice(at, at + STRIP) for at in range(start, stop, STRIP)]


def silu(half):
    curve = jnp.tanh(half)
    value = (half + half * curve).astype(bf16)
    half, curve = half.astype(bf16), curve.astype(bf16)
    return value, (0.5 + 0.5 * curve) * (1.0 + half * (1.0 - curve))


def center(values):
    values = values - jnp.mean(values, axis=-1, keepdims=True)
    return values, lax.rsqrt(jnp.mean(values * values, axis=-1, keepdims=True) + epsilon)


def pull_normalize(change, normed, scale):
    return scale * (
        change
        - jnp.mean(change, axis=-1, keepdims=True)
        - normed * jnp.mean(change * normed, axis=-1, keepdims=True)
    )


def pickers(slots, slot_ref, leaf_ref, leaves):
    count = slot_ref.shape[1]
    picker = lax.broadcasted_iota(jnp.int32, (slots, count), 0) == slot_ref[...]
    trees = leaf_ref.shape[0]
    each = leaves // trees
    spots = lax.broadcasted_iota(jnp.int32, (each, count), 0)
    onehot = [(spots == leaf_ref[t : t + 1, :]).astype(f32).astype(bf16) for t in range(trees)]
    return picker.astype(f32).astype(bf16), jnp.concatenate(onehot, axis=0)


def permute_rows(chunks, source, target):
    for place, chunk in enumerate(chunks):
        start = pl.multiple_of(chunk * ROWS, ROWS)
        target[place * ROWS : (place + 1) * ROWS, :] = source[pl.ds(start, ROWS), :]


def zero_one(condition):
    return jnp.where(condition, 1.0, 0.0).astype(bf16)


def to_tiles(rows):
    parts = rows.shape[1] // BLOCK
    shape = (rows.shape[0] * parts, rows.shape[0])
    row, column = (lax.broadcasted_iota(jnp.int32, shape, axis) for axis in (0, 1))
    total = jnp.zeros((shape[0], BLOCK), f32)
    for part in range(parts):
        place = zero_one(row == column * parts + part)
        total = total + mm(place, rows[:, part * BLOCK : (part + 1) * BLOCK])
    return total.astype(bf16)


def from_tiles(block, width):
    parts = width // BLOCK
    shape = (block.shape[0] // parts, block.shape[0])
    row, column = (lax.broadcasted_iota(jnp.int32, shape, axis) for axis in (0, 1))
    pieces = [mm(zero_one(column == row * parts + part), block) for part in range(parts)]
    return jnp.concatenate(pieces, axis=1).astype(bf16)


def lookup_kernel(asked_ref, table_ref, rows_ref, chosen_ref):
    count, each = asked_ref.shape
    owned, width = table_ref.shape
    parts = width // BLOCK
    many = count * each * parts
    spot = lax.broadcasted_iota(jnp.int32, (count, owned), 1)
    row = lax.broadcasted_iota(jnp.int32, (many, count), 0)
    device = lax.broadcasted_iota(jnp.int32, (many, count), 1)
    chosen = jnp.zeros((many, owned), f32)
    for k in range(each):
        base = (device * each + k) * parts
        here = zero_one(jnp.logical_and(row >= base, row < base + parts))
        chosen = chosen + mm(here, zero_one(spot == asked_ref[:, k : k + 1]))
    chosen_ref[...] = chosen.astype(bf16)
    part_of = lax.broadcasted_iota(jnp.int32, (many, owned), 0) & (parts - 1)
    total = jnp.zeros((many, BLOCK), f32)
    for part in range(parts):
        mine = jnp.where(part_of == part, chosen, 0.0).astype(bf16)
        total = total + mm(mine, table_ref[:, part * BLOCK : (part + 1) * BLOCK])
    rows_ref[...] = total.astype(bf16)


def run_lookup(asked, table):
    vmem = pl.BlockSpec(memory_space=pltpu.VMEM)
    shape = jax.ShapeDtypeStruct
    many = asked.shape[0] * asked.shape[1] * table.shape[1] // BLOCK
    return pl.pallas_call(
        lookup_kernel,
        name="lookup",
        out_shape=(
            shape((many, BLOCK), bf16),
            shape((many, table.shape[0]), bf16),
        ),
        in_specs=[vmem, vmem],
        out_specs=(vmem,) * 2,
        compiler_params=pltpu.CompilerParams(vmem_limit_bytes=16 * 2**20),
    )(asked, table)


def layer_kernel(
    me_ref, lengths_ref, slot_ref, leaf_ref, rows_ref, table_hbm, in_hbm, out_hbm, tangent_hbm,
    output_hbm, d_rows_ref, keep_hbm, send_hbm, keep_late_hbm, send_late_hbm,
    inputs, gated, d_pre, grads, output,
    normed, turned, moved, hidden, slope, weights, weights_slope, mixed, d_mixed,
    d_score, d_gated, allowed, allowed_scale, keys_t, values_t, d_inputs, leaf_grad, table, w_in, w_out, tangent, sems, out_sems,
):
    count, width = inputs.shape
    head = width // HEADS
    half_scale = 0.5 * head ** (-0.5)
    half_rows = width // 2
    copies = [
        pltpu.make_async_copy(source, target, sems.at[k])
        for k, (source, target) in enumerate(
            ((table_hbm, table), (in_hbm, w_in), (out_hbm, w_out), (tangent_hbm, tangent))
        )
    ]
    for copy in copies:
        copy.start()
    leaving = []

    def leave(source, target):
        copy = pltpu.make_async_copy(source, target, out_sems.at[len(leaving)])
        copy.start()
        leaving.append(copy)

    rows = from_tiles(rows_ref[...], width)
    picker, onehot = pickers(rows.shape[0], slot_ref, leaf_ref, table.shape[0])
    ends = []
    total = 0
    for place in range(lengths_ref.shape[1]):
        total = total + lengths_ref[0, place]
        ends.append(total)
    for start, low, high in spans(count):
        at = slice(start, start + BLOCK)
        row = start + lax.broadcasted_iota(jnp.int32, (BLOCK, high - low), 0)
        column = low + lax.broadcasted_iota(jnp.int32, (BLOCK, high - low), 1)
        first = jnp.zeros_like(row)
        for end in ends[:-1]:
            first = jnp.where(row >= end, end, first)
        seen = jnp.logical_and(column >= first, column <= row)
        allowed[at, low:high] = jnp.where(seen, 1.0, 0.0).astype(bf16)
        allowed_scale[at, low:high] = jnp.where(seen, 2.0 * half_scale, 0.0).astype(bf16)
    copies[0].wait()
    inputs[...] = (mm_tn(picker, rows) + mm_tn(onehot, table[...])).astype(bf16)
    for at in strips(0, count):
        values, scale = center(inputs[at, :].astype(f32))
        normed[at, :] = (values * scale).astype(bf16)
    turned[...] = normed[...].T
    copies[1].wait()
    for start in range(0, 4 * width, 2 * BLOCK):
        to = slice(start, start + 2 * BLOCK)
        halves = mm(normed[...], w_in[:, to]) * 0.5
        for at in strips(0, count):
            value, slope_at = silu(halves[at, :])
            hidden[at, to] = value
            slope[at, to] = slope_at
    keys_t[...] = hidden[:, 3 * width :].T
    values_t[...] = hidden[:, width : 2 * width].T
    for start, low, high in spans(count):
        at = slice(start, start + BLOCK)
        end = start // (2 * BLOCK) * 2 * BLOCK + 2 * BLOCK
        for out in (slice(0, low), slice(high, end)):
            if out.start < out.stop:
                nothing = jnp.zeros((HEADS, BLOCK, out.stop - out.start), bf16)
                weights[:, at, out] = nothing
                d_score[:, at, out] = nothing
    for h in range(HEADS):
        own = slice(h * head, (h + 1) * head)
        value_at = slice(width + h * head, width + (h + 1) * head)
        query_at = slice(2 * width + h * head, 2 * width + (h + 1) * head)
        key_at = slice(3 * width + h * head, 3 * width + (h + 1) * head)
        for start, low, high in spans(count):
            at = slice(start, start + BLOCK)
            halves = mm(hidden[at, query_at], keys_t[own, low:high]) * half_scale
            for strip in strips(0, BLOCK):
                to = slice(start + strip.start, start + strip.stop)
                value, slope_at = silu(halves[strip, :])
                weights[h, to, low:high] = value * allowed[to, low:high]
                weights_slope[h, to, low:high] = slope_at * allowed_scale[to, low:high]
        for start in range(0, count, 2 * BLOCK):
            at = slice(start, start + 2 * BLOCK)
            high = start + 2 * BLOCK
            mixed[at, h * head : (h + 1) * head] = mm(
                weights[h, at, :high], hidden[:high, value_at]
            )
    copies[2].wait()
    copies[3].wait()
    d_gated[...] = mm_nt(tangent[...], w_out[...]).astype(bf16)
    for at in strips(0, count):
        values, scale = center(mixed[at, :])
        values = values * scale
        gates = hidden[at, :width].astype(f32)
        change = d_gated[at, :].astype(f32)
        gated[at, :] = (values * gates).astype(bf16)
        d_pre[at, :width] = (change * values).astype(bf16) * slope[at, :width]
        d_mixed[at, :] = pull_normalize(change * gates, values, scale).astype(bf16)
    for h in range(HEADS):
        own = slice(h * head, (h + 1) * head)
        value_at = slice(width + h * head, width + (h + 1) * head)
        query_at = slice(2 * width + h * head, 2 * width + (h + 1) * head)
        key_at = slice(3 * width + h * head, 3 * width + (h + 1) * head)
        for start, low, high in spans(count):
            at = slice(start, start + BLOCK)
            d_weights = mm(d_mixed[at, own], values_t[own, low:high]).astype(bf16)
            d_score[h, at, low:high] = d_weights * weights_slope[h, at, low:high]
        for start in range(0, count, 2 * BLOCK):
            at = slice(start, start + 2 * BLOCK)
            high = start + 2 * BLOCK
            d_query = mm(d_score[h, at, :high], hidden[:high, key_at])
            d_pre[at, query_at] = d_query.astype(bf16) * slope[at, query_at]
            d_key = mm_tn(d_score[h, start:, at], hidden[start:, query_at])
            d_pre[at, key_at] = d_key.astype(bf16) * slope[at, key_at]
            d_value = mm_tn(weights[h, start:, at], d_mixed[start:, own])
            d_pre[at, value_at] = d_value.astype(bf16) * slope[at, value_at]
    me = me_ref[0]
    early, late = chunk_order(me, EARLY), chunk_order(me, LATE, SHARED)
    permute_rows(early, turned, moved)
    for start in range(0, 4 * width, 2 * BLOCK):
        to = slice(start, start + 2 * BLOCK)
        grads[:, to] = mm(moved[...], d_pre[:, to]).astype(bf16)
    leave(grads.at[half_rows:, :SPLIT], send_hbm)
    leave(grads.at[:half_rows, :SPLIT], keep_hbm)
    turned[...] = gated[...].T
    permute_rows(late, turned, moved)
    grads[:, 4 * width : 5 * width] = mm(moved[...], tangent[...]).astype(bf16)
    output[...] = (mm(gated[...], w_out[...]) + inputs[...].astype(f32)).astype(bf16)
    leave(output, output_hbm)
    normed_change = mm_nt(d_pre[...], w_in[...])
    for at in strips(0, count):
        values, scale = center(inputs[at, :].astype(f32))
        change = pull_normalize(normed_change[at, :], values * scale, scale)
        d_inputs[at, :] = (change + tangent[at, :].astype(f32)).astype(bf16)
    leaves = table.shape[0]
    d_leaf = mm(onehot, d_inputs[...]).astype(bf16)
    leaf_grad[:leaves, :] = d_leaf[:, : width // 2]
    leaf_grad[leaves:, :] = d_leaf[:, width // 2 :]
    permute_rows(late, leaf_grad, grads.at[:, 5 * width :])
    leave(grads.at[half_rows:, SPLIT:], send_late_hbm)
    leave(grads.at[:half_rows, SPLIT:], keep_late_hbm)
    d_rows_ref[...] = to_tiles(mm(picker, d_inputs[...]).astype(bf16))
    for copy in leaving:
        copy.wait()


def run_layer(me, lengths, slot, leaf, rows, table, w_in, w_out, tangent):
    count, width = tangent.shape
    smem = pl.BlockSpec(memory_space=pltpu.SMEM)
    vmem = pl.BlockSpec(memory_space=pltpu.VMEM)
    hbm = pl.BlockSpec(memory_space=pltpu.HBM)
    shape = jax.ShapeDtypeStruct
    columns = 5 * width + width // 2
    return pl.pallas_call(
        layer_kernel,
        name="layer",
        out_shape=(
            shape((count, width), bf16),
            shape(rows.shape, bf16),
            shape((width // 2, SPLIT), bf16),
            shape((width // 2, SPLIT), bf16),
            shape((width // 2, columns - SPLIT), bf16),
            shape((width // 2, columns - SPLIT), bf16),
        ),
        in_specs=[smem, smem] + [vmem] * 3 + [hbm] * 4,
        out_specs=(hbm, vmem, hbm, hbm, hbm, hbm),
        scratch_shapes=[
            pltpu.VMEM((count, width), bf16),
            pltpu.VMEM((count, width), bf16),
            pltpu.VMEM((count, 4 * width), bf16),
            pltpu.VMEM((width, columns), bf16),
            pltpu.VMEM((count, width), bf16),
            pltpu.VMEM((count, width), bf16),
            pltpu.VMEM((width, count), bf16),
            pltpu.VMEM((width, count), bf16),
            pltpu.VMEM((count, 4 * width), bf16),
            pltpu.VMEM((count, 4 * width), bf16),
            pltpu.VMEM((HEADS, count, count), bf16),
            pltpu.VMEM((HEADS, count, count), bf16),
            pltpu.VMEM((count, width), f32),
            pltpu.VMEM((count, width), bf16),
            pltpu.VMEM((HEADS, count, count), bf16),
            pltpu.VMEM((count, width), bf16),
            pltpu.VMEM((count, count), bf16),
            pltpu.VMEM((count, count), bf16),
            pltpu.VMEM((width, count), bf16),
            pltpu.VMEM((width, count), bf16),
            pltpu.VMEM((count, width), bf16),
            pltpu.VMEM((width, width // 2), bf16),
            pltpu.VMEM(table.shape, bf16),
            pltpu.VMEM(w_in.shape, bf16),
            pltpu.VMEM(w_out.shape, bf16),
            pltpu.VMEM(tangent.shape, bf16),
            pltpu.SemaphoreType.DMA((4,)),
            pltpu.SemaphoreType.DMA((5,)),
        ],
        compiler_params=pltpu.CompilerParams(vmem_limit_bytes=LAYER_VMEM),
        cost_estimate=pl.CostEstimate(flops=6 * 10**9, bytes_accessed=10**7, transcendentals=10**6),
    )(me, lengths, slot, leaf, rows, table, w_in, w_out, tangent)


def finish_kernel(
    me_ref, chosen_ref, returned_ref, early_own, early_other, late_own, late_other,
    table_hbm, leaf_hbm, in_hbm, out_hbm, grads, table, sems,
):
    width, columns = grads.shape
    leaves = leaf_hbm.shape[0]
    me = me_ref[0]
    half_rows = width // 2
    leaving = []

    def leave(source, target):
        copy = pltpu.make_async_copy(source, target, sems.at[len(leaving)])
        copy.start()
        leaving.append(copy)

    early, late = chunk_order(me, EARLY), chunk_order(me, LATE, SHARED)

    def place(chunks, own, other, low, high, at):
        for spot, chunk in enumerate(chunks):
            source = own if spot * ROWS < half_rows else other
            row = spot * ROWS % half_rows
            start = pl.multiple_of(chunk * ROWS, ROWS)
            grads[pl.ds(start, ROWS), at + low : at + high] = source[
                row : row + ROWS, low:high
            ].astype(f32)

    place(late, late_own, late_other, 0, width, SPLIT)
    leave(grads.at[:, SPLIT : SPLIT + width], out_hbm)
    place(late, late_own, late_other, width, columns - SPLIT, SPLIT)
    for half in range(2):
        leave(
            grads.at[half * leaves : (half + 1) * leaves, SPLIT + width :],
            leaf_hbm.at[:, half * (width // 2) : (half + 1) * (width // 2)],
        )
    parts = width // BLOCK
    part_of = lax.broadcasted_iota(jnp.int32, chosen_ref.shape, 0) & (parts - 1)
    for part in range(parts):
        mine = jnp.where(part_of == part, chosen_ref[...].astype(f32), 0.0).astype(bf16)
        table[:, part * BLOCK : (part + 1) * BLOCK] = mm_tn(mine, returned_ref[...])
    leave(table, table_hbm)
    for low in range(0, SPLIT, width):
        place(early, early_own, early_other, low, low + width, 0)
        leave(grads.at[:, low : low + width], in_hbm.at[:, low : low + width])
    for copy in leaving:
        copy.wait()


def run_finish(me, chosen, returned, early_own, early_other, late_own, late_other, leaves):
    smem = pl.BlockSpec(memory_space=pltpu.SMEM)
    vmem = pl.BlockSpec(memory_space=pltpu.VMEM)
    hbm = pl.BlockSpec(memory_space=pltpu.HBM)
    shape = jax.ShapeDtypeStruct
    width = early_own.shape[1] // 4
    return pl.pallas_call(
        finish_kernel,
        name="finish",
        out_shape=(
            shape((chosen.shape[1], width), f32),
            shape((leaves, width), f32),
            shape((width, 4 * width), f32),
            shape((width, width), f32),
        ),
        in_specs=[smem] + [vmem] * 6,
        out_specs=(hbm,) * 4,
        scratch_shapes=[
            pltpu.VMEM((width, early_own.shape[1] + late_own.shape[1]), f32),
            pltpu.VMEM((chosen.shape[1], width), f32),
            pltpu.SemaphoreType.DMA((8,)),
        ],
        compiler_params=pltpu.CompilerParams(vmem_limit_bytes=32 * 2**20),
    )(me, chosen, returned, early_own, early_other, late_own, late_other)


def load_kernel(*refs):
    for source, target in zip(refs[: len(refs) // 2], refs[len(refs) // 2 :]):
        target[...] = source[...]


def run_load(*arrays):
    vmem = pl.BlockSpec(memory_space=pltpu.VMEM)
    return pl.pallas_call(
        load_kernel,
        name="load",
        out_shape=tuple(jax.ShapeDtypeStruct(array.shape, array.dtype) for array in arrays),
        in_specs=[vmem] * len(arrays),
        out_specs=(vmem,) * len(arrays),
        compiler_params=pltpu.CompilerParams(vmem_limit_bytes=8 * 2**20),
        cost_estimate=pl.CostEstimate(flops=0, bytes_accessed=4 * 2**20, transcendentals=0),
    )(*arrays)


def merge_kernel(keep_ref, other_ref, *outs):
    rows = outs[0].shape[0]
    for part, out in enumerate(outs):
        at = slice(part * rows, (part + 1) * rows)
        out[...] = (keep_ref[at, :].astype(f32) + other_ref[at, :].astype(f32)).astype(bf16)


def run_merge(keep, other, parts):
    vmem = pl.BlockSpec(memory_space=pltpu.VMEM)
    part = jax.ShapeDtypeStruct((keep.shape[0] // parts, keep.shape[1]), bf16)
    return pl.pallas_call(
        merge_kernel,
        name="merge",
        out_shape=(part,) * parts,
        in_specs=[vmem] * 2,
        out_specs=(vmem,) * parts,
        compiler_params=pltpu.CompilerParams(vmem_limit_bytes=8 * 2**20),
    )(keep, other)


def exchange(blocks):
    return lax.all_to_all(blocks, ("dp", "rep"), split_axis=0, concat_axis=0, tiled=True)


def swap(block, mask, count):
    return lax.ppermute(block, ("dp", "rep"), [(i, i ^ mask) for i in range(count)])


def add(parts):
    return sum(part.astype(f32) for part in parts)


def shares(parts, group):
    size = 2 ** len(group)
    rows = parts[0].shape[0] // size
    return [
        add(part[digit * rows : (digit + 1) * rows] for part in parts).astype(bf16)
        for digit in range(1, size)
    ]


def swap_all(blocks, group, count):
    return [
        swap(block, mask_of(group, digit), count) for digit, block in enumerate(blocks, start=1)
    ]


def extend(parts, got):
    return [part[: got[0].shape[0]] for part in parts] + got


def split_up(parts, group, count):
    return extend(parts, swap_all(shares(parts, group), group, count))


def sum_with(block, group, count):
    return block.astype(f32) + swap(block, mask_of(group, 1), count).astype(f32)


def join(block, group, count):
    pieces = swap_all([block] * (2 ** len(group) - 1), group, count)
    return jnp.concatenate([block] + pieces, axis=0)


def reduce_and_gather(early, late, d_rows, count):
    _, near, far = EARLY
    _, first, second = LATE
    early_other, late_other = swap(early[1], 1, count), swap(late[1], 1, count)
    early_own, late_own = run_load(early[0], late[0])
    early, *early_blocks = run_merge(early_own, early_other, 2 ** len(near))
    late, *late_blocks = run_merge(late_own, late_other, 2 ** len(first))
    early_blocks, late_blocks = lax.optimization_barrier((early_blocks, late_blocks))
    early_got = swap_all(early_blocks, near, count)
    late = [late] + swap_all(late_blocks, first, count)
    late_got = swap_all(shares(late, second), second, count)
    early_got[0], late, d_rows = lax.optimization_barrier((early_got[0], late, d_rows))
    returned = exchange(d_rows)
    early_got, late = lax.optimization_barrier((early_got, extend(late, late_got)))
    early, late = split_up([early] + early_got, far, count), add(late).astype(bf16)
    late = sum_with(late, SHARED[0], count).astype(bf16)
    early, late = add(early), sum_with(late, SHARED[1], count)
    reach = CHUNKS
    while reach < count:
        early, late = early + swap(early, reach, count), late + swap(late, reach, count)
        reach *= 2
    early, returned = lax.optimization_barrier(((early * (1.0 / count)).astype(bf16), returned))
    early = join(early, far, count)
    early, late = lax.optimization_barrier((early, (late * (1.0 / count)).astype(bf16)))
    pieces = swap_all([early] * (2 ** len(near) - 1), near, count)
    late = join(join(late, second, count), first, count)
    pieces, late = lax.optimization_barrier((pieces, late))
    early = jnp.concatenate([early] + pieces, axis=0)
    return returned, early, swap(early, 1, count), late, swap(late, 1, count)


def on_device(
    item_table, requests, event_slot, lengths, leaf_ids, leaf_table, w_in, w_out, cotangent
):
    count = lax.axis_size("dp") * lax.axis_size("rep")
    place = lax.axis_index(("dp", "rep")).astype(jnp.int32)
    me = (place & (CHUNKS - 1)).reshape(1)
    slot = event_slot.reshape(1, -1)
    leaf = leaf_ids.T
    asked = exchange(requests[0])
    (table,) = run_load(item_table)
    fetched, chosen = run_lookup(asked, table)
    arrived = exchange(fetched)
    output, d_rows, keep, send, keep_late, send_late = run_layer(
        me, lengths, slot, leaf, arrived, leaf_table, w_in, w_out, cotangent
    )
    returned, early, early_other, late, late_other = reduce_and_gather(
        (keep, send), (keep_late, send_late), d_rows, count
    )
    table_grad, leaf_mean, in_mean, out_mean = run_finish(
        me, chosen, returned, early, early_other, late, late_other, leaf_table.shape[0]
    )
    return (output, table_grad, leaf_mean, in_mean, out_mean)


def solution(mesh):
    return jax.shard_map(
        on_device,
        mesh=mesh,
        in_specs=(
            P(("dp", "rep"), None),
            P(("dp", "rep"), None, None),
            P(("dp", "rep")),
            P(("dp", "rep"), None),
            P(("dp", "rep"), None),
            P(),
            P(),
            P(),
            P(("dp", "rep"), None),
        ),
        out_specs=(P(("dp", "rep"), None), P(("dp", "rep"), None), P(), P(), P()),
        check_vma=False,
    )
```

```python
import functools
import jax
import jax.numpy as jnp
from jax import lax
from jax.experimental import pallas as pl
from jax.experimental.pallas import tpu as pltpu
from jax.sharding import PartitionSpec as P

HEADS = 4
MAXLEN = 256
BLOCK = 128
ROWS = 16
epsilon = 1e-06
f32 = jnp.float32
bf16 = jnp.bfloat16

EARLY = ((0,), (1, 2), (3, 4))
LATE = ((0,), (3,), (4,))
SHARED = ((2,), (1,))
SPLIT = 2048
CHUNKS = 32
STRIP = 32
LAYER_VMEM = 56 * 2**20


def dot(a, b, contract):
    return lax.dot_general(a, b, ((contract[0], contract[1]), ((), ())), preferred_element_type=f32)


def mm(a, b):
    return dot(a, b, ((1,), (0,)))


def mm_nt(a, b):
    return dot(a, b, ((1,), (1,)))


def mm_tn(a, b):
    return dot(a, b, ((0,), (0,)))


def mask_of(group, digit):
    return sum(((digit >> k) & 1) << bit for k, bit in enumerate(group))


def chunk_order(me, route, shared=()):
    masks = [0]
    for group in route + shared:
        masks = [mask ^ mask_of(group, digit) for mask in masks for digit in range(2 ** len(group))]
    for group in shared:
        me = me & ~mask_of(group, 1)
    return [me ^ mask for mask in masks]


def spans(count):
    for start in range(0, count, BLOCK):
        low = max(0, start - (MAXLEN - 1)) // BLOCK * BLOCK
        yield start, low, start + BLOCK


def strips(start, stop):
    return [slice(at, at + STRIP) for at in range(start, stop, STRIP)]


def silu(half):
    curve = jnp.tanh(half)
    value = (half + half * curve).astype(bf16)
    half, curve = half.astype(bf16), curve.astype(bf16)
    return value, (0.5 + 0.5 * curve) * (1.0 + half * (1.0 - curve))


def center(values):
    values = values - jnp.mean(values, axis=-1, keepdims=True)
    return values, lax.rsqrt(jnp.mean(values * values, axis=-1, keepdims=True) + epsilon)


def pull_normalize(change, normed, scale):
    return scale * (
        change
        - jnp.mean(change, axis=-1, keepdims=True)
        - normed * jnp.mean(change * normed, axis=-1, keepdims=True)
    )


def pickers(slots, slot_ref, leaf_ref, leaves):
    count = slot_ref.shape[1]
    picker = lax.broadcasted_iota(jnp.int32, (slots, count), 0) == slot_ref[...]
    trees = leaf_ref.shape[0]
    each = leaves // trees
    spots = lax.broadcasted_iota(jnp.int32, (each, count), 0)
    onehot = [(spots == leaf_ref[t : t + 1, :]).astype(f32).astype(bf16) for t in range(trees)]
    return picker.astype(f32).astype(bf16), jnp.concatenate(onehot, axis=0)


def permute_rows(chunks, source, target):
    for place, chunk in enumerate(chunks):
        start = pl.multiple_of(chunk * ROWS, ROWS)
        target[place * ROWS : (place + 1) * ROWS, :] = source[pl.ds(start, ROWS), :]


def zero_one(condition):
    return jnp.where(condition, 1.0, 0.0).astype(bf16)


def to_tiles(rows):
    parts = rows.shape[1] // BLOCK
    shape = (rows.shape[0] * parts, rows.shape[0])
    row, column = (lax.broadcasted_iota(jnp.int32, shape, axis) for axis in (0, 1))
    total = jnp.zeros((shape[0], BLOCK), f32)
    for part in range(parts):
        place = zero_one(row == column * parts + part)
        total = total + mm(place, rows[:, part * BLOCK : (part + 1) * BLOCK])
    return total.astype(bf16)


def from_tiles(block, width):
    parts = width // BLOCK
    shape = (block.shape[0] // parts, block.shape[0])
    row, column = (lax.broadcasted_iota(jnp.int32, shape, axis) for axis in (0, 1))
    pieces = [mm(zero_one(column == row * parts + part), block) for part in range(parts)]
    return jnp.concatenate(pieces, axis=1).astype(bf16)


def lookup_kernel(asked_ref, table_ref, rows_ref, chosen_ref):
    count, each = asked_ref.shape
    owned, width = table_ref.shape
    parts = width // BLOCK
    many = count * each * parts
    spot = lax.broadcasted_iota(jnp.int32, (count, owned), 1)
    row = lax.broadcasted_iota(jnp.int32, (many, count), 0)
    device = lax.broadcasted_iota(jnp.int32, (many, count), 1)
    here, wanted = [], []
    for k in range(each):
        base = (device * each + k) * parts
        here.append(zero_one(jnp.logical_and(row >= base, row < base + parts)))
        wanted.append(zero_one(spot == asked_ref[:, k : k + 1]))
    chosen = mm(jnp.concatenate(here, axis=1), jnp.concatenate(wanted, axis=0))
    chosen_ref[...] = chosen.astype(bf16)
    part_of = lax.broadcasted_iota(jnp.int32, (many, owned), 0) & (parts - 1)
    mine = [jnp.where(part_of == part, chosen, 0.0).astype(bf16) for part in range(parts)]
    blocks = [table_ref[:, part * BLOCK : (part + 1) * BLOCK] for part in range(parts)]
    total = mm(jnp.concatenate(mine, axis=1), jnp.concatenate(blocks, axis=0))
    rows_ref[...] = total.astype(bf16)


def run_lookup(asked, table):
    vmem = pl.BlockSpec(memory_space=pltpu.VMEM)
    shape = jax.ShapeDtypeStruct
    many = asked.shape[0] * asked.shape[1] * table.shape[1] // BLOCK
    return pl.pallas_call(
        lookup_kernel,
        name="lookup",
        out_shape=(
            shape((many, BLOCK), bf16),
            shape((many, table.shape[0]), bf16),
        ),
        in_specs=[vmem, vmem],
        out_specs=(vmem,) * 2,
        compiler_params=pltpu.CompilerParams(vmem_limit_bytes=16 * 2**20),
    )(asked, table)


def layer_kernel(
    me_ref, lengths_ref, slot_ref, leaf_ref, rows_ref, table_hbm, in_hbm, out_hbm, tangent_hbm,
    output_hbm, d_rows_ref, keep_hbm, send_hbm, keep_late_hbm, send_late_hbm,
    inputs, gated, d_pre, grads, output,
    normed, turned, moved, hidden, slope, weights, weights_slope, mixed, d_mixed,
    d_score, d_gated, allowed, allowed_scale, keys_t, values_t, d_inputs, leaf_grad, table, w_in, w_out, tangent, sems, out_sems,
):
    count, width = inputs.shape
    head = width // HEADS
    half_scale = 0.5 * head ** (-0.5)
    half_rows = width // 2
    copies = [
        pltpu.make_async_copy(source, target, sems.at[k])
        for k, (source, target) in enumerate(
            ((table_hbm, table), (in_hbm, w_in), (out_hbm, w_out), (tangent_hbm, tangent))
        )
    ]
    for copy in copies:
        copy.start()
    leaving = []

    def leave(source, target):
        copy = pltpu.make_async_copy(source, target, out_sems.at[len(leaving)])
        copy.start()
        leaving.append(copy)

    rows = from_tiles(rows_ref[...], width)
    picker, onehot = pickers(rows.shape[0], slot_ref, leaf_ref, table.shape[0])
    ends = []
    total = 0
    for place in range(lengths_ref.shape[1]):
        total = total + lengths_ref[0, place]
        ends.append(total)
    for start, low, high in spans(count):
        at = slice(start, start + BLOCK)
        row = start + lax.broadcasted_iota(jnp.int32, (BLOCK, high - low), 0)
        column = low + lax.broadcasted_iota(jnp.int32, (BLOCK, high - low), 1)
        first = jnp.zeros_like(row)
        for end in ends[:-1]:
            first = jnp.where(row >= end, end, first)
        seen = jnp.logical_and(column >= first, column <= row)
        allowed[at, low:high] = jnp.where(seen, 1.0, 0.0).astype(bf16)
        allowed_scale[at, low:high] = jnp.where(seen, 2.0 * half_scale, 0.0).astype(bf16)
    copies[0].wait()
    inputs[...] = (mm_tn(picker, rows) + mm_tn(onehot, table[...])).astype(bf16)
    for at in strips(0, count):
        values, scale = center(inputs[at, :].astype(f32))
        normed[at, :] = (values * scale).astype(bf16)
    turned[...] = normed[...].T
    copies[1].wait()
    for start in range(0, 4 * width, 2 * BLOCK):
        to = slice(start, start + 2 * BLOCK)
        halves = mm(normed[...], w_in[:, to]) * 0.5
        for at in strips(0, count):
            value, slope_at = silu(halves[at, :])
            hidden[at, to] = value
            slope[at, to] = slope_at
    keys_t[...] = hidden[:, 3 * width :].T
    values_t[...] = hidden[:, width : 2 * width].T
    for start, low, high in spans(count):
        at = slice(start, start + BLOCK)
        end = start // (2 * BLOCK) * 2 * BLOCK + 2 * BLOCK
        for out in (slice(0, low), slice(high, end)):
            if out.start < out.stop:
                nothing = jnp.zeros((HEADS, BLOCK, out.stop - out.start), bf16)
                weights[:, at, out] = nothing
                d_score[:, at, out] = nothing
    for h in range(HEADS):
        own = slice(h * head, (h + 1) * head)
        value_at = slice(width + h * head, width + (h + 1) * head)
        query_at = slice(2 * width + h * head, 2 * width + (h + 1) * head)
        key_at = slice(3 * width + h * head, 3 * width + (h + 1) * head)
        for start, low, high in spans(count):
            at = slice(start, start + BLOCK)
            halves = mm(hidden[at, query_at], keys_t[own, low:high]) * half_scale
            for strip in strips(0, BLOCK):
                to = slice(start + strip.start, start + strip.stop)
                value, slope_at = silu(halves[strip, :])
                weights[h, to, low:high] = value * allowed[to, low:high]
                weights_slope[h, to, low:high] = slope_at * allowed_scale[to, low:high]
        for start in range(0, count, 2 * BLOCK):
            at = slice(start, start + 2 * BLOCK)
            high = start + 2 * BLOCK
            mixed[at, h * head : (h + 1) * head] = mm(
                weights[h, at, :high], hidden[:high, value_at]
            )
    copies[2].wait()
    copies[3].wait()
    d_gated[...] = mm_nt(tangent[...], w_out[...]).astype(bf16)
    for at in strips(0, count):
        values, scale = center(mixed[at, :])
        values = values * scale
        gates = hidden[at, :width].astype(f32)
        change = d_gated[at, :].astype(f32)
        gated[at, :] = (values * gates).astype(bf16)
        d_pre[at, :width] = (change * values).astype(bf16) * slope[at, :width]
        d_mixed[at, :] = pull_normalize(change * gates, values, scale).astype(bf16)
    for h in range(HEADS):
        own = slice(h * head, (h + 1) * head)
        value_at = slice(width + h * head, width + (h + 1) * head)
        query_at = slice(2 * width + h * head, 2 * width + (h + 1) * head)
        key_at = slice(3 * width + h * head, 3 * width + (h + 1) * head)
        for start, low, high in spans(count):
            at = slice(start, start + BLOCK)
            d_weights = mm(d_mixed[at, own], values_t[own, low:high]).astype(bf16)
            d_score[h, at, low:high] = d_weights * weights_slope[h, at, low:high]
        for start in range(0, count, 2 * BLOCK):
            at = slice(start, start + 2 * BLOCK)
            high = start + 2 * BLOCK
            d_query = mm(d_score[h, at, :high], hidden[:high, key_at])
            d_pre[at, query_at] = d_query.astype(bf16) * slope[at, query_at]
            d_key = mm_tn(d_score[h, start:, at], hidden[start:, query_at])
            d_pre[at, key_at] = d_key.astype(bf16) * slope[at, key_at]
            d_value = mm_tn(weights[h, start:, at], d_mixed[start:, own])
            d_pre[at, value_at] = d_value.astype(bf16) * slope[at, value_at]
    me = me_ref[0]
    early, late = chunk_order(me, EARLY), chunk_order(me, LATE, SHARED)
    permute_rows(early, turned, moved)
    for start in range(0, 4 * width, 2 * BLOCK):
        to = slice(start, start + 2 * BLOCK)
        grads[:, to] = mm(moved[...], d_pre[:, to]).astype(bf16)
    leave(grads.at[half_rows:, :SPLIT], send_hbm)
    leave(grads.at[:half_rows, :SPLIT], keep_hbm)
    turned[...] = gated[...].T
    permute_rows(late, turned, moved)
    grads[:, 4 * width : 5 * width] = mm(moved[...], tangent[...]).astype(bf16)
    output[...] = (mm(gated[...], w_out[...]) + inputs[...].astype(f32)).astype(bf16)
    leave(output, output_hbm)
    normed_change = mm_nt(d_pre[...], w_in[...])
    for at in strips(0, count):
        values, scale = center(inputs[at, :].astype(f32))
        change = pull_normalize(normed_change[at, :], values * scale, scale)
        d_inputs[at, :] = (change + tangent[at, :].astype(f32)).astype(bf16)
    leaves = table.shape[0]
    d_leaf = mm(onehot, d_inputs[...]).astype(bf16)
    leaf_grad[:leaves, :] = d_leaf[:, : width // 2]
    leaf_grad[leaves:, :] = d_leaf[:, width // 2 :]
    permute_rows(late, leaf_grad, grads.at[:, 5 * width :])
    leave(grads.at[half_rows:, SPLIT:], send_late_hbm)
    leave(grads.at[:half_rows, SPLIT:], keep_late_hbm)
    d_rows_ref[...] = to_tiles(mm(picker, d_inputs[...]).astype(bf16))
    for copy in leaving:
        copy.wait()


def run_layer(me, lengths, slot, leaf, rows, table, w_in, w_out, tangent):
    count, width = tangent.shape
    smem = pl.BlockSpec(memory_space=pltpu.SMEM)
    vmem = pl.BlockSpec(memory_space=pltpu.VMEM)
    hbm = pl.BlockSpec(memory_space=pltpu.HBM)
    shape = jax.ShapeDtypeStruct
    columns = 5 * width + width // 2
    return pl.pallas_call(
        layer_kernel,
        name="layer",
        out_shape=(
            shape((count, width), bf16),
            shape(rows.shape, bf16),
            shape((width // 2, SPLIT), bf16),
            shape((width // 2, SPLIT), bf16),
            shape((width // 2, columns - SPLIT), bf16),
            shape((width // 2, columns - SPLIT), bf16),
        ),
        in_specs=[smem, smem] + [vmem] * 3 + [hbm] * 4,
        out_specs=(hbm, vmem, hbm, hbm, hbm, hbm),
        scratch_shapes=[
            pltpu.VMEM((count, width), bf16),
            pltpu.VMEM((count, width), bf16),
            pltpu.VMEM((count, 4 * width), bf16),
            pltpu.VMEM((width, columns), bf16),
            pltpu.VMEM((count, width), bf16),
            pltpu.VMEM((count, width), bf16),
            pltpu.VMEM((width, count), bf16),
            pltpu.VMEM((width, count), bf16),
            pltpu.VMEM((count, 4 * width), bf16),
            pltpu.VMEM((count, 4 * width), bf16),
            pltpu.VMEM((HEADS, count, count), bf16),
            pltpu.VMEM((HEADS, count, count), bf16),
            pltpu.VMEM((count, width), f32),
            pltpu.VMEM((count, width), bf16),
            pltpu.VMEM((HEADS, count, count), bf16),
            pltpu.VMEM((count, width), bf16),
            pltpu.VMEM((count, count), bf16),
            pltpu.VMEM((count, count), bf16),
            pltpu.VMEM((width, count), bf16),
            pltpu.VMEM((width, count), bf16),
            pltpu.VMEM((count, width), bf16),
            pltpu.VMEM((width, width // 2), bf16),
            pltpu.VMEM(table.shape, bf16),
            pltpu.VMEM(w_in.shape, bf16),
            pltpu.VMEM(w_out.shape, bf16),
            pltpu.VMEM(tangent.shape, bf16),
            pltpu.SemaphoreType.DMA((4,)),
            pltpu.SemaphoreType.DMA((5,)),
        ],
        compiler_params=pltpu.CompilerParams(vmem_limit_bytes=LAYER_VMEM),
        cost_estimate=pl.CostEstimate(flops=6 * 10**9, bytes_accessed=10**7, transcendentals=10**6),
    )(me, lengths, slot, leaf, rows, table, w_in, w_out, tangent)


def write_chunks(me, half, early_ref, late_ref, leaf_hbm, in_hbm, out_hbm, grads, sems):
    width = in_hbm.shape[0]
    leaves = leaf_hbm.shape[0]
    places = early_ref.shape[0] // ROWS
    early, late = chunk_order(me, EARLY), chunk_order(me, LATE, SHARED)
    leaving = []

    def leave(source, target):
        copy = pltpu.make_async_copy(source, target, sems.at[len(leaving)])
        copy.start()
        leaving.append(copy)

    for place in range(places):
        at = slice(place * ROWS, (place + 1) * ROWS)
        grads[at, :SPLIT] = early_ref[at, :].astype(f32)
        start = pl.multiple_of(early[half * places + place] * ROWS, ROWS)
        leave(grads.at[at, :SPLIT], in_hbm.at[pl.ds(start, ROWS), :])
        grads[at, SPLIT:] = late_ref[at, :].astype(f32)
        start = pl.multiple_of(late[half * places + place] * ROWS, ROWS)
        leave(grads.at[at, SPLIT : SPLIT + width], out_hbm.at[pl.ds(start, ROWS), :])
        side = (start >= leaves).astype(jnp.int32)
        start = pl.multiple_of(start - side * leaves, ROWS)
        column = pl.multiple_of(side * (width // 2), width // 2)
        leave(
            grads.at[at, SPLIT + width :],
            leaf_hbm.at[pl.ds(start, ROWS), pl.ds(column, width // 2)],
        )
    return leaving


def finish_own_kernel(
    me_ref, chosen_ref, returned_ref, early_ref, late_ref,
    table_ref, leaf_hbm, in_hbm, out_hbm, grads, sems,
):
    leaving = write_chunks(
        me_ref[0], 0, early_ref, late_ref, leaf_hbm, in_hbm, out_hbm, grads, sems
    )
    parts = table_ref.shape[1] // BLOCK
    part_of = lax.broadcasted_iota(jnp.int32, chosen_ref.shape, 0) & (parts - 1)
    for part in range(parts):
        mine = jnp.where(part_of == part, chosen_ref[...].astype(f32), 0.0).astype(bf16)
        table_ref[:, part * BLOCK : (part + 1) * BLOCK] = mm_tn(mine, returned_ref[...])
    for copy in leaving:
        copy.wait()


def finish_other_kernel(
    me_ref, early_ref, late_ref, leaf_in, in_in, out_in, leaf_hbm, in_hbm, out_hbm, grads, sems
):
    leaving = write_chunks(
        me_ref[0], 1, early_ref, late_ref, leaf_hbm, in_hbm, out_hbm, grads, sems
    )
    for copy in leaving:
        copy.wait()


def finish_scratch(early, late):
    return [
        pltpu.VMEM((early.shape[0], early.shape[1] + late.shape[1]), f32),
        pltpu.SemaphoreType.DMA((3 * early.shape[0] // ROWS,)),
    ]


def run_finish(me, chosen, returned, early_own, early_other, late_own, late_other, leaves):
    smem = pl.BlockSpec(memory_space=pltpu.SMEM)
    vmem = pl.BlockSpec(memory_space=pltpu.VMEM)
    hbm = pl.BlockSpec(memory_space=pltpu.HBM)
    width = early_own.shape[1] // 4
    shapes = tuple(
        jax.ShapeDtypeStruct(shape, f32)
        for shape in (
            (chosen.shape[1], width), (leaves, width), (width, 4 * width), (width, width)
        )
    )
    table, *written = pl.pallas_call(
        finish_own_kernel,
        name="finish_own",
        out_shape=shapes,
        in_specs=[smem] + [vmem] * 4,
        out_specs=(vmem, hbm, hbm, hbm),
        scratch_shapes=finish_scratch(early_own, late_own),
        compiler_params=pltpu.CompilerParams(vmem_limit_bytes=16 * 2**20),
        cost_estimate=pl.CostEstimate(flops=10**8, bytes_accessed=5 * 10**6, transcendentals=0),
    )(me, chosen, returned, early_own, late_own)
    written = pl.pallas_call(
        finish_other_kernel,
        name="finish_other",
        out_shape=shapes[1:],
        in_specs=[smem] + [vmem] * 2 + [hbm] * 3,
        out_specs=(hbm,) * 3,
        scratch_shapes=finish_scratch(early_own, late_own),
        input_output_aliases={3: 0, 4: 1, 5: 2},
        compiler_params=pltpu.CompilerParams(vmem_limit_bytes=16 * 2**20),
        cost_estimate=pl.CostEstimate(flops=0, bytes_accessed=5 * 10**6, transcendentals=0),
    )(me, early_other, late_other, *written)
    return (table, *written)


def load_kernel(*refs):
    for source, target in zip(refs[: len(refs) // 2], refs[len(refs) // 2 :]):
        target[...] = source[...]


def run_load(*arrays):
    vmem = pl.BlockSpec(memory_space=pltpu.VMEM)
    return pl.pallas_call(
        load_kernel,
        name="load",
        out_shape=tuple(jax.ShapeDtypeStruct(array.shape, array.dtype) for array in arrays),
        in_specs=[vmem] * len(arrays),
        out_specs=(vmem,) * len(arrays),
        compiler_params=pltpu.CompilerParams(vmem_limit_bytes=8 * 2**20),
        cost_estimate=pl.CostEstimate(flops=0, bytes_accessed=4 * 2**20, transcendentals=0),
    )(*arrays)


def merge_kernel(keep_ref, other_ref, *outs):
    rows = outs[0].shape[0]
    for part, out in enumerate(outs):
        at = slice(part * rows, (part + 1) * rows)
        out[...] = (keep_ref[at, :].astype(f32) + other_ref[at, :].astype(f32)).astype(bf16)


def run_merge(keep, other, parts):
    vmem = pl.BlockSpec(memory_space=pltpu.VMEM)
    part = jax.ShapeDtypeStruct((keep.shape[0] // parts, keep.shape[1]), bf16)
    return pl.pallas_call(
        merge_kernel,
        name="merge",
        out_shape=(part,) * parts,
        in_specs=[vmem] * 2,
        out_specs=(vmem,) * parts,
        compiler_params=pltpu.CompilerParams(vmem_limit_bytes=8 * 2**20),
    )(keep, other)


def exchange(blocks):
    return lax.all_to_all(blocks, ("dp", "rep"), split_axis=0, concat_axis=0, tiled=True)


def swap(block, mask, count):
    return lax.ppermute(block, ("dp", "rep"), [(i, i ^ mask) for i in range(count)])


def add(parts):
    return sum(part.astype(f32) for part in parts)


def shares(parts, group):
    size = 2 ** len(group)
    rows = parts[0].shape[0] // size
    return [
        add(part[digit * rows : (digit + 1) * rows] for part in parts).astype(bf16)
        for digit in range(1, size)
    ]


def swap_all(blocks, group, count):
    return [
        swap(block, mask_of(group, digit), count) for digit, block in enumerate(blocks, start=1)
    ]


def extend(parts, got):
    return [part[: got[0].shape[0]] for part in parts] + got


def split_up(parts, group, count):
    return extend(parts, swap_all(shares(parts, group), group, count))


def sum_with(block, group, count):
    return block.astype(f32) + swap(block, mask_of(group, 1), count).astype(f32)


def join(block, group, count):
    pieces = swap_all([block] * (2 ** len(group) - 1), group, count)
    return jnp.concatenate([block] + pieces, axis=0)


def reduce_and_gather(early, late, d_rows, count):
    _, near, far = EARLY
    _, first, second = LATE
    early_other, late_other = swap(early[1], 1, count), swap(late[1], 1, count)
    early_own, late_own = run_load(early[0], late[0])
    early, *early_blocks = run_merge(early_own, early_other, 2 ** len(near))
    late, *late_blocks = run_merge(late_own, late_other, 2 ** len(first))
    early_blocks, late_blocks = lax.optimization_barrier((early_blocks, late_blocks))
    early_got = swap_all(early_blocks, near, count)
    late = [late] + swap_all(late_blocks, first, count)
    late_got = swap_all(shares(late, second), second, count)
    early_got[0], late, d_rows = lax.optimization_barrier((early_got[0], late, d_rows))
    returned = exchange(d_rows)
    early_got, late = lax.optimization_barrier((early_got, extend(late, late_got)))
    early, late = split_up([early] + early_got, far, count), add(late).astype(bf16)
    late = sum_with(late, SHARED[0], count).astype(bf16)
    early, late = add(early), sum_with(late, SHARED[1], count)
    reach = CHUNKS
    while reach < count:
        early, late = early + swap(early, reach, count), late + swap(late, reach, count)
        reach *= 2
    early, returned = lax.optimization_barrier(((early * (1.0 / count)).astype(bf16), returned))
    early = join(early, far, count)
    early, late = lax.optimization_barrier((early, (late * (1.0 / count)).astype(bf16)))
    pieces = swap_all([early] * (2 ** len(near) - 1), near, count)
    late = join(join(late, second, count), first, count)
    pieces, late = lax.optimization_barrier((pieces, late))
    early = jnp.concatenate([early] + pieces, axis=0)
    return returned, early, swap(early, 1, count), late, swap(late, 1, count)


def on_device(
    item_table, requests, event_slot, lengths, leaf_ids, leaf_table, w_in, w_out, cotangent
):
    count = lax.axis_size("dp") * lax.axis_size("rep")
    place = lax.axis_index(("dp", "rep")).astype(jnp.int32)
    me = (place & (CHUNKS - 1)).reshape(1)
    slot = event_slot.reshape(1, -1)
    leaf = leaf_ids.T
    asked = exchange(requests[0])
    (table,) = run_load(item_table)
    fetched, chosen = run_lookup(asked, table)
    arrived = exchange(fetched)
    output, d_rows, keep, send, keep_late, send_late = run_layer(
        me, lengths, slot, leaf, arrived, leaf_table, w_in, w_out, cotangent
    )
    returned, early, early_other, late, late_other = reduce_and_gather(
        (keep, send), (keep_late, send_late), d_rows, count
    )
    table_grad, leaf_mean, in_mean, out_mean = run_finish(
        me, chosen, returned, early, early_other, late, late_other, leaf_table.shape[0]
    )
    return (output, table_grad, leaf_mean, in_mean, out_mean)


def solution(mesh):
    return jax.shard_map(
        on_device,
        mesh=mesh,
        in_specs=(
            P(("dp", "rep"), None),
            P(("dp", "rep"), None, None),
            P(("dp", "rep")),
            P(("dp", "rep"), None),
            P(("dp", "rep"), None),
            P(),
            P(),
            P(),
            P(("dp", "rep"), None),
        ),
        out_specs=(P(("dp", "rep"), None), P(("dp", "rep"), None), P(), P(), P()),
        check_vma=False,
    )
```

```python
import functools
import jax
import jax.numpy as jnp
from jax import lax
from jax.experimental import pallas as pl
from jax.experimental.pallas import tpu as pltpu
from jax.sharding import PartitionSpec as P

HEADS = 4
MAXLEN = 256
BLOCK = 128
ROWS = 16
epsilon = 1e-06
f32 = jnp.float32
bf16 = jnp.bfloat16

EARLY = ((0,), (1, 2), (3, 4))
LATE = ((0,), (3,), (4,))
SHARED = ((2,), (1,))
SPLIT = 2048
CHUNKS = 32
STRIP = 32
LAYER_VMEM = 56 * 2**20


def dot(a, b, contract):
    return lax.dot_general(a, b, ((contract[0], contract[1]), ((), ())), preferred_element_type=f32)


def mm(a, b):
    return dot(a, b, ((1,), (0,)))


def mm_nt(a, b):
    return dot(a, b, ((1,), (1,)))


def mm_tn(a, b):
    return dot(a, b, ((0,), (0,)))


def mask_of(group, digit):
    return sum(((digit >> k) & 1) << bit for k, bit in enumerate(group))


def chunk_order(me, route, shared=()):
    masks = [0]
    for group in route + shared:
        masks = [mask ^ mask_of(group, digit) for mask in masks for digit in range(2 ** len(group))]
    for group in shared:
        me = me & ~mask_of(group, 1)
    return [me ^ mask for mask in masks]


def spans(count):
    for start in range(0, count, BLOCK):
        low = max(0, start - (MAXLEN - 1)) // BLOCK * BLOCK
        yield start, low, start + BLOCK


def strips(start, stop):
    return [slice(at, at + STRIP) for at in range(start, stop, STRIP)]


def silu(half):
    curve = jnp.tanh(half)
    value = (half + half * curve).astype(bf16)
    half, curve = half.astype(bf16), curve.astype(bf16)
    return value, (0.5 + 0.5 * curve) * (1.0 + half * (1.0 - curve))


def center(values):
    values = values - jnp.mean(values, axis=-1, keepdims=True)
    return values, lax.rsqrt(jnp.mean(values * values, axis=-1, keepdims=True) + epsilon)


def pull_normalize(change, normed, scale):
    return scale * (
        change
        - jnp.mean(change, axis=-1, keepdims=True)
        - normed * jnp.mean(change * normed, axis=-1, keepdims=True)
    )


def pickers(slots, slot_ref, leaf_ref, leaves):
    count = slot_ref.shape[1]
    picker = lax.broadcasted_iota(jnp.int32, (slots, count), 0) == slot_ref[...]
    trees = leaf_ref.shape[0]
    each = leaves // trees
    spots = lax.broadcasted_iota(jnp.int32, (each, count), 0)
    onehot = [(spots == leaf_ref[t : t + 1, :]).astype(f32).astype(bf16) for t in range(trees)]
    return picker.astype(f32).astype(bf16), jnp.concatenate(onehot, axis=0)


def permute_rows(chunks, source, target):
    for place, chunk in enumerate(chunks):
        start = pl.multiple_of(chunk * ROWS, ROWS)
        target[place * ROWS : (place + 1) * ROWS, :] = source[pl.ds(start, ROWS), :]


def zero_one(condition):
    return jnp.where(condition, 1.0, 0.0).astype(bf16)


def to_tiles(rows):
    parts = rows.shape[1] // BLOCK
    shape = (rows.shape[0] * parts, rows.shape[0])
    row, column = (lax.broadcasted_iota(jnp.int32, shape, axis) for axis in (0, 1))
    total = jnp.zeros((shape[0], BLOCK), f32)
    for part in range(parts):
        place = zero_one(row == column * parts + part)
        total = total + mm(place, rows[:, part * BLOCK : (part + 1) * BLOCK])
    return total.astype(bf16)


def from_tiles(block, width):
    parts = width // BLOCK
    shape = (block.shape[0] // parts, block.shape[0])
    row, column = (lax.broadcasted_iota(jnp.int32, shape, axis) for axis in (0, 1))
    pieces = [mm(zero_one(column == row * parts + part), block) for part in range(parts)]
    return jnp.concatenate(pieces, axis=1).astype(bf16)


def lookup_kernel(asked_ref, table_ref, rows_ref, chosen_ref):
    count, each = asked_ref.shape
    owned, width = table_ref.shape
    parts = width // BLOCK
    many = count * each * parts
    spot = lax.broadcasted_iota(jnp.int32, (count, owned), 1)
    row = lax.broadcasted_iota(jnp.int32, (many, count), 0)
    device = lax.broadcasted_iota(jnp.int32, (many, count), 1)
    here, wanted = [], []
    for k in range(each):
        base = (device * each + k) * parts
        here.append(zero_one(jnp.logical_and(row >= base, row < base + parts)))
        wanted.append(zero_one(spot == asked_ref[:, k : k + 1]))
    chosen = mm(jnp.concatenate(here, axis=1), jnp.concatenate(wanted, axis=0))
    chosen_ref[...] = chosen.astype(bf16)
    part_of = lax.broadcasted_iota(jnp.int32, (many, owned), 0) & (parts - 1)
    mine = [jnp.where(part_of == part, chosen, 0.0).astype(bf16) for part in range(parts)]
    blocks = [table_ref[:, part * BLOCK : (part + 1) * BLOCK] for part in range(parts)]
    total = mm(jnp.concatenate(mine, axis=1), jnp.concatenate(blocks, axis=0))
    rows_ref[...] = total.astype(bf16)


def run_lookup(asked, table):
    vmem = pl.BlockSpec(memory_space=pltpu.VMEM)
    shape = jax.ShapeDtypeStruct
    many = asked.shape[0] * asked.shape[1] * table.shape[1] // BLOCK
    return pl.pallas_call(
        lookup_kernel,
        name="lookup",
        out_shape=(
            shape((many, BLOCK), bf16),
            shape((many, table.shape[0]), bf16),
        ),
        in_specs=[vmem, vmem],
        out_specs=(vmem,) * 2,
        compiler_params=pltpu.CompilerParams(vmem_limit_bytes=16 * 2**20),
    )(asked, table)


def start_all(sems, *pairs):
    copies = [
        pltpu.make_async_copy(source, target, sems.at[k])
        for k, (source, target) in enumerate(pairs)
    ]
    for copy in copies:
        copy.start()
    return copies


def prepare_kernel(
    lengths_ref, slot_ref, leaf_ref, table_hbm, out_hbm, tangent_hbm,
    picker_ref, onehot_ref, leaf_sum_ref, allowed, allowed_scale, d_gated_ref,
    table, w_out, tangent, sems,
):
    count, width = d_gated_ref.shape
    half_scale = 0.5 * (width // HEADS) ** (-0.5)
    loads = start_all(sems, (table_hbm, table), (out_hbm, w_out), (tangent_hbm, tangent))
    picker, onehot = pickers(picker_ref.shape[0], slot_ref, leaf_ref, table.shape[0])
    picker_ref[...] = picker
    onehot_ref[...] = onehot
    ends = []
    total = 0
    for place in range(lengths_ref.shape[1]):
        total = total + lengths_ref[0, place]
        ends.append(total)
    allowed[...] = jnp.zeros_like(allowed)
    allowed_scale[...] = jnp.zeros_like(allowed_scale)
    for start, low, high in spans(count):
        at = slice(start, start + BLOCK)
        row = start + lax.broadcasted_iota(jnp.int32, (BLOCK, high - low), 0)
        column = low + lax.broadcasted_iota(jnp.int32, (BLOCK, high - low), 1)
        first = jnp.zeros_like(row)
        for end in ends[:-1]:
            first = jnp.where(row >= end, end, first)
        seen = jnp.logical_and(column >= first, column <= row)
        allowed[at, low:high] = jnp.where(seen, 1.0, 0.0).astype(bf16)
        allowed_scale[at, low:high] = jnp.where(seen, 2.0 * half_scale, 0.0).astype(bf16)
    loads[0].wait()
    leaf_sum_ref[...] = mm_tn(onehot, table[...])
    loads[1].wait()
    loads[2].wait()
    d_gated_ref[...] = mm_nt(tangent[...], w_out[...]).astype(bf16)


def run_prepare(lengths, slot, leaf, table, w_out, tangent, slots):
    count, width = tangent.shape
    smem = pl.BlockSpec(memory_space=pltpu.SMEM)
    vmem = pl.BlockSpec(memory_space=pltpu.VMEM)
    hbm = pl.BlockSpec(memory_space=pltpu.HBM)
    shape = jax.ShapeDtypeStruct
    return pl.pallas_call(
        prepare_kernel,
        name="prepare",
        out_shape=(
            shape((slots, count), bf16),
            shape((table.shape[0], count), bf16),
            shape((count, width), f32),
            shape((count, count), bf16),
            shape((count, count), bf16),
            shape((count, width), bf16),
        ),
        in_specs=[smem, vmem, vmem] + [hbm] * 3,
        out_specs=(vmem,) * 6,
        scratch_shapes=[
            pltpu.VMEM(table.shape, bf16),
            pltpu.VMEM(w_out.shape, bf16),
            pltpu.VMEM(tangent.shape, bf16),
            pltpu.SemaphoreType.DMA((3,)),
        ],
        compiler_params=pltpu.CompilerParams(vmem_limit_bytes=LAYER_VMEM),
        cost_estimate=pl.CostEstimate(flops=6 * 10**8, bytes_accessed=5 * 10**6, transcendentals=0),
    )(lengths, slot, leaf, table, w_out, tangent)


def layer_kernel(
    me_ref, rows_hbm, picker_hbm, onehot_hbm, leaf_sum_hbm, allowed_hbm, allowed_scale_hbm,
    d_gated_hbm, in_hbm, tangent_hbm,
    inputs_hbm, gated_hbm, d_rows_ref, keep_hbm, send_hbm, keep_late_hbm, send_late_hbm,
    inputs, gated, d_pre, grads,
    normed, turned, moved, hidden, slope, weights, weights_slope, mixed, d_mixed,
    d_score, rows, picker, onehot, leaf_sum, allowed, allowed_scale, d_gated, w_in, tangent,
    keys_t, values_t, d_inputs, leaf_grad, sems, out_sems,
):
    count, width = inputs.shape
    head = width // HEADS
    half_scale = 0.5 * head ** (-0.5)
    half_rows = width // 2
    loads = start_all(
        sems,
        (rows_hbm, rows), (picker_hbm, picker), (leaf_sum_hbm, leaf_sum), (in_hbm, w_in),
        (allowed_hbm, allowed), (allowed_scale_hbm, allowed_scale), (d_gated_hbm, d_gated),
        (tangent_hbm, tangent), (onehot_hbm, onehot),
    )
    leaving = []

    def leave(source, target):
        copy = pltpu.make_async_copy(source, target, out_sems.at[len(leaving)])
        copy.start()
        leaving.append(copy)

    for load in loads[:3]:
        load.wait()
    fetched = from_tiles(rows[...], width)
    inputs[...] = (mm_tn(picker[...], fetched) + leaf_sum[...]).astype(bf16)
    leave(inputs, inputs_hbm)
    for at in strips(0, count):
        values, scale = center(inputs[at, :].astype(f32))
        normed[at, :] = (values * scale).astype(bf16)
    turned[...] = normed[...].T
    loads[3].wait()
    for start in range(0, 4 * width, 2 * BLOCK):
        to = slice(start, start + 2 * BLOCK)
        halves = mm(normed[...], w_in[:, to]) * 0.5
        for at in strips(0, count):
            value, slope_at = silu(halves[at, :])
            hidden[at, to] = value
            slope[at, to] = slope_at
    for load in loads[4:]:
        load.wait()
    keys_t[...] = hidden[:, 3 * width :].T
    values_t[...] = hidden[:, width : 2 * width].T
    for start, low, high in spans(count):
        at = slice(start, start + BLOCK)
        end = start // (2 * BLOCK) * 2 * BLOCK + 2 * BLOCK
        for out in (slice(0, low), slice(high, end)):
            if out.start < out.stop:
                nothing = jnp.zeros((HEADS, BLOCK, out.stop - out.start), bf16)
                weights[:, at, out] = nothing
                d_score[:, at, out] = nothing
    for h in range(HEADS):
        own = slice(h * head, (h + 1) * head)
        value_at = slice(width + h * head, width + (h + 1) * head)
        query_at = slice(2 * width + h * head, 2 * width + (h + 1) * head)
        key_at = slice(3 * width + h * head, 3 * width + (h + 1) * head)
        for start, low, high in spans(count):
            at = slice(start, start + BLOCK)
            halves = mm(hidden[at, query_at], keys_t[own, low:high]) * half_scale
            for strip in strips(0, BLOCK):
                to = slice(start + strip.start, start + strip.stop)
                value, slope_at = silu(halves[strip, :])
                weights[h, to, low:high] = value * allowed[to, low:high]
                weights_slope[h, to, low:high] = slope_at * allowed_scale[to, low:high]
        for start in range(0, count, 2 * BLOCK):
            at = slice(start, start + 2 * BLOCK)
            high = start + 2 * BLOCK
            mixed[at, h * head : (h + 1) * head] = mm(
                weights[h, at, :high], hidden[:high, value_at]
            )
    for at in strips(0, count):
        values, scale = center(mixed[at, :])
        values = values * scale
        gates = hidden[at, :width].astype(f32)
        change = d_gated[at, :].astype(f32)
        gated[at, :] = (values * gates).astype(bf16)
        d_pre[at, :width] = (change * values).astype(bf16) * slope[at, :width]
        d_mixed[at, :] = pull_normalize(change * gates, values, scale).astype(bf16)
    for h in range(HEADS):
        own = slice(h * head, (h + 1) * head)
        value_at = slice(width + h * head, width + (h + 1) * head)
        query_at = slice(2 * width + h * head, 2 * width + (h + 1) * head)
        key_at = slice(3 * width + h * head, 3 * width + (h + 1) * head)
        for start, low, high in spans(count):
            at = slice(start, start + BLOCK)
            d_weights = mm(d_mixed[at, own], values_t[own, low:high]).astype(bf16)
            d_score[h, at, low:high] = d_weights * weights_slope[h, at, low:high]
        for start in range(0, count, 2 * BLOCK):
            at = slice(start, start + 2 * BLOCK)
            high = start + 2 * BLOCK
            d_query = mm(d_score[h, at, :high], hidden[:high, key_at])
            d_pre[at, query_at] = d_query.astype(bf16) * slope[at, query_at]
            d_key = mm_tn(d_score[h, start:, at], hidden[start:, query_at])
            d_pre[at, key_at] = d_key.astype(bf16) * slope[at, key_at]
            d_value = mm_tn(weights[h, start:, at], d_mixed[start:, own])
            d_pre[at, value_at] = d_value.astype(bf16) * slope[at, value_at]
    me = me_ref[0]
    early, late = chunk_order(me, EARLY), chunk_order(me, LATE, SHARED)
    permute_rows(early, turned, moved)
    for start in range(0, 4 * width, 2 * BLOCK):
        to = slice(start, start + 2 * BLOCK)
        grads[:, to] = mm(moved[...], d_pre[:, to]).astype(bf16)
    leave(grads.at[half_rows:, :SPLIT], send_hbm)
    leave(grads.at[:half_rows, :SPLIT], keep_hbm)
    leave(gated, gated_hbm)
    turned[...] = gated[...].T
    permute_rows(late, turned, moved)
    grads[:, 4 * width : 5 * width] = mm(moved[...], tangent[...]).astype(bf16)
    normed_change = mm_nt(d_pre[...], w_in[...])
    for at in strips(0, count):
        values, scale = center(inputs[at, :].astype(f32))
        change = pull_normalize(normed_change[at, :], values * scale, scale)
        d_inputs[at, :] = (change + tangent[at, :].astype(f32)).astype(bf16)
    leaves = onehot.shape[0]
    d_leaf = mm(onehot[...], d_inputs[...]).astype(bf16)
    leaf_grad[:leaves, :] = d_leaf[:, : width // 2]
    leaf_grad[leaves:, :] = d_leaf[:, width // 2 :]
    permute_rows(late, leaf_grad, grads.at[:, 5 * width :])
    leave(grads.at[half_rows:, SPLIT:], send_late_hbm)
    leave(grads.at[:half_rows, SPLIT:], keep_late_hbm)
    d_rows_ref[...] = to_tiles(mm(picker[...], d_inputs[...]).astype(bf16))
    for copy in leaving:
        copy.wait()


def run_layer(me, rows, prepared, w_in, tangent):
    picker, onehot, leaf_sum, allowed, allowed_scale, d_gated = prepared
    count, width = tangent.shape
    smem = pl.BlockSpec(memory_space=pltpu.SMEM)
    vmem = pl.BlockSpec(memory_space=pltpu.VMEM)
    hbm = pl.BlockSpec(memory_space=pltpu.HBM)
    shape = jax.ShapeDtypeStruct
    columns = 5 * width + width // 2
    operands = (
        rows, picker, onehot, leaf_sum, allowed, allowed_scale, d_gated, w_in, tangent
    )
    return pl.pallas_call(
        layer_kernel,
        name="layer",
        out_shape=(
            shape((count, width), bf16),
            shape((count, width), bf16),
            shape(rows.shape, bf16),
            shape((width // 2, SPLIT), bf16),
            shape((width // 2, SPLIT), bf16),
            shape((width // 2, columns - SPLIT), bf16),
            shape((width // 2, columns - SPLIT), bf16),
        ),
        in_specs=[smem] + [hbm] * 9,
        out_specs=(hbm, hbm, vmem) + (hbm,) * 4,
        scratch_shapes=[
            pltpu.VMEM((count, width), bf16),
            pltpu.VMEM((count, width), bf16),
            pltpu.VMEM((count, 4 * width), bf16),
            pltpu.VMEM((width, columns), bf16),
            pltpu.VMEM((count, width), bf16),
            pltpu.VMEM((width, count), bf16),
            pltpu.VMEM((width, count), bf16),
            pltpu.VMEM((count, 4 * width), bf16),
            pltpu.VMEM((count, 4 * width), bf16),
            pltpu.VMEM((HEADS, count, count), bf16),
            pltpu.VMEM((HEADS, count, count), bf16),
            pltpu.VMEM((count, width), f32),
            pltpu.VMEM((count, width), bf16),
            pltpu.VMEM((HEADS, count, count), bf16),
        ]
        + [
            pltpu.VMEM(array.shape, array.dtype)
            for array in (
                rows, picker, onehot, leaf_sum, allowed, allowed_scale, d_gated, w_in, tangent
            )
        ]
        + [
            pltpu.VMEM((width, count), bf16),
            pltpu.VMEM((width, count), bf16),
            pltpu.VMEM((count, width), bf16),
            pltpu.VMEM((width, width // 2), bf16),
            pltpu.SemaphoreType.DMA((9,)),
            pltpu.SemaphoreType.DMA((6,)),
        ],
        compiler_params=pltpu.CompilerParams(vmem_limit_bytes=LAYER_VMEM),
        cost_estimate=pl.CostEstimate(flops=5 * 10**9, bytes_accessed=10**7, transcendentals=10**6),
    )(me, *operands)


def write_chunks(me, half, early_ref, late_ref, leaf_hbm, in_hbm, out_hbm, grads, sems):
    width = in_hbm.shape[0]
    leaves = leaf_hbm.shape[0]
    places = early_ref.shape[0] // ROWS
    early, late = chunk_order(me, EARLY), chunk_order(me, LATE, SHARED)
    leaving = []

    def leave(source, target):
        copy = pltpu.make_async_copy(source, target, sems.at[len(leaving)])
        copy.start()
        leaving.append(copy)

    for place in range(places):
        at = slice(place * ROWS, (place + 1) * ROWS)
        grads[at, :SPLIT] = early_ref[at, :].astype(f32)
        start = pl.multiple_of(early[half * places + place] * ROWS, ROWS)
        leave(grads.at[at, :SPLIT], in_hbm.at[pl.ds(start, ROWS), :])
        grads[at, SPLIT:] = late_ref[at, :].astype(f32)
        start = pl.multiple_of(late[half * places + place] * ROWS, ROWS)
        leave(grads.at[at, SPLIT : SPLIT + width], out_hbm.at[pl.ds(start, ROWS), :])
        side = (start >= leaves).astype(jnp.int32)
        start = pl.multiple_of(start - side * leaves, ROWS)
        column = pl.multiple_of(side * (width // 2), width // 2)
        leave(
            grads.at[at, SPLIT + width :],
            leaf_hbm.at[pl.ds(start, ROWS), pl.ds(column, width // 2)],
        )
    return leaving


def finish_own_kernel(
    me_ref, chosen_ref, returned_ref, early_ref, late_ref,
    table_ref, leaf_hbm, in_hbm, out_hbm, grads, sems,
):
    leaving = write_chunks(
        me_ref[0], 0, early_ref, late_ref, leaf_hbm, in_hbm, out_hbm, grads, sems
    )
    parts = table_ref.shape[1] // BLOCK
    part_of = lax.broadcasted_iota(jnp.int32, chosen_ref.shape, 0) & (parts - 1)
    for part in range(parts):
        mine = jnp.where(part_of == part, chosen_ref[...].astype(f32), 0.0).astype(bf16)
        table_ref[:, part * BLOCK : (part + 1) * BLOCK] = mm_tn(mine, returned_ref[...])
    for copy in leaving:
        copy.wait()


def finish_other_kernel(
    me_ref, early_ref, late_ref, leaf_in, in_in, out_in, leaf_hbm, in_hbm, out_hbm, grads, sems
):
    leaving = write_chunks(
        me_ref[0], 1, early_ref, late_ref, leaf_hbm, in_hbm, out_hbm, grads, sems
    )
    for copy in leaving:
        copy.wait()


def finish_scratch(early, late):
    return [
        pltpu.VMEM((early.shape[0], early.shape[1] + late.shape[1]), f32),
        pltpu.SemaphoreType.DMA((3 * early.shape[0] // ROWS,)),
    ]


def run_finish(me, chosen, returned, early_own, early_other, late_own, late_other, leaves):
    smem = pl.BlockSpec(memory_space=pltpu.SMEM)
    vmem = pl.BlockSpec(memory_space=pltpu.VMEM)
    hbm = pl.BlockSpec(memory_space=pltpu.HBM)
    width = early_own.shape[1] // 4
    shapes = tuple(
        jax.ShapeDtypeStruct(shape, f32)
        for shape in (
            (chosen.shape[1], width), (leaves, width), (width, 4 * width), (width, width)
        )
    )
    table, *written = pl.pallas_call(
        finish_own_kernel,
        name="finish_own",
        out_shape=shapes,
        in_specs=[smem] + [vmem] * 4,
        out_specs=(vmem, hbm, hbm, hbm),
        scratch_shapes=finish_scratch(early_own, late_own),
        compiler_params=pltpu.CompilerParams(vmem_limit_bytes=16 * 2**20),
        cost_estimate=pl.CostEstimate(flops=10**8, bytes_accessed=5 * 10**6, transcendentals=0),
    )(me, chosen, returned, early_own, late_own)
    written = pl.pallas_call(
        finish_other_kernel,
        name="finish_other",
        out_shape=shapes[1:],
        in_specs=[smem] + [vmem] * 2 + [hbm] * 3,
        out_specs=(hbm,) * 3,
        scratch_shapes=finish_scratch(early_own, late_own),
        input_output_aliases={3: 0, 4: 1, 5: 2},
        compiler_params=pltpu.CompilerParams(vmem_limit_bytes=16 * 2**20),
        cost_estimate=pl.CostEstimate(flops=0, bytes_accessed=5 * 10**6, transcendentals=0),
    )(me, early_other, late_other, *written)
    return (table, *written)


def load_kernel(*refs):
    for source, target in zip(refs[: len(refs) // 2], refs[len(refs) // 2 :]):
        target[...] = source[...]


def run_load(*arrays):
    vmem = pl.BlockSpec(memory_space=pltpu.VMEM)
    return pl.pallas_call(
        load_kernel,
        name="load",
        out_shape=tuple(jax.ShapeDtypeStruct(array.shape, array.dtype) for array in arrays),
        in_specs=[vmem] * len(arrays),
        out_specs=(vmem,) * len(arrays),
        compiler_params=pltpu.CompilerParams(vmem_limit_bytes=8 * 2**20),
        cost_estimate=pl.CostEstimate(flops=0, bytes_accessed=4 * 2**20, transcendentals=0),
    )(*arrays)


def merge_kernel(keep_ref, other_ref, *outs):
    rows = outs[0].shape[0]
    for part, out in enumerate(outs):
        at = slice(part * rows, (part + 1) * rows)
        out[...] = (keep_ref[at, :].astype(f32) + other_ref[at, :].astype(f32)).astype(bf16)


def run_merge(keep, other, parts):
    vmem = pl.BlockSpec(memory_space=pltpu.VMEM)
    part = jax.ShapeDtypeStruct((keep.shape[0] // parts, keep.shape[1]), bf16)
    return pl.pallas_call(
        merge_kernel,
        name="merge",
        out_shape=(part,) * parts,
        in_specs=[vmem] * 2,
        out_specs=(vmem,) * parts,
        compiler_params=pltpu.CompilerParams(vmem_limit_bytes=8 * 2**20),
    )(keep, other)


def exchange(blocks):
    return lax.all_to_all(blocks, ("dp", "rep"), split_axis=0, concat_axis=0, tiled=True)


def swap(block, mask, count):
    return lax.ppermute(block, ("dp", "rep"), [(i, i ^ mask) for i in range(count)])


def add(parts):
    return sum(part.astype(f32) for part in parts)


def shares(parts, group):
    size = 2 ** len(group)
    rows = parts[0].shape[0] // size
    return [
        add(part[digit * rows : (digit + 1) * rows] for part in parts).astype(bf16)
        for digit in range(1, size)
    ]


def swap_all(blocks, group, count):
    return [
        swap(block, mask_of(group, digit), count) for digit, block in enumerate(blocks, start=1)
    ]


def extend(parts, got):
    return [part[: got[0].shape[0]] for part in parts] + got


def split_up(parts, group, count):
    return extend(parts, swap_all(shares(parts, group), group, count))


def sum_with(block, group, count):
    return block.astype(f32) + swap(block, mask_of(group, 1), count).astype(f32)


def join(block, group, count):
    pieces = swap_all([block] * (2 ** len(group) - 1), group, count)
    return jnp.concatenate([block] + pieces, axis=0)


def reduce_and_gather(early, late, d_rows, inputs, gated, w_out, count):
    _, near, far = EARLY
    _, first, second = LATE
    early_other, late_other = swap(early[1], 1, count), swap(late[1], 1, count)
    early_own, late_own = run_load(early[0], late[0])
    early, *early_blocks = run_merge(early_own, early_other, 2 ** len(near))
    late, *late_blocks = run_merge(late_own, late_other, 2 ** len(first))
    early_blocks, late_blocks = lax.optimization_barrier((early_blocks, late_blocks))
    early_got = swap_all(early_blocks, near, count)
    late = [late] + swap_all(late_blocks, first, count)
    late_got = swap_all(shares(late, second), second, count)
    early_got[0], late, d_rows = lax.optimization_barrier((early_got[0], late, d_rows))
    returned = exchange(d_rows)
    early_got, late = lax.optimization_barrier((early_got, extend(late, late_got)))
    early, late = split_up([early] + early_got, far, count), add(late).astype(bf16)
    late = sum_with(late, SHARED[0], count).astype(bf16)
    early, late = add(early), sum_with(late, SHARED[1], count)
    reach = CHUNKS
    while reach < count:
        early, late = early + swap(early, reach, count), late + swap(late, reach, count)
        reach *= 2
    early, returned = lax.optimization_barrier(((early * (1.0 / count)).astype(bf16), returned))
    early = join(early, far, count)
    early, late = lax.optimization_barrier((early, (late * (1.0 / count)).astype(bf16)))
    pieces = swap_all([early] * (2 ** len(near) - 1), near, count)
    late, gated = lax.optimization_barrier((join(late, second, count), gated))
    output = (mm(gated, w_out) + inputs.astype(f32)).astype(bf16)
    late = join(late, first, count)
    pieces, late, output = lax.optimization_barrier((pieces, late, output))
    early = jnp.concatenate([early] + pieces, axis=0)
    return returned, early, swap(early, 1, count), late, swap(late, 1, count), output


def on_device(
    item_table, requests, event_slot, lengths, leaf_ids, leaf_table, w_in, w_out, cotangent
):
    count = lax.axis_size("dp") * lax.axis_size("rep")
    place = lax.axis_index(("dp", "rep")).astype(jnp.int32)
    me = (place & (CHUNKS - 1)).reshape(1)
    slot = event_slot.reshape(1, -1)
    leaf = leaf_ids.T
    asked = exchange(requests[0])
    (table,) = run_load(item_table)
    fetched, chosen = run_lookup(asked, table)
    arrived = exchange(fetched)
    prepared = run_prepare(
        lengths, slot, leaf, leaf_table, w_out, cotangent, requests.shape[1] * requests.shape[2]
    )
    inputs, gated, d_rows, *halves = run_layer(me, arrived, prepared, w_in, cotangent)
    returned, early, early_other, late, late_other, output = reduce_and_gather(
        halves[:2], halves[2:], d_rows, inputs, gated, w_out, count
    )
    table_grad, leaf_mean, in_mean, out_mean = run_finish(
        me, chosen, returned, early, early_other, late, late_other, leaf_table.shape[0]
    )
    return (output, table_grad, leaf_mean, in_mean, out_mean)


def solution(mesh):
    return jax.shard_map(
        on_device,
        mesh=mesh,
        in_specs=(
            P(("dp", "rep"), None),
            P(("dp", "rep"), None, None),
            P(("dp", "rep")),
            P(("dp", "rep"), None),
            P(("dp", "rep"), None),
            P(),
            P(),
            P(),
            P(("dp", "rep"), None),
        ),
        out_specs=(P(("dp", "rep"), None), P(("dp", "rep"), None), P(), P(), P()),
        check_vma=False,
    )
```

```python
import functools
import jax
import jax.numpy as jnp
from jax import lax
from jax.experimental import pallas as pl
from jax.experimental.pallas import tpu as pltpu
from jax.sharding import PartitionSpec as P

HEADS = 4
MAXLEN = 256
BLOCK = 128
ROWS = 16
epsilon = 1e-06
f32 = jnp.float32
bf16 = jnp.bfloat16

EARLY = ((0,), (1, 2), (3, 4))
LATE = ((0,), (3,), (4,))
SHARED = ((2,), (1,))
SPLIT = 1920
CHUNKS = 32
STRIP = 32
LAYER_VMEM = 56 * 2**20


def dot(a, b, contract):
    return lax.dot_general(a, b, ((contract[0], contract[1]), ((), ())), preferred_element_type=f32)


def mm(a, b):
    return dot(a, b, ((1,), (0,)))


def mm_nt(a, b):
    return dot(a, b, ((1,), (1,)))


def mm_tn(a, b):
    return dot(a, b, ((0,), (0,)))


def mask_of(group, digit):
    return sum(((digit >> k) & 1) << bit for k, bit in enumerate(group))


def chunk_order(me, route, shared=()):
    masks = [0]
    for group in route + shared:
        masks = [mask ^ mask_of(group, digit) for mask in masks for digit in range(2 ** len(group))]
    for group in shared:
        me = me & ~mask_of(group, 1)
    return [me ^ mask for mask in masks]


def spans(count):
    for start in range(0, count, BLOCK):
        low = max(0, start - (MAXLEN - 1)) // BLOCK * BLOCK
        yield start, low, start + BLOCK


def strips(start, stop):
    return [slice(at, at + STRIP) for at in range(start, stop, STRIP)]


def silu(half):
    curve = jnp.tanh(half)
    value = (half + half * curve).astype(bf16)
    half, curve = half.astype(bf16), curve.astype(bf16)
    return value, (0.5 + 0.5 * curve) * (1.0 + half * (1.0 - curve))


def center(values):
    values = values - jnp.mean(values, axis=-1, keepdims=True)
    return values, lax.rsqrt(jnp.mean(values * values, axis=-1, keepdims=True) + epsilon)


def pull_normalize(change, normed, scale):
    return scale * (
        change
        - jnp.mean(change, axis=-1, keepdims=True)
        - normed * jnp.mean(change * normed, axis=-1, keepdims=True)
    )


def pickers(slots, slot_ref, leaf_ref, leaves):
    count = slot_ref.shape[1]
    picker = lax.broadcasted_iota(jnp.int32, (slots, count), 0) == slot_ref[...]
    trees = leaf_ref.shape[0]
    each = leaves // trees
    spots = lax.broadcasted_iota(jnp.int32, (each, count), 0)
    onehot = [(spots == leaf_ref[t : t + 1, :]).astype(f32).astype(bf16) for t in range(trees)]
    return picker.astype(f32).astype(bf16), jnp.concatenate(onehot, axis=0)


def permute_rows(chunks, source, target):
    for place, chunk in enumerate(chunks):
        start = pl.multiple_of(chunk * ROWS, ROWS)
        target[place * ROWS : (place + 1) * ROWS, :] = source[pl.ds(start, ROWS), :]


def zero_one(condition):
    return jnp.where(condition, 1.0, 0.0).astype(bf16)


def to_tiles(rows):
    parts = rows.shape[1] // BLOCK
    shape = (rows.shape[0] * parts, rows.shape[0])
    row, column = (lax.broadcasted_iota(jnp.int32, shape, axis) for axis in (0, 1))
    total = jnp.zeros((shape[0], BLOCK), f32)
    for part in range(parts):
        place = zero_one(row == column * parts + part)
        total = total + mm(place, rows[:, part * BLOCK : (part + 1) * BLOCK])
    return total.astype(bf16)


def from_tiles(block, width):
    parts = width // BLOCK
    shape = (block.shape[0] // parts, block.shape[0])
    row, column = (lax.broadcasted_iota(jnp.int32, shape, axis) for axis in (0, 1))
    pieces = [mm(zero_one(column == row * parts + part), block) for part in range(parts)]
    return jnp.concatenate(pieces, axis=1).astype(bf16)


def lookup_kernel(asked_ref, table_ref, rows_ref, chosen_ref):
    count, each = asked_ref.shape
    owned, width = table_ref.shape
    parts = width // BLOCK
    many = count * each * parts
    spot = lax.broadcasted_iota(jnp.int32, (count, owned), 1)
    row = lax.broadcasted_iota(jnp.int32, (many, count), 0)
    device = lax.broadcasted_iota(jnp.int32, (many, count), 1)
    here, wanted = [], []
    for k in range(each):
        base = (device * each + k) * parts
        here.append(zero_one(jnp.logical_and(row >= base, row < base + parts)))
        wanted.append(zero_one(spot == asked_ref[:, k : k + 1]))
    chosen = mm(jnp.concatenate(here, axis=1), jnp.concatenate(wanted, axis=0))
    chosen_ref[...] = chosen.astype(bf16)
    part_of = lax.broadcasted_iota(jnp.int32, (many, owned), 0) & (parts - 1)
    mine = [jnp.where(part_of == part, chosen, 0.0).astype(bf16) for part in range(parts)]
    blocks = [table_ref[:, part * BLOCK : (part + 1) * BLOCK] for part in range(parts)]
    total = mm(jnp.concatenate(mine, axis=1), jnp.concatenate(blocks, axis=0))
    rows_ref[...] = total.astype(bf16)


def run_lookup(asked, table):
    vmem = pl.BlockSpec(memory_space=pltpu.VMEM)
    shape = jax.ShapeDtypeStruct
    many = asked.shape[0] * asked.shape[1] * table.shape[1] // BLOCK
    return pl.pallas_call(
        lookup_kernel,
        name="lookup",
        out_shape=(
            shape((many, BLOCK), bf16),
            shape((many, table.shape[0]), bf16),
        ),
        in_specs=[vmem, vmem],
        out_specs=(vmem,) * 2,
        compiler_params=pltpu.CompilerParams(vmem_limit_bytes=16 * 2**20),
    )(asked, table)


def layer_kernel(
    me_ref, lengths_ref, slot_ref, leaf_ref, rows_ref, table_hbm, in_hbm, out_hbm, tangent_hbm,
    output_hbm, d_rows_ref, keep_hbm, send_hbm, keep_late_hbm, send_late_hbm,
    inputs, gated, d_pre, grads, output,
    normed, turned, moved, moved_late, turned_gated, moved_gated, hidden, slope, weights, weights_slope, mixed, d_mixed,
    d_score, d_gated, allowed, allowed_scale, keys_t, values_t, d_inputs, leaf_grad, table, w_in, w_out, tangent, sems, out_sems,
):
    count, width = inputs.shape
    head = width // HEADS
    half_scale = 0.5 * head ** (-0.5)
    half_rows = width // 2
    copies = [
        pltpu.make_async_copy(source, target, sems.at[k])
        for k, (source, target) in enumerate(
            ((table_hbm, table), (in_hbm, w_in), (out_hbm, w_out), (tangent_hbm, tangent))
        )
    ]
    for copy in copies:
        copy.start()
    leaving = []

    def leave(source, target):
        copy = pltpu.make_async_copy(source, target, out_sems.at[len(leaving)])
        copy.start()
        leaving.append(copy)

    rows = from_tiles(rows_ref[...], width)
    picker, onehot = pickers(rows.shape[0], slot_ref, leaf_ref, table.shape[0])
    ends = []
    total = 0
    for place in range(lengths_ref.shape[1]):
        total = total + lengths_ref[0, place]
        ends.append(total)
    for start, low, high in spans(count):
        at = slice(start, start + BLOCK)
        row = start + lax.broadcasted_iota(jnp.int32, (BLOCK, high - low), 0)
        column = low + lax.broadcasted_iota(jnp.int32, (BLOCK, high - low), 1)
        first = jnp.zeros_like(row)
        for end in ends[:-1]:
            first = jnp.where(row >= end, end, first)
        seen = jnp.logical_and(column >= first, column <= row)
        allowed[at, low:high] = jnp.where(seen, 1.0, 0.0).astype(bf16)
        allowed_scale[at, low:high] = jnp.where(seen, 2.0 * half_scale, 0.0).astype(bf16)
    copies[0].wait()
    inputs[...] = (mm_tn(picker, rows) + mm_tn(onehot, table[...])).astype(bf16)
    for at in strips(0, count):
        values, scale = center(inputs[at, :].astype(f32))
        normed[at, :] = (values * scale).astype(bf16)
    turned[...] = normed[...].T
    copies[1].wait()
    for start in range(0, 4 * width, 2 * BLOCK):
        to = slice(start, start + 2 * BLOCK)
        halves = mm(normed[...], w_in[:, to]) * 0.5
        for at in strips(0, count):
            value, slope_at = silu(halves[at, :])
            hidden[at, to] = value
            slope[at, to] = slope_at
    keys_t[...] = hidden[:, 3 * width :].T
    values_t[...] = hidden[:, width : 2 * width].T
    for start, low, high in spans(count):
        at = slice(start, start + BLOCK)
        end = start // (2 * BLOCK) * 2 * BLOCK + 2 * BLOCK
        for out in (slice(0, low), slice(high, end)):
            if out.start < out.stop:
                nothing = jnp.zeros((HEADS, BLOCK, out.stop - out.start), bf16)
                weights[:, at, out] = nothing
                d_score[:, at, out] = nothing
    for h in range(HEADS):
        own = slice(h * head, (h + 1) * head)
        value_at = slice(width + h * head, width + (h + 1) * head)
        query_at = slice(2 * width + h * head, 2 * width + (h + 1) * head)
        key_at = slice(3 * width + h * head, 3 * width + (h + 1) * head)
        for start, low, high in spans(count):
            at = slice(start, start + BLOCK)
            halves = mm(hidden[at, query_at], keys_t[own, low:high]) * half_scale
            for strip in strips(0, BLOCK):
                to = slice(start + strip.start, start + strip.stop)
                value, slope_at = silu(halves[strip, :])
                weights[h, to, low:high] = value * allowed[to, low:high]
                weights_slope[h, to, low:high] = slope_at * allowed_scale[to, low:high]
        for start in range(0, count, 2 * BLOCK):
            at = slice(start, start + 2 * BLOCK)
            high = start + 2 * BLOCK
            mixed[at, h * head : (h + 1) * head] = mm(
                weights[h, at, :high], hidden[:high, value_at]
            )
    copies[2].wait()
    copies[3].wait()
    d_gated[...] = mm_nt(tangent[...], w_out[...]).astype(bf16)
    for at in strips(0, count):
        values, scale = center(mixed[at, :])
        values = values * scale
        gates = hidden[at, :width].astype(f32)
        change = d_gated[at, :].astype(f32)
        gated[at, :] = (values * gates).astype(bf16)
        d_pre[at, :width] = (change * values).astype(bf16) * slope[at, :width]
        d_mixed[at, :] = pull_normalize(change * gates, values, scale).astype(bf16)
    for h in range(HEADS):
        own = slice(h * head, (h + 1) * head)
        value_at = slice(width + h * head, width + (h + 1) * head)
        query_at = slice(2 * width + h * head, 2 * width + (h + 1) * head)
        key_at = slice(3 * width + h * head, 3 * width + (h + 1) * head)
        for start, low, high in spans(count):
            at = slice(start, start + BLOCK)
            d_weights = mm(d_mixed[at, own], values_t[own, low:high]).astype(bf16)
            d_score[h, at, low:high] = d_weights * weights_slope[h, at, low:high]
        for start in range(0, count, 2 * BLOCK):
            at = slice(start, start + 2 * BLOCK)
            high = start + 2 * BLOCK
            d_query = mm(d_score[h, at, :high], hidden[:high, key_at])
            d_pre[at, query_at] = d_query.astype(bf16) * slope[at, query_at]
            d_key = mm_tn(d_score[h, start:, at], hidden[start:, query_at])
            d_pre[at, key_at] = d_key.astype(bf16) * slope[at, key_at]
            d_value = mm_tn(weights[h, start:, at], d_mixed[start:, own])
            d_pre[at, value_at] = d_value.astype(bf16) * slope[at, value_at]
    me = me_ref[0]
    early, late = chunk_order(me, EARLY), chunk_order(me, LATE, SHARED)
    permute_rows(early, turned, moved)
    permute_rows(late, turned, moved_late)
    for start in range(0, SPLIT, 2 * BLOCK):
        to = slice(start, min(start + 2 * BLOCK, SPLIT))
        grads[:, to] = mm(moved[...], d_pre[:, to]).astype(bf16)
    grads[:, SPLIT : 4 * width] = mm(moved_late[...], d_pre[:, SPLIT:]).astype(bf16)
    leave(grads.at[half_rows:, :SPLIT], send_hbm)
    leave(grads.at[:half_rows, :SPLIT], keep_hbm)
    turned_gated[...] = gated[...].T
    permute_rows(late, turned_gated, moved_gated)
    grads[:, 4 * width : 5 * width] = mm(moved_gated[...], tangent[...]).astype(bf16)
    output[...] = (mm(gated[...], w_out[...]) + inputs[...].astype(f32)).astype(bf16)
    leave(output, output_hbm)
    normed_change = mm_nt(d_pre[...], w_in[...])
    for at in strips(0, count):
        values, scale = center(inputs[at, :].astype(f32))
        change = pull_normalize(normed_change[at, :], values * scale, scale)
        d_inputs[at, :] = (change + tangent[at, :].astype(f32)).astype(bf16)
    leaves = table.shape[0]
    d_leaf = mm(onehot, d_inputs[...]).astype(bf16)
    leaf_grad[:leaves, :] = d_leaf[:, : width // 2]
    leaf_grad[leaves:, :] = d_leaf[:, width // 2 :]
    permute_rows(late, leaf_grad, grads.at[:, 5 * width :])
    leave(grads.at[half_rows:, SPLIT:], send_late_hbm)
    leave(grads.at[:half_rows, SPLIT:], keep_late_hbm)
    d_rows_ref[...] = to_tiles(mm(picker, d_inputs[...]).astype(bf16))
    for copy in leaving:
        copy.wait()


def run_layer(me, lengths, slot, leaf, rows, table, w_in, w_out, tangent):
    count, width = tangent.shape
    smem = pl.BlockSpec(memory_space=pltpu.SMEM)
    vmem = pl.BlockSpec(memory_space=pltpu.VMEM)
    hbm = pl.BlockSpec(memory_space=pltpu.HBM)
    shape = jax.ShapeDtypeStruct
    columns = 5 * width + width // 2
    return pl.pallas_call(
        layer_kernel,
        name="layer",
        out_shape=(
            shape((count, width), bf16),
            shape(rows.shape, bf16),
            shape((width // 2, SPLIT), bf16),
            shape((width // 2, SPLIT), bf16),
            shape((width // 2, columns - SPLIT), bf16),
            shape((width // 2, columns - SPLIT), bf16),
        ),
        in_specs=[smem, smem] + [vmem] * 3 + [hbm] * 4,
        out_specs=(hbm, vmem, hbm, hbm, hbm, hbm),
        scratch_shapes=[
            pltpu.VMEM((count, width), bf16),
            pltpu.VMEM((count, width), bf16),
            pltpu.VMEM((count, 4 * width), bf16),
            pltpu.VMEM((width, columns), bf16),
            pltpu.VMEM((count, width), bf16),
            pltpu.VMEM((count, width), bf16),
            pltpu.VMEM((width, count), bf16),
            pltpu.VMEM((width, count), bf16),
            pltpu.VMEM((width, count), bf16),
            pltpu.VMEM((width, count), bf16),
            pltpu.VMEM((width, count), bf16),
            pltpu.VMEM((count, 4 * width), bf16),
            pltpu.VMEM((count, 4 * width), bf16),
            pltpu.VMEM((HEADS, count, count), bf16),
            pltpu.VMEM((HEADS, count, count), bf16),
            pltpu.VMEM((count, width), f32),
            pltpu.VMEM((count, width), bf16),
            pltpu.VMEM((HEADS, count, count), bf16),
            pltpu.VMEM((count, width), bf16),
            pltpu.VMEM((count, count), bf16),
            pltpu.VMEM((count, count), bf16),
            pltpu.VMEM((width, count), bf16),
            pltpu.VMEM((width, count), bf16),
            pltpu.VMEM((count, width), bf16),
            pltpu.VMEM((width, width // 2), bf16),
            pltpu.VMEM(table.shape, bf16),
            pltpu.VMEM(w_in.shape, bf16),
            pltpu.VMEM(w_out.shape, bf16),
            pltpu.VMEM(tangent.shape, bf16),
            pltpu.SemaphoreType.DMA((4,)),
            pltpu.SemaphoreType.DMA((5,)),
        ],
        compiler_params=pltpu.CompilerParams(vmem_limit_bytes=LAYER_VMEM),
        cost_estimate=pl.CostEstimate(flops=6 * 10**9, bytes_accessed=10**7, transcendentals=10**6),
    )(me, lengths, slot, leaf, rows, table, w_in, w_out, tangent)


def write_chunks(me, half, early_ref, late_ref, leaf_hbm, in_hbm, out_hbm, grads, sems):
    width = in_hbm.shape[0]
    leaves = leaf_hbm.shape[0]
    places = early_ref.shape[0] // ROWS
    early, late = chunk_order(me, EARLY), chunk_order(me, LATE, SHARED)
    leaving = []

    def leave(source, target):
        copy = pltpu.make_async_copy(source, target, sems.at[len(leaving)])
        copy.start()
        leaving.append(copy)

    for place in range(places):
        at = slice(place * ROWS, (place + 1) * ROWS)
        grads[at, :SPLIT] = early_ref[at, :].astype(f32)
        start = pl.multiple_of(early[half * places + place] * ROWS, ROWS)
        leave(grads.at[at, :SPLIT], in_hbm.at[pl.ds(start, ROWS), :SPLIT])
        grads[at, SPLIT:] = late_ref[at, :].astype(f32)
        start = pl.multiple_of(late[half * places + place] * ROWS, ROWS)
        leave(grads.at[at, SPLIT : 4 * width], in_hbm.at[pl.ds(start, ROWS), SPLIT:])
        leave(grads.at[at, 4 * width : 5 * width], out_hbm.at[pl.ds(start, ROWS), :])
        side = (start >= leaves).astype(jnp.int32)
        start = pl.multiple_of(start - side * leaves, ROWS)
        column = pl.multiple_of(side * (width // 2), width // 2)
        leave(
            grads.at[at, 5 * width :],
            leaf_hbm.at[pl.ds(start, ROWS), pl.ds(column, width // 2)],
        )
    return leaving


def finish_own_kernel(
    me_ref, chosen_ref, returned_ref, early_ref, late_ref,
    table_ref, leaf_hbm, in_hbm, out_hbm, grads, sems,
):
    leaving = write_chunks(
        me_ref[0], 0, early_ref, late_ref, leaf_hbm, in_hbm, out_hbm, grads, sems
    )
    parts = table_ref.shape[1] // BLOCK
    part_of = lax.broadcasted_iota(jnp.int32, chosen_ref.shape, 0) & (parts - 1)
    for part in range(parts):
        mine = jnp.where(part_of == part, chosen_ref[...].astype(f32), 0.0).astype(bf16)
        table_ref[:, part * BLOCK : (part + 1) * BLOCK] = mm_tn(mine, returned_ref[...])
    for copy in leaving:
        copy.wait()


def finish_other_kernel(
    me_ref, early_ref, late_ref, leaf_in, in_in, out_in, leaf_hbm, in_hbm, out_hbm, grads, sems
):
    leaving = write_chunks(
        me_ref[0], 1, early_ref, late_ref, leaf_hbm, in_hbm, out_hbm, grads, sems
    )
    for copy in leaving:
        copy.wait()


def finish_scratch(early, late):
    return [
        pltpu.VMEM((early.shape[0], early.shape[1] + late.shape[1]), f32),
        pltpu.SemaphoreType.DMA((4 * early.shape[0] // ROWS,)),
    ]


def run_finish(me, chosen, returned, early_own, early_other, late_own, late_other, leaves, width):
    smem = pl.BlockSpec(memory_space=pltpu.SMEM)
    vmem = pl.BlockSpec(memory_space=pltpu.VMEM)
    hbm = pl.BlockSpec(memory_space=pltpu.HBM)
    shapes = tuple(
        jax.ShapeDtypeStruct(shape, f32)
        for shape in (
            (chosen.shape[1], width), (leaves, width), (width, 4 * width), (width, width)
        )
    )
    table, *written = pl.pallas_call(
        finish_own_kernel,
        name="finish_own",
        out_shape=shapes,
        in_specs=[smem] + [vmem] * 4,
        out_specs=(vmem, hbm, hbm, hbm),
        scratch_shapes=finish_scratch(early_own, late_own),
        compiler_params=pltpu.CompilerParams(vmem_limit_bytes=16 * 2**20),
        cost_estimate=pl.CostEstimate(flops=10**8, bytes_accessed=5 * 10**6, transcendentals=0),
    )(me, chosen, returned, early_own, late_own)
    written = pl.pallas_call(
        finish_other_kernel,
        name="finish_other",
        out_shape=shapes[1:],
        in_specs=[smem] + [vmem] * 2 + [hbm] * 3,
        out_specs=(hbm,) * 3,
        scratch_shapes=finish_scratch(early_own, late_own),
        input_output_aliases={3: 0, 4: 1, 5: 2},
        compiler_params=pltpu.CompilerParams(vmem_limit_bytes=16 * 2**20),
        cost_estimate=pl.CostEstimate(flops=0, bytes_accessed=5 * 10**6, transcendentals=0),
    )(me, early_other, late_other, *written)
    return (table, *written)


def load_kernel(*refs):
    for source, target in zip(refs[: len(refs) // 2], refs[len(refs) // 2 :]):
        target[...] = source[...]


def run_load(*arrays):
    vmem = pl.BlockSpec(memory_space=pltpu.VMEM)
    return pl.pallas_call(
        load_kernel,
        name="load",
        out_shape=tuple(jax.ShapeDtypeStruct(array.shape, array.dtype) for array in arrays),
        in_specs=[vmem] * len(arrays),
        out_specs=(vmem,) * len(arrays),
        compiler_params=pltpu.CompilerParams(vmem_limit_bytes=8 * 2**20),
        cost_estimate=pl.CostEstimate(flops=0, bytes_accessed=4 * 2**20, transcendentals=0),
    )(*arrays)


def merge_kernel(keep_ref, other_ref, *outs):
    rows = outs[0].shape[0]
    for part, out in enumerate(outs):
        at = slice(part * rows, (part + 1) * rows)
        out[...] = (keep_ref[at, :].astype(f32) + other_ref[at, :].astype(f32)).astype(bf16)


def run_merge(keep, other, parts):
    vmem = pl.BlockSpec(memory_space=pltpu.VMEM)
    part = jax.ShapeDtypeStruct((keep.shape[0] // parts, keep.shape[1]), bf16)
    return pl.pallas_call(
        merge_kernel,
        name="merge",
        out_shape=(part,) * parts,
        in_specs=[vmem] * 2,
        out_specs=(vmem,) * parts,
        compiler_params=pltpu.CompilerParams(vmem_limit_bytes=8 * 2**20),
    )(keep, other)


def exchange(blocks):
    return lax.all_to_all(blocks, ("dp", "rep"), split_axis=0, concat_axis=0, tiled=True)


def swap(block, mask, count):
    return lax.ppermute(block, ("dp", "rep"), [(i, i ^ mask) for i in range(count)])


def add(parts):
    return sum(part.astype(f32) for part in parts)


def shares(parts, group):
    size = 2 ** len(group)
    rows = parts[0].shape[0] // size
    return [
        add(part[digit * rows : (digit + 1) * rows] for part in parts).astype(bf16)
        for digit in range(1, size)
    ]


def swap_all(blocks, group, count):
    return [
        swap(block, mask_of(group, digit), count) for digit, block in enumerate(blocks, start=1)
    ]


def extend(parts, got):
    return [part[: got[0].shape[0]] for part in parts] + got


def split_up(parts, group, count):
    return extend(parts, swap_all(shares(parts, group), group, count))


def sum_with(block, group, count):
    return block.astype(f32) + swap(block, mask_of(group, 1), count).astype(f32)


def join(block, group, count):
    pieces = swap_all([block] * (2 ** len(group) - 1), group, count)
    return jnp.concatenate([block] + pieces, axis=0)


def reduce_and_gather(early, late, d_rows, count):
    _, near, far = EARLY
    _, first, second = LATE
    early_other, late_other = swap(early[1], 1, count), swap(late[1], 1, count)
    early_own, late_own = run_load(early[0], late[0])
    early, *early_blocks = run_merge(early_own, early_other, 2 ** len(near))
    late, *late_blocks = run_merge(late_own, late_other, 2 ** len(first))
    early_blocks, late_blocks = lax.optimization_barrier((early_blocks, late_blocks))
    early_got = swap_all(early_blocks, near, count)
    late = [late] + swap_all(late_blocks, first, count)
    late_got = swap_all(shares(late, second), second, count)
    early_got[0], late, d_rows = lax.optimization_barrier((early_got[0], late, d_rows))
    returned = exchange(d_rows)
    early_got, late = lax.optimization_barrier((early_got, extend(late, late_got)))
    early, late = split_up([early] + early_got, far, count), add(late).astype(bf16)
    late = sum_with(late, SHARED[0], count).astype(bf16)
    early, late = add(early), sum_with(late, SHARED[1], count)
    reach = CHUNKS
    while reach < count:
        early, late = early + swap(early, reach, count), late + swap(late, reach, count)
        reach *= 2
    early, returned = lax.optimization_barrier(((early * (1.0 / count)).astype(bf16), returned))
    early = join(early, far, count)
    early, late = lax.optimization_barrier((early, (late * (1.0 / count)).astype(bf16)))
    pieces = swap_all([early] * (2 ** len(near) - 1), near, count)
    late = join(join(late, second, count), first, count)
    pieces, late = lax.optimization_barrier((pieces, late))
    early = jnp.concatenate([early] + pieces, axis=0)
    return returned, early, swap(early, 1, count), late, swap(late, 1, count)


def on_device(
    item_table, requests, event_slot, lengths, leaf_ids, leaf_table, w_in, w_out, cotangent
):
    count = lax.axis_size("dp") * lax.axis_size("rep")
    place = lax.axis_index(("dp", "rep")).astype(jnp.int32)
    me = (place & (CHUNKS - 1)).reshape(1)
    slot = event_slot.reshape(1, -1)
    leaf = leaf_ids.T
    asked = exchange(requests[0])
    (table,) = run_load(item_table)
    fetched, chosen = run_lookup(asked, table)
    arrived = exchange(fetched)
    output, d_rows, keep, send, keep_late, send_late = run_layer(
        me, lengths, slot, leaf, arrived, leaf_table, w_in, w_out, cotangent
    )
    returned, early, early_other, late, late_other = reduce_and_gather(
        (keep, send), (keep_late, send_late), d_rows, count
    )
    table_grad, leaf_mean, in_mean, out_mean = run_finish(
        me, chosen, returned, early, early_other, late, late_other, *leaf_table.shape
    )
    return (output, table_grad, leaf_mean, in_mean, out_mean)


def solution(mesh):
    return jax.shard_map(
        on_device,
        mesh=mesh,
        in_specs=(
            P(("dp", "rep"), None),
            P(("dp", "rep"), None, None),
            P(("dp", "rep")),
            P(("dp", "rep"), None),
            P(("dp", "rep"), None),
            P(),
            P(),
            P(),
            P(("dp", "rep"), None),
        ),
        out_specs=(P(("dp", "rep"), None), P(("dp", "rep"), None), P(), P(), P()),
        check_vma=False,
    )
```

```python
import functools
import jax
import jax.numpy as jnp
from jax import lax
from jax.experimental import pallas as pl
from jax.experimental.pallas import tpu as pltpu
from jax.sharding import PartitionSpec as P

HEADS = 4
MAXLEN = 256
BLOCK = 128
ROWS = 16
epsilon = 1e-06
f32 = jnp.float32
bf16 = jnp.bfloat16

EARLY = ((0,), (1, 2), (3, 4))
LATE = ((0,), (3,), (4,))
SHARED = ((2,), (1,))
SPLIT = 2048
CHUNKS = 32
STRIP = 32
LAYER_VMEM = 56 * 2**20


def dot(a, b, contract):
    return lax.dot_general(a, b, ((contract[0], contract[1]), ((), ())), preferred_element_type=f32)


def mm(a, b):
    return dot(a, b, ((1,), (0,)))


def mm_nt(a, b):
    return dot(a, b, ((1,), (1,)))


def mm_tn(a, b):
    return dot(a, b, ((0,), (0,)))


def mask_of(group, digit):
    return sum(((digit >> k) & 1) << bit for k, bit in enumerate(group))


def chunk_order(me, route, shared=()):
    masks = [0]
    for group in route + shared:
        masks = [mask ^ mask_of(group, digit) for mask in masks for digit in range(2 ** len(group))]
    for group in shared:
        me = me & ~mask_of(group, 1)
    return [me ^ mask for mask in masks]


def spans(count):
    for start in range(0, count, BLOCK):
        low = max(0, start - (MAXLEN - 1)) // BLOCK * BLOCK
        yield start, low, start + BLOCK


def strips(start, stop):
    return [slice(at, at + STRIP) for at in range(start, stop, STRIP)]


def silu(half):
    curve = jnp.tanh(half)
    value = (half + half * curve).astype(bf16)
    half, curve = half.astype(bf16), curve.astype(bf16)
    return value, (0.5 + 0.5 * curve) * (1.0 + half * (1.0 - curve))


def center(values):
    values = values - jnp.mean(values, axis=-1, keepdims=True)
    return values, lax.rsqrt(jnp.mean(values * values, axis=-1, keepdims=True) + epsilon)


def pull_normalize(change, normed, scale):
    return scale * (
        change
        - jnp.mean(change, axis=-1, keepdims=True)
        - normed * jnp.mean(change * normed, axis=-1, keepdims=True)
    )


def pickers(slots, slot_ref, leaf_ref, leaves):
    count = slot_ref.shape[1]
    picker = lax.broadcasted_iota(jnp.int32, (slots, count), 0) == slot_ref[...]
    trees = leaf_ref.shape[0]
    each = leaves // trees
    spots = lax.broadcasted_iota(jnp.int32, (each, count), 0)
    onehot = [(spots == leaf_ref[t : t + 1, :]).astype(f32).astype(bf16) for t in range(trees)]
    return picker.astype(f32).astype(bf16), jnp.concatenate(onehot, axis=0)


def permute_rows(chunks, source, target):
    for place, chunk in enumerate(chunks):
        start = pl.multiple_of(chunk * ROWS, ROWS)
        target[place * ROWS : (place + 1) * ROWS, :] = source[pl.ds(start, ROWS), :]


def zero_one(condition):
    return jnp.where(condition, 1.0, 0.0).astype(bf16)


def to_tiles(rows):
    parts = rows.shape[1] // BLOCK
    shape = (rows.shape[0] * parts, rows.shape[0])
    row, column = (lax.broadcasted_iota(jnp.int32, shape, axis) for axis in (0, 1))
    total = jnp.zeros((shape[0], BLOCK), f32)
    for part in range(parts):
        place = zero_one(row == column * parts + part)
        total = total + mm(place, rows[:, part * BLOCK : (part + 1) * BLOCK])
    return total.astype(bf16)


def from_tiles(block, width):
    parts = width // BLOCK
    shape = (block.shape[0] // parts, block.shape[0])
    row, column = (lax.broadcasted_iota(jnp.int32, shape, axis) for axis in (0, 1))
    pieces = [mm(zero_one(column == row * parts + part), block) for part in range(parts)]
    return jnp.concatenate(pieces, axis=1).astype(bf16)


def lookup_kernel(asked_ref, table_ref, rows_ref, chosen_ref):
    count, each = asked_ref.shape
    owned, width = table_ref.shape
    parts = width // BLOCK
    many = count * each * parts
    spot = lax.broadcasted_iota(jnp.int32, (count, owned), 1)
    row = lax.broadcasted_iota(jnp.int32, (many, count), 0)
    device = lax.broadcasted_iota(jnp.int32, (many, count), 1)
    here, wanted = [], []
    for k in range(each):
        base = (device * each + k) * parts
        here.append(zero_one(jnp.logical_and(row >= base, row < base + parts)))
        wanted.append(zero_one(spot == asked_ref[:, k : k + 1]))
    chosen = mm(jnp.concatenate(here, axis=1), jnp.concatenate(wanted, axis=0))
    chosen_ref[...] = chosen.astype(bf16)
    part_of = lax.broadcasted_iota(jnp.int32, (many, owned), 0) & (parts - 1)
    mine = [jnp.where(part_of == part, chosen, 0.0).astype(bf16) for part in range(parts)]
    blocks = [table_ref[:, part * BLOCK : (part + 1) * BLOCK] for part in range(parts)]
    total = mm(jnp.concatenate(mine, axis=1), jnp.concatenate(blocks, axis=0))
    rows_ref[...] = total.astype(bf16)


def run_lookup(asked, table):
    vmem = pl.BlockSpec(memory_space=pltpu.VMEM)
    shape = jax.ShapeDtypeStruct
    many = asked.shape[0] * asked.shape[1] * table.shape[1] // BLOCK
    return pl.pallas_call(
        lookup_kernel,
        name="lookup",
        out_shape=(
            shape((many, BLOCK), bf16),
            shape((many, table.shape[0]), bf16),
        ),
        in_specs=[vmem, vmem],
        out_specs=(vmem,) * 2,
        compiler_params=pltpu.CompilerParams(vmem_limit_bytes=16 * 2**20),
    )(asked, table)


def layer_kernel(
    me_ref, lengths_ref, slot_ref, leaf_ref, rows_ref, table_hbm, in_hbm, out_hbm, tangent_hbm,
    output_hbm, d_rows_ref, keep_hbm, send_hbm, keep_late_hbm, send_late_hbm,
    inputs, gated, d_pre, grads, output,
    normed, turned, moved, turned_gated, moved_gated, hidden, slope, weights, weights_slope, mixed, d_mixed,
    d_score, d_gated, allowed, allowed_scale, keys_t, values_t, d_inputs, leaf_grad, table, w_in, w_out, tangent, sems, out_sems,
):
    count, width = inputs.shape
    head = width // HEADS
    half_scale = 0.5 * head ** (-0.5)
    half_rows = width // 2
    copies = [
        pltpu.make_async_copy(source, target, sems.at[k])
        for k, (source, target) in enumerate(
            ((table_hbm, table), (in_hbm, w_in), (out_hbm, w_out), (tangent_hbm, tangent))
        )
    ]
    for copy in copies:
        copy.start()
    leaving = []

    def leave(source, target):
        copy = pltpu.make_async_copy(source, target, out_sems.at[len(leaving)])
        copy.start()
        leaving.append(copy)

    rows = from_tiles(rows_ref[...], width)
    picker, onehot = pickers(rows.shape[0], slot_ref, leaf_ref, table.shape[0])
    ends = []
    total = 0
    for place in range(lengths_ref.shape[1]):
        total = total + lengths_ref[0, place]
        ends.append(total)
    for start, low, high in spans(count):
        at = slice(start, start + BLOCK)
        row = start + lax.broadcasted_iota(jnp.int32, (BLOCK, high - low), 0)
        column = low + lax.broadcasted_iota(jnp.int32, (BLOCK, high - low), 1)
        first = jnp.zeros_like(row)
        for end in ends[:-1]:
            first = jnp.where(row >= end, end, first)
        seen = jnp.logical_and(column >= first, column <= row)
        allowed[at, low:high] = jnp.where(seen, 1.0, 0.0).astype(bf16)
        allowed_scale[at, low:high] = jnp.where(seen, 2.0 * half_scale, 0.0).astype(bf16)
    copies[0].wait()
    inputs[...] = (mm_tn(picker, rows) + mm_tn(onehot, table[...])).astype(bf16)
    for at in strips(0, count):
        values, scale = center(inputs[at, :].astype(f32))
        normed[at, :] = (values * scale).astype(bf16)
    turned[...] = normed[...].T
    copies[1].wait()
    for start in range(0, 4 * width, 2 * BLOCK):
        to = slice(start, start + 2 * BLOCK)
        halves = mm(normed[...], w_in[:, to]) * 0.5
        for at in strips(0, count):
            value, slope_at = silu(halves[at, :])
            hidden[at, to] = value
            slope[at, to] = slope_at
    keys_t[...] = hidden[:, 3 * width :].T
    values_t[...] = hidden[:, width : 2 * width].T
    for start, low, high in spans(count):
        at = slice(start, start + BLOCK)
        end = start // (2 * BLOCK) * 2 * BLOCK + 2 * BLOCK
        for out in (slice(0, low), slice(high, end)):
            if out.start < out.stop:
                nothing = jnp.zeros((HEADS, BLOCK, out.stop - out.start), bf16)
                weights[:, at, out] = nothing
                d_score[:, at, out] = nothing
    for h in range(HEADS):
        own = slice(h * head, (h + 1) * head)
        value_at = slice(width + h * head, width + (h + 1) * head)
        query_at = slice(2 * width + h * head, 2 * width + (h + 1) * head)
        key_at = slice(3 * width + h * head, 3 * width + (h + 1) * head)
        for start, low, high in spans(count):
            at = slice(start, start + BLOCK)
            halves = mm(hidden[at, query_at], keys_t[own, low:high]) * half_scale
            for strip in strips(0, BLOCK):
                to = slice(start + strip.start, start + strip.stop)
                value, slope_at = silu(halves[strip, :])
                weights[h, to, low:high] = value * allowed[to, low:high]
                weights_slope[h, to, low:high] = slope_at * allowed_scale[to, low:high]
        for start in range(0, count, 2 * BLOCK):
            at = slice(start, start + 2 * BLOCK)
            high = start + 2 * BLOCK
            mixed[at, h * head : (h + 1) * head] = mm(
                weights[h, at, :high], hidden[:high, value_at]
            )
    copies[2].wait()
    copies[3].wait()
    d_gated[...] = mm_nt(tangent[...], w_out[...]).astype(bf16)
    for at in strips(0, count):
        values, scale = center(mixed[at, :])
        values = values * scale
        gates = hidden[at, :width].astype(f32)
        change = d_gated[at, :].astype(f32)
        gated[at, :] = (values * gates).astype(bf16)
        d_pre[at, :width] = (change * values).astype(bf16) * slope[at, :width]
        d_mixed[at, :] = pull_normalize(change * gates, values, scale).astype(bf16)
    for h in range(HEADS):
        own = slice(h * head, (h + 1) * head)
        value_at = slice(width + h * head, width + (h + 1) * head)
        query_at = slice(2 * width + h * head, 2 * width + (h + 1) * head)
        key_at = slice(3 * width + h * head, 3 * width + (h + 1) * head)
        for start, low, high in spans(count):
            at = slice(start, start + BLOCK)
            d_weights = mm(d_mixed[at, own], values_t[own, low:high]).astype(bf16)
            d_score[h, at, low:high] = d_weights * weights_slope[h, at, low:high]
        for start in range(0, count, 2 * BLOCK):
            at = slice(start, start + 2 * BLOCK)
            high = start + 2 * BLOCK
            d_query = mm(d_score[h, at, :high], hidden[:high, key_at])
            d_pre[at, query_at] = d_query.astype(bf16) * slope[at, query_at]
            d_key = mm_tn(d_score[h, start:, at], hidden[start:, query_at])
            d_pre[at, key_at] = d_key.astype(bf16) * slope[at, key_at]
            d_value = mm_tn(weights[h, start:, at], d_mixed[start:, own])
            d_pre[at, value_at] = d_value.astype(bf16) * slope[at, value_at]
    me = me_ref[0]
    early, late = chunk_order(me, EARLY), chunk_order(me, LATE, SHARED)
    permute_rows(early, turned, moved)
    for start in range(0, 4 * width, 2 * BLOCK):
        to = slice(start, start + 2 * BLOCK)
        grads[:, to] = mm(moved[...], d_pre[:, to]).astype(bf16)
    leave(grads.at[half_rows:, :SPLIT], send_hbm)
    leave(grads.at[:half_rows, :SPLIT], keep_hbm)
    turned_gated[...] = gated[...].T
    permute_rows(late, turned_gated, moved_gated)
    grads[:, 4 * width : 5 * width] = mm(moved_gated[...], tangent[...]).astype(bf16)
    output[...] = (mm(gated[...], w_out[...]) + inputs[...].astype(f32)).astype(bf16)
    leave(output, output_hbm)
    normed_change = mm_nt(d_pre[...], w_in[...])
    for at in strips(0, count):
        values, scale = center(inputs[at, :].astype(f32))
        change = pull_normalize(normed_change[at, :], values * scale, scale)
        d_inputs[at, :] = (change + tangent[at, :].astype(f32)).astype(bf16)
    leaves = table.shape[0]
    d_leaf = mm(onehot, d_inputs[...]).astype(bf16)
    leaf_grad[:leaves, :] = d_leaf[:, : width // 2]
    leaf_grad[leaves:, :] = d_leaf[:, width // 2 :]
    permute_rows(late, leaf_grad, grads.at[:, 5 * width :])
    leave(grads.at[half_rows:, SPLIT:], send_late_hbm)
    leave(grads.at[:half_rows, SPLIT:], keep_late_hbm)
    d_rows_ref[...] = to_tiles(mm(picker, d_inputs[...]).astype(bf16))
    for copy in leaving:
        copy.wait()


def run_layer(me, lengths, slot, leaf, rows, table, w_in, w_out, tangent):
    count, width = tangent.shape
    smem = pl.BlockSpec(memory_space=pltpu.SMEM)
    vmem = pl.BlockSpec(memory_space=pltpu.VMEM)
    hbm = pl.BlockSpec(memory_space=pltpu.HBM)
    shape = jax.ShapeDtypeStruct
    columns = 5 * width + width // 2
    return pl.pallas_call(
        layer_kernel,
        name="layer",
        out_shape=(
            shape((count, width), bf16),
            shape(rows.shape, bf16),
            shape((width // 2, SPLIT), bf16),
            shape((width // 2, SPLIT), bf16),
            shape((width // 2, columns - SPLIT), bf16),
            shape((width // 2, columns - SPLIT), bf16),
        ),
        in_specs=[smem, smem] + [vmem] * 3 + [hbm] * 4,
        out_specs=(hbm, vmem, hbm, hbm, hbm, hbm),
        scratch_shapes=[
            pltpu.VMEM((count, width), bf16),
            pltpu.VMEM((count, width), bf16),
            pltpu.VMEM((count, 4 * width), bf16),
            pltpu.VMEM((width, columns), bf16),
            pltpu.VMEM((count, width), bf16),
            pltpu.VMEM((count, width), bf16),
            pltpu.VMEM((width, count), bf16),
            pltpu.VMEM((width, count), bf16),
            pltpu.VMEM((width, count), bf16),
            pltpu.VMEM((width, count), bf16),
            pltpu.VMEM((count, 4 * width), bf16),
            pltpu.VMEM((count, 4 * width), bf16),
            pltpu.VMEM((HEADS, count, count), bf16),
            pltpu.VMEM((HEADS, count, count), bf16),
            pltpu.VMEM((count, width), f32),
            pltpu.VMEM((count, width), bf16),
            pltpu.VMEM((HEADS, count, count), bf16),
            pltpu.VMEM((count, width), bf16),
            pltpu.VMEM((count, count), bf16),
            pltpu.VMEM((count, count), bf16),
            pltpu.VMEM((width, count), bf16),
            pltpu.VMEM((width, count), bf16),
            pltpu.VMEM((count, width), bf16),
            pltpu.VMEM((width, width // 2), bf16),
            pltpu.VMEM(table.shape, bf16),
            pltpu.VMEM(w_in.shape, bf16),
            pltpu.VMEM(w_out.shape, bf16),
            pltpu.VMEM(tangent.shape, bf16),
            pltpu.SemaphoreType.DMA((4,)),
            pltpu.SemaphoreType.DMA((5,)),
        ],
        compiler_params=pltpu.CompilerParams(vmem_limit_bytes=LAYER_VMEM),
        cost_estimate=pl.CostEstimate(flops=6 * 10**9, bytes_accessed=10**7, transcendentals=10**6),
    )(me, lengths, slot, leaf, rows, table, w_in, w_out, tangent)


def write_chunks(me, half, early_ref, late_ref, leaf_hbm, in_hbm, out_hbm, grads, sems):
    width = in_hbm.shape[0]
    leaves = leaf_hbm.shape[0]
    places = early_ref.shape[0] // ROWS
    early, late = chunk_order(me, EARLY), chunk_order(me, LATE, SHARED)
    leaving = []

    def leave(source, target):
        copy = pltpu.make_async_copy(source, target, sems.at[len(leaving)])
        copy.start()
        leaving.append(copy)

    for place in range(places):
        at = slice(place * ROWS, (place + 1) * ROWS)
        grads[at, :SPLIT] = early_ref[at, :].astype(f32)
        start = pl.multiple_of(early[half * places + place] * ROWS, ROWS)
        leave(grads.at[at, :SPLIT], in_hbm.at[pl.ds(start, ROWS), :])
        grads[at, SPLIT:] = late_ref[at, :].astype(f32)
        start = pl.multiple_of(late[half * places + place] * ROWS, ROWS)
        leave(grads.at[at, SPLIT : SPLIT + width], out_hbm.at[pl.ds(start, ROWS), :])
        side = (start >= leaves).astype(jnp.int32)
        start = pl.multiple_of(start - side * leaves, ROWS)
        column = pl.multiple_of(side * (width // 2), width // 2)
        leave(
            grads.at[at, SPLIT + width :],
            leaf_hbm.at[pl.ds(start, ROWS), pl.ds(column, width // 2)],
        )
    return leaving


def finish_own_kernel(
    me_ref, chosen_ref, returned_ref, early_ref, late_ref,
    table_ref, leaf_hbm, in_hbm, out_hbm, grads, sems,
):
    leaving = write_chunks(
        me_ref[0], 0, early_ref, late_ref, leaf_hbm, in_hbm, out_hbm, grads, sems
    )
    parts = table_ref.shape[1] // BLOCK
    part_of = lax.broadcasted_iota(jnp.int32, chosen_ref.shape, 0) & (parts - 1)
    for part in range(parts):
        mine = jnp.where(part_of == part, chosen_ref[...].astype(f32), 0.0).astype(bf16)
        table_ref[:, part * BLOCK : (part + 1) * BLOCK] = mm_tn(mine, returned_ref[...])
    for copy in leaving:
        copy.wait()


def finish_other_kernel(
    me_ref, early_ref, late_ref, leaf_in, in_in, out_in, leaf_hbm, in_hbm, out_hbm, grads, sems
):
    leaving = write_chunks(
        me_ref[0], 1, early_ref, late_ref, leaf_hbm, in_hbm, out_hbm, grads, sems
    )
    for copy in leaving:
        copy.wait()


def finish_scratch(early, late):
    return [
        pltpu.VMEM((early.shape[0], early.shape[1] + late.shape[1]), f32),
        pltpu.SemaphoreType.DMA((3 * early.shape[0] // ROWS,)),
    ]


def run_finish(me, chosen, returned, early_own, early_other, late_own, late_other, leaves):
    smem = pl.BlockSpec(memory_space=pltpu.SMEM)
    vmem = pl.BlockSpec(memory_space=pltpu.VMEM)
    hbm = pl.BlockSpec(memory_space=pltpu.HBM)
    width = early_own.shape[1] // 4
    shapes = tuple(
        jax.ShapeDtypeStruct(shape, f32)
        for shape in (
            (chosen.shape[1], width), (leaves, width), (width, 4 * width), (width, width)
        )
    )
    table, *written = pl.pallas_call(
        finish_own_kernel,
        name="finish_own",
        out_shape=shapes,
        in_specs=[smem] + [vmem] * 4,
        out_specs=(vmem, hbm, hbm, hbm),
        scratch_shapes=finish_scratch(early_own, late_own),
        compiler_params=pltpu.CompilerParams(vmem_limit_bytes=16 * 2**20),
        cost_estimate=pl.CostEstimate(flops=10**8, bytes_accessed=5 * 10**6, transcendentals=0),
    )(me, chosen, returned, early_own, late_own)
    written = pl.pallas_call(
        finish_other_kernel,
        name="finish_other",
        out_shape=shapes[1:],
        in_specs=[smem] + [vmem] * 2 + [hbm] * 3,
        out_specs=(hbm,) * 3,
        scratch_shapes=finish_scratch(early_own, late_own),
        input_output_aliases={3: 0, 4: 1, 5: 2},
        compiler_params=pltpu.CompilerParams(vmem_limit_bytes=16 * 2**20),
        cost_estimate=pl.CostEstimate(flops=0, bytes_accessed=5 * 10**6, transcendentals=0),
    )(me, early_other, late_other, *written)
    return (table, *written)


def load_kernel(*refs):
    for source, target in zip(refs[: len(refs) // 2], refs[len(refs) // 2 :]):
        target[...] = source[...]


def run_load(*arrays):
    vmem = pl.BlockSpec(memory_space=pltpu.VMEM)
    return pl.pallas_call(
        load_kernel,
        name="load",
        out_shape=tuple(jax.ShapeDtypeStruct(array.shape, array.dtype) for array in arrays),
        in_specs=[vmem] * len(arrays),
        out_specs=(vmem,) * len(arrays),
        compiler_params=pltpu.CompilerParams(vmem_limit_bytes=8 * 2**20),
        cost_estimate=pl.CostEstimate(flops=0, bytes_accessed=4 * 2**20, transcendentals=0),
    )(*arrays)


def merge_kernel(keep_ref, other_ref, *outs):
    rows = outs[0].shape[0]
    for part, out in enumerate(outs):
        at = slice(part * rows, (part + 1) * rows)
        out[...] = (keep_ref[at, :].astype(f32) + other_ref[at, :].astype(f32)).astype(bf16)


def run_merge(keep, other, parts):
    vmem = pl.BlockSpec(memory_space=pltpu.VMEM)
    part = jax.ShapeDtypeStruct((keep.shape[0] // parts, keep.shape[1]), bf16)
    return pl.pallas_call(
        merge_kernel,
        name="merge",
        out_shape=(part,) * parts,
        in_specs=[vmem] * 2,
        out_specs=(vmem,) * parts,
        compiler_params=pltpu.CompilerParams(vmem_limit_bytes=8 * 2**20),
    )(keep, other)


def exchange(blocks):
    return lax.all_to_all(blocks, ("dp", "rep"), split_axis=0, concat_axis=0, tiled=True)


def swap(block, mask, count):
    return lax.ppermute(block, ("dp", "rep"), [(i, i ^ mask) for i in range(count)])


def add(parts):
    return sum(part.astype(f32) for part in parts)


def shares(parts, group):
    size = 2 ** len(group)
    rows = parts[0].shape[0] // size
    return [
        add(part[digit * rows : (digit + 1) * rows] for part in parts).astype(bf16)
        for digit in range(1, size)
    ]


def swap_all(blocks, group, count):
    return [
        swap(block, mask_of(group, digit), count) for digit, block in enumerate(blocks, start=1)
    ]


def extend(parts, got):
    return [part[: got[0].shape[0]] for part in parts] + got


def split_up(parts, group, count):
    return extend(parts, swap_all(shares(parts, group), group, count))


def sum_with(block, group, count):
    return block.astype(f32) + swap(block, mask_of(group, 1), count).astype(f32)


def join(block, group, count):
    pieces = swap_all([block] * (2 ** len(group) - 1), group, count)
    return jnp.concatenate([block] + pieces, axis=0)


def reduce_and_gather(early, late, d_rows, count):
    _, near, far = EARLY
    _, first, second = LATE
    early_other, late_other = swap(early[1], 1, count), swap(late[1], 1, count)
    early_own, late_own = run_load(early[0], late[0])
    early, *early_blocks = run_merge(early_own, early_other, 2 ** len(near))
    late, *late_blocks = run_merge(late_own, late_other, 2 ** len(first))
    early_blocks, late_blocks = lax.optimization_barrier((early_blocks, late_blocks))
    early_got = swap_all(early_blocks, near, count)
    late = [late] + swap_all(late_blocks, first, count)
    late_got = swap_all(shares(late, second), second, count)
    early_got[0], late, d_rows = lax.optimization_barrier((early_got[0], late, d_rows))
    returned = exchange(d_rows)
    early_got, late = lax.optimization_barrier((early_got, extend(late, late_got)))
    early, late = split_up([early] + early_got, far, count), add(late).astype(bf16)
    late = sum_with(late, SHARED[0], count).astype(bf16)
    early, late = add(early), sum_with(late, SHARED[1], count)
    reach = CHUNKS
    while reach < count:
        early, late = early + swap(early, reach, count), late + swap(late, reach, count)
        reach *= 2
    early, returned = lax.optimization_barrier(((early * (1.0 / count)).astype(bf16), returned))
    early = join(early, far, count)
    early, late = lax.optimization_barrier((early, (late * (1.0 / count)).astype(bf16)))
    pieces = swap_all([early] * (2 ** len(near) - 1), near, count)
    late = join(join(late, second, count), first, count)
    pieces, late = lax.optimization_barrier((pieces, late))
    early = jnp.concatenate([early] + pieces, axis=0)
    return returned, early, swap(early, 1, count), late, swap(late, 1, count)


def on_device(
    item_table, requests, event_slot, lengths, leaf_ids, leaf_table, w_in, w_out, cotangent
):
    count = lax.axis_size("dp") * lax.axis_size("rep")
    place = lax.axis_index(("dp", "rep")).astype(jnp.int32)
    me = (place & (CHUNKS - 1)).reshape(1)
    slot = event_slot.reshape(1, -1)
    leaf = leaf_ids.T
    asked = exchange(requests[0])
    (table,) = run_load(item_table)
    fetched, chosen = run_lookup(asked, table)
    arrived = exchange(fetched)
    output, d_rows, keep, send, keep_late, send_late = run_layer(
        me, lengths, slot, leaf, arrived, leaf_table, w_in, w_out, cotangent
    )
    returned, early, early_other, late, late_other = reduce_and_gather(
        (keep, send), (keep_late, send_late), d_rows, count
    )
    table_grad, leaf_mean, in_mean, out_mean = run_finish(
        me, chosen, returned, early, early_other, late, late_other, leaf_table.shape[0]
    )
    return (output, table_grad, leaf_mean, in_mean, out_mean)


def solution(mesh):
    return jax.shard_map(
        on_device,
        mesh=mesh,
        in_specs=(
            P(("dp", "rep"), None),
            P(("dp", "rep"), None, None),
            P(("dp", "rep")),
            P(("dp", "rep"), None),
            P(("dp", "rep"), None),
            P(),
            P(),
            P(),
            P(("dp", "rep"), None),
        ),
        out_specs=(P(("dp", "rep"), None), P(("dp", "rep"), None), P(), P(), P()),
        check_vma=False,
    )
```

```python
import functools
import jax
import jax.numpy as jnp
from jax import lax
from jax.experimental import pallas as pl
from jax.experimental.pallas import tpu as pltpu
from jax.sharding import PartitionSpec as P

HEADS = 4
MAXLEN = 256
BLOCK = 128
SPAN = 256
ROWS = 16
epsilon = 1e-06
f32 = jnp.float32
bf16 = jnp.bfloat16

EARLY = ((0,), (1, 2), (3, 4))
LATE = ((0,), (3,), (4,))
SHARED = ((2,), (1,))
SPLIT = 2048
CHUNKS = 32
STRIP = 32
LAYER_VMEM = 56 * 2**20


def dot(a, b, contract):
    return lax.dot_general(a, b, ((contract[0], contract[1]), ((), ())), preferred_element_type=f32)


def mm(a, b):
    return dot(a, b, ((1,), (0,)))


def mm_nt(a, b):
    return dot(a, b, ((1,), (1,)))


def mm_tn(a, b):
    return dot(a, b, ((0,), (0,)))


def mask_of(group, digit):
    return sum(((digit >> k) & 1) << bit for k, bit in enumerate(group))


def chunk_order(me, route, shared=()):
    masks = [0]
    for group in route + shared:
        masks = [mask ^ mask_of(group, digit) for mask in masks for digit in range(2 ** len(group))]
    for group in shared:
        me = me & ~mask_of(group, 1)
    return [me ^ mask for mask in masks]


def spans(count):
    for start in range(0, count, SPAN):
        low = max(0, start - (MAXLEN - 1)) // BLOCK * BLOCK
        yield start, low, start + SPAN


def strips(start, stop):
    return [slice(at, at + STRIP) for at in range(start, stop, STRIP)]


def silu(half):
    curve = jnp.tanh(half)
    value = (half + half * curve).astype(bf16)
    half, curve = half.astype(bf16), curve.astype(bf16)
    return value, (0.5 + 0.5 * curve) * (1.0 + half * (1.0 - curve))


def center(values):
    values = values - jnp.mean(values, axis=-1, keepdims=True)
    return values, lax.rsqrt(jnp.mean(values * values, axis=-1, keepdims=True) + epsilon)


def pull_normalize(change, normed, scale):
    return scale * (
        change
        - jnp.mean(change, axis=-1, keepdims=True)
        - normed * jnp.mean(change * normed, axis=-1, keepdims=True)
    )


def pickers(slots, slot_ref, leaf_ref, leaves):
    count = slot_ref.shape[1]
    picker = lax.broadcasted_iota(jnp.int32, (slots, count), 0) == slot_ref[...]
    trees = leaf_ref.shape[0]
    each = leaves // trees
    spots = lax.broadcasted_iota(jnp.int32, (each, count), 0)
    onehot = [(spots == leaf_ref[t : t + 1, :]).astype(f32).astype(bf16) for t in range(trees)]
    return picker.astype(f32).astype(bf16), jnp.concatenate(onehot, axis=0)


def permute_rows(chunks, source, target):
    for place, chunk in enumerate(chunks):
        start = pl.multiple_of(chunk * ROWS, ROWS)
        target[place * ROWS : (place + 1) * ROWS, :] = source[pl.ds(start, ROWS), :]


def zero_one(condition):
    return jnp.where(condition, 1.0, 0.0).astype(bf16)


def to_tiles(rows):
    parts = rows.shape[1] // BLOCK
    shape = (rows.shape[0] * parts, rows.shape[0])
    row, column = (lax.broadcasted_iota(jnp.int32, shape, axis) for axis in (0, 1))
    total = jnp.zeros((shape[0], BLOCK), f32)
    for part in range(parts):
        place = zero_one(row == column * parts + part)
        total = total + mm(place, rows[:, part * BLOCK : (part + 1) * BLOCK])
    return total.astype(bf16)


def from_tiles(block, width):
    parts = width // BLOCK
    shape = (block.shape[0] // parts, block.shape[0])
    row, column = (lax.broadcasted_iota(jnp.int32, shape, axis) for axis in (0, 1))
    pieces = [mm(zero_one(column == row * parts + part), block) for part in range(parts)]
    return jnp.concatenate(pieces, axis=1).astype(bf16)


def lookup_kernel(asked_ref, table_ref, rows_ref, chosen_ref):
    count, each = asked_ref.shape
    owned, width = table_ref.shape
    parts = width // BLOCK
    many = count * each * parts
    spot = lax.broadcasted_iota(jnp.int32, (count, owned), 1)
    row = lax.broadcasted_iota(jnp.int32, (many, count), 0)
    device = lax.broadcasted_iota(jnp.int32, (many, count), 1)
    here, wanted = [], []
    for k in range(each):
        base = (device * each + k) * parts
        here.append(zero_one(jnp.logical_and(row >= base, row < base + parts)))
        wanted.append(zero_one(spot == asked_ref[:, k : k + 1]))
    chosen = mm(jnp.concatenate(here, axis=1), jnp.concatenate(wanted, axis=0))
    chosen_ref[...] = chosen.astype(bf16)
    part_of = lax.broadcasted_iota(jnp.int32, (many, owned), 0) & (parts - 1)
    mine = [jnp.where(part_of == part, chosen, 0.0).astype(bf16) for part in range(parts)]
    blocks = [table_ref[:, part * BLOCK : (part + 1) * BLOCK] for part in range(parts)]
    total = mm(jnp.concatenate(mine, axis=1), jnp.concatenate(blocks, axis=0))
    rows_ref[...] = total.astype(bf16)


def run_lookup(asked, table):
    vmem = pl.BlockSpec(memory_space=pltpu.VMEM)
    shape = jax.ShapeDtypeStruct
    many = asked.shape[0] * asked.shape[1] * table.shape[1] // BLOCK
    return pl.pallas_call(
        lookup_kernel,
        name="lookup",
        out_shape=(
            shape((many, BLOCK), bf16),
            shape((many, table.shape[0]), bf16),
        ),
        in_specs=[vmem, vmem],
        out_specs=(vmem,) * 2,
        compiler_params=pltpu.CompilerParams(vmem_limit_bytes=16 * 2**20),
    )(asked, table)


def layer_kernel(
    me_ref, lengths_ref, slot_ref, leaf_ref, rows_ref, table_hbm, in_hbm, out_hbm, tangent_hbm,
    output_hbm, d_rows_ref, keep_hbm, send_hbm, keep_late_hbm, send_late_hbm,
    inputs, gated, d_pre, grads, output,
    normed, turned, moved, turned_gated, moved_gated, hidden, slope, weights, weights_slope, mixed, d_mixed,
    d_score, d_gated, allowed, allowed_scale, keys_t, values_t, d_inputs, leaf_grad, table, w_in, w_out, tangent, sems, out_sems,
):
    count, width = inputs.shape
    head = width // HEADS
    half_scale = 0.5 * head ** (-0.5)
    half_rows = width // 2
    copies = [
        pltpu.make_async_copy(source, target, sems.at[k])
        for k, (source, target) in enumerate(
            ((table_hbm, table), (in_hbm, w_in), (out_hbm, w_out), (tangent_hbm, tangent))
        )
    ]
    for copy in copies:
        copy.start()
    leaving = []

    def leave(source, target):
        copy = pltpu.make_async_copy(source, target, out_sems.at[len(leaving)])
        copy.start()
        leaving.append(copy)

    rows = from_tiles(rows_ref[...], width)
    picker, onehot = pickers(rows.shape[0], slot_ref, leaf_ref, table.shape[0])
    ends = []
    total = 0
    for place in range(lengths_ref.shape[1]):
        total = total + lengths_ref[0, place]
        ends.append(total)
    for start, low, high in spans(count):
        at = slice(start, start + SPAN)
        row = start + lax.broadcasted_iota(jnp.int32, (SPAN, high - low), 0)
        column = low + lax.broadcasted_iota(jnp.int32, (SPAN, high - low), 1)
        first = jnp.zeros_like(row)
        for end in ends[:-1]:
            first = jnp.where(row >= end, end, first)
        seen = jnp.logical_and(column >= first, column <= row)
        allowed[at, low:high] = jnp.where(seen, 1.0, 0.0).astype(bf16)
        allowed_scale[at, low:high] = jnp.where(seen, 2.0 * half_scale, 0.0).astype(bf16)
    copies[0].wait()
    inputs[...] = (mm_tn(picker, rows) + mm_tn(onehot, table[...])).astype(bf16)
    for at in strips(0, count):
        values, scale = center(inputs[at, :].astype(f32))
        normed[at, :] = (values * scale).astype(bf16)
    turned[...] = normed[...].T
    copies[1].wait()
    for start in range(0, 4 * width, 2 * BLOCK):
        to = slice(start, start + 2 * BLOCK)
        halves = mm(normed[...], w_in[:, to]) * 0.5
        for at in strips(0, count):
            value, slope_at = silu(halves[at, :])
            hidden[at, to] = value
            slope[at, to] = slope_at
    keys_t[...] = hidden[:, 3 * width :].T
    values_t[...] = hidden[:, width : 2 * width].T
    for start, low, high in spans(count):
        at = slice(start, start + SPAN)
        end = start // (2 * BLOCK) * 2 * BLOCK + 2 * BLOCK
        for out in (slice(0, low), slice(high, end)):
            if out.start < out.stop:
                nothing = jnp.zeros((HEADS, SPAN, out.stop - out.start), bf16)
                weights[:, at, out] = nothing
                d_score[:, at, out] = nothing
    for h in range(HEADS):
        own = slice(h * head, (h + 1) * head)
        value_at = slice(width + h * head, width + (h + 1) * head)
        query_at = slice(2 * width + h * head, 2 * width + (h + 1) * head)
        key_at = slice(3 * width + h * head, 3 * width + (h + 1) * head)
        for start, low, high in spans(count):
            at = slice(start, start + SPAN)
            halves = mm(hidden[at, query_at], keys_t[own, low:high]) * half_scale
            for strip in strips(0, SPAN):
                to = slice(start + strip.start, start + strip.stop)
                value, slope_at = silu(halves[strip, :])
                weights[h, to, low:high] = value * allowed[to, low:high]
                weights_slope[h, to, low:high] = slope_at * allowed_scale[to, low:high]
        for start in range(0, count, 2 * BLOCK):
            at = slice(start, start + 2 * BLOCK)
            high = start + 2 * BLOCK
            mixed[at, h * head : (h + 1) * head] = mm(
                weights[h, at, :high], hidden[:high, value_at]
            )
    copies[2].wait()
    copies[3].wait()
    d_gated[...] = mm_nt(tangent[...], w_out[...]).astype(bf16)
    for at in strips(0, count):
        values, scale = center(mixed[at, :])
        values = values * scale
        gates = hidden[at, :width].astype(f32)
        change = d_gated[at, :].astype(f32)
        gated[at, :] = (values * gates).astype(bf16)
        d_pre[at, :width] = (change * values).astype(bf16) * slope[at, :width]
        d_mixed[at, :] = pull_normalize(change * gates, values, scale).astype(bf16)
    for h in range(HEADS):
        own = slice(h * head, (h + 1) * head)
        value_at = slice(width + h * head, width + (h + 1) * head)
        query_at = slice(2 * width + h * head, 2 * width + (h + 1) * head)
        key_at = slice(3 * width + h * head, 3 * width + (h + 1) * head)
        for start, low, high in spans(count):
            at = slice(start, start + SPAN)
            d_weights = mm(d_mixed[at, own], values_t[own, low:high]).astype(bf16)
            d_score[h, at, low:high] = d_weights * weights_slope[h, at, low:high]
        for start in range(0, count, 2 * BLOCK):
            at = slice(start, start + 2 * BLOCK)
            high = start + 2 * BLOCK
            d_query = mm(d_score[h, at, :high], hidden[:high, key_at])
            d_pre[at, query_at] = d_query.astype(bf16) * slope[at, query_at]
            d_key = mm_tn(d_score[h, start:, at], hidden[start:, query_at])
            d_pre[at, key_at] = d_key.astype(bf16) * slope[at, key_at]
            d_value = mm_tn(weights[h, start:, at], d_mixed[start:, own])
            d_pre[at, value_at] = d_value.astype(bf16) * slope[at, value_at]
    me = me_ref[0]
    early, late = chunk_order(me, EARLY), chunk_order(me, LATE, SHARED)
    permute_rows(early, turned, moved)
    for start in range(0, 4 * width, 2 * BLOCK):
        to = slice(start, start + 2 * BLOCK)
        grads[:, to] = mm(moved[...], d_pre[:, to]).astype(bf16)
    leave(grads.at[half_rows:, :SPLIT], send_hbm)
    leave(grads.at[:half_rows, :SPLIT], keep_hbm)
    turned_gated[...] = gated[...].T
    permute_rows(late, turned_gated, moved_gated)
    grads[:, 4 * width : 5 * width] = mm(moved_gated[...], tangent[...]).astype(bf16)
    output[...] = (mm(gated[...], w_out[...]) + inputs[...].astype(f32)).astype(bf16)
    leave(output, output_hbm)
    normed_change = mm_nt(d_pre[...], w_in[...])
    for at in strips(0, count):
        values, scale = center(inputs[at, :].astype(f32))
        change = pull_normalize(normed_change[at, :], values * scale, scale)
        d_inputs[at, :] = (change + tangent[at, :].astype(f32)).astype(bf16)
    leaves = table.shape[0]
    d_leaf = mm(onehot, d_inputs[...]).astype(bf16)
    leaf_grad[:leaves, :] = d_leaf[:, : width // 2]
    leaf_grad[leaves:, :] = d_leaf[:, width // 2 :]
    permute_rows(late, leaf_grad, grads.at[:, 5 * width :])
    leave(grads.at[half_rows:, SPLIT:], send_late_hbm)
    leave(grads.at[:half_rows, SPLIT:], keep_late_hbm)
    d_rows_ref[...] = to_tiles(mm(picker, d_inputs[...]).astype(bf16))
    for copy in leaving:
        copy.wait()


def run_layer(me, lengths, slot, leaf, rows, table, w_in, w_out, tangent):
    count, width = tangent.shape
    smem = pl.BlockSpec(memory_space=pltpu.SMEM)
    vmem = pl.BlockSpec(memory_space=pltpu.VMEM)
    hbm = pl.BlockSpec(memory_space=pltpu.HBM)
    shape = jax.ShapeDtypeStruct
    columns = 5 * width + width // 2
    return pl.pallas_call(
        layer_kernel,
        name="layer",
        out_shape=(
            shape((count, width), bf16),
            shape(rows.shape, bf16),
            shape((width // 2, SPLIT), bf16),
            shape((width // 2, SPLIT), bf16),
            shape((width // 2, columns - SPLIT), bf16),
            shape((width // 2, columns - SPLIT), bf16),
        ),
        in_specs=[smem, smem] + [vmem] * 3 + [hbm] * 4,
        out_specs=(hbm, vmem, hbm, hbm, hbm, hbm),
        scratch_shapes=[
            pltpu.VMEM((count, width), bf16),
            pltpu.VMEM((count, width), bf16),
            pltpu.VMEM((count, 4 * width), bf16),
            pltpu.VMEM((width, columns), bf16),
            pltpu.VMEM((count, width), bf16),
            pltpu.VMEM((count, width), bf16),
            pltpu.VMEM((width, count), bf16),
            pltpu.VMEM((width, count), bf16),
            pltpu.VMEM((width, count), bf16),
            pltpu.VMEM((width, count), bf16),
            pltpu.VMEM((count, 4 * width), bf16),
            pltpu.VMEM((count, 4 * width), bf16),
            pltpu.VMEM((HEADS, count, count), bf16),
            pltpu.VMEM((HEADS, count, count), bf16),
            pltpu.VMEM((count, width), f32),
            pltpu.VMEM((count, width), bf16),
            pltpu.VMEM((HEADS, count, count), bf16),
            pltpu.VMEM((count, width), bf16),
            pltpu.VMEM((count, count), bf16),
            pltpu.VMEM((count, count), bf16),
            pltpu.VMEM((width, count), bf16),
            pltpu.VMEM((width, count), bf16),
            pltpu.VMEM((count, width), bf16),
            pltpu.VMEM((width, width // 2), bf16),
            pltpu.VMEM(table.shape, bf16),
            pltpu.VMEM(w_in.shape, bf16),
            pltpu.VMEM(w_out.shape, bf16),
            pltpu.VMEM(tangent.shape, bf16),
            pltpu.SemaphoreType.DMA((4,)),
            pltpu.SemaphoreType.DMA((5,)),
        ],
        compiler_params=pltpu.CompilerParams(vmem_limit_bytes=LAYER_VMEM),
        cost_estimate=pl.CostEstimate(flops=6 * 10**9, bytes_accessed=10**7, transcendentals=10**6),
    )(me, lengths, slot, leaf, rows, table, w_in, w_out, tangent)


def write_chunks(me, half, early_ref, late_ref, leaf_hbm, in_hbm, out_hbm, grads, sems):
    width = in_hbm.shape[0]
    leaves = leaf_hbm.shape[0]
    places = early_ref.shape[0] // ROWS
    early, late = chunk_order(me, EARLY), chunk_order(me, LATE, SHARED)
    leaving = []

    def leave(source, target):
        copy = pltpu.make_async_copy(source, target, sems.at[len(leaving)])
        copy.start()
        leaving.append(copy)

    for place in range(places):
        at = slice(place * ROWS, (place + 1) * ROWS)
        grads[at, :SPLIT] = early_ref[at, :].astype(f32)
        start = pl.multiple_of(early[half * places + place] * ROWS, ROWS)
        leave(grads.at[at, :SPLIT], in_hbm.at[pl.ds(start, ROWS), :])
        grads[at, SPLIT:] = late_ref[at, :].astype(f32)
        start = pl.multiple_of(late[half * places + place] * ROWS, ROWS)
        leave(grads.at[at, SPLIT : SPLIT + width], out_hbm.at[pl.ds(start, ROWS), :])
        side = (start >= leaves).astype(jnp.int32)
        start = pl.multiple_of(start - side * leaves, ROWS)
        column = pl.multiple_of(side * (width // 2), width // 2)
        leave(
            grads.at[at, SPLIT + width :],
            leaf_hbm.at[pl.ds(start, ROWS), pl.ds(column, width // 2)],
        )
    return leaving


def finish_own_kernel(
    me_ref, chosen_ref, returned_ref, early_ref, late_ref,
    table_ref, leaf_hbm, in_hbm, out_hbm, grads, sems,
):
    leaving = write_chunks(
        me_ref[0], 0, early_ref, late_ref, leaf_hbm, in_hbm, out_hbm, grads, sems
    )
    parts = table_ref.shape[1] // BLOCK
    part_of = lax.broadcasted_iota(jnp.int32, chosen_ref.shape, 0) & (parts - 1)
    for part in range(parts):
        mine = jnp.where(part_of == part, chosen_ref[...].astype(f32), 0.0).astype(bf16)
        table_ref[:, part * BLOCK : (part + 1) * BLOCK] = mm_tn(mine, returned_ref[...])
    for copy in leaving:
        copy.wait()


def finish_other_kernel(
    me_ref, early_ref, late_ref, leaf_in, in_in, out_in, leaf_hbm, in_hbm, out_hbm, grads, sems
):
    leaving = write_chunks(
        me_ref[0], 1, early_ref, late_ref, leaf_hbm, in_hbm, out_hbm, grads, sems
    )
    for copy in leaving:
        copy.wait()


def finish_scratch(early, late):
    return [
        pltpu.VMEM((early.shape[0], early.shape[1] + late.shape[1]), f32),
        pltpu.SemaphoreType.DMA((3 * early.shape[0] // ROWS,)),
    ]


def run_finish(me, chosen, returned, early_own, early_other, late_own, late_other, leaves):
    smem = pl.BlockSpec(memory_space=pltpu.SMEM)
    vmem = pl.BlockSpec(memory_space=pltpu.VMEM)
    hbm = pl.BlockSpec(memory_space=pltpu.HBM)
    width = early_own.shape[1] // 4
    shapes = tuple(
        jax.ShapeDtypeStruct(shape, f32)
        for shape in (
            (chosen.shape[1], width), (leaves, width), (width, 4 * width), (width, width)
        )
    )
    table, *written = pl.pallas_call(
        finish_own_kernel,
        name="finish_own",
        out_shape=shapes,
        in_specs=[smem] + [vmem] * 4,
        out_specs=(vmem, hbm, hbm, hbm),
        scratch_shapes=finish_scratch(early_own, late_own),
        compiler_params=pltpu.CompilerParams(vmem_limit_bytes=16 * 2**20),
        cost_estimate=pl.CostEstimate(flops=10**8, bytes_accessed=5 * 10**6, transcendentals=0),
    )(me, chosen, returned, early_own, late_own)
    written = pl.pallas_call(
        finish_other_kernel,
        name="finish_other",
        out_shape=shapes[1:],
        in_specs=[smem] + [vmem] * 2 + [hbm] * 3,
        out_specs=(hbm,) * 3,
        scratch_shapes=finish_scratch(early_own, late_own),
        input_output_aliases={3: 0, 4: 1, 5: 2},
        compiler_params=pltpu.CompilerParams(vmem_limit_bytes=16 * 2**20),
        cost_estimate=pl.CostEstimate(flops=0, bytes_accessed=5 * 10**6, transcendentals=0),
    )(me, early_other, late_other, *written)
    return (table, *written)


def load_kernel(*refs):
    for source, target in zip(refs[: len(refs) // 2], refs[len(refs) // 2 :]):
        target[...] = source[...]


def run_load(*arrays):
    vmem = pl.BlockSpec(memory_space=pltpu.VMEM)
    return pl.pallas_call(
        load_kernel,
        name="load",
        out_shape=tuple(jax.ShapeDtypeStruct(array.shape, array.dtype) for array in arrays),
        in_specs=[vmem] * len(arrays),
        out_specs=(vmem,) * len(arrays),
        compiler_params=pltpu.CompilerParams(vmem_limit_bytes=8 * 2**20),
        cost_estimate=pl.CostEstimate(flops=0, bytes_accessed=4 * 2**20, transcendentals=0),
    )(*arrays)


def merge_kernel(keep_ref, other_ref, *outs):
    rows = outs[0].shape[0]
    for part, out in enumerate(outs):
        at = slice(part * rows, (part + 1) * rows)
        out[...] = (keep_ref[at, :].astype(f32) + other_ref[at, :].astype(f32)).astype(bf16)


def run_merge(keep, other, parts):
    vmem = pl.BlockSpec(memory_space=pltpu.VMEM)
    part = jax.ShapeDtypeStruct((keep.shape[0] // parts, keep.shape[1]), bf16)
    return pl.pallas_call(
        merge_kernel,
        name="merge",
        out_shape=(part,) * parts,
        in_specs=[vmem] * 2,
        out_specs=(vmem,) * parts,
        compiler_params=pltpu.CompilerParams(vmem_limit_bytes=8 * 2**20),
    )(keep, other)


def exchange(blocks):
    return lax.all_to_all(blocks, ("dp", "rep"), split_axis=0, concat_axis=0, tiled=True)


def swap(block, mask, count):
    return lax.ppermute(block, ("dp", "rep"), [(i, i ^ mask) for i in range(count)])


def add(parts):
    return sum(part.astype(f32) for part in parts)


def shares(parts, group):
    size = 2 ** len(group)
    rows = parts[0].shape[0] // size
    return [
        add(part[digit * rows : (digit + 1) * rows] for part in parts).astype(bf16)
        for digit in range(1, size)
    ]


def swap_all(blocks, group, count):
    return [
        swap(block, mask_of(group, digit), count) for digit, block in enumerate(blocks, start=1)
    ]


def extend(parts, got):
    return [part[: got[0].shape[0]] for part in parts] + got


def split_up(parts, group, count):
    return extend(parts, swap_all(shares(parts, group), group, count))


def sum_with(block, group, count):
    return block.astype(f32) + swap(block, mask_of(group, 1), count).astype(f32)


def join(block, group, count):
    pieces = swap_all([block] * (2 ** len(group) - 1), group, count)
    return jnp.concatenate([block] + pieces, axis=0)


def reduce_and_gather(early, late, d_rows, count):
    _, near, far = EARLY
    _, first, second = LATE
    early_other, late_other = swap(early[1], 1, count), swap(late[1], 1, count)
    early_own, late_own = run_load(early[0], late[0])
    early, *early_blocks = run_merge(early_own, early_other, 2 ** len(near))
    late, *late_blocks = run_merge(late_own, late_other, 2 ** len(first))
    early_blocks, late_blocks = lax.optimization_barrier((early_blocks, late_blocks))
    early_got = swap_all(early_blocks, near, count)
    late = [late] + swap_all(late_blocks, first, count)
    late_got = swap_all(shares(late, second), second, count)
    early_got[0], late, d_rows = lax.optimization_barrier((early_got[0], late, d_rows))
    returned = exchange(d_rows)
    early_got, late = lax.optimization_barrier((early_got, extend(late, late_got)))
    early, late = split_up([early] + early_got, far, count), add(late).astype(bf16)
    late = sum_with(late, SHARED[0], count).astype(bf16)
    early, late = add(early), sum_with(late, SHARED[1], count)
    reach = CHUNKS
    while reach < count:
        early, late = early + swap(early, reach, count), late + swap(late, reach, count)
        reach *= 2
    early, returned = lax.optimization_barrier(((early * (1.0 / count)).astype(bf16), returned))
    early = join(early, far, count)
    early, late = lax.optimization_barrier((early, (late * (1.0 / count)).astype(bf16)))
    pieces = swap_all([early] * (2 ** len(near) - 1), near, count)
    late = join(join(late, second, count), first, count)
    pieces, late = lax.optimization_barrier((pieces, late))
    early = jnp.concatenate([early] + pieces, axis=0)
    return returned, early, swap(early, 1, count), late, swap(late, 1, count)


def on_device(
    item_table, requests, event_slot, lengths, leaf_ids, leaf_table, w_in, w_out, cotangent
):
    count = lax.axis_size("dp") * lax.axis_size("rep")
    place = lax.axis_index(("dp", "rep")).astype(jnp.int32)
    me = (place & (CHUNKS - 1)).reshape(1)
    slot = event_slot.reshape(1, -1)
    leaf = leaf_ids.T
    asked = exchange(requests[0])
    (table,) = run_load(item_table)
    fetched, chosen = run_lookup(asked, table)
    arrived = exchange(fetched)
    output, d_rows, keep, send, keep_late, send_late = run_layer(
        me, lengths, slot, leaf, arrived, leaf_table, w_in, w_out, cotangent
    )
    returned, early, early_other, late, late_other = reduce_and_gather(
        (keep, send), (keep_late, send_late), d_rows, count
    )
    table_grad, leaf_mean, in_mean, out_mean = run_finish(
        me, chosen, returned, early, early_other, late, late_other, leaf_table.shape[0]
    )
    return (output, table_grad, leaf_mean, in_mean, out_mean)


def solution(mesh):
    return jax.shard_map(
        on_device,
        mesh=mesh,
        in_specs=(
            P(("dp", "rep"), None),
            P(("dp", "rep"), None, None),
            P(("dp", "rep")),
            P(("dp", "rep"), None),
            P(("dp", "rep"), None),
            P(),
            P(),
            P(),
            P(("dp", "rep"), None),
        ),
        out_specs=(P(("dp", "rep"), None), P(("dp", "rep"), None), P(), P(), P()),
        check_vma=False,
    )
```

```python
import functools
import jax
import jax.numpy as jnp
from jax import lax
from jax.experimental import pallas as pl
from jax.experimental.pallas import tpu as pltpu
from jax.sharding import PartitionSpec as P

HEADS = 4
MAXLEN = 256
BLOCK = 128
ROWS = 16
epsilon = 1e-06
f32 = jnp.float32
bf16 = jnp.bfloat16

EARLY = ((0,), (1, 2), (3, 4))
LATE = ((0,), (3,), (4,))
SHARED = ((2,), (1,))
SPLIT = 2048
CHUNKS = 32
STRIP = 32
LAYER_VMEM = 56 * 2**20


def dot(a, b, contract):
    return lax.dot_general(a, b, ((contract[0], contract[1]), ((), ())), preferred_element_type=f32)


def mm(a, b):
    return dot(a, b, ((1,), (0,)))


def mm_nt(a, b):
    return dot(a, b, ((1,), (1,)))


def mm_tn(a, b):
    return dot(a, b, ((0,), (0,)))


def mask_of(group, digit):
    return sum(((digit >> k) & 1) << bit for k, bit in enumerate(group))


def chunk_order(me, route, shared=()):
    masks = [0]
    for group in route + shared:
        masks = [mask ^ mask_of(group, digit) for mask in masks for digit in range(2 ** len(group))]
    for group in shared:
        me = me & ~mask_of(group, 1)
    return [me ^ mask for mask in masks]


def spans(count):
    for start in range(0, count, BLOCK):
        low = max(0, start - (MAXLEN - 1)) // BLOCK * BLOCK
        yield start, low, start + BLOCK


def strips(start, stop):
    return [slice(at, at + STRIP) for at in range(start, stop, STRIP)]


def silu(half):
    curve = jnp.tanh(half)
    value = (half + half * curve).astype(bf16)
    half, curve = half.astype(bf16), curve.astype(bf16)
    return value, (0.5 + 0.5 * curve) * (1.0 + half * (1.0 - curve))


def center(values):
    values = values - jnp.mean(values, axis=-1, keepdims=True)
    return values, lax.rsqrt(jnp.mean(values * values, axis=-1, keepdims=True) + epsilon)


def pull_normalize(change, normed, scale):
    return scale * (
        change
        - jnp.mean(change, axis=-1, keepdims=True)
        - normed * jnp.mean(change * normed, axis=-1, keepdims=True)
    )


def pickers(slots, slot_ref, leaf_ref, leaves):
    count = slot_ref.shape[1]
    picker = lax.broadcasted_iota(jnp.int32, (slots, count), 0) == slot_ref[...]
    trees = leaf_ref.shape[0]
    each = leaves // trees
    spots = lax.broadcasted_iota(jnp.int32, (each, count), 0)
    onehot = [(spots == leaf_ref[t : t + 1, :]).astype(f32).astype(bf16) for t in range(trees)]
    return picker.astype(f32).astype(bf16), jnp.concatenate(onehot, axis=0)


def permute_rows(chunks, source, target):
    for place, chunk in enumerate(chunks):
        start = pl.multiple_of(chunk * ROWS, ROWS)
        target[place * ROWS : (place + 1) * ROWS, :] = source[pl.ds(start, ROWS), :]


def zero_one(condition):
    return jnp.where(condition, 1.0, 0.0).astype(bf16)


def to_tiles(rows):
    parts = rows.shape[1] // BLOCK
    shape = (rows.shape[0] * parts, rows.shape[0])
    row, column = (lax.broadcasted_iota(jnp.int32, shape, axis) for axis in (0, 1))
    total = jnp.zeros((shape[0], BLOCK), f32)
    for part in range(parts):
        place = zero_one(row == column * parts + part)
        total = total + mm(place, rows[:, part * BLOCK : (part + 1) * BLOCK])
    return total.astype(bf16)


def from_tiles(block, width):
    parts = width // BLOCK
    shape = (block.shape[0] // parts, block.shape[0])
    row, column = (lax.broadcasted_iota(jnp.int32, shape, axis) for axis in (0, 1))
    pieces = [mm(zero_one(column == row * parts + part), block) for part in range(parts)]
    return jnp.concatenate(pieces, axis=1).astype(bf16)


def lookup_kernel(asked_ref, table_ref, rows_ref, chosen_ref, spread):
    count, each = asked_ref.shape
    owned, width = table_ref.shape
    parts = width // BLOCK
    many = count * each * parts
    spot = lax.broadcasted_iota(jnp.int32, (count, owned), 1)
    row = lax.broadcasted_iota(jnp.int32, (many, count), 0)
    device = lax.broadcasted_iota(jnp.int32, (many, count), 1)
    here, wanted = [], []
    for k in range(each):
        base = (device * each + k) * parts
        here.append(zero_one(jnp.logical_and(row >= base, row < base + parts)))
        wanted.append(zero_one(spot == asked_ref[:, k : k + 1]))
    chosen = mm(jnp.concatenate(here, axis=1), jnp.concatenate(wanted, axis=0))
    chosen_ref[...] = chosen.astype(bf16)
    for k in range(each):
        rows = mm(wanted[k], table_ref[...])
        for part in range(parts):
            spread[pl.ds(k * parts + part, count, stride=each * parts), :] = rows[
                :, part * BLOCK : (part + 1) * BLOCK
            ]
    rows_ref[...] = spread[...].astype(bf16)


def run_lookup(asked, table):
    vmem = pl.BlockSpec(memory_space=pltpu.VMEM)
    shape = jax.ShapeDtypeStruct
    many = asked.shape[0] * asked.shape[1] * table.shape[1] // BLOCK
    return pl.pallas_call(
        lookup_kernel,
        name="lookup",
        out_shape=(
            shape((many, BLOCK), bf16),
            shape((many, table.shape[0]), bf16),
        ),
        in_specs=[vmem, vmem],
        out_specs=(vmem,) * 2,
        scratch_shapes=[pltpu.VMEM((many, BLOCK), f32)],
        compiler_params=pltpu.CompilerParams(vmem_limit_bytes=16 * 2**20),
    )(asked, table)


def layer_kernel(
    me_ref, lengths_ref, slot_ref, leaf_ref, rows_ref, table_hbm, in_hbm, out_hbm, tangent_hbm,
    output_hbm, d_rows_ref, keep_hbm, send_hbm, keep_late_hbm, send_late_hbm,
    inputs, gated, d_pre, grads, output,
    normed, turned, moved, turned_gated, moved_gated, hidden, slope, weights, weights_slope, mixed, d_mixed,
    d_score, d_gated, allowed, allowed_scale, keys_t, values_t, d_inputs, leaf_grad, table, w_in, w_out, tangent, sems, out_sems,
):
    count, width = inputs.shape
    head = width // HEADS
    half_scale = 0.5 * head ** (-0.5)
    half_rows = width // 2
    copies = [
        pltpu.make_async_copy(source, target, sems.at[k])
        for k, (source, target) in enumerate(
            ((table_hbm, table), (in_hbm, w_in), (out_hbm, w_out), (tangent_hbm, tangent))
        )
    ]
    for copy in copies:
        copy.start()
    leaving = []

    def leave(source, target):
        copy = pltpu.make_async_copy(source, target, out_sems.at[len(leaving)])
        copy.start()
        leaving.append(copy)

    rows = from_tiles(rows_ref[...], width)
    picker, onehot = pickers(rows.shape[0], slot_ref, leaf_ref, table.shape[0])
    ends = []
    total = 0
    for place in range(lengths_ref.shape[1]):
        total = total + lengths_ref[0, place]
        ends.append(total)
    for start, low, high in spans(count):
        at = slice(start, start + BLOCK)
        row = start + lax.broadcasted_iota(jnp.int32, (BLOCK, high - low), 0)
        column = low + lax.broadcasted_iota(jnp.int32, (BLOCK, high - low), 1)
        first = jnp.zeros_like(row)
        for end in ends[:-1]:
            first = jnp.where(row >= end, end, first)
        seen = jnp.logical_and(column >= first, column <= row)
        allowed[at, low:high] = jnp.where(seen, 1.0, 0.0).astype(bf16)
        allowed_scale[at, low:high] = jnp.where(seen, 2.0 * half_scale, 0.0).astype(bf16)
    copies[0].wait()
    inputs[...] = (mm_tn(picker, rows) + mm_tn(onehot, table[...])).astype(bf16)
    for at in strips(0, count):
        values, scale = center(inputs[at, :].astype(f32))
        normed[at, :] = (values * scale).astype(bf16)
    turned[...] = normed[...].T
    copies[1].wait()
    for start in range(0, 4 * width, 2 * BLOCK):
        to = slice(start, start + 2 * BLOCK)
        halves = mm(normed[...], w_in[:, to]) * 0.5
        for at in strips(0, count):
            value, slope_at = silu(halves[at, :])
            hidden[at, to] = value
            slope[at, to] = slope_at
    keys_t[...] = hidden[:, 3 * width :].T
    values_t[...] = hidden[:, width : 2 * width].T
    for start, low, high in spans(count):
        at = slice(start, start + BLOCK)
        end = start // (2 * BLOCK) * 2 * BLOCK + 2 * BLOCK
        for out in (slice(0, low), slice(high, end)):
            if out.start < out.stop:
                nothing = jnp.zeros((HEADS, BLOCK, out.stop - out.start), bf16)
                weights[:, at, out] = nothing
                d_score[:, at, out] = nothing
    for h in range(HEADS):
        own = slice(h * head, (h + 1) * head)
        value_at = slice(width + h * head, width + (h + 1) * head)
        query_at = slice(2 * width + h * head, 2 * width + (h + 1) * head)
        key_at = slice(3 * width + h * head, 3 * width + (h + 1) * head)
        for start, low, high in spans(count):
            at = slice(start, start + BLOCK)
            halves = mm(hidden[at, query_at], keys_t[own, low:high]) * half_scale
            for strip in strips(0, BLOCK):
                to = slice(start + strip.start, start + strip.stop)
                value, slope_at = silu(halves[strip, :])
                weights[h, to, low:high] = value * allowed[to, low:high]
                weights_slope[h, to, low:high] = slope_at * allowed_scale[to, low:high]
        for start in range(0, count, 2 * BLOCK):
            at = slice(start, start + 2 * BLOCK)
            high = start + 2 * BLOCK
            mixed[at, h * head : (h + 1) * head] = mm(
                weights[h, at, :high], hidden[:high, value_at]
            )
    copies[2].wait()
    copies[3].wait()
    d_gated[...] = mm_nt(tangent[...], w_out[...]).astype(bf16)
    for at in strips(0, count):
        values, scale = center(mixed[at, :])
        values = values * scale
        gates = hidden[at, :width].astype(f32)
        change = d_gated[at, :].astype(f32)
        gated[at, :] = (values * gates).astype(bf16)
        d_pre[at, :width] = (change * values).astype(bf16) * slope[at, :width]
        d_mixed[at, :] = pull_normalize(change * gates, values, scale).astype(bf16)
    for h in range(HEADS):
        own = slice(h * head, (h + 1) * head)
        value_at = slice(width + h * head, width + (h + 1) * head)
        query_at = slice(2 * width + h * head, 2 * width + (h + 1) * head)
        key_at = slice(3 * width + h * head, 3 * width + (h + 1) * head)
        for start, low, high in spans(count):
            at = slice(start, start + BLOCK)
            d_weights = mm(d_mixed[at, own], values_t[own, low:high]).astype(bf16)
            d_score[h, at, low:high] = d_weights * weights_slope[h, at, low:high]
        for start in range(0, count, 2 * BLOCK):
            at = slice(start, start + 2 * BLOCK)
            high = start + 2 * BLOCK
            d_query = mm(d_score[h, at, :high], hidden[:high, key_at])
            d_pre[at, query_at] = d_query.astype(bf16) * slope[at, query_at]
            d_key = mm_tn(d_score[h, start:, at], hidden[start:, query_at])
            d_pre[at, key_at] = d_key.astype(bf16) * slope[at, key_at]
            d_value = mm_tn(weights[h, start:, at], d_mixed[start:, own])
            d_pre[at, value_at] = d_value.astype(bf16) * slope[at, value_at]
    me = me_ref[0]
    early, late = chunk_order(me, EARLY), chunk_order(me, LATE, SHARED)
    permute_rows(early, turned, moved)
    for start in range(0, 4 * width, 2 * BLOCK):
        to = slice(start, start + 2 * BLOCK)
        grads[:, to] = mm(moved[...], d_pre[:, to]).astype(bf16)
    leave(grads.at[half_rows:, :SPLIT], send_hbm)
    leave(grads.at[:half_rows, :SPLIT], keep_hbm)
    turned_gated[...] = gated[...].T
    permute_rows(late, turned_gated, moved_gated)
    grads[:, 4 * width : 5 * width] = mm(moved_gated[...], tangent[...]).astype(bf16)
    output[...] = (mm(gated[...], w_out[...]) + inputs[...].astype(f32)).astype(bf16)
    leave(output, output_hbm)
    normed_change = mm_nt(d_pre[...], w_in[...])
    for at in strips(0, count):
        values, scale = center(inputs[at, :].astype(f32))
        change = pull_normalize(normed_change[at, :], values * scale, scale)
        d_inputs[at, :] = (change + tangent[at, :].astype(f32)).astype(bf16)
    leaves = table.shape[0]
    d_leaf = mm(onehot, d_inputs[...]).astype(bf16)
    leaf_grad[:leaves, :] = d_leaf[:, : width // 2]
    leaf_grad[leaves:, :] = d_leaf[:, width // 2 :]
    permute_rows(late, leaf_grad, grads.at[:, 5 * width :])
    leave(grads.at[half_rows:, SPLIT:], send_late_hbm)
    leave(grads.at[:half_rows, SPLIT:], keep_late_hbm)
    d_rows_ref[...] = to_tiles(mm(picker, d_inputs[...]).astype(bf16))
    for copy in leaving:
        copy.wait()


def run_layer(me, lengths, slot, leaf, rows, table, w_in, w_out, tangent):
    count, width = tangent.shape
    smem = pl.BlockSpec(memory_space=pltpu.SMEM)
    vmem = pl.BlockSpec(memory_space=pltpu.VMEM)
    hbm = pl.BlockSpec(memory_space=pltpu.HBM)
    shape = jax.ShapeDtypeStruct
    columns = 5 * width + width // 2
    return pl.pallas_call(
        layer_kernel,
        name="layer",
        out_shape=(
            shape((count, width), bf16),
            shape(rows.shape, bf16),
            shape((width // 2, SPLIT), bf16),
            shape((width // 2, SPLIT), bf16),
            shape((width // 2, columns - SPLIT), bf16),
            shape((width // 2, columns - SPLIT), bf16),
        ),
        in_specs=[smem, smem] + [vmem] * 3 + [hbm] * 4,
        out_specs=(hbm, vmem, hbm, hbm, hbm, hbm),
        scratch_shapes=[
            pltpu.VMEM((count, width), bf16),
            pltpu.VMEM((count, width), bf16),
            pltpu.VMEM((count, 4 * width), bf16),
            pltpu.VMEM((width, columns), bf16),
            pltpu.VMEM((count, width), bf16),
            pltpu.VMEM((count, width), bf16),
            pltpu.VMEM((width, count), bf16),
            pltpu.VMEM((width, count), bf16),
            pltpu.VMEM((width, count), bf16),
            pltpu.VMEM((width, count), bf16),
            pltpu.VMEM((count, 4 * width), bf16),
            pltpu.VMEM((count, 4 * width), bf16),
            pltpu.VMEM((HEADS, count, count), bf16),
            pltpu.VMEM((HEADS, count, count), bf16),
            pltpu.VMEM((count, width), f32),
            pltpu.VMEM((count, width), bf16),
            pltpu.VMEM((HEADS, count, count), bf16),
            pltpu.VMEM((count, width), bf16),
            pltpu.VMEM((count, count), bf16),
            pltpu.VMEM((count, count), bf16),
            pltpu.VMEM((width, count), bf16),
            pltpu.VMEM((width, count), bf16),
            pltpu.VMEM((count, width), bf16),
            pltpu.VMEM((width, width // 2), bf16),
            pltpu.VMEM(table.shape, bf16),
            pltpu.VMEM(w_in.shape, bf16),
            pltpu.VMEM(w_out.shape, bf16),
            pltpu.VMEM(tangent.shape, bf16),
            pltpu.SemaphoreType.DMA((4,)),
            pltpu.SemaphoreType.DMA((5,)),
        ],
        compiler_params=pltpu.CompilerParams(vmem_limit_bytes=LAYER_VMEM),
        cost_estimate=pl.CostEstimate(flops=6 * 10**9, bytes_accessed=10**7, transcendentals=10**6),
    )(me, lengths, slot, leaf, rows, table, w_in, w_out, tangent)


def write_chunks(me, half, early_ref, late_ref, leaf_hbm, in_hbm, out_hbm, grads, sems):
    width = in_hbm.shape[0]
    leaves = leaf_hbm.shape[0]
    places = early_ref.shape[0] // ROWS
    early, late = chunk_order(me, EARLY), chunk_order(me, LATE, SHARED)
    leaving = []

    def leave(source, target):
        copy = pltpu.make_async_copy(source, target, sems.at[len(leaving)])
        copy.start()
        leaving.append(copy)

    for place in range(places):
        at = slice(place * ROWS, (place + 1) * ROWS)
        grads[at, :SPLIT] = early_ref[at, :].astype(f32)
        start = pl.multiple_of(early[half * places + place] * ROWS, ROWS)
        leave(grads.at[at, :SPLIT], in_hbm.at[pl.ds(start, ROWS), :])
        grads[at, SPLIT:] = late_ref[at, :].astype(f32)
        start = pl.multiple_of(late[half * places + place] * ROWS, ROWS)
        leave(grads.at[at, SPLIT : SPLIT + width], out_hbm.at[pl.ds(start, ROWS), :])
        side = (start >= leaves).astype(jnp.int32)
        start = pl.multiple_of(start - side * leaves, ROWS)
        column = pl.multiple_of(side * (width // 2), width // 2)
        leave(
            grads.at[at, SPLIT + width :],
            leaf_hbm.at[pl.ds(start, ROWS), pl.ds(column, width // 2)],
        )
    return leaving


def finish_own_kernel(
    me_ref, chosen_ref, returned_ref, early_ref, late_ref,
    table_ref, leaf_hbm, in_hbm, out_hbm, grads, sems,
):
    leaving = write_chunks(
        me_ref[0], 0, early_ref, late_ref, leaf_hbm, in_hbm, out_hbm, grads, sems
    )
    parts = table_ref.shape[1] // BLOCK
    part_of = lax.broadcasted_iota(jnp.int32, chosen_ref.shape, 0) & (parts - 1)
    for part in range(parts):
        mine = jnp.where(part_of == part, chosen_ref[...].astype(f32), 0.0).astype(bf16)
        table_ref[:, part * BLOCK : (part + 1) * BLOCK] = mm_tn(mine, returned_ref[...])
    for copy in leaving:
        copy.wait()


def finish_other_kernel(
    me_ref, early_ref, late_ref, leaf_in, in_in, out_in, leaf_hbm, in_hbm, out_hbm, grads, sems
):
    leaving = write_chunks(
        me_ref[0], 1, early_ref, late_ref, leaf_hbm, in_hbm, out_hbm, grads, sems
    )
    for copy in leaving:
        copy.wait()


def finish_scratch(early, late):
    return [
        pltpu.VMEM((early.shape[0], early.shape[1] + late.shape[1]), f32),
        pltpu.SemaphoreType.DMA((3 * early.shape[0] // ROWS,)),
    ]


def run_finish(me, chosen, returned, early_own, early_other, late_own, late_other, leaves):
    smem = pl.BlockSpec(memory_space=pltpu.SMEM)
    vmem = pl.BlockSpec(memory_space=pltpu.VMEM)
    hbm = pl.BlockSpec(memory_space=pltpu.HBM)
    width = early_own.shape[1] // 4
    shapes = tuple(
        jax.ShapeDtypeStruct(shape, f32)
        for shape in (
            (chosen.shape[1], width), (leaves, width), (width, 4 * width), (width, width)
        )
    )
    table, *written = pl.pallas_call(
        finish_own_kernel,
        name="finish_own",
        out_shape=shapes,
        in_specs=[smem] + [vmem] * 4,
        out_specs=(vmem, hbm, hbm, hbm),
        scratch_shapes=finish_scratch(early_own, late_own),
        compiler_params=pltpu.CompilerParams(vmem_limit_bytes=16 * 2**20),
        cost_estimate=pl.CostEstimate(flops=10**8, bytes_accessed=5 * 10**6, transcendentals=0),
    )(me, chosen, returned, early_own, late_own)
    written = pl.pallas_call(
        finish_other_kernel,
        name="finish_other",
        out_shape=shapes[1:],
        in_specs=[smem] + [vmem] * 2 + [hbm] * 3,
        out_specs=(hbm,) * 3,
        scratch_shapes=finish_scratch(early_own, late_own),
        input_output_aliases={3: 0, 4: 1, 5: 2},
        compiler_params=pltpu.CompilerParams(vmem_limit_bytes=16 * 2**20),
        cost_estimate=pl.CostEstimate(flops=0, bytes_accessed=5 * 10**6, transcendentals=0),
    )(me, early_other, late_other, *written)
    return (table, *written)


def load_kernel(*refs):
    for source, target in zip(refs[: len(refs) // 2], refs[len(refs) // 2 :]):
        target[...] = source[...]


def run_load(*arrays):
    vmem = pl.BlockSpec(memory_space=pltpu.VMEM)
    return pl.pallas_call(
        load_kernel,
        name="load",
        out_shape=tuple(jax.ShapeDtypeStruct(array.shape, array.dtype) for array in arrays),
        in_specs=[vmem] * len(arrays),
        out_specs=(vmem,) * len(arrays),
        compiler_params=pltpu.CompilerParams(vmem_limit_bytes=8 * 2**20),
        cost_estimate=pl.CostEstimate(flops=0, bytes_accessed=4 * 2**20, transcendentals=0),
    )(*arrays)


def merge_kernel(keep_ref, other_ref, *outs):
    rows = outs[0].shape[0]
    for part, out in enumerate(outs):
        at = slice(part * rows, (part + 1) * rows)
        out[...] = (keep_ref[at, :].astype(f32) + other_ref[at, :].astype(f32)).astype(bf16)


def run_merge(keep, other, parts):
    vmem = pl.BlockSpec(memory_space=pltpu.VMEM)
    part = jax.ShapeDtypeStruct((keep.shape[0] // parts, keep.shape[1]), bf16)
    return pl.pallas_call(
        merge_kernel,
        name="merge",
        out_shape=(part,) * parts,
        in_specs=[vmem] * 2,
        out_specs=(vmem,) * parts,
        compiler_params=pltpu.CompilerParams(vmem_limit_bytes=8 * 2**20),
    )(keep, other)


def exchange(blocks):
    return lax.all_to_all(blocks, ("dp", "rep"), split_axis=0, concat_axis=0, tiled=True)


def swap(block, mask, count):
    return lax.ppermute(block, ("dp", "rep"), [(i, i ^ mask) for i in range(count)])


def add(parts):
    return sum(part.astype(f32) for part in parts)


def shares(parts, group):
    size = 2 ** len(group)
    rows = parts[0].shape[0] // size
    return [
        add(part[digit * rows : (digit + 1) * rows] for part in parts).astype(bf16)
        for digit in range(1, size)
    ]


def swap_all(blocks, group, count):
    return [
        swap(block, mask_of(group, digit), count) for digit, block in enumerate(blocks, start=1)
    ]


def extend(parts, got):
    return [part[: got[0].shape[0]] for part in parts] + got


def split_up(parts, group, count):
    return extend(parts, swap_all(shares(parts, group), group, count))


def sum_with(block, group, count):
    return block.astype(f32) + swap(block, mask_of(group, 1), count).astype(f32)


def join(block, group, count):
    pieces = swap_all([block] * (2 ** len(group) - 1), group, count)
    return jnp.concatenate([block] + pieces, axis=0)


def reduce_and_gather(early, late, d_rows, count):
    _, near, far = EARLY
    _, first, second = LATE
    early_other, late_other = swap(early[1], 1, count), swap(late[1], 1, count)
    early_own, late_own = run_load(early[0], late[0])
    early, *early_blocks = run_merge(early_own, early_other, 2 ** len(near))
    late, *late_blocks = run_merge(late_own, late_other, 2 ** len(first))
    early_blocks, late_blocks = lax.optimization_barrier((early_blocks, late_blocks))
    early_got = swap_all(early_blocks, near, count)
    late = [late] + swap_all(late_blocks, first, count)
    late_got = swap_all(shares(late, second), second, count)
    early_got[0], late, d_rows = lax.optimization_barrier((early_got[0], late, d_rows))
    returned = exchange(d_rows)
    early_got, late = lax.optimization_barrier((early_got, extend(late, late_got)))
    early, late = split_up([early] + early_got, far, count), add(late).astype(bf16)
    late = sum_with(late, SHARED[0], count).astype(bf16)
    early, late = add(early), sum_with(late, SHARED[1], count)
    reach = CHUNKS
    while reach < count:
        early, late = early + swap(early, reach, count), late + swap(late, reach, count)
        reach *= 2
    early, returned = lax.optimization_barrier(((early * (1.0 / count)).astype(bf16), returned))
    early = join(early, far, count)
    early, late = lax.optimization_barrier((early, (late * (1.0 / count)).astype(bf16)))
    pieces = swap_all([early] * (2 ** len(near) - 1), near, count)
    late = join(join(late, second, count), first, count)
    pieces, late = lax.optimization_barrier((pieces, late))
    early = jnp.concatenate([early] + pieces, axis=0)
    return returned, early, swap(early, 1, count), late, swap(late, 1, count)


def on_device(
    item_table, requests, event_slot, lengths, leaf_ids, leaf_table, w_in, w_out, cotangent
):
    count = lax.axis_size("dp") * lax.axis_size("rep")
    place = lax.axis_index(("dp", "rep")).astype(jnp.int32)
    me = (place & (CHUNKS - 1)).reshape(1)
    slot = event_slot.reshape(1, -1)
    leaf = leaf_ids.T
    asked = exchange(requests[0])
    (table,) = run_load(item_table)
    fetched, chosen = run_lookup(asked, table)
    arrived = exchange(fetched)
    output, d_rows, keep, send, keep_late, send_late = run_layer(
        me, lengths, slot, leaf, arrived, leaf_table, w_in, w_out, cotangent
    )
    returned, early, early_other, late, late_other = reduce_and_gather(
        (keep, send), (keep_late, send_late), d_rows, count
    )
    table_grad, leaf_mean, in_mean, out_mean = run_finish(
        me, chosen, returned, early, early_other, late, late_other, leaf_table.shape[0]
    )
    return (output, table_grad, leaf_mean, in_mean, out_mean)


def solution(mesh):
    return jax.shard_map(
        on_device,
        mesh=mesh,
        in_specs=(
            P(("dp", "rep"), None),
            P(("dp", "rep"), None, None),
            P(("dp", "rep")),
            P(("dp", "rep"), None),
            P(("dp", "rep"), None),
            P(),
            P(),
            P(),
            P(("dp", "rep"), None),
        ),
        out_specs=(P(("dp", "rep"), None), P(("dp", "rep"), None), P(), P(), P()),
        check_vma=False,
    )
```
